32 devices in a mesh: batch: 2 (over x), seq: 16 (over z, y, core).
Axes of the slice: x: 2, y: 2, z: 4, core: 2. Of those that a mesh axis runs over, the one named last changes fastest.
Arguments:
- tokens: bfloat16 [2, 8192, 1152], P('batch', 'seq'), may hold values from -6 to 6
- cotangent: bfloat16 [2, 8192, 1152], P('batch', 'seq'), may hold values from -6 to 6
- doc_ids: int32 [2, 8192], P('batch'), may hold values from 0 to 7, never falling along the last dimension, each value on 1 to 2048 neighbouring positions
- w_query: bfloat16 [1152, 1024], P(('batch', 'seq')), may hold values from -0.1875 to 0.1875
- w_key: bfloat16 [1152, 256], P(('batch', 'seq')), may hold values from -0.1875 to 0.1875
- w_value: bfloat16 [1152, 256], P(('batch', 'seq')), may hold values from -0.1875 to 0.1875
- w_out: bfloat16 [1024, 1152], P(('batch', 'seq')), may hold values from -0.1875 to 0.1875
- w_gate: bfloat16 [1152, 6912], P(('batch', 'seq')), may hold values from -0.1875 to 0.1875
- w_up: bfloat16 [1152, 6912], P(('batch', 'seq')), may hold values from -0.1875 to 0.1875
- w_down: bfloat16 [6912, 1152], P(('batch', 'seq')), may hold values from -0.078125 to 0.078125
- gain_attn_in: bfloat16 [1152], P(('batch', 'seq')), may hold values from 0.25 to 1.75
- gain_attn_out: bfloat16 [1152], P(('batch', 'seq')), may hold values from 0.25 to 1.75
- gain_mlp_in: bfloat16 [1152], P(('batch', 'seq')), may hold values from 0.25 to 1.75
- gain_mlp_out: bfloat16 [1152], P(('batch', 'seq')), may hold values from 0.25 to 1.75
- gain_query: bfloat16 [256], P(('batch', 'seq')), may hold values from 0.25 to 1.75
- gain_key: bfloat16 [256], P(('batch', 'seq')), may hold values from 0.25 to 1.75
Outputs:
- layer_out: bfloat16 [2, 8192, 1152], P('batch', 'seq')
- grad_tokens: bfloat16 [2, 8192, 1152], P('batch', 'seq')
- grad_w_query: float32 [1152, 1024], P(('batch', 'seq'))
- grad_w_key: float32 [1152, 256], P(('batch', 'seq'))
- grad_w_value: float32 [1152, 256], P(('batch', 'seq'))
- grad_w_out: float32 [1024, 1152], P(('batch', 'seq'))
- grad_w_gate: float32 [1152, 6912], P(('batch', 'seq'))
- grad_w_up: float32 [1152, 6912], P(('batch', 'seq'))
- grad_w_down: float32 [6912, 1152], P(('batch', 'seq'))
- grad_gain_attn_in: float32 [1152], P(('batch', 'seq'))
- grad_gain_attn_out: float32 [1152], P(('batch', 'seq'))
- grad_gain_mlp_in: float32 [1152], P(('batch', 'seq'))
- grad_gain_mlp_out: float32 [1152], P(('batch', 'seq'))
- grad_gain_query: float32 [256], P(('batch', 'seq'))
- grad_gain_key: float32 [256], P(('batch', 'seq'))
The draws below stay inside these ranges and needn't reach their ends.
Inputs may be any that keep to these rules, and one draw needn't show every extreme that they name: `doc_ids`: within each sequence the ids never fall; each of the 8 documents holds 1 to 2048 tokens, and one holds exactly 2048.
All inputs are finite; a program needn't handle non-finite values.
Results may differ from the reference program's by a relative error of at most 0.018.
Values may be sent and summed in bfloat16 or wider, within the bound.
No kernel may reach another device: no remote copies, remote signals or barrier semaphores. Data moves between devices by JAX's collectives and lax.ppermute only.
A program may use at most 384 MiB of HBM per device.

```python
import math
import jax
import jax.numpy as jnp
import numpy as np
from jax import lax

D = 1152
HEADS = 4
HEAD = 256
FF = 6912
WINDOW = 512
DOCS = 8
SEQS = 2
LENGTH = 8192


def level_of(stream_key, dims, split, least, high):
    loudness = 1.0
    for axis_at, parts in split:
        draws = jax.random.uniform(jax.random.fold_in(jax.random.fold_in(stream_key, 6), axis_at), (parts,), jnp.float32, least / len(split), high / len(split))
        loudness = loudness * jnp.repeat(jnp.exp(draws), dims[axis_at] // parts).reshape((-1,) + (1,) * (len(dims) - 1 - axis_at))
    return loudness


def length_profile(count, total, bound, skew):
    portions = [(1 << 20) // math.isqrt(rank ** skew) + 1 for rank in range(2, count + 1)]
    spare, counts = total - bound - (count - 1), [1] * (count - 1)
    while spare > 0:
        movable = [i for i in range(count - 1) if counts[i] < bound]
        pool, left = sum([portions[i] for i in movable]), spare
        for i in movable:
            addition = min(bound - counts[i], max(1, left * portions[i] // pool), spare)
            counts[i] = counts[i] + addition
            spare = spare - addition
    return np.array([bound] + counts)


def uneven_parts(key, count, total, most, lean):
    if count == 2:
        one = jax.random.randint(key, (), max(1, total - most), min(most, total - 1) + 1)
        return jnp.stack([one, total - one])
    tallies = jnp.asarray(length_profile(count, total, most, lean), jnp.int32)
    pairs = (count - 1) // 2
    giver, receiver = tallies[1:1 + 2 * pairs:2], tallies[2:2 + 2 * pairs:2]
    margin = jnp.minimum(giver - 1, most - receiver)
    shifted = jax.random.randint(jax.random.fold_in(key, 1), (pairs,), 0, 1 << 20) % (margin + 1)
    tallies = tallies.at[1:1 + 2 * pairs:2].set(giver - shifted).at[2:2 + 2 * pairs:2].set(receiver + shifted)
    return tallies[jax.random.permutation(jax.random.fold_in(key, 2), count)]


def bell_draw(key, dims, spread, most, cuts=(), kind=jnp.bfloat16):
    array = jax.random.normal(key, dims, jnp.float32) * spread
    if len(cuts) > 0:
        array = level_of(key, dims, cuts, -0.22, 0.18) * array
    return jnp.clip(array, min=-most, max=most).astype(kind)


def setup_inputs(seed: int = 0) -> dict:
    key_of = jax.random.split(jax.random.key(seed), 17)
    tokens = bell_draw(key_of[0], (SEQS, LENGTH, D), 1.0, 6.0, ((0, 2), (1, 16)))
    cotangent = bell_draw(key_of[1], (SEQS, LENGTH, D), 1.0, 6.0, ((0, 2), (1, 16)))
    doc_ids = jax.vmap(lambda own: jnp.searchsorted(jnp.cumsum(uneven_parts(own, DOCS, LENGTH, LENGTH // 4, 0)), jnp.arange(LENGTH), side="right"))(jax.random.split(key_of[2], SEQS)).reshape((SEQS, LENGTH)).astype(jnp.int32)
    w_query = bell_draw(key_of[3], (D, HEADS * HEAD), D ** -0.5, 0.1875, ((0, 32),))
    w_key = bell_draw(key_of[4], (D, HEAD), D ** -0.5, 0.1875, ((0, 32),))
    w_value = bell_draw(key_of[5], (D, HEAD), D ** -0.5, 0.1875, ((0, 32),))
    w_out = bell_draw(key_of[6], (HEADS * HEAD, D), (HEADS * HEAD) ** -0.5, 0.1875, ((0, 32),))
    w_gate = bell_draw(key_of[7], (D, FF), D ** -0.5, 0.1875, ((0, 32),))
    w_up = bell_draw(key_of[8], (D, FF), D ** -0.5, 0.1875, ((0, 32),))
    w_down = bell_draw(key_of[9], (FF, D), FF ** -0.5, 0.078125, ((0, 32),))
    gain_attn_in = jnp.clip(1.0 + 0.15 * jax.random.normal(key_of[10], (D,), jnp.float32), 0.25, 1.75).astype(jnp.bfloat16)
    gain_attn_out = jnp.clip(1.0 + 0.15 * jax.random.normal(key_of[11], (D,), jnp.float32), 0.25, 1.75).astype(jnp.bfloat16)
    gain_mlp_in = jnp.clip(1.0 + 0.15 * jax.random.normal(key_of[12], (D,), jnp.float32), 0.25, 1.75).astype(jnp.bfloat16)
    gain_mlp_out = jnp.clip(1.0 + 0.15 * jax.random.normal(key_of[13], (D,), jnp.float32), 0.25, 1.75).astype(jnp.bfloat16)
    gain_query = jnp.clip(1.0 + 0.15 * jax.random.normal(key_of[14], (HEAD,), jnp.float32), 0.25, 1.75).astype(jnp.bfloat16)
    gain_key = jnp.clip(1.0 + 0.15 * jax.random.normal(key_of[15], (HEAD,), jnp.float32), 0.25, 1.75).astype(jnp.bfloat16)
    return dict(tokens=tokens, cotangent=cotangent, doc_ids=doc_ids, w_query=w_query, w_key=w_key, w_value=w_value, w_out=w_out, w_gate=w_gate, w_up=w_up, w_down=w_down, gain_attn_in=gain_attn_in, gain_attn_out=gain_attn_out, gain_mlp_in=gain_mlp_in, gain_mlp_out=gain_mlp_out, gain_query=gain_query, gain_key=gain_key)


EPSILON = 1e-06
ROPE_BASE = 10000.0
HIGHEST = lax.Precision.HIGHEST

@jax.custom_vjp
def low(v):
    return lax.optimization_barrier(v.astype(jnp.bfloat16)).astype(jnp.float32)

@jax.custom_vjp
def low_back(v):
    return v

def low_keep(v):
    return (low(v), None)

def low_pass(kept, grad):
    return (grad,)

def back_keep(v):
    return (v, None)

def back_low(kept, grad):
    return (low(grad),)
low.defvjp(low_keep, low_pass)
low_back.defvjp(back_keep, back_low)

def norm_gain(values, gain_vec):
    return values * lax.rsqrt(lax.optimization_barrier(jnp.mean(values * values, axis=-1, keepdims=True)) + EPSILON) * gain_vec

def rotate(values, cosine_table, sine_table):
    half_size = values.shape[-1] // 2
    turned = jnp.concatenate([-values[..., half_size:], values[..., :half_size]], axis=-1)
    return values * cosine_table + turned * sine_table

def rope_tables(first_row, row_count, head_size):
    places = (first_row + jnp.arange(row_count, dtype=jnp.int32)).astype(jnp.float32)
    frequency = ROPE_BASE ** (-(jnp.arange(head_size // 2, dtype=jnp.float32) * 2.0) / head_size)
    angles = places[:, None] * frequency[None, :]
    angles = jnp.concatenate([angles, angles], axis=-1)
    return (jnp.cos(angles), jnp.sin(angles))

def product(left_side, right_side):
    return jnp.dot(left_side, right_side, precision=HIGHEST, preferred_element_type=jnp.float32)

def block_mask(query_ids, key_ids, window_rows):
    query_place = window_rows + jnp.arange(window_rows, dtype=jnp.int32)
    key_place = jnp.arange(2 * window_rows, dtype=jnp.int32)
    distance = query_place[:, None] - key_place[None, :]
    same_doc = query_ids[:, None] == key_ids[None, :]
    return (distance >= 0) & (distance < window_rows) & same_doc

def attend(queries, keys, values, ids_pad, window_rows, attn_scale):
    row_count, head_count, head_size = queries.shape
    key_pad = jnp.concatenate([jnp.zeros((window_rows, head_size), keys.dtype), keys])
    value_pad = jnp.concatenate([jnp.zeros((window_rows, head_size), values.dtype), values])

    def one_block(block_index):
        block_start = block_index * window_rows
        query_part = lax.dynamic_slice_in_dim(queries, block_start, window_rows, 0)
        key_part = lax.dynamic_slice_in_dim(key_pad, block_start, 2 * window_rows, 0)
        value_part = lax.dynamic_slice_in_dim(value_pad, block_start, 2 * window_rows, 0)
        query_ids = lax.dynamic_slice_in_dim(ids_pad, block_start + window_rows, window_rows, 0)
        key_ids = lax.dynamic_slice_in_dim(ids_pad, block_start, 2 * window_rows, 0)
        allowed = block_mask(query_ids, key_ids, window_rows)
        scores = low_back(jnp.einsum('qhd,kd->hqk', query_part, key_part, precision=HIGHEST) * attn_scale)
        scores = jnp.where(allowed[None], scores, -1e+30)
        probabilities = low(jax.nn.softmax(scores, axis=-1))
        return jnp.einsum('hqk,kd->qhd', probabilities, value_part, precision=HIGHEST)
    results = lax.map(jax.checkpoint(one_block), jnp.arange(row_count // window_rows, dtype=jnp.int32))
    return results.reshape(row_count, head_count * head_size)

def layer(layer_in, ids_pad, cosine_table, sine_table, w_query, w_key, w_value, w_out, w_gate, w_up, w_down, gain_attn_in, gain_attn_out, gain_mlp_in, gain_mlp_out, gain_query, gain_key):
    row_count = layer_in.shape[0]
    normed = low(norm_gain(layer_in, gain_attn_in))
    query_raw = low_back(product(normed, w_query)).reshape(row_count, HEADS, HEAD)
    key_raw = low_back(product(normed, w_key))
    value_raw = low_back(product(normed, w_value))
    queries = low(rotate(norm_gain(query_raw, gain_query), cosine_table[:, None, :], sine_table[:, None, :]))
    keys = low(rotate(norm_gain(key_raw, gain_key), cosine_table, sine_table))
    values = low(value_raw)
    attended = low(low_back(attend(queries, keys, values, ids_pad, WINDOW, HEAD ** (-0.5))))
    branch = low_back(product(attended, w_out))
    middle = layer_in + norm_gain(branch, gain_attn_out)
    normed_mlp = low(norm_gain(middle, gain_mlp_in))
    gate_raw = low_back(product(normed_mlp, w_gate))
    up_raw = low_back(product(normed_mlp, w_up))
    hidden = low(jax.nn.gelu(gate_raw, approximate=True) * up_raw)
    mixed = low_back(product(hidden, w_down))
    return middle + norm_gain(mixed, gain_mlp_out)

def reference(tokens, cotangent, doc_ids, w_query, w_key, w_value, w_out, w_gate, w_up, w_down, gain_attn_in, gain_attn_out, gain_mlp_in, gain_mlp_out, gain_query, gain_key):
    params = tuple((member.astype(jnp.float32) for member in (w_query, w_key, w_value, w_out, w_gate, w_up, w_down, gain_attn_in, gain_attn_out, gain_mlp_in, gain_mlp_out, gain_query, gain_key)))
    cosine_table, sine_table = rope_tables(0, LENGTH, HEAD)

    def per_sequence(totals, item):
        sequence_in, sequence_grad, sequence_ids = item
        ids_pad = jnp.concatenate([jnp.full((WINDOW,), -1, jnp.int32), sequence_ids.astype(jnp.int32)])

        def forward(layer_in, *weight_list):
            return layer(layer_in, ids_pad, cosine_table, sine_table, *weight_list)
        layer_out, pullback = jax.vjp(forward, sequence_in.astype(jnp.float32), *params)
        grads = pullback(sequence_grad.astype(jnp.float32))
        totals = tuple((running + addend for running, addend in zip(totals, grads[1:])))
        return (totals, (layer_out.astype(jnp.bfloat16), grads[0].astype(jnp.bfloat16)))
    start_totals = tuple((jnp.zeros_like(member) for member in params))
    totals, (layer_outs, grad_ins) = lax.scan(per_sequence, start_totals, (tokens, cotangent, doc_ids))
    return (layer_outs, grad_ins, totals[0], totals[1], totals[2], totals[3], totals[4], totals[5], totals[6], totals[7], totals[8], totals[9], totals[10], totals[11], totals[12])
```

```python
import jax
import jax.numpy as jnp
from jax import lax
from jax.sharding import Mesh
from jax.sharding import PartitionSpec as P

HEAD = 256
WINDOW = 512
EPSILON = 1e-06
ROPE_BASE = 10000.0
ALL = ("x", "g", "y", "c")
PLANE = ("x", "y", "c")
BF = jnp.bfloat16
F32 = jnp.float32


def norm_gain(values, gain_vec):
    return (
        values * lax.rsqrt(jnp.mean(values * values, axis=-1, keepdims=True) + EPSILON) * gain_vec
    )


def rotate(values, cosine_table, sine_table):
    half_size = values.shape[-1] // 2
    turned = jnp.concatenate([-values[..., half_size:], values[..., :half_size]], axis=-1)
    return values * cosine_table + turned * sine_table


def rope_tables(first_row, row_count, head_size):
    places = (first_row + jnp.arange(row_count, dtype=jnp.int32)).astype(F32)
    frequency = ROPE_BASE ** (-(jnp.arange(head_size // 2, dtype=F32) * 2.0) / head_size)
    angles = places[:, None] * frequency[None, :]
    angles = jnp.concatenate([angles, angles], axis=-1)
    return (jnp.cos(angles), jnp.sin(angles))


def prepare_query(raw_value, gain_vec, cosine_table, sine_table):
    split_heads = raw_value.reshape(raw_value.shape[0], -1, gain_vec.shape[0])
    return rotate(
        norm_gain(split_heads, gain_vec), cosine_table[:, None, :], sine_table[:, None, :]
    )


def prepare_key(raw_value, gain_vec, cosine_table, sine_table):
    return rotate(norm_gain(raw_value, gain_vec), cosine_table, sine_table)


def matmul(left_side, right_side):
    return jnp.dot(left_side, right_side, preferred_element_type=F32)


def over_rows(left_side, right_side):
    return lax.dot_general(
        left_side, right_side, (((0,), (0,)), ((), ())), preferred_element_type=F32
    )


def by_transpose(left_side, right_side):
    return lax.dot_general(
        left_side, right_side, (((1,), (1,)), ((), ())), preferred_element_type=F32
    )


def block_mask(ids_pad, rows):
    query_place = rows + jnp.arange(rows, dtype=jnp.int32)
    key_place = jnp.arange(2 * rows, dtype=jnp.int32)
    distance = query_place[:, None] - key_place[None, :]
    same_doc = ids_pad[rows:][:, None] == ids_pad[None, :]
    return (distance >= 0) & (distance < WINDOW) & same_doc


def attend_forward(queries, key_pad, value_pad, allowed, attn_scale):
    row_count, head_count, head_size = queries.shape
    scores = jnp.einsum("qhd,kd->hqk", queries, key_pad, preferred_element_type=F32) * attn_scale
    scores = jnp.where(allowed[None], scores, -1e30)
    row_max = jnp.max(scores, axis=-1, keepdims=True)
    weights = jnp.exp(scores - row_max)
    row_total = jnp.sum(weights, axis=-1, keepdims=True)
    probabilities = (weights / row_total).astype(BF)
    attended = jnp.einsum("hqk,kd->qhd", probabilities, value_pad, preferred_element_type=F32)
    return (
        attended.reshape(row_count, head_count * head_size),
        (row_max + jnp.log(row_total))[..., 0],
    )


def attend_backward(queries, key_pad, value_pad, allowed, log_total, grad_attended, attn_scale):
    row_count, head_count, head_size = queries.shape
    grad_part = grad_attended.reshape(row_count, head_count, head_size)
    scores = jnp.einsum("qhd,kd->hqk", queries, key_pad, preferred_element_type=F32) * attn_scale
    probabilities = jnp.where(allowed[None], jnp.exp(scores - log_total[..., None]), 0.0)
    grad_prob = jnp.einsum("qhd,kd->hqk", grad_part, value_pad, preferred_element_type=F32)
    inner_sum = jnp.sum(probabilities * grad_prob, axis=-1, keepdims=True)
    grad_score = (probabilities * (grad_prob - inner_sum)).astype(BF)
    grad_query = (
        jnp.einsum("hqk,kd->qhd", grad_score, key_pad, preferred_element_type=F32) * attn_scale
    )
    grad_key = (
        jnp.einsum("hqk,qhd->kd", grad_score, queries, preferred_element_type=F32) * attn_scale
    )
    grad_value = jnp.einsum(
        "hqk,qhd->kd", probabilities.astype(BF), grad_part, preferred_element_type=F32
    )
    return (grad_query, grad_key, grad_value)


def swap(array, axis):
    return lax.ppermute(array, axis, [(0, 1), (1, 0)])


def plane_gather(own):
    half = own.shape[0] // 2
    from_x = swap(own, "x")
    from_y = swap(own, "y")
    far_top = swap(from_x[:half], "y")
    far_low = swap(from_y[half:], "x")
    mine = jnp.concatenate([own, from_x, from_y, far_top, far_low])
    return jnp.concatenate([mine, swap(mine, "c")])


def plane_reduce(parts):
    rows = parts.shape[0] // 8
    half = rows // 2
    mine = parts[: 4 * rows].astype(F32) + swap(parts[4 * rows :].astype(BF), "c").astype(F32)
    own, to_x, to_y, far = (mine[i * rows : (i + 1) * rows] for i in range(4))
    far = far.astype(BF)
    top = swap(far[:half], "y").astype(F32)
    low = swap(far[half:], "x").astype(F32)
    to_x = jnp.concatenate([to_x[:half] + top, to_x[half:]]).astype(BF)
    to_y = jnp.concatenate([to_y[:half], to_y[half:] + low]).astype(BF)
    return own + swap(to_x, "x").astype(F32) + swap(to_y, "y").astype(F32)


def on_device(
    tokens,
    cotangent,
    doc_ids,
    w_query,
    w_key,
    w_value,
    w_out,
    w_gate,
    w_up,
    w_down,
    gain_attn_in,
    gain_attn_out,
    gain_mlp_in,
    gain_mlp_out,
    gain_query,
    gain_key,
):
    row_count = tokens.shape[1]
    width = tokens.shape[2]
    devices = lax.axis_size(ALL)
    groups = lax.axis_size("g")
    members = lax.axis_size(PLANE)
    shard_rows = w_query.shape[0]
    head_rows = gain_query.shape[0]
    hidden_all = w_gate.shape[1]
    hidden_own = hidden_all // members
    piece = hidden_own // groups
    q_cols, k_cols = w_query.shape[1], w_key.shape[1]
    qkv_cols = q_cols + 2 * k_cols
    attn_scale = HEAD ** (-0.5)

    def gain_columns(d_gains, h_gains):
        columns = list(d_gains) + [
            jnp.pad(h, ((0, 0), (0, shard_rows - head_rows))) for h in h_gains
        ]
        block = jnp.stack(columns, axis=-1)
        return jnp.pad(block, ((0, 0), (0, 0), (0, 128 - len(columns))))

    gains = gain_columns(
        [g[None] for g in (gain_attn_in, gain_attn_out, gain_mlp_in, gain_mlp_out)],
        [gain_query[None], gain_key[None]],
    )
    packed = jnp.concatenate([w_query, w_key, w_value, gains[0]], axis=1)
    packed = lax.all_gather(packed, ALL, axis=0)
    w_o = lax.all_gather(w_out, ALL, axis=0, tiled=True)
    gain_block = packed[:, :, qkv_cols:].astype(F32)
    d_gains = gain_block[:, :, :4].reshape(width, 4).T
    g_attn_in, g_attn_out, g_mlp_in, g_mlp_out = (d_gains[i : i + 1] for i in range(4))
    g_query = gain_block[:, :head_rows, 4].reshape(HEAD)
    g_key = gain_block[:, :head_rows, 5].reshape(HEAD)
    w_qkv = packed[:, :, :qkv_cols].reshape(width, qkv_cols)

    down = lax.all_gather(w_down, "g", axis=0, tiled=True)

    def spread(weight):
        cut = weight.reshape(shard_rows, 2, groups, members // 2, piece)
        return cut.transpose(1, 3, 0, 2, 4).reshape(members, shard_rows, hidden_own)

    sent = jnp.stack([spread(w_gate), spread(w_up)], axis=1)
    sent = lax.all_to_all(sent, PLANE, split_axis=0, concat_axis=0, tiled=True)
    sent = sent.transpose(1, 0, 2, 3).reshape(2, members * shard_rows, hidden_own)
    both = lax.all_gather(sent, "g", axis=0)
    both = both.reshape(groups, 2, 2, members // 2 * shard_rows, hidden_own)
    gate = both[:, 0].transpose(1, 0, 2, 3).reshape(width, hidden_own)
    up = both[:, 1].transpose(1, 0, 2, 3).reshape(width, hidden_own)

    seq_place = lax.axis_index(("g", "y", "c"))
    seq_size = lax.axis_size(("g", "y", "c"))
    first_row = seq_place * row_count
    ids_all = doc_ids[0]
    ids_own = lax.dynamic_slice_in_dim(ids_all, first_row, row_count, 0)
    ids_prev = lax.dynamic_slice_in_dim(
        ids_all, jnp.maximum(first_row - row_count, 0), row_count, 0
    )
    ids_prev = jnp.where(seq_place > 0, ids_prev, -1)
    ids_pad = jnp.concatenate([ids_prev, ids_own])
    allowed = block_mask(ids_pad, row_count)
    cosine_table, sine_table = rope_tables(first_row, row_count, HEAD)
    layer_in = tokens[0].astype(F32)
    grad_out = cotangent[0].astype(F32)

    normed = norm_gain(layer_in, g_attn_in).astype(BF)
    qkv_raw = matmul(normed, w_qkv)
    query_raw = qkv_raw[:, :q_cols]
    key_raw = qkv_raw[:, q_cols : q_cols + k_cols]
    queries = prepare_query(query_raw, g_query, cosine_table, sine_table).astype(BF)
    keys = prepare_key(key_raw, g_key, cosine_table, sine_table).astype(BF)
    values = qkv_raw[:, q_cols + k_cols :].astype(BF)
    key_value = jnp.concatenate([keys, values], axis=1)
    halo = lax.ppermute(key_value, ("g", "y", "c"), [(i, i + 1) for i in range(seq_size - 1)])
    key_pad = jnp.concatenate([halo[:, :k_cols], keys])
    value_pad = jnp.concatenate([halo[:, k_cols:], values])
    attended, log_total = attend_forward(queries, key_pad, value_pad, allowed, attn_scale)
    attended = attended.astype(BF)
    branch = matmul(attended, w_o)
    middle = layer_in + norm_gain(branch, g_attn_out)
    normed_mlp = norm_gain(middle, g_mlp_in).astype(BF)

    normed_all = plane_gather(normed_mlp)
    gate_raw = matmul(normed_all, gate)
    up_raw = matmul(normed_all, up)
    gelu, gelu_pull = jax.vjp(lambda u: jax.nn.gelu(u, approximate=True), gate_raw)
    hidden = (gelu * up_raw).astype(BF)
    slope = gelu_pull(up_raw)[0].astype(BF)
    gelu = gelu.astype(BF)
    mixed = plane_reduce(matmul(hidden, down))
    layer_out = middle + norm_gain(mixed, g_mlp_out)

    _, pullback = jax.vjp(norm_gain, mixed, g_mlp_out)
    grad_mixed, grad_gain_mlp_out = pullback(grad_out)
    grad_mixed_all = plane_gather(grad_mixed.astype(BF))
    grad_down = over_rows(hidden, grad_mixed_all).astype(BF)
    grad_down = lax.psum_scatter(grad_down, "g", scatter_dimension=0, tiled=True)
    grad_hidden = by_transpose(grad_mixed_all, down)
    grad_gate = (grad_hidden * slope.astype(F32)).astype(BF)
    grad_up = (grad_hidden * gelu.astype(F32)).astype(BF)

    def collect(term):
        term = term.astype(BF).reshape(2, groups, members // 2 * shard_rows, hidden_own)
        term = term.transpose(1, 0, 2, 3).reshape(groups * members * shard_rows, hidden_own)
        term = lax.psum_scatter(term, "g", scatter_dimension=0, tiled=True)
        term = term.reshape(members, shard_rows, hidden_own)
        term = lax.all_to_all(term, PLANE, split_axis=0, concat_axis=0, tiled=True)
        term = term.reshape(2, members // 2, shard_rows, groups, piece)
        return term.transpose(2, 0, 3, 1, 4).reshape(shard_rows, hidden_all).astype(F32)

    grad_w_gate = collect(over_rows(normed_all, grad_gate))
    grad_w_up = collect(over_rows(normed_all, grad_up))
    grad_normed_mlp = plane_reduce(by_transpose(grad_gate, gate) + by_transpose(grad_up, up))
    _, pullback = jax.vjp(norm_gain, middle, g_mlp_in)
    grad_from_mlp, grad_gain_mlp_in = pullback(grad_normed_mlp)
    grad_middle = grad_out + grad_from_mlp

    _, pullback = jax.vjp(norm_gain, branch, g_attn_out)
    grad_branch, grad_gain_attn_out = pullback(grad_middle)
    grad_branch = grad_branch.astype(BF)
    grad_w_out = lax.psum_scatter(
        over_rows(attended, grad_branch).astype(BF), ALL, scatter_dimension=0, tiled=True
    )
    grad_attended = by_transpose(grad_branch, w_o).astype(BF)
    grad_queries, grad_key_pad, grad_value_pad = attend_backward(
        queries, key_pad, value_pad, allowed, log_total, grad_attended, attn_scale
    )
    returned = lax.ppermute(
        jnp.concatenate([grad_key_pad[:row_count], grad_value_pad[:row_count]], axis=1).astype(BF),
        ("g", "y", "c"),
        [(i + 1, i) for i in range(seq_size - 1)],
    ).astype(F32)
    grad_keys = grad_key_pad[row_count:] + returned[:, :k_cols]
    grad_values = grad_value_pad[row_count:] + returned[:, k_cols:]
    _, pullback = jax.vjp(
        lambda raw, gain: prepare_key(raw, gain, cosine_table, sine_table), key_raw, g_key
    )
    grad_key_raw, grad_gain_key = pullback(grad_keys)
    _, pullback = jax.vjp(
        lambda raw, gain: prepare_query(raw, gain, cosine_table, sine_table), query_raw, g_query
    )
    grad_query_raw, grad_gain_query = pullback(grad_queries)
    grad_qkv_raw = jnp.concatenate([grad_query_raw, grad_key_raw, grad_values], axis=1).astype(BF)
    grad_w_qkv = over_rows(normed, grad_qkv_raw).astype(BF)
    grad_normed = by_transpose(grad_qkv_raw, w_qkv)
    _, pullback = jax.vjp(norm_gain, layer_in, g_attn_in)
    grad_from_attn, grad_gain_attn_in = pullback(grad_normed)
    grad_in = grad_middle + grad_from_attn

    terms = gain_columns(
        [
            g.reshape(devices, shard_rows)
            for g in (grad_gain_attn_in, grad_gain_attn_out, grad_gain_mlp_in, grad_gain_mlp_out)
        ],
        [g.reshape(devices, head_rows) for g in (grad_gain_query, grad_gain_key)],
    ).astype(BF)
    terms = jnp.concatenate([grad_w_qkv.reshape(devices, shard_rows, qkv_cols), terms], axis=2)
    share = lax.psum_scatter(terms, ALL, scatter_dimension=0, tiled=True)[0].astype(F32)
    return (
        layer_out.astype(BF)[None],
        grad_in.astype(BF)[None],
        share[:, :q_cols],
        share[:, q_cols : q_cols + k_cols],
        share[:, q_cols + k_cols : qkv_cols],
        grad_w_out.astype(F32),
        grad_w_gate,
        grad_w_up,
        grad_down.astype(F32),
        share[:, qkv_cols],
        share[:, qkv_cols + 1],
        share[:, qkv_cols + 2],
        share[:, qkv_cols + 3],
        share[:head_rows, qkv_cols + 4],
        share[:head_rows, qkv_cols + 5],
    )


def solution(mesh):
    batch, seq = mesh.devices.shape
    fine = Mesh(mesh.devices.reshape(batch, seq // 4, 2, 2), ALL)
    rows = ("g", "y", "c")
    return jax.shard_map(
        on_device,
        mesh=fine,
        in_specs=(P("x", rows, None),) * 2
        + (P("x", None),)
        + (P(ALL, None),) * 7
        + (P(ALL),) * 6,
        out_specs=(P("x", rows, None),) * 2 + (P(ALL, None),) * 7 + (P(ALL),) * 6,
        check_vma=False,
    )
```

```python
import jax
import jax.numpy as jnp
from jax import lax
from jax.sharding import Mesh
from jax.sharding import PartitionSpec as P

HEAD = 256
WINDOW = 512
EPSILON = 1e-06
ROPE_BASE = 10000.0
ALL = ("x", "g", "y", "c")
PLANE = ("x", "y", "c")
BF = jnp.bfloat16
F32 = jnp.float32


def norm_gain(values, gain_vec):
    return (
        values * lax.rsqrt(jnp.mean(values * values, axis=-1, keepdims=True) + EPSILON) * gain_vec
    )


def rotate(values, cosine_table, sine_table):
    half_size = values.shape[-1] // 2
    turned = jnp.concatenate([-values[..., half_size:], values[..., :half_size]], axis=-1)
    return values * cosine_table + turned * sine_table


def rope_tables(first_row, row_count, head_size):
    places = (first_row + jnp.arange(row_count, dtype=jnp.int32)).astype(F32)
    frequency = ROPE_BASE ** (-(jnp.arange(head_size // 2, dtype=F32) * 2.0) / head_size)
    angles = places[:, None] * frequency[None, :]
    angles = jnp.concatenate([angles, angles], axis=-1)
    return (jnp.cos(angles), jnp.sin(angles))


def prepare_query(raw_value, gain_vec, cosine_table, sine_table):
    split_heads = raw_value.reshape(raw_value.shape[0], -1, gain_vec.shape[0])
    return rotate(
        norm_gain(split_heads, gain_vec), cosine_table[:, None, :], sine_table[:, None, :]
    )


def prepare_key(raw_value, gain_vec, cosine_table, sine_table):
    return rotate(norm_gain(raw_value, gain_vec), cosine_table, sine_table)


def matmul(left_side, right_side):
    return jnp.dot(left_side, right_side, preferred_element_type=F32)


def over_rows(left_side, right_side):
    return lax.dot_general(
        left_side, right_side, (((0,), (0,)), ((), ())), preferred_element_type=F32
    )


def by_transpose(left_side, right_side):
    return lax.dot_general(
        left_side, right_side, (((1,), (1,)), ((), ())), preferred_element_type=F32
    )


def block_mask(ids_pad, rows):
    query_place = rows + jnp.arange(rows, dtype=jnp.int32)
    key_place = jnp.arange(2 * rows, dtype=jnp.int32)
    distance = query_place[:, None] - key_place[None, :]
    same_doc = ids_pad[rows:][:, None] == ids_pad[None, :]
    return (distance >= 0) & (distance < WINDOW) & same_doc


def attend_forward(queries, key_pad, value_pad, allowed, attn_scale):
    row_count, head_count, head_size = queries.shape
    scores = jnp.einsum("qhd,kd->hqk", queries, key_pad, preferred_element_type=F32) * attn_scale
    scores = jnp.where(allowed[None], scores, -1e30)
    row_max = jnp.max(scores, axis=-1, keepdims=True)
    weights = jnp.exp(scores - row_max)
    row_total = jnp.sum(weights, axis=-1, keepdims=True)
    probabilities = (weights / row_total).astype(BF)
    attended = jnp.einsum("hqk,kd->qhd", probabilities, value_pad, preferred_element_type=F32)
    return (
        attended.reshape(row_count, head_count * head_size),
        (row_max + jnp.log(row_total))[..., 0],
    )


def attend_backward(queries, key_pad, value_pad, allowed, log_total, grad_attended, attn_scale):
    row_count, head_count, head_size = queries.shape
    grad_part = grad_attended.reshape(row_count, head_count, head_size)
    scores = jnp.einsum("qhd,kd->hqk", queries, key_pad, preferred_element_type=F32) * attn_scale
    probabilities = jnp.where(allowed[None], jnp.exp(scores - log_total[..., None]), 0.0)
    grad_prob = jnp.einsum("qhd,kd->hqk", grad_part, value_pad, preferred_element_type=F32)
    inner_sum = jnp.sum(probabilities * grad_prob, axis=-1, keepdims=True)
    grad_score = (probabilities * (grad_prob - inner_sum)).astype(BF)
    grad_query = (
        jnp.einsum("hqk,kd->qhd", grad_score, key_pad, preferred_element_type=F32) * attn_scale
    )
    grad_key = (
        jnp.einsum("hqk,qhd->kd", grad_score, queries, preferred_element_type=F32) * attn_scale
    )
    grad_value = jnp.einsum(
        "hqk,qhd->kd", probabilities.astype(BF), grad_part, preferred_element_type=F32
    )
    return (grad_query, grad_key, grad_value)


def swap(array, axis):
    return lax.ppermute(array, axis, [(0, 1), (1, 0)])


def plane_gather(own):
    half = own.shape[0] // 2
    from_x = swap(own, "x")
    from_y = swap(own, "y")
    far_top = swap(from_x[:half], "y")
    far_low = swap(from_y[half:], "x")
    mine = jnp.concatenate([own, from_x, from_y, far_top, far_low])
    return jnp.concatenate([mine, swap(mine, "c")])


def plane_reduce(parts):
    rows = parts.shape[0] // 8
    half = rows // 2
    mine = parts[: 4 * rows].astype(F32) + swap(parts[4 * rows :].astype(BF), "c").astype(F32)
    own, to_x, to_y, far = (mine[i * rows : (i + 1) * rows] for i in range(4))
    far = far.astype(BF)
    top = swap(far[:half], "y").astype(F32)
    low = swap(far[half:], "x").astype(F32)
    to_x = jnp.concatenate([to_x[:half] + top, to_x[half:]]).astype(BF)
    to_y = jnp.concatenate([to_y[:half], to_y[half:] + low]).astype(BF)
    return own + swap(to_x, "x").astype(F32) + swap(to_y, "y").astype(F32)


def in_order(own, other, place):
    both = jnp.concatenate([own[None], other[None], own[None]])
    return lax.dynamic_slice_in_dim(both, place, 2, 0)


def group_gather(own):
    size = lax.axis_size("g")
    parts = [own] + [
        lax.ppermute(own, "g", [((i + k) % size, i) for i in range(size)]) for k in range(1, size)
    ]
    both = jnp.stack(parts + parts[:-1])
    place = lax.axis_index("g")
    return lax.dynamic_slice_in_dim(both, lax.rem(size - place, size), size, 0)


def plane_weights(blocks):
    x, y = lax.axis_index("x"), lax.axis_index("y")
    half = blocks.shape[0] // 2
    first, second = blocks[:half], blocks[half:]
    first = in_order(first, swap(first, "x"), x)
    second = in_order(second, swap(second, "y"), y)
    first = in_order(first, swap(first, "y"), y)
    second = in_order(second, swap(second, "x"), x)
    first = first.transpose(1, 2, 0, 3, 4)
    second = second.transpose(0, 2, 1, 3, 4)
    return jnp.concatenate([first, second], axis=1)


def fold(term, axis, dim):
    place = lax.axis_index(axis)
    mine = lax.dynamic_index_in_dim(term, place, dim, keepdims=False)
    other = lax.dynamic_index_in_dim(term, 1 - place, dim, keepdims=False)
    return (mine.astype(F32) + swap(other.astype(BF), axis).astype(F32)).astype(BF)


def plane_terms(term):
    half = term.shape[1] // 2
    first = fold(fold(term[:, :half], "x", 0), "y", 1)
    second = fold(fold(term[:, half:], "y", 2), "x", 0)
    term = jnp.concatenate([first, second])
    term = term.reshape(-1, term.shape[-1])
    return lax.psum_scatter(term, "g", scatter_dimension=0, tiled=True)


def on_device(
    tokens,
    cotangent,
    doc_ids,
    w_query,
    w_key,
    w_value,
    w_out,
    w_gate,
    w_up,
    w_down,
    gain_attn_in,
    gain_attn_out,
    gain_mlp_in,
    gain_mlp_out,
    gain_query,
    gain_key,
):
    row_count = tokens.shape[1]
    width = tokens.shape[2]
    devices = lax.axis_size(ALL)
    groups = lax.axis_size("g")
    members = lax.axis_size(PLANE)
    shard_rows = w_query.shape[0]
    head_rows = gain_query.shape[0]
    hidden_all = w_gate.shape[1]
    hidden_own = hidden_all // members
    piece = hidden_own // groups
    q_cols, k_cols = w_query.shape[1], w_key.shape[1]
    attn_scale = HEAD ** (-0.5)

    def gain_columns(d_gains, h_gains):
        columns = list(d_gains) + [
            jnp.pad(h, ((0, 0), (0, shard_rows - head_rows))) for h in h_gains
        ]
        block = jnp.stack(columns, axis=-1)
        return jnp.pad(block, ((0, 0), (0, 0), (0, 128 - len(columns))))

    core = lax.axis_index("c")
    half_cols = q_cols // 2 + k_cols + 128
    gains = gain_columns(
        [g[None] for g in (gain_attn_in, gain_attn_out, gain_mlp_in, gain_mlp_out)],
        [gain_query[None], gain_key[None]],
    )
    halves = jnp.stack(
        [
            jnp.concatenate([w_query[:, : q_cols // 2], w_key, gains[0]], axis=1),
            jnp.concatenate([w_query[:, q_cols // 2 :], w_value, jnp.zeros_like(gains[0])], axis=1),
        ]
    )
    mine = lax.dynamic_index_in_dim(halves, core, 0, keepdims=False)
    other = lax.dynamic_index_in_dim(halves, 1 - core, 0, keepdims=False)
    mine = in_order(mine, swap(other, "c"), core).reshape(2 * shard_rows, half_cols)
    mine = plane_weights(group_gather(mine)).reshape(width, half_cols)
    w_first, w_second = in_order(mine, swap(mine, "c"), core)
    gain_block = w_first[:, q_cols // 2 + k_cols :].astype(F32)
    d_gains = gain_block[:, :4].T
    g_attn_in, g_attn_out, g_mlp_in, g_mlp_out = (d_gains[i : i + 1] for i in range(4))
    h_gains = gain_block[:, 4:6].reshape(devices, shard_rows, 2)[:, :head_rows]
    g_query = h_gains[:, :, 0].reshape(HEAD)
    g_key = h_gains[:, :, 1].reshape(HEAD)
    w_first = w_first[:, : q_cols // 2 + k_cols]
    w_second = w_second[:, : q_cols // 2 + k_cols]

    down = lax.all_gather(jnp.concatenate([w_down, w_out]), "g", axis=0)
    w_o = plane_weights(down[:, w_down.shape[0] :])
    down = down[:, : w_down.shape[0]].reshape(-1, width)
    w_o = in_order(w_o, swap(w_o, "c"), core).transpose(1, 2, 3, 0, 4, 5).reshape(q_cols, width)

    def spread(weight):
        cut = weight.reshape(shard_rows, 2, groups, members // 2, piece)
        return cut.transpose(1, 3, 0, 2, 4).reshape(members, shard_rows, hidden_own)

    sent = jnp.stack([spread(w_gate), spread(w_up)], axis=1)
    sent = lax.all_to_all(sent, PLANE, split_axis=0, concat_axis=0, tiled=True)
    sent = sent.transpose(1, 0, 2, 3).reshape(2, members * shard_rows, hidden_own)
    both = lax.all_gather(sent, "g", axis=0)
    both = both.reshape(groups, 2, 2, members // 2 * shard_rows, hidden_own)
    gate = both[:, 0].transpose(1, 0, 2, 3).reshape(width, hidden_own)
    up = both[:, 1].transpose(1, 0, 2, 3).reshape(width, hidden_own)

    seq_place = lax.axis_index(("g", "y", "c"))
    seq_size = lax.axis_size(("g", "y", "c"))
    first_row = seq_place * row_count
    ids_all = doc_ids[0]
    ids_own = lax.dynamic_slice_in_dim(ids_all, first_row, row_count, 0)
    ids_prev = lax.dynamic_slice_in_dim(
        ids_all, jnp.maximum(first_row - row_count, 0), row_count, 0
    )
    ids_prev = jnp.where(seq_place > 0, ids_prev, -1)
    ids_pad = jnp.concatenate([ids_prev, ids_own])
    allowed = block_mask(ids_pad, row_count)
    cosine_table, sine_table = rope_tables(first_row, row_count, HEAD)
    layer_in = tokens[0].astype(F32)
    grad_out = cotangent[0].astype(F32)

    normed = norm_gain(layer_in, g_attn_in).astype(BF)
    raw_first = matmul(normed, w_first)
    raw_second = matmul(normed, w_second)
    query_raw = jnp.concatenate([raw_first[:, : q_cols // 2], raw_second[:, : q_cols // 2]], axis=1)
    key_raw = raw_first[:, q_cols // 2 :]
    queries = prepare_query(query_raw, g_query, cosine_table, sine_table).astype(BF)
    keys = prepare_key(key_raw, g_key, cosine_table, sine_table).astype(BF)
    values = raw_second[:, q_cols // 2 :].astype(BF)
    key_value = jnp.concatenate([keys, values], axis=1)
    halo = lax.ppermute(key_value, ("g", "y", "c"), [(i, i + 1) for i in range(seq_size - 1)])
    key_pad = jnp.concatenate([halo[:, :k_cols], keys])
    value_pad = jnp.concatenate([halo[:, k_cols:], values])
    attended, log_total = attend_forward(queries, key_pad, value_pad, allowed, attn_scale)
    attended = attended.astype(BF)
    branch = matmul(attended, w_o)
    middle = layer_in + norm_gain(branch, g_attn_out)
    normed_mlp = norm_gain(middle, g_mlp_in).astype(BF)

    normed_all = plane_gather(normed_mlp)
    gate_raw = matmul(normed_all, gate)
    up_raw = matmul(normed_all, up)
    gelu, gelu_pull = jax.vjp(lambda u: jax.nn.gelu(u, approximate=True), gate_raw)
    hidden = (gelu * up_raw).astype(BF)
    slope = gelu_pull(up_raw)[0].astype(BF)
    gelu = gelu.astype(BF)
    mixed = plane_reduce(matmul(hidden, down))
    layer_out = middle + norm_gain(mixed, g_mlp_out)

    _, pullback = jax.vjp(norm_gain, mixed, g_mlp_out)
    grad_mixed, grad_gain_mlp_out = pullback(grad_out)
    grad_mixed_all = plane_gather(grad_mixed.astype(BF))
    grad_down = over_rows(hidden, grad_mixed_all).astype(BF)
    grad_down = lax.psum_scatter(grad_down, "g", scatter_dimension=0, tiled=True)
    grad_hidden = by_transpose(grad_mixed_all, down)
    grad_gate = (grad_hidden * slope.astype(F32)).astype(BF)
    grad_up = (grad_hidden * gelu.astype(F32)).astype(BF)

    def collect(term):
        term = term.astype(BF).reshape(2, groups, members // 2 * shard_rows, hidden_own)
        term = term.transpose(1, 0, 2, 3).reshape(groups * members * shard_rows, hidden_own)
        term = lax.psum_scatter(term, "g", scatter_dimension=0, tiled=True)
        term = term.reshape(members, shard_rows, hidden_own)
        term = lax.all_to_all(term, PLANE, split_axis=0, concat_axis=0, tiled=True)
        term = term.reshape(2, members // 2, shard_rows, groups, piece)
        return term.transpose(2, 0, 3, 1, 4).reshape(shard_rows, hidden_all).astype(F32)

    grad_w_gate = collect(over_rows(normed_all, grad_gate))
    grad_w_up = collect(over_rows(normed_all, grad_up))
    grad_normed_mlp = plane_reduce(by_transpose(grad_gate, gate) + by_transpose(grad_up, up))
    _, pullback = jax.vjp(norm_gain, middle, g_mlp_in)
    grad_from_mlp, grad_gain_mlp_in = pullback(grad_normed_mlp)
    grad_middle = grad_out + grad_from_mlp

    _, pullback = jax.vjp(norm_gain, branch, g_attn_out)
    grad_branch, grad_gain_attn_out = pullback(grad_middle)
    grad_branch = grad_branch.astype(BF)
    grad_w_out = over_rows(attended, grad_branch).astype(BF)
    grad_w_out = grad_w_out.reshape(2, groups, 2, 2, w_out.shape[0], width)
    grad_w_out = plane_terms(fold(grad_w_out, "c", 3))
    grad_attended = by_transpose(grad_branch, w_o).astype(BF)
    grad_queries, grad_key_pad, grad_value_pad = attend_backward(
        queries, key_pad, value_pad, allowed, log_total, grad_attended, attn_scale
    )
    returned = lax.ppermute(
        jnp.concatenate([grad_key_pad[:row_count], grad_value_pad[:row_count]], axis=1).astype(BF),
        ("g", "y", "c"),
        [(i + 1, i) for i in range(seq_size - 1)],
    ).astype(F32)
    grad_keys = grad_key_pad[row_count:] + returned[:, :k_cols]
    grad_values = grad_value_pad[row_count:] + returned[:, k_cols:]
    _, pullback = jax.vjp(
        lambda raw, gain: prepare_key(raw, gain, cosine_table, sine_table), key_raw, g_key
    )
    grad_key_raw, grad_gain_key = pullback(grad_keys)
    _, pullback = jax.vjp(
        lambda raw, gain: prepare_query(raw, gain, cosine_table, sine_table), query_raw, g_query
    )
    grad_query_raw, grad_gain_query = pullback(grad_queries)
    grad_query_raw = grad_query_raw.astype(BF)
    grad_first = jnp.concatenate([grad_query_raw[:, : q_cols // 2], grad_key_raw.astype(BF)], axis=1)
    grad_second = jnp.concatenate([grad_query_raw[:, q_cols // 2 :], grad_values.astype(BF)], axis=1)
    grad_w_first = over_rows(normed, grad_first).astype(BF)
    grad_w_second = over_rows(normed, grad_second).astype(BF)
    grad_normed = by_transpose(grad_first, w_first) + by_transpose(grad_second, w_second)
    _, pullback = jax.vjp(norm_gain, layer_in, g_attn_in)
    grad_from_attn, grad_gain_attn_in = pullback(grad_normed)
    grad_in = grad_middle + grad_from_attn

    terms = gain_columns(
        [
            g.reshape(devices, shard_rows)
            for g in (grad_gain_attn_in, grad_gain_attn_out, grad_gain_mlp_in, grad_gain_mlp_out)
        ],
        [g.reshape(devices, head_rows) for g in (grad_gain_query, grad_gain_key)],
    ).astype(BF)
    terms = terms.reshape(width, 128)
    terms = jnp.stack(
        [
            jnp.concatenate([grad_w_first, terms], axis=1),
            jnp.concatenate([grad_w_second, jnp.zeros_like(terms)], axis=1),
        ]
    )
    share = plane_terms(fold(terms, "c", 0).reshape(2, groups, 2, 2 * shard_rows, half_cols))
    share = share.reshape(2, shard_rows, half_cols)
    mine = lax.dynamic_index_in_dim(share, core, 0, keepdims=False)
    other = lax.dynamic_index_in_dim(share, 1 - core, 0, keepdims=False)
    first, second = in_order(mine, swap(other, "c"), core).astype(F32)
    half = q_cols // 2
    d_terms = first[:, half + k_cols :]
    return (
        layer_out.astype(BF)[None],
        grad_in.astype(BF)[None],
        jnp.concatenate([first[:, :half], second[:, :half]], axis=1),
        first[:, half : half + k_cols],
        second[:, half : half + k_cols],
        grad_w_out.astype(F32),
        grad_w_gate,
        grad_w_up,
        grad_down.astype(F32),
        d_terms[:, 0],
        d_terms[:, 1],
        d_terms[:, 2],
        d_terms[:, 3],
        d_terms[:head_rows, 4],
        d_terms[:head_rows, 5],
    )


def solution(mesh):
    batch, seq = mesh.devices.shape
    fine = Mesh(mesh.devices.reshape(batch, seq // 4, 2, 2), ALL)
    rows = ("g", "y", "c")
    return jax.shard_map(
        on_device,
        mesh=fine,
        in_specs=(P("x", rows, None),) * 2
        + (P("x", None),)
        + (P(ALL, None),) * 7
        + (P(ALL),) * 6,
        out_specs=(P("x", rows, None),) * 2 + (P(ALL, None),) * 7 + (P(ALL),) * 6,
        check_vma=False,
    )
```

```python
import jax
import jax.numpy as jnp
from jax import lax
from jax.experimental import pallas as pl
from jax.experimental.pallas import tpu as pltpu
from jax.sharding import Mesh
from jax.sharding import PartitionSpec as P

HEAD = 256
WINDOW = 512
EPSILON = 1e-06
ROPE_BASE = 10000.0
ALL = ("x", "g", "y", "c")
PLANE = ("x", "y", "c")
BF = jnp.bfloat16
F32 = jnp.float32


def norm_gain(values, gain_vec):
    return (
        values * lax.rsqrt(jnp.mean(values * values, axis=-1, keepdims=True) + EPSILON) * gain_vec
    )


def rotate(values, cosine_table, sine_table):
    half_size = values.shape[-1] // 2
    turned = jnp.concatenate([-values[..., half_size:], values[..., :half_size]], axis=-1)
    return values * cosine_table + turned * sine_table


def rope_tables(first_row, row_count, head_size):
    places = (first_row + jnp.arange(row_count, dtype=jnp.int32)).astype(F32)
    frequency = ROPE_BASE ** (-(jnp.arange(head_size // 2, dtype=F32) * 2.0) / head_size)
    angles = places[:, None] * frequency[None, :]
    angles = jnp.concatenate([angles, angles], axis=-1)
    return (jnp.cos(angles), jnp.sin(angles))


def prepare_query(raw_value, gain_vec, cosine_table, sine_table):
    split_heads = raw_value.reshape(raw_value.shape[0], -1, gain_vec.shape[0])
    return rotate(
        norm_gain(split_heads, gain_vec), cosine_table[:, None, :], sine_table[:, None, :]
    )


def prepare_key(raw_value, gain_vec, cosine_table, sine_table):
    return rotate(norm_gain(raw_value, gain_vec), cosine_table, sine_table)


def matmul(left_side, right_side):
    return jnp.dot(left_side, right_side, preferred_element_type=F32)


def over_rows(left_side, right_side):
    return lax.dot_general(
        left_side, right_side, (((0,), (0,)), ((), ())), preferred_element_type=F32
    )


def by_transpose(left_side, right_side):
    return lax.dot_general(
        left_side, right_side, (((1,), (1,)), ((), ())), preferred_element_type=F32
    )


def block_mask(ids_pad, rows):
    query_place = rows + jnp.arange(rows, dtype=jnp.int32)
    key_place = jnp.arange(2 * rows, dtype=jnp.int32)
    distance = query_place[:, None] - key_place[None, :]
    same_doc = ids_pad[rows:][:, None] == ids_pad[None, :]
    return (distance >= 0) & (distance < WINDOW) & same_doc


def attend_forward(queries, key_pad, value_pad, allowed, attn_scale):
    row_count, head_count, head_size = queries.shape
    scores = jnp.einsum("qhd,kd->hqk", queries, key_pad, preferred_element_type=F32) * attn_scale
    scores = jnp.where(allowed[None], scores, -1e30)
    row_max = jnp.max(scores, axis=-1, keepdims=True)
    weights = jnp.exp(scores - row_max)
    row_total = jnp.sum(weights, axis=-1, keepdims=True)
    probabilities = (weights / row_total).astype(BF)
    attended = jnp.einsum("hqk,kd->qhd", probabilities, value_pad, preferred_element_type=F32)
    return (
        attended.reshape(row_count, head_count * head_size),
        (row_max + jnp.log(row_total))[..., 0],
    )


def attend_backward(queries, key_pad, value_pad, allowed, log_total, grad_attended, attn_scale):
    row_count, head_count, head_size = queries.shape
    grad_part = grad_attended.reshape(row_count, head_count, head_size)
    scores = jnp.einsum("qhd,kd->hqk", queries, key_pad, preferred_element_type=F32) * attn_scale
    probabilities = jnp.where(allowed[None], jnp.exp(scores - log_total[..., None]), 0.0)
    grad_prob = jnp.einsum("qhd,kd->hqk", grad_part, value_pad, preferred_element_type=F32)
    inner_sum = jnp.sum(probabilities * grad_prob, axis=-1, keepdims=True)
    grad_score = (probabilities * (grad_prob - inner_sum)).astype(BF)
    grad_query = (
        jnp.einsum("hqk,kd->qhd", grad_score, key_pad, preferred_element_type=F32) * attn_scale
    )
    grad_key = (
        jnp.einsum("hqk,qhd->kd", grad_score, queries, preferred_element_type=F32) * attn_scale
    )
    grad_value = jnp.einsum(
        "hqk,qhd->kd", probabilities.astype(BF), grad_part, preferred_element_type=F32
    )
    return (grad_query, grad_key, grad_value)


def swap(array, axis):
    return lax.ppermute(array, axis, [(0, 1), (1, 0)])


GELU_A = 0.7978845608028654
GELU_B = 0.044715
TILE = 512
PARAMS = pltpu.CompilerParams(vmem_limit_bytes=58 << 20)


def whole_block(shape):
    return pl.BlockSpec(shape, lambda i: (0,) * len(shape), pipeline_mode=pl.Buffered(1))


def row_block(rows, columns):
    return pl.BlockSpec((rows, columns), lambda i: (i, 0))


def mlp_forward_kernel(normed, gate_up, down, hidden, gelu, slope, mixed):
    own = down.shape[0]
    raw = matmul(normed[...], gate_up[...])
    gate_raw, up_raw = raw[:, :own], raw[:, own:]
    square = gate_raw * gate_raw
    bend = jnp.tanh(GELU_A * (gate_raw + GELU_B * square * gate_raw))
    half = 0.5 + 0.5 * bend
    active = gate_raw * half
    turn = 0.5 * gate_raw * (1.0 - bend * bend) * (GELU_A * (1.0 + 3.0 * GELU_B * square))
    low = (active * up_raw).astype(BF)
    hidden[...] = low
    gelu[...] = active.astype(BF)
    slope[...] = ((half + turn) * up_raw).astype(BF)
    mixed[...] = matmul(low, down[...]).astype(BF)


def mlp_forward(normed, gate_up, down):
    rows, width = normed.shape
    own = down.shape[0]
    flat = jax.ShapeDtypeStruct((rows, own), BF)
    return pl.pallas_call(
        mlp_forward_kernel,
        grid=(rows // TILE,),
        in_specs=[row_block(TILE, width), whole_block(gate_up.shape), whole_block(down.shape)],
        out_specs=[row_block(TILE, own)] * 3 + [row_block(TILE, width)],
        out_shape=[flat, flat, flat, jax.ShapeDtypeStruct((rows, width), BF)],
        compiler_params=PARAMS,
        cost_estimate=pl.CostEstimate(
            flops=6 * rows * width * own, bytes_accessed=rows * (4 * width + 6 * own), transcendentals=0
        ),
    )(normed, gate_up, down)


def mlp_backward_kernel(grad_mixed, gelu, slope, gate_up, down, grad_raw, grad_normed):
    own = down.shape[0]
    grad_hidden = by_transpose(grad_mixed[...], down[...])
    grad_gate = (grad_hidden * slope[...].astype(F32)).astype(BF)
    grad_up = (grad_hidden * gelu[...].astype(F32)).astype(BF)
    grad_raw[:, :own] = grad_gate
    grad_raw[:, own:] = grad_up
    grad_normed[...] = (
        by_transpose(grad_gate, gate_up[:, :own]) + by_transpose(grad_up, gate_up[:, own:])
    ).astype(BF)


def mlp_backward(grad_mixed, gelu, slope, gate_up, down):
    rows, width = grad_mixed.shape
    own = down.shape[0]
    return pl.pallas_call(
        mlp_backward_kernel,
        grid=(rows // TILE,),
        in_specs=[
            row_block(TILE, width),
            row_block(TILE, own),
            row_block(TILE, own),
            whole_block(gate_up.shape),
            whole_block(down.shape),
        ],
        out_specs=[row_block(TILE, 2 * own), row_block(TILE, width)],
        out_shape=[
            jax.ShapeDtypeStruct((rows, 2 * own), BF),
            jax.ShapeDtypeStruct((rows, width), BF),
        ],
        compiler_params=PARAMS,
        cost_estimate=pl.CostEstimate(
            flops=6 * rows * width * own, bytes_accessed=rows * (4 * width + 8 * own), transcendentals=0
        ),
    )(grad_mixed, gelu, slope, gate_up, down)


def down_terms_kernel(*refs):
    *ins, out = refs
    half = len(ins) // 2
    total = over_rows(ins[0][...], ins[half][...])
    for left, right in zip(ins[1:half], ins[half + 1 :]):
        total = total + over_rows(left[...], right[...])
    out[...] = total.astype(BF)


def down_terms(hidden, grad_mixed):
    own, width = hidden[0].shape[1], grad_mixed[0].shape[1]
    rows = sum(part.shape[0] for part in hidden)
    return pl.pallas_call(
        down_terms_kernel,
        grid=(own // 128,),
        in_specs=[pl.BlockSpec((part.shape[0], 128), lambda i: (0, i)) for part in hidden]
        + [whole_block(part.shape) for part in grad_mixed],
        out_specs=row_block(128, width),
        out_shape=jax.ShapeDtypeStruct((own, width), BF),
        compiler_params=PARAMS,
        cost_estimate=pl.CostEstimate(
            flops=2 * rows * width * own, bytes_accessed=2 * rows * (width + own), transcendentals=0
        ),
    )(*hidden, *grad_mixed)


def gate_terms_kernel(*refs):
    *ins, out = refs
    half = len(ins) // 2
    total = over_rows(ins[0][...], ins[half][...])
    for left, right in zip(ins[1:half], ins[half + 1 :]):
        total = total + over_rows(left[...], right[...])
    total = total.astype(BF)
    groups, sides, rows, _ = out.shape
    for side in range(sides):
        for group in range(groups):
            first = (side * groups + group) * rows
            out[group, side] = total[first : first + rows]


def gate_terms(normed, grad_raw, groups):
    width, both = normed[0].shape[1], grad_raw[0].shape[1]
    rows = sum(part.shape[0] for part in normed)
    shape = (groups, 2, width // (2 * groups))
    return pl.pallas_call(
        gate_terms_kernel,
        grid=(both // 256,),
        in_specs=[whole_block(part.shape) for part in normed]
        + [pl.BlockSpec((part.shape[0], 256), lambda i: (0, i)) for part in grad_raw],
        out_specs=pl.BlockSpec(shape + (256,), lambda i: (0, 0, 0, i)),
        out_shape=jax.ShapeDtypeStruct(shape + (both,), BF),
        compiler_params=PARAMS,
        cost_estimate=pl.CostEstimate(
            flops=2 * rows * width * both, bytes_accessed=2 * rows * (width + both), transcendentals=0
        ),
    )(*normed, *grad_raw)


def with_core(part):
    return jnp.concatenate([part, swap(part, "c")])


def plane_gather(own):
    half = own.shape[0] // 2
    from_x = swap(own, "x")
    from_y = swap(own, "y")
    far_top = swap(from_x[:half], "y")
    far_low = swap(from_y[half:], "x")
    near = jnp.concatenate([from_x, from_y])
    far = jnp.concatenate([far_top, far_low])
    return [with_core(own), with_core(near), with_core(far)]


def core_sum(part):
    half = part.shape[0] // 2
    return part[:half].astype(F32) + swap(part[half:], "c").astype(F32)


def plane_reduce(own, near, far):
    far = core_sum(far).astype(BF)
    rows = far.shape[0]
    half = rows // 2
    top = swap(far[:half], "y").astype(F32)
    low = swap(far[half:], "x").astype(F32)
    near = core_sum(near)
    to_x = jnp.concatenate([near[:half] + top, near[half:rows]]).astype(BF)
    to_y = jnp.concatenate([near[rows : rows + half], near[rows + half :] + low]).astype(BF)
    own = core_sum(own)
    return own + swap(to_x, "x").astype(F32) + swap(to_y, "y").astype(F32)


def in_order(own, other, place):
    both = jnp.concatenate([own[None], other[None], own[None]])
    return lax.dynamic_slice_in_dim(both, place, 2, 0)


def group_gather(own):
    size = lax.axis_size("g")
    parts = [own] + [
        lax.ppermute(own, "g", [((i + k) % size, i) for i in range(size)]) for k in range(1, size)
    ]
    both = jnp.stack(parts + parts[:-1])
    place = lax.axis_index("g")
    return lax.dynamic_slice_in_dim(both, lax.rem(size - place, size), size, 0)


def plane_weights(blocks):
    x, y = lax.axis_index("x"), lax.axis_index("y")
    half = blocks.shape[0] // 2
    first, second = blocks[:half], blocks[half:]
    first = in_order(first, swap(first, "x"), x)
    second = in_order(second, swap(second, "y"), y)
    first = in_order(first, swap(first, "y"), y)
    second = in_order(second, swap(second, "x"), x)
    first = first.transpose(1, 2, 0, 3, 4)
    second = second.transpose(0, 2, 1, 3, 4)
    return jnp.concatenate([first, second], axis=1)


def fold(term, axis, dim):
    place = lax.axis_index(axis)
    mine = lax.dynamic_index_in_dim(term, place, dim, keepdims=False)
    other = lax.dynamic_index_in_dim(term, 1 - place, dim, keepdims=False)
    return (mine.astype(F32) + swap(other.astype(BF), axis).astype(F32)).astype(BF)


def plane_terms(term):
    half = term.shape[1] // 2
    first = fold(fold(term[:, :half], "x", 0), "y", 1)
    second = fold(fold(term[:, half:], "y", 2), "x", 0)
    term = jnp.concatenate([first, second])
    term = term.reshape(-1, term.shape[-1])
    return lax.psum_scatter(term, "g", scatter_dimension=0, tiled=True)


def on_device(
    tokens,
    cotangent,
    doc_ids,
    w_query,
    w_key,
    w_value,
    w_out,
    w_gate,
    w_up,
    w_down,
    gain_attn_in,
    gain_attn_out,
    gain_mlp_in,
    gain_mlp_out,
    gain_query,
    gain_key,
):
    row_count = tokens.shape[1]
    width = tokens.shape[2]
    devices = lax.axis_size(ALL)
    groups = lax.axis_size("g")
    members = lax.axis_size(PLANE)
    shard_rows = w_query.shape[0]
    head_rows = gain_query.shape[0]
    hidden_all = w_gate.shape[1]
    hidden_own = hidden_all // members
    hidden_pad = -(-hidden_own // 128) * 128
    piece = hidden_own // groups
    q_cols, k_cols = w_query.shape[1], w_key.shape[1]
    attn_scale = HEAD ** (-0.5)

    def gain_columns(d_gains, h_gains):
        columns = list(d_gains) + [
            jnp.pad(h, ((0, 0), (0, shard_rows - head_rows))) for h in h_gains
        ]
        block = jnp.stack(columns, axis=-1)
        return jnp.pad(block, ((0, 0), (0, 0), (0, 128 - len(columns))))

    core = lax.axis_index("c")
    half_cols = q_cols // 2 + k_cols + 128
    gains = gain_columns(
        [g[None] for g in (gain_attn_in, gain_attn_out, gain_mlp_in, gain_mlp_out)],
        [gain_query[None], gain_key[None]],
    )
    halves = jnp.stack(
        [
            jnp.concatenate([w_query[:, : q_cols // 2], w_key, gains[0]], axis=1),
            jnp.concatenate([w_query[:, q_cols // 2 :], w_value, jnp.zeros_like(gains[0])], axis=1),
        ]
    )
    mine = lax.dynamic_index_in_dim(halves, core, 0, keepdims=False)
    other = lax.dynamic_index_in_dim(halves, 1 - core, 0, keepdims=False)
    mine = in_order(mine, swap(other, "c"), core).reshape(2 * shard_rows, half_cols)
    mine = plane_weights(group_gather(mine)).reshape(width, half_cols)
    w_first, w_second = in_order(mine, swap(mine, "c"), core)
    gain_block = w_first[:, q_cols // 2 + k_cols :].astype(F32)
    d_gains = gain_block[:, :4].T
    g_attn_in, g_attn_out, g_mlp_in, g_mlp_out = (d_gains[i : i + 1] for i in range(4))
    h_gains = gain_block[:, 4:6].reshape(devices, shard_rows, 2)[:, :head_rows]
    g_query = h_gains[:, :, 0].reshape(HEAD)
    g_key = h_gains[:, :, 1].reshape(HEAD)
    w_first = w_first[:, : q_cols // 2 + k_cols]
    w_second = w_second[:, : q_cols // 2 + k_cols]

    down = lax.all_gather(jnp.concatenate([w_down, w_out]), "g", axis=0)
    w_o = plane_weights(down[:, w_down.shape[0] :])
    down = down[:, : w_down.shape[0]].reshape(-1, width)
    down = jnp.pad(down, ((0, hidden_pad - hidden_own), (0, 0)))
    w_o = in_order(w_o, swap(w_o, "c"), core).transpose(1, 2, 3, 0, 4, 5).reshape(q_cols, width)

    def spread(weight):
        cut = weight.reshape(shard_rows, 2, groups, members // 2, piece)
        cut = cut.transpose(1, 3, 0, 2, 4).reshape(members, shard_rows, hidden_own)
        return jnp.pad(cut, ((0, 0), (0, 0), (0, hidden_pad - hidden_own)))

    sent = jnp.concatenate([spread(w_gate), spread(w_up)], axis=2)
    sent = lax.all_to_all(sent, PLANE, split_axis=0, concat_axis=0, tiled=True)
    sent = sent.reshape(members * shard_rows, 2 * hidden_pad)
    both = lax.all_gather(sent, "g", axis=0)
    both = both.reshape(groups, 2, members // 2 * shard_rows, 2 * hidden_pad)
    gate_up = both.transpose(1, 0, 2, 3).reshape(width, 2 * hidden_pad)

    seq_place = lax.axis_index(("g", "y", "c"))
    seq_size = lax.axis_size(("g", "y", "c"))
    first_row = seq_place * row_count
    ids_all = doc_ids[0]
    ids_own = lax.dynamic_slice_in_dim(ids_all, first_row, row_count, 0)
    ids_prev = lax.dynamic_slice_in_dim(
        ids_all, jnp.maximum(first_row - row_count, 0), row_count, 0
    )
    ids_prev = jnp.where(seq_place > 0, ids_prev, -1)
    ids_pad = jnp.concatenate([ids_prev, ids_own])
    allowed = block_mask(ids_pad, row_count)
    cosine_table, sine_table = rope_tables(first_row, row_count, HEAD)
    layer_in = tokens[0].astype(F32)
    grad_out = cotangent[0].astype(F32)

    normed = norm_gain(layer_in, g_attn_in).astype(BF)
    raw_first = matmul(normed, w_first)
    raw_second = matmul(normed, w_second)
    query_raw = jnp.concatenate([raw_first[:, : q_cols // 2], raw_second[:, : q_cols // 2]], axis=1)
    key_raw = raw_first[:, q_cols // 2 :]
    queries = prepare_query(query_raw, g_query, cosine_table, sine_table).astype(BF)
    keys = prepare_key(key_raw, g_key, cosine_table, sine_table).astype(BF)
    values = raw_second[:, q_cols // 2 :].astype(BF)
    key_value = jnp.concatenate([keys, values], axis=1)
    halo = lax.ppermute(key_value, ("g", "y", "c"), [(i, i + 1) for i in range(seq_size - 1)])
    key_pad = jnp.concatenate([halo[:, :k_cols], keys])
    value_pad = jnp.concatenate([halo[:, k_cols:], values])
    attended, log_total = attend_forward(queries, key_pad, value_pad, allowed, attn_scale)
    attended = attended.astype(BF)
    branch = matmul(attended, w_o)
    middle = layer_in + norm_gain(branch, g_attn_out)
    normed_mlp = norm_gain(middle, g_mlp_in).astype(BF)

    normed_all = plane_gather(normed_mlp)
    results = [mlp_forward(part, gate_up, down) for part in normed_all]
    mixed = plane_reduce(*(r[3] for r in results))
    layer_out = middle + norm_gain(mixed, g_mlp_out)

    _, pullback = jax.vjp(norm_gain, mixed, g_mlp_out)
    grad_mixed, grad_gain_mlp_out = pullback(grad_out)
    grad_mixed_all = plane_gather(grad_mixed.astype(BF))
    grads = [
        mlp_backward(part, r[1], r[2], gate_up, down) for part, r in zip(grad_mixed_all, results)
    ]
    grad_down = down_terms([r[0] for r in results], grad_mixed_all)[:hidden_own]
    grad_down = lax.psum_scatter(grad_down, "g", scatter_dimension=0, tiled=True)
    term = gate_terms(normed_all, [g[0] for g in grads], groups)
    term = term.reshape(groups * members * shard_rows, 2 * hidden_pad)
    term = lax.psum_scatter(term, "g", scatter_dimension=0, tiled=True)
    term = term.reshape(members, shard_rows, 2 * hidden_pad)
    term = lax.all_to_all(term, PLANE, split_axis=0, concat_axis=0, tiled=True)

    def collect(cut):
        cut = cut[:, :, :hidden_own].reshape(2, members // 2, shard_rows, groups, piece)
        return cut.transpose(2, 0, 3, 1, 4).reshape(shard_rows, hidden_all).astype(F32)

    grad_w_gate = collect(term[:, :, :hidden_pad])
    grad_w_up = collect(term[:, :, hidden_pad:])
    grad_normed_mlp = plane_reduce(*(g[1] for g in grads))
    _, pullback = jax.vjp(norm_gain, middle, g_mlp_in)
    grad_from_mlp, grad_gain_mlp_in = pullback(grad_normed_mlp)
    grad_middle = grad_out + grad_from_mlp

    _, pullback = jax.vjp(norm_gain, branch, g_attn_out)
    grad_branch, grad_gain_attn_out = pullback(grad_middle)
    grad_branch = grad_branch.astype(BF)
    grad_w_out = over_rows(attended, grad_branch).astype(BF)
    grad_w_out = grad_w_out.reshape(2, groups, 2, 2, w_out.shape[0], width)
    grad_w_out = plane_terms(fold(grad_w_out, "c", 3))
    grad_attended = by_transpose(grad_branch, w_o).astype(BF)
    grad_queries, grad_key_pad, grad_value_pad = attend_backward(
        queries, key_pad, value_pad, allowed, log_total, grad_attended, attn_scale
    )
    returned = lax.ppermute(
        jnp.concatenate([grad_key_pad[:row_count], grad_value_pad[:row_count]], axis=1).astype(BF),
        ("g", "y", "c"),
        [(i + 1, i) for i in range(seq_size - 1)],
    ).astype(F32)
    grad_keys = grad_key_pad[row_count:] + returned[:, :k_cols]
    grad_values = grad_value_pad[row_count:] + returned[:, k_cols:]
    _, pullback = jax.vjp(
        lambda raw, gain: prepare_key(raw, gain, cosine_table, sine_table), key_raw, g_key
    )
    grad_key_raw, grad_gain_key = pullback(grad_keys)
    _, pullback = jax.vjp(
        lambda raw, gain: prepare_query(raw, gain, cosine_table, sine_table), query_raw, g_query
    )
    grad_query_raw, grad_gain_query = pullback(grad_queries)
    grad_query_raw = grad_query_raw.astype(BF)
    grad_first = jnp.concatenate([grad_query_raw[:, : q_cols // 2], grad_key_raw.astype(BF)], axis=1)
    grad_second = jnp.concatenate([grad_query_raw[:, q_cols // 2 :], grad_values.astype(BF)], axis=1)
    grad_w_first = over_rows(normed, grad_first).astype(BF)
    grad_w_second = over_rows(normed, grad_second).astype(BF)
    grad_normed = by_transpose(grad_first, w_first) + by_transpose(grad_second, w_second)
    _, pullback = jax.vjp(norm_gain, layer_in, g_attn_in)
    grad_from_attn, grad_gain_attn_in = pullback(grad_normed)
    grad_in = grad_middle + grad_from_attn

    terms = gain_columns(
        [
            g.reshape(devices, shard_rows)
            for g in (grad_gain_attn_in, grad_gain_attn_out, grad_gain_mlp_in, grad_gain_mlp_out)
        ],
        [g.reshape(devices, head_rows) for g in (grad_gain_query, grad_gain_key)],
    ).astype(BF)
    terms = terms.reshape(width, 128)
    terms = jnp.stack(
        [
            jnp.concatenate([grad_w_first, terms], axis=1),
            jnp.concatenate([grad_w_second, jnp.zeros_like(terms)], axis=1),
        ]
    )
    share = plane_terms(fold(terms, "c", 0).reshape(2, groups, 2, 2 * shard_rows, half_cols))
    share = share.reshape(2, shard_rows, half_cols)
    mine = lax.dynamic_index_in_dim(share, core, 0, keepdims=False)
    other = lax.dynamic_index_in_dim(share, 1 - core, 0, keepdims=False)
    first, second = in_order(mine, swap(other, "c"), core).astype(F32)
    half = q_cols // 2
    d_terms = first[:, half + k_cols :]
    return (
        layer_out.astype(BF)[None],
        grad_in.astype(BF)[None],
        jnp.concatenate([first[:, :half], second[:, :half]], axis=1),
        first[:, half : half + k_cols],
        second[:, half : half + k_cols],
        grad_w_out.astype(F32),
        grad_w_gate,
        grad_w_up,
        grad_down.astype(F32),
        d_terms[:, 0],
        d_terms[:, 1],
        d_terms[:, 2],
        d_terms[:, 3],
        d_terms[:head_rows, 4],
        d_terms[:head_rows, 5],
    )


def solution(mesh):
    batch, seq = mesh.devices.shape
    fine = Mesh(mesh.devices.reshape(batch, seq // 4, 2, 2), ALL)
    rows = ("g", "y", "c")
    return jax.shard_map(
        on_device,
        mesh=fine,
        in_specs=(P("x", rows, None),) * 2
        + (P("x", None),)
        + (P(ALL, None),) * 7
        + (P(ALL),) * 6,
        out_specs=(P("x", rows, None),) * 2 + (P(ALL, None),) * 7 + (P(ALL),) * 6,
        check_vma=False,
    )
```

```python
import jax
import jax.numpy as jnp
from jax import lax
from jax.experimental import pallas as pl
from jax.experimental.pallas import tpu as pltpu
from jax.sharding import Mesh
from jax.sharding import PartitionSpec as P

HEAD = 256
WINDOW = 512
EPSILON = 1e-06
ROPE_BASE = 10000.0
ALL = ("x", "g", "y", "c")
PLANE = ("x", "y", "c")
BF = jnp.bfloat16
F32 = jnp.float32


def norm_gain(values, gain_vec):
    return (
        values * lax.rsqrt(jnp.mean(values * values, axis=-1, keepdims=True) + EPSILON) * gain_vec
    )


def rotate(values, cosine_table, sine_table):
    half_size = values.shape[-1] // 2
    turned = jnp.concatenate([-values[..., half_size:], values[..., :half_size]], axis=-1)
    return values * cosine_table + turned * sine_table


def rope_tables(first_row, row_count, head_size):
    places = (first_row + jnp.arange(row_count, dtype=jnp.int32)).astype(F32)
    frequency = ROPE_BASE ** (-(jnp.arange(head_size // 2, dtype=F32) * 2.0) / head_size)
    angles = places[:, None] * frequency[None, :]
    angles = jnp.concatenate([angles, angles], axis=-1)
    return (jnp.cos(angles), jnp.sin(angles))


def prepare_query(raw_value, gain_vec, cosine_table, sine_table):
    split_heads = raw_value.reshape(raw_value.shape[0], -1, gain_vec.shape[0])
    return rotate(
        norm_gain(split_heads, gain_vec), cosine_table[:, None, :], sine_table[:, None, :]
    )


def prepare_key(raw_value, gain_vec, cosine_table, sine_table):
    return rotate(norm_gain(raw_value, gain_vec), cosine_table, sine_table)


def matmul(left_side, right_side):
    return jnp.dot(left_side, right_side, preferred_element_type=F32)


def over_rows(left_side, right_side):
    return lax.dot_general(
        left_side, right_side, (((0,), (0,)), ((), ())), preferred_element_type=F32
    )


def by_transpose(left_side, right_side):
    return lax.dot_general(
        left_side, right_side, (((1,), (1,)), ((), ())), preferred_element_type=F32
    )


def block_mask(ids_pad, rows):
    query_place = rows + jnp.arange(rows, dtype=jnp.int32)
    key_place = jnp.arange(2 * rows, dtype=jnp.int32)
    distance = query_place[:, None] - key_place[None, :]
    same_doc = ids_pad[rows:][:, None] == ids_pad[None, :]
    return (distance >= 0) & (distance < WINDOW) & same_doc


def attend_forward(queries, key_pad, value_pad, allowed, attn_scale):
    row_count, head_count, head_size = queries.shape
    scores = jnp.einsum("qhd,kd->hqk", queries, key_pad, preferred_element_type=F32) * attn_scale
    scores = jnp.where(allowed[None], scores, -1e30)
    row_max = jnp.max(scores, axis=-1, keepdims=True)
    weights = jnp.exp(scores - row_max)
    row_total = jnp.sum(weights, axis=-1, keepdims=True)
    probabilities = (weights / row_total).astype(BF)
    attended = jnp.einsum("hqk,kd->qhd", probabilities, value_pad, preferred_element_type=F32)
    return (
        attended.reshape(row_count, head_count * head_size),
        (row_max + jnp.log(row_total))[..., 0],
    )


def attend_backward(queries, key_pad, value_pad, allowed, log_total, grad_attended, attn_scale):
    row_count, head_count, head_size = queries.shape
    grad_part = grad_attended.reshape(row_count, head_count, head_size)
    scores = jnp.einsum("qhd,kd->hqk", queries, key_pad, preferred_element_type=F32) * attn_scale
    probabilities = jnp.where(allowed[None], jnp.exp(scores - log_total[..., None]), 0.0)
    grad_prob = jnp.einsum("qhd,kd->hqk", grad_part, value_pad, preferred_element_type=F32)
    inner_sum = jnp.sum(probabilities * grad_prob, axis=-1, keepdims=True)
    grad_score = (probabilities * (grad_prob - inner_sum)).astype(BF)
    grad_query = (
        jnp.einsum("hqk,kd->qhd", grad_score, key_pad, preferred_element_type=F32) * attn_scale
    )
    grad_key = (
        jnp.einsum("hqk,qhd->kd", grad_score, queries, preferred_element_type=F32) * attn_scale
    )
    grad_value = jnp.einsum(
        "hqk,qhd->kd", probabilities.astype(BF), grad_part, preferred_element_type=F32
    )
    return (grad_query, grad_key, grad_value)


def swap(array, axis):
    return lax.ppermute(array, axis, [(0, 1), (1, 0)])


GELU_A = 0.7978845608028654
GELU_B = 0.044715
TILE = 512
PARAMS = pltpu.CompilerParams(vmem_limit_bytes=58 << 20)


def whole_block(shape):
    return pl.BlockSpec(shape, lambda i: (0,) * len(shape), pipeline_mode=pl.Buffered(1))


def row_block(rows, columns):
    return pl.BlockSpec((rows, columns), lambda i: (i, 0))


def mlp_forward_kernel(normed, gate_up, down, _, hidden, gelu, slope, mixed):
    own = down.shape[0]
    raw = matmul(normed[...], gate_up[...])
    gate_raw, up_raw = raw[:, :own], raw[:, own:]
    square = gate_raw * gate_raw
    bend = jnp.tanh(GELU_A * (gate_raw + GELU_B * square * gate_raw))
    half = 0.5 + 0.5 * bend
    active = gate_raw * half
    turn = 0.5 * gate_raw * (1.0 - bend * bend) * (GELU_A * (1.0 + 3.0 * GELU_B * square))
    low = (active * up_raw).astype(BF)
    hidden[...] = low
    gelu[...] = active.astype(BF)
    slope[...] = ((half + turn) * up_raw).astype(BF)
    mixed[...] = matmul(low, down[...]).astype(BF)


def mlp_forward(normed, gate_up, down, earlier):
    rows, width = normed.shape
    own = down.shape[0]
    flat = jax.ShapeDtypeStruct((rows, own), BF)
    return pl.pallas_call(
        mlp_forward_kernel,
        grid=(rows // TILE,),
        in_specs=[
            row_block(TILE, width),
            whole_block(gate_up.shape),
            whole_block(down.shape),
            pl.BlockSpec(memory_space=pl.ANY),
        ],
        out_specs=[row_block(TILE, own)] * 3 + [row_block(TILE, width)],
        out_shape=[flat, flat, flat, jax.ShapeDtypeStruct((rows, width), BF)],
        compiler_params=PARAMS,
        cost_estimate=pl.CostEstimate(
            flops=6 * rows * width * own, bytes_accessed=rows * (4 * width + 6 * own), transcendentals=0
        ),
    )(normed, gate_up, down, earlier)


def mlp_backward_kernel(grad_mixed, gelu, slope, gate_up, down, _, grad_raw, grad_normed):
    own = down.shape[0]
    grad_hidden = by_transpose(grad_mixed[...], down[...])
    grad_gate = (grad_hidden * slope[...].astype(F32)).astype(BF)
    grad_up = (grad_hidden * gelu[...].astype(F32)).astype(BF)
    grad_raw[:, :own] = grad_gate
    grad_raw[:, own:] = grad_up
    grad_normed[...] = (
        by_transpose(grad_gate, gate_up[:, :own]) + by_transpose(grad_up, gate_up[:, own:])
    ).astype(BF)


def mlp_backward(grad_mixed, gelu, slope, gate_up, down, earlier):
    rows, width = grad_mixed.shape
    own = down.shape[0]
    return pl.pallas_call(
        mlp_backward_kernel,
        grid=(rows // TILE,),
        in_specs=[
            row_block(TILE, width),
            row_block(TILE, own),
            row_block(TILE, own),
            whole_block(gate_up.shape),
            whole_block(down.shape),
            pl.BlockSpec(memory_space=pl.ANY),
        ],
        out_specs=[row_block(TILE, 2 * own), row_block(TILE, width)],
        out_shape=[
            jax.ShapeDtypeStruct((rows, 2 * own), BF),
            jax.ShapeDtypeStruct((rows, width), BF),
        ],
        compiler_params=PARAMS,
        cost_estimate=pl.CostEstimate(
            flops=6 * rows * width * own, bytes_accessed=rows * (4 * width + 8 * own), transcendentals=0
        ),
    )(grad_mixed, gelu, slope, gate_up, down, earlier)


def down_terms_kernel(*refs):
    *ins, out = refs
    half = len(ins) // 2
    total = over_rows(ins[0][...], ins[half][...])
    for left, right in zip(ins[1:half], ins[half + 1 :]):
        total = total + over_rows(left[...], right[...])
    out[...] = total.astype(BF)


def down_terms(hidden, grad_mixed):
    own, width = hidden[0].shape[1], grad_mixed[0].shape[1]
    rows = sum(part.shape[0] for part in hidden)
    return pl.pallas_call(
        down_terms_kernel,
        grid=(own // 128,),
        in_specs=[pl.BlockSpec((part.shape[0], 128), lambda i: (0, i)) for part in hidden]
        + [whole_block(part.shape) for part in grad_mixed],
        out_specs=row_block(128, width),
        out_shape=jax.ShapeDtypeStruct((own, width), BF),
        compiler_params=PARAMS,
        cost_estimate=pl.CostEstimate(
            flops=2 * rows * width * own, bytes_accessed=2 * rows * (width + own), transcendentals=0
        ),
    )(*hidden, *grad_mixed)


def gate_terms_kernel(*refs):
    *ins, out = refs
    half = len(ins) // 2
    total = over_rows(ins[0][...], ins[half][...])
    for left, right in zip(ins[1:half], ins[half + 1 :]):
        total = total + over_rows(left[...], right[...])
    total = total.astype(BF)
    groups, sides, rows, _ = out.shape
    for side in range(sides):
        for group in range(groups):
            first = (side * groups + group) * rows
            out[group, side] = total[first : first + rows]


def gate_terms(normed, grad_raw, groups):
    width, both = normed[0].shape[1], grad_raw[0].shape[1]
    rows = sum(part.shape[0] for part in normed)
    shape = (groups, 2, width // (2 * groups))
    return pl.pallas_call(
        gate_terms_kernel,
        grid=(both // 256,),
        in_specs=[whole_block(part.shape) for part in normed]
        + [pl.BlockSpec((part.shape[0], 256), lambda i: (0, i)) for part in grad_raw],
        out_specs=pl.BlockSpec(shape + (256,), lambda i: (0, 0, 0, i)),
        out_shape=jax.ShapeDtypeStruct(shape + (both,), BF),
        compiler_params=PARAMS,
        cost_estimate=pl.CostEstimate(
            flops=2 * rows * width * both, bytes_accessed=2 * rows * (width + both), transcendentals=0
        ),
    )(*normed, *grad_raw)


def after(value, *earlier):
    return lax.optimization_barrier((value, *earlier))[0]


def with_core(part):
    return jnp.concatenate([part, swap(part, "c")])


def plane_gather(own):
    half = own.shape[0] // 2
    from_x = swap(own, "x")
    from_y = swap(own, "y")
    far_top = swap(from_x[:half], "y")
    far_low = swap(from_y[half:], "x")
    near = jnp.concatenate([from_x, from_y])
    far = jnp.concatenate([far_top, far_low])
    return [with_core(own), with_core(near), with_core(far)]


def core_sum(part):
    half = part.shape[0] // 2
    return part[:half].astype(F32) + swap(part[half:], "c").astype(F32)


def plane_reduce(own, near, far):
    far = core_sum(far).astype(BF)
    rows = far.shape[0]
    half = rows // 2
    top = swap(far[:half], "y").astype(F32)
    low = swap(far[half:], "x").astype(F32)
    near = core_sum(near)
    to_x = jnp.concatenate([near[:half] + top, near[half:rows]]).astype(BF)
    to_y = jnp.concatenate([near[rows : rows + half], near[rows + half :] + low]).astype(BF)
    own = core_sum(own)
    return own + swap(to_x, "x").astype(F32) + swap(to_y, "y").astype(F32)


def in_order(own, other, place):
    both = jnp.concatenate([own[None], other[None], own[None]])
    return lax.dynamic_slice_in_dim(both, place, 2, 0)


def group_gather(own):
    size = lax.axis_size("g")
    parts = [own] + [
        lax.ppermute(own, "g", [((i + k) % size, i) for i in range(size)]) for k in range(1, size)
    ]
    both = jnp.stack(parts + parts[:-1])
    place = lax.axis_index("g")
    return lax.dynamic_slice_in_dim(both, lax.rem(size - place, size), size, 0)


def plane_weights(blocks):
    x, y = lax.axis_index("x"), lax.axis_index("y")
    half = blocks.shape[0] // 2
    first, second = blocks[:half], blocks[half:]
    first = in_order(first, swap(first, "x"), x)
    second = in_order(second, swap(second, "y"), y)
    first = in_order(first, swap(first, "y"), y)
    second = in_order(second, swap(second, "x"), x)
    first = first.transpose(1, 2, 0, 3, 4)
    second = second.transpose(0, 2, 1, 3, 4)
    return jnp.concatenate([first, second], axis=1)


def fold(term, axis, dim):
    place = lax.axis_index(axis)
    mine = lax.dynamic_index_in_dim(term, place, dim, keepdims=False)
    other = lax.dynamic_index_in_dim(term, 1 - place, dim, keepdims=False)
    return (mine.astype(F32) + swap(other.astype(BF), axis).astype(F32)).astype(BF)


def plane_terms(term, earlier):
    half = term.shape[1] // 2
    first = fold(fold(term[:, :half], "x", 0), "y", 1)
    second = fold(fold(term[:, half:], "y", 2), "x", 0)
    term = jnp.concatenate([first, second])
    term = after(term.reshape(-1, term.shape[-1]), earlier)
    return lax.psum_scatter(term, "g", scatter_dimension=0, tiled=True)


def on_device(
    tokens,
    cotangent,
    doc_ids,
    w_query,
    w_key,
    w_value,
    w_out,
    w_gate,
    w_up,
    w_down,
    gain_attn_in,
    gain_attn_out,
    gain_mlp_in,
    gain_mlp_out,
    gain_query,
    gain_key,
):
    row_count = tokens.shape[1]
    width = tokens.shape[2]
    devices = lax.axis_size(ALL)
    groups = lax.axis_size("g")
    members = lax.axis_size(PLANE)
    shard_rows = w_query.shape[0]
    head_rows = gain_query.shape[0]
    hidden_all = w_gate.shape[1]
    hidden_own = hidden_all // members
    hidden_pad = -(-hidden_own // 128) * 128
    piece = hidden_own // groups
    q_cols, k_cols = w_query.shape[1], w_key.shape[1]
    attn_scale = HEAD ** (-0.5)

    def gain_columns(d_gains, h_gains):
        columns = list(d_gains) + [
            jnp.pad(h, ((0, 0), (0, shard_rows - head_rows))) for h in h_gains
        ]
        block = jnp.stack(columns, axis=-1)
        return jnp.pad(block, ((0, 0), (0, 0), (0, 128 - len(columns))))

    def spread(weight):
        cut = weight.reshape(shard_rows, 2, groups, members // 2, piece)
        cut = cut.transpose(1, 3, 0, 2, 4).reshape(members, shard_rows, hidden_own)
        return jnp.pad(cut, ((0, 0), (0, 0), (0, hidden_pad - hidden_own)))

    sent = jnp.concatenate([spread(w_gate), spread(w_up)], axis=2)
    sent = lax.all_to_all(sent, PLANE, split_axis=0, concat_axis=0, tiled=True)
    sent = sent.reshape(members * shard_rows, 2 * hidden_pad)
    core = lax.axis_index("c")
    half_cols = q_cols // 2 + k_cols + 128
    gains = gain_columns(
        [g[None] for g in (gain_attn_in, gain_attn_out, gain_mlp_in, gain_mlp_out)],
        [gain_query[None], gain_key[None]],
    )
    halves = jnp.stack(
        [
            jnp.concatenate([w_query[:, : q_cols // 2], w_key, gains[0]], axis=1),
            jnp.concatenate([w_query[:, q_cols // 2 :], w_value, jnp.zeros_like(gains[0])], axis=1),
        ]
    )
    mine = lax.dynamic_index_in_dim(halves, core, 0, keepdims=False)
    other = lax.dynamic_index_in_dim(halves, 1 - core, 0, keepdims=False)
    mine = in_order(mine, swap(other, "c"), core).reshape(2 * shard_rows, half_cols)
    mine, sent = lax.optimization_barrier((group_gather(mine), sent))
    mine = plane_weights(mine).reshape(width, half_cols)
    w_first, w_second = in_order(mine, swap(mine, "c"), core)
    gain_block = w_first[:, q_cols // 2 + k_cols :].astype(F32)
    d_gains = gain_block[:, :4].T
    g_attn_in, g_attn_out, g_mlp_in, g_mlp_out = (d_gains[i : i + 1] for i in range(4))
    h_gains = gain_block[:, 4:6].reshape(devices, shard_rows, 2)[:, :head_rows]
    g_query = h_gains[:, :, 0].reshape(HEAD)
    g_key = h_gains[:, :, 1].reshape(HEAD)
    w_first = w_first[:, : q_cols // 2 + k_cols]
    w_second = w_second[:, : q_cols // 2 + k_cols]

    down = lax.all_gather(jnp.concatenate([w_down, w_out]), "g", axis=0)
    w_o = plane_weights(down[:, w_down.shape[0] :])
    down = down[:, : w_down.shape[0]].reshape(-1, width)
    down = jnp.pad(down, ((0, hidden_pad - hidden_own), (0, 0)))
    w_o = in_order(w_o, swap(w_o, "c"), core).transpose(1, 2, 3, 0, 4, 5).reshape(q_cols, width)

    both = lax.all_gather(sent, "g", axis=0)
    both = both.reshape(groups, 2, members // 2 * shard_rows, 2 * hidden_pad)
    gate_up = both.transpose(1, 0, 2, 3).reshape(width, 2 * hidden_pad)

    seq_place = lax.axis_index(("g", "y", "c"))
    seq_size = lax.axis_size(("g", "y", "c"))
    first_row = seq_place * row_count
    ids_all = doc_ids[0]
    ids_own = lax.dynamic_slice_in_dim(ids_all, first_row, row_count, 0)
    ids_prev = lax.dynamic_slice_in_dim(
        ids_all, jnp.maximum(first_row - row_count, 0), row_count, 0
    )
    ids_prev = jnp.where(seq_place > 0, ids_prev, -1)
    ids_pad = jnp.concatenate([ids_prev, ids_own])
    allowed = block_mask(ids_pad, row_count)
    cosine_table, sine_table = rope_tables(first_row, row_count, HEAD)
    layer_in = tokens[0].astype(F32)
    grad_out = cotangent[0].astype(F32)

    normed = norm_gain(layer_in, g_attn_in).astype(BF)
    raw_first = matmul(normed, w_first)
    raw_second = matmul(normed, w_second)
    query_raw = jnp.concatenate([raw_first[:, : q_cols // 2], raw_second[:, : q_cols // 2]], axis=1)
    key_raw = raw_first[:, q_cols // 2 :]
    queries = prepare_query(query_raw, g_query, cosine_table, sine_table).astype(BF)
    keys = prepare_key(key_raw, g_key, cosine_table, sine_table).astype(BF)
    values = raw_second[:, q_cols // 2 :].astype(BF)
    key_value = jnp.concatenate([keys, values], axis=1)
    halo = lax.ppermute(key_value, ("g", "y", "c"), [(i, i + 1) for i in range(seq_size - 1)])
    key_pad = jnp.concatenate([halo[:, :k_cols], keys])
    value_pad = jnp.concatenate([halo[:, k_cols:], values])
    attended, log_total = attend_forward(queries, key_pad, value_pad, allowed, attn_scale)
    attended = attended.astype(BF)
    branch = matmul(attended, w_o)
    middle = layer_in + norm_gain(branch, g_attn_out)
    normed_mlp = norm_gain(middle, g_mlp_in).astype(BF)

    normed_all = plane_gather(normed_mlp)
    far_result = mlp_forward(normed_all[2], gate_up, down, normed_all[2])
    near_result = mlp_forward(normed_all[1], gate_up, down, far_result[3])
    own_result = mlp_forward(normed_all[0], gate_up, down, near_result[3])
    results = [own_result, near_result, far_result]
    mixed = plane_reduce(*(r[3] for r in results))
    layer_out = middle + norm_gain(mixed, g_mlp_out)

    _, pullback = jax.vjp(norm_gain, mixed, g_mlp_out)
    grad_mixed, grad_gain_mlp_out = pullback(grad_out)
    grad_mixed_all = plane_gather(grad_mixed.astype(BF))
    grads = []
    earlier = down
    for part, result in zip(grad_mixed_all, results):
        grads.append(mlp_backward(part, result[1], result[2], gate_up, down, earlier))
        earlier = grads[-1][1]
    grad_down = down_terms([r[0] for r in results], grad_mixed_all)[:hidden_own]
    grad_down_terms = grad_down
    grad_down = lax.psum_scatter(grad_down, "g", scatter_dimension=0, tiled=True)
    term = gate_terms(normed_all, [g[0] for g in grads], groups)
    gate_up_terms = term
    term = after(term.reshape(groups * members * shard_rows, 2 * hidden_pad), grad_down)
    term = lax.psum_scatter(term, "g", scatter_dimension=0, tiled=True)
    gate_up_share = term
    term = term.reshape(members, shard_rows, 2 * hidden_pad)
    term = lax.all_to_all(term, PLANE, split_axis=0, concat_axis=0, tiled=True)

    def collect(cut):
        cut = cut[:, :, :hidden_own].reshape(2, members // 2, shard_rows, groups, piece)
        return cut.transpose(2, 0, 3, 1, 4).reshape(shard_rows, hidden_all).astype(F32)

    grad_w_gate = collect(term[:, :, :hidden_pad])
    grad_w_up = collect(term[:, :, hidden_pad:])
    grad_normed_mlp = plane_reduce(*(g[1] for g in grads))
    grad_normed_mlp = after(grad_normed_mlp, grad_down_terms, gate_up_terms)
    _, pullback = jax.vjp(norm_gain, middle, g_mlp_in)
    grad_from_mlp, grad_gain_mlp_in = pullback(grad_normed_mlp)
    grad_middle = grad_out + grad_from_mlp

    _, pullback = jax.vjp(norm_gain, branch, g_attn_out)
    grad_branch, grad_gain_attn_out = pullback(grad_middle)
    grad_branch = grad_branch.astype(BF)
    grad_w_out = over_rows(attended, grad_branch).astype(BF)
    grad_w_out = grad_w_out.reshape(2, groups, 2, 2, w_out.shape[0], width)
    grad_w_out = plane_terms(fold(grad_w_out, "c", 3), gate_up_share)
    grad_attended = by_transpose(grad_branch, w_o).astype(BF)
    grad_queries, grad_key_pad, grad_value_pad = attend_backward(
        queries, key_pad, value_pad, allowed, log_total, grad_attended, attn_scale
    )
    returned = lax.ppermute(
        jnp.concatenate([grad_key_pad[:row_count], grad_value_pad[:row_count]], axis=1).astype(BF),
        ("g", "y", "c"),
        [(i + 1, i) for i in range(seq_size - 1)],
    ).astype(F32)
    grad_keys = grad_key_pad[row_count:] + returned[:, :k_cols]
    grad_values = grad_value_pad[row_count:] + returned[:, k_cols:]
    _, pullback = jax.vjp(
        lambda raw, gain: prepare_key(raw, gain, cosine_table, sine_table), key_raw, g_key
    )
    grad_key_raw, grad_gain_key = pullback(grad_keys)
    _, pullback = jax.vjp(
        lambda raw, gain: prepare_query(raw, gain, cosine_table, sine_table), query_raw, g_query
    )
    grad_query_raw, grad_gain_query = pullback(grad_queries)
    grad_query_raw = after(grad_query_raw.astype(BF), grad_down)
    grad_first = jnp.concatenate([grad_query_raw[:, : q_cols // 2], grad_key_raw.astype(BF)], axis=1)
    grad_second = jnp.concatenate([grad_query_raw[:, q_cols // 2 :], grad_values.astype(BF)], axis=1)
    grad_w_first = over_rows(normed, grad_first).astype(BF)
    grad_w_second = over_rows(normed, grad_second).astype(BF)
    grad_normed = by_transpose(grad_first, w_first) + by_transpose(grad_second, w_second)
    _, pullback = jax.vjp(norm_gain, layer_in, g_attn_in)
    grad_from_attn, grad_gain_attn_in = pullback(grad_normed)
    grad_in = grad_middle + grad_from_attn

    terms = gain_columns(
        [
            g.reshape(devices, shard_rows)
            for g in (grad_gain_attn_in, grad_gain_attn_out, grad_gain_mlp_in, grad_gain_mlp_out)
        ],
        [g.reshape(devices, head_rows) for g in (grad_gain_query, grad_gain_key)],
    ).astype(BF)
    terms = terms.reshape(width, 128)
    terms = jnp.stack(
        [
            jnp.concatenate([grad_w_first, terms], axis=1),
            jnp.concatenate([grad_w_second, jnp.zeros_like(terms)], axis=1),
        ]
    )
    terms = fold(terms, "c", 0).reshape(2, groups, 2, 2 * shard_rows, half_cols)
    share = plane_terms(terms, grad_w_out)
    share = share.reshape(2, shard_rows, half_cols)
    mine = lax.dynamic_index_in_dim(share, core, 0, keepdims=False)
    other = lax.dynamic_index_in_dim(share, 1 - core, 0, keepdims=False)
    first, second = in_order(mine, swap(other, "c"), core).astype(F32)
    half = q_cols // 2
    d_terms = first[:, half + k_cols :]
    return (
        layer_out.astype(BF)[None],
        grad_in.astype(BF)[None],
        jnp.concatenate([first[:, :half], second[:, :half]], axis=1),
        first[:, half : half + k_cols],
        second[:, half : half + k_cols],
        grad_w_out.astype(F32),
        grad_w_gate,
        grad_w_up,
        grad_down.astype(F32),
        d_terms[:, 0],
        d_terms[:, 1],
        d_terms[:, 2],
        d_terms[:, 3],
        d_terms[:head_rows, 4],
        d_terms[:head_rows, 5],
    )


def solution(mesh):
    batch, seq = mesh.devices.shape
    fine = Mesh(mesh.devices.reshape(batch, seq // 4, 2, 2), ALL)
    rows = ("g", "y", "c")
    return jax.shard_map(
        on_device,
        mesh=fine,
        in_specs=(P("x", rows, None),) * 2
        + (P("x", None),)
        + (P(ALL, None),) * 7
        + (P(ALL),) * 6,
        out_specs=(P("x", rows, None),) * 2 + (P(ALL, None),) * 7 + (P(ALL),) * 6,
        check_vma=False,
    )
```

```python
import functools

import jax
import jax.numpy as jnp
from jax import lax
from jax.experimental import pallas as pl
from jax.experimental.pallas import tpu as pltpu
from jax.sharding import Mesh
from jax.sharding import PartitionSpec as P

HEAD = 256
WINDOW = 512
EPSILON = 1e-06
ROPE_BASE = 10000.0
ALL = ("x", "g", "y", "c")
PLANE = ("x", "y", "c")
BF = jnp.bfloat16
F32 = jnp.float32


def norm_gain(values, gain_vec):
    return (
        values * lax.rsqrt(jnp.mean(values * values, axis=-1, keepdims=True) + EPSILON) * gain_vec
    )


def rope_tables(first_row, row_count, head_size):
    places = (first_row + jnp.arange(row_count, dtype=jnp.int32)).astype(F32)
    frequency = ROPE_BASE ** (-(jnp.arange(head_size // 2, dtype=F32) * 2.0) / head_size)
    angles = places[:, None] * frequency[None, :]
    return (jnp.cos(angles), jnp.sin(angles))


def matmul(left_side, right_side):
    return jnp.dot(left_side, right_side, preferred_element_type=F32)


def over_rows(left_side, right_side):
    return lax.dot_general(
        left_side, right_side, (((0,), (0,)), ((), ())), preferred_element_type=F32
    )


def by_transpose(left_side, right_side):
    return lax.dot_general(
        left_side, right_side, (((1,), (1,)), ((), ())), preferred_element_type=F32
    )


def swap(array, axis):
    return lax.ppermute(array, axis, [(0, 1), (1, 0)])


GELU_A = 0.7978845608028654
GELU_B = 0.044715
TILE = 512
PARAMS = pltpu.CompilerParams(vmem_limit_bytes=58 << 20)


def whole_block(shape):
    return pl.BlockSpec(shape, lambda i: (0,) * len(shape), pipeline_mode=pl.Buffered(1))


def row_block(rows, columns):
    return pl.BlockSpec((rows, columns), lambda i: (i, 0))


def mlp_forward_kernel(normed, gate_up, down, _, hidden, gelu, slope, mixed):
    own = down.shape[0]
    raw = matmul(normed[...], gate_up[...])
    gate_raw, up_raw = raw[:, :own], raw[:, own:]
    square = gate_raw * gate_raw
    bend = jnp.tanh(GELU_A * (gate_raw + GELU_B * square * gate_raw))
    half = 0.5 + 0.5 * bend
    active = gate_raw * half
    turn = 0.5 * gate_raw * (1.0 - bend * bend) * (GELU_A * (1.0 + 3.0 * GELU_B * square))
    low = (active * up_raw).astype(BF)
    hidden[...] = low
    gelu[...] = active.astype(BF)
    slope[...] = ((half + turn) * up_raw).astype(BF)
    mixed[...] = matmul(low, down[...]).astype(BF)


def mlp_forward(normed, gate_up, down, earlier):
    rows, width = normed.shape
    own = down.shape[0]
    flat = jax.ShapeDtypeStruct((rows, own), BF)
    return pl.pallas_call(
        mlp_forward_kernel,
        grid=(rows // TILE,),
        in_specs=[
            row_block(TILE, width),
            whole_block(gate_up.shape),
            whole_block(down.shape),
            pl.BlockSpec(memory_space=pl.ANY),
        ],
        out_specs=[row_block(TILE, own)] * 3 + [row_block(TILE, width)],
        out_shape=[flat, flat, flat, jax.ShapeDtypeStruct((rows, width), BF)],
        compiler_params=PARAMS,
        cost_estimate=pl.CostEstimate(
            flops=6 * rows * width * own, bytes_accessed=rows * (4 * width + 6 * own), transcendentals=0
        ),
    )(normed, gate_up, down, earlier)


def mlp_backward_kernel(grad_mixed, gelu, slope, gate_up, down, _, grad_raw, grad_normed):
    own = down.shape[0]
    grad_hidden = by_transpose(grad_mixed[...], down[...])
    grad_gate = (grad_hidden * slope[...].astype(F32)).astype(BF)
    grad_up = (grad_hidden * gelu[...].astype(F32)).astype(BF)
    grad_raw[:, :own] = grad_gate
    grad_raw[:, own:] = grad_up
    grad_normed[...] = (
        by_transpose(grad_gate, gate_up[:, :own]) + by_transpose(grad_up, gate_up[:, own:])
    ).astype(BF)


def mlp_backward(grad_mixed, gelu, slope, gate_up, down, earlier):
    rows, width = grad_mixed.shape
    own = down.shape[0]
    return pl.pallas_call(
        mlp_backward_kernel,
        grid=(rows // TILE,),
        in_specs=[
            row_block(TILE, width),
            row_block(TILE, own),
            row_block(TILE, own),
            whole_block(gate_up.shape),
            whole_block(down.shape),
            pl.BlockSpec(memory_space=pl.ANY),
        ],
        out_specs=[row_block(TILE, 2 * own), row_block(TILE, width)],
        out_shape=[
            jax.ShapeDtypeStruct((rows, 2 * own), BF),
            jax.ShapeDtypeStruct((rows, width), BF),
        ],
        compiler_params=PARAMS,
        cost_estimate=pl.CostEstimate(
            flops=6 * rows * width * own, bytes_accessed=rows * (4 * width + 8 * own), transcendentals=0
        ),
    )(grad_mixed, gelu, slope, gate_up, down, earlier)


def down_terms_kernel(*refs):
    *ins, out = refs
    half = len(ins) // 2
    total = over_rows(ins[0][...], ins[half][...])
    for left, right in zip(ins[1:half], ins[half + 1 :]):
        total = total + over_rows(left[...], right[...])
    out[...] = total.astype(BF)


def down_terms(hidden, grad_mixed, keep):
    own, width = hidden[0].shape[1], grad_mixed[0].shape[1]
    rows = sum(part.shape[0] for part in hidden)
    return pl.pallas_call(
        down_terms_kernel,
        grid=(own // 128,),
        in_specs=[pl.BlockSpec((part.shape[0], 128), lambda i: (0, i)) for part in hidden]
        + [whole_block(part.shape) for part in grad_mixed],
        out_specs=row_block(128, width),
        out_shape=jax.ShapeDtypeStruct((keep, width), BF),
        compiler_params=PARAMS,
        cost_estimate=pl.CostEstimate(
            flops=2 * rows * width * own, bytes_accessed=2 * rows * (width + own), transcendentals=0
        ),
    )(*hidden, *grad_mixed)


def gate_terms_kernel(*refs):
    *ins, _, out = refs
    half = len(ins) // 2
    total = over_rows(ins[0][...], ins[half][...])
    for left, right in zip(ins[1:half], ins[half + 1 :]):
        total = total + over_rows(left[...], right[...])
    total = total.astype(BF)
    groups, sides, rows, _ = out.shape
    for side in range(sides):
        for group in range(groups):
            first = (side * groups + group) * rows
            out[group, side] = total[first : first + rows]


def gate_terms(normed, grad_raw, groups, earlier):
    width, both = normed[0].shape[1], grad_raw[0].shape[1]
    rows = sum(part.shape[0] for part in normed)
    shape = (groups, 2, width // (2 * groups))
    return pl.pallas_call(
        gate_terms_kernel,
        grid=(both // 256,),
        in_specs=[whole_block(part.shape) for part in normed]
        + [pl.BlockSpec((part.shape[0], 256), lambda i: (0, i)) for part in grad_raw]
        + [pl.BlockSpec(memory_space=pl.ANY)],
        out_specs=pl.BlockSpec(shape + (256,), lambda i: (0, 0, 0, i)),
        out_shape=jax.ShapeDtypeStruct(shape + (both,), BF),
        compiler_params=PARAMS,
        cost_estimate=pl.CostEstimate(
            flops=2 * rows * width * both, bytes_accessed=2 * rows * (width + both), transcendentals=0
        ),
    )(*normed, *grad_raw, earlier)


def after(value, *earlier):
    return lax.optimization_barrier((value, *earlier))[0]


def with_core(part):
    return jnp.concatenate([part, swap(part, "c")])


def core_sum(part):
    half = part.shape[0] // 2
    return part[:half].astype(F32) + swap(part[half:], "c").astype(F32)


def send_far(far):
    half = far.shape[0] // 2
    return swap(far[:half], "y").astype(F32), swap(far[half:], "x").astype(F32)


def sum_near(near, top, low):
    near = core_sum(near)
    rows = near.shape[0] // 2
    half = rows // 2
    to_x = jnp.concatenate([near[:half] + top, near[half:rows]]).astype(BF)
    to_y = jnp.concatenate([near[rows : rows + half], near[rows + half :] + low]).astype(BF)
    return to_x, to_y


def sum_own(own, to_x, to_y):
    return core_sum(own) + swap(to_x, "x").astype(F32) + swap(to_y, "y").astype(F32)


def in_order(own, other, place):
    both = jnp.concatenate([own[None], other[None], own[None]])
    return lax.dynamic_slice_in_dim(both, place, 2, 0)


def group_gather(own):
    size = lax.axis_size("g")
    parts = [own] + [
        lax.ppermute(own, "g", [((i + k) % size, i) for i in range(size)]) for k in range(1, size)
    ]
    both = jnp.stack(parts + parts[:-1])
    place = lax.axis_index("g")
    return lax.dynamic_slice_in_dim(both, lax.rem(size - place, size), size, 0)


def plane_weights(blocks):
    x, y = lax.axis_index("x"), lax.axis_index("y")
    half = blocks.shape[0] // 2
    first, second = blocks[:half], blocks[half:]
    first = in_order(first, swap(first, "x"), x)
    second = in_order(second, swap(second, "y"), y)
    first = in_order(first, swap(first, "y"), y)
    second = in_order(second, swap(second, "x"), x)
    first = first.transpose(1, 2, 0, 3, 4)
    second = second.transpose(0, 2, 1, 3, 4)
    return jnp.concatenate([first, second], axis=1)


def fold(term, axis, dim):
    place = lax.axis_index(axis)
    mine = lax.dynamic_index_in_dim(term, place, dim, keepdims=False)
    other = lax.dynamic_index_in_dim(term, 1 - place, dim, keepdims=False)
    return (mine.astype(F32) + swap(other.astype(BF), axis).astype(F32)).astype(BF)


def plane_terms(term):
    half = term.shape[1] // 2
    first = fold(fold(term[:, :half], "x", 0), "y", 1)
    second = fold(fold(term[:, half:], "y", 2), "x", 0)
    return jnp.concatenate([first, second])


def rms_scale(values):
    return lax.rsqrt(jnp.mean(values * values, axis=-1, keepdims=True) + EPSILON)


def rms_backward(values, scale, gain, grad):
    weighted = grad * gain
    inner = jnp.mean(weighted * values, axis=-1, keepdims=True)
    terms = jnp.sum(grad * values * scale, axis=0, keepdims=True)
    return weighted * scale - values * (scale * scale * scale * inner), terms


def turn_forward(values, cosine, sine):
    half = cosine.shape[1]
    low, high = values[:, :half], values[:, half:]
    return jnp.concatenate([low * cosine - high * sine, high * cosine + low * sine], axis=1)


def turn_backward(grad, cosine, sine):
    half = cosine.shape[1]
    low, high = grad[:, :half], grad[:, half:]
    return jnp.concatenate([low * cosine + high * sine, high * cosine - low * sine], axis=1)


def gain_places(width, columns, shard_rows):
    heads = columns // (width // shard_rows)
    row = lax.broadcasted_iota(jnp.int32, (width, columns), 0)
    column = lax.broadcasted_iota(jnp.int32, (width, columns), 1)
    place = (column // heads) * shard_rows + lax.rem(column, heads)
    return jnp.where(row == place, 1.0, 0.0).astype(BF)


def project_kernel(
    shard_rows, core, tokens, own, other, cosine, sine,
    normed, query_raw, key_raw, queries, key_value, d_gains, h_gains,
):
    width = tokens.shape[1]
    k_cols = key_raw.shape[1]
    half = query_raw.shape[1] // 2
    first_is_own = core[0] == 0
    block = jnp.where(
        first_is_own, own[:, half + k_cols :].astype(F32), other[:, half + k_cols :].astype(F32)
    )
    flat = block.T[:8]
    d_gains[...] = flat
    chosen = matmul(flat.astype(BF), gain_places(width, k_cols, shard_rows))
    h_gains[...] = chosen
    values = tokens[...].astype(F32)
    low = (values * rms_scale(values) * flat[0:1]).astype(BF)
    normed[...] = low
    raw_own = matmul(low, own[:, : half + k_cols])
    raw_other = matmul(low, other[:, : half + k_cols])
    first = jnp.where(first_is_own, raw_own, raw_other)
    second = jnp.where(first_is_own, raw_other, raw_own)
    raw_query = jnp.concatenate([first[:, :half], second[:, :half]], axis=1)
    raw_key = first[:, half:]
    query_raw[...] = raw_query
    key_raw[...] = raw_key
    cos, sin = cosine[...], sine[...]
    for head in range(2 * half // k_cols):
        at = slice(head * k_cols, (head + 1) * k_cols)
        part = raw_query[:, at]
        part = part * rms_scale(part) * chosen[4:5]
        queries[:, at] = turn_forward(part, cos, sin).astype(BF)
    part = raw_key * rms_scale(raw_key) * chosen[5:6]
    key_value[:, :k_cols] = turn_forward(part, cos, sin).astype(BF)
    key_value[:, k_cols:] = second[:, half:].astype(BF)


def project(core, tokens, own, other, cosine, sine, shard_rows, q_cols, k_cols):
    rows, width = tokens.shape
    vmem = pl.BlockSpec(memory_space=pltpu.VMEM)
    return pl.pallas_call(
        functools.partial(project_kernel, shard_rows),
        in_specs=[pl.BlockSpec(memory_space=pltpu.SMEM)] + [vmem] * 5,
        out_specs=[vmem] * 7,
        out_shape=[
            jax.ShapeDtypeStruct((rows, width), BF),
            jax.ShapeDtypeStruct((rows, q_cols), F32),
            jax.ShapeDtypeStruct((rows, k_cols), F32),
            jax.ShapeDtypeStruct((rows, q_cols), BF),
            jax.ShapeDtypeStruct((rows, 2 * k_cols), BF),
            jax.ShapeDtypeStruct((8, width), F32),
            jax.ShapeDtypeStruct((8, k_cols), F32),
        ],
        compiler_params=PARAMS,
        cost_estimate=pl.CostEstimate(
            flops=2 * rows * width * (q_cols + 2 * k_cols), bytes_accessed=16 * rows * width, transcendentals=0
        ),
    )(core, tokens, own, other, cosine, sine)


def tile_mask(first, rows, first_key, keys, query_ids, key_ids, pad):
    query_place = pad + first + lax.broadcasted_iota(jnp.int32, (rows, keys), 0)
    key_place = first_key + lax.broadcasted_iota(jnp.int32, (rows, keys), 1)
    distance = query_place - key_place
    same_doc = query_ids[first : first + rows, :] == key_ids[:, first_key : first_key + keys]
    return (distance >= 0) & (distance < WINDOW) & same_doc


def attend_kernel(
    scale, queries, halo, key_value, query_ids, key_ids, w_o, tokens, d_gains,
    attended, log_total, branch, middle, normed_mlp, keys, values,
):
    pad, k_cols = halo.shape[0], halo.shape[1] // 2
    rows, q_cols = queries.shape
    keys[:pad] = halo[:, :k_cols]
    keys[pad:] = key_value[:, :k_cols]
    values[:pad] = halo[:, k_cols:]
    values[pad:] = key_value[:, k_cols:]
    tile = rows // 2
    span = pad + tile
    lane = lax.broadcasted_iota(jnp.int32, (tile, 128), 1)
    for first in (0, tile):
        at = slice(first, first + tile)
        seen = slice(first, first + span)
        allowed = tile_mask(first, tile, first, span, query_ids, key_ids, pad)
        logs = jnp.zeros((tile, 128), F32)
        for head in range(q_cols // k_cols):
            columns = slice(head * k_cols, (head + 1) * k_cols)
            scores = by_transpose(queries[at, columns], keys[seen]) * scale
            scores = jnp.where(allowed, scores, -1e30)
            row_max = jnp.max(scores, axis=-1, keepdims=True)
            weights = jnp.exp(scores - row_max)
            row_total = jnp.sum(weights, axis=-1, keepdims=True)
            probabilities = (weights * (1.0 / row_total)).astype(BF)
            attended[at, columns] = matmul(probabilities, values[seen]).astype(BF)
            logs = jnp.where(lane == head, row_max + jnp.log(row_total), logs)
        log_total[at] = logs
    out = matmul(attended[...], w_o[...])
    branch[...] = out
    total = tokens[...].astype(F32) + out * rms_scale(out) * d_gains[1:2]
    middle[...] = total
    normed_mlp[...] = (total * rms_scale(total) * d_gains[2:3]).astype(BF)


def attend(queries, halo, key_value, query_ids, key_ids, w_o, tokens, d_gains, scale):
    rows, q_cols = queries.shape
    width = tokens.shape[1]
    k_cols = halo.shape[1] // 2
    pad = halo.shape[0]
    vmem = pl.BlockSpec(memory_space=pltpu.VMEM)
    return pl.pallas_call(
        functools.partial(attend_kernel, scale),
        in_specs=[vmem] * 8,
        out_specs=[vmem] * 5,
        out_shape=[
            jax.ShapeDtypeStruct((rows, q_cols), BF),
            jax.ShapeDtypeStruct((rows, 128), F32),
            jax.ShapeDtypeStruct((rows, width), F32),
            jax.ShapeDtypeStruct((rows, width), F32),
            jax.ShapeDtypeStruct((rows, width), BF),
        ],
        scratch_shapes=[pltpu.VMEM((pad + rows, k_cols), BF), pltpu.VMEM((pad + rows, k_cols), BF)],
        compiler_params=PARAMS,
        cost_estimate=pl.CostEstimate(
            flops=2 * rows * q_cols * (width + 2 * (pad + rows)), bytes_accessed=20 * rows * width, transcendentals=0
        ),
    )(queries, halo, key_value, query_ids, key_ids, w_o, tokens, d_gains)


def attend_backward_kernel(
    scale, grad_normed_mlp, cotangent, middle, branch, d_gains, w_o,
    queries, halo, key_value, query_ids, key_ids, log_total,
    grad_middle, grad_branch, grad_queries, grad_key_value, returned, terms,
    keys, values, grad_keys, grad_values, grad_attended,
):
    pad, k_cols = halo.shape[0], halo.shape[1] // 2
    rows, q_cols = queries.shape
    total = middle[...]
    from_mlp, mlp_terms = rms_backward(total, rms_scale(total), d_gains[2:3], grad_normed_mlp[...])
    grad_total = cotangent[...].astype(F32) + from_mlp
    grad_middle[...] = grad_total
    out = branch[...]
    grad_out, out_terms = rms_backward(out, rms_scale(out), d_gains[1:2], grad_total)
    low = grad_out.astype(BF)
    grad_branch[...] = low
    terms[...] = jnp.concatenate([out_terms, mlp_terms, jnp.zeros((6, out.shape[1]), F32)], axis=0)
    grad_attended[...] = by_transpose(low, w_o[...]).astype(BF)
    keys[:pad] = halo[:, :k_cols]
    keys[pad:] = key_value[:, :k_cols]
    values[:pad] = halo[:, k_cols:]
    values[pad:] = key_value[:, k_cols:]
    grad_keys[...] = jnp.zeros_like(grad_keys)
    grad_values[...] = jnp.zeros_like(grad_values)
    tile = rows // 2
    span = pad + tile
    for first in (0, tile):
        at = slice(first, first + tile)
        seen = slice(first, first + span)
        allowed = tile_mask(first, tile, first, span, query_ids, key_ids, pad)
        key_total = jnp.zeros((span, k_cols), F32)
        value_total = jnp.zeros((span, k_cols), F32)
        for head in range(q_cols // k_cols):
            columns = slice(head * k_cols, (head + 1) * k_cols)
            query = queries[at, columns]
            grad = grad_attended[at, columns]
            scores = by_transpose(query, keys[seen]) * scale
            probabilities = jnp.where(
                allowed, jnp.exp(scores - log_total[at, head : head + 1]), 0.0
            )
            grad_prob = by_transpose(grad, values[seen])
            inner = jnp.sum(probabilities * grad_prob, axis=-1, keepdims=True)
            grad_score = (probabilities * (grad_prob - inner)).astype(BF)
            grad_queries[at, columns] = matmul(grad_score, keys[seen]) * scale
            key_total = key_total + over_rows(grad_score, query)
            value_total = value_total + over_rows(probabilities.astype(BF), grad)
        grad_keys[seen] = grad_keys[seen] + key_total * scale
        grad_values[seen] = grad_values[seen] + value_total
    returned[:, :k_cols] = grad_keys[:pad].astype(BF)
    returned[:, k_cols:] = grad_values[:pad].astype(BF)
    grad_key_value[:, :k_cols] = grad_keys[pad:]
    grad_key_value[:, k_cols:] = grad_values[pad:]


def attend_backward(
    grad_normed_mlp, cotangent, middle, branch, d_gains, w_o,
    queries, halo, key_value, query_ids, key_ids, log_total, scale,
):
    rows, q_cols = queries.shape
    width = middle.shape[1]
    k_cols = halo.shape[1] // 2
    pad = halo.shape[0]
    vmem = pl.BlockSpec(memory_space=pltpu.VMEM)
    return pl.pallas_call(
        functools.partial(attend_backward_kernel, scale),
        in_specs=[vmem] * 12,
        out_specs=[vmem] * 6,
        out_shape=[
            jax.ShapeDtypeStruct((rows, width), F32),
            jax.ShapeDtypeStruct((rows, width), BF),
            jax.ShapeDtypeStruct((rows, q_cols), F32),
            jax.ShapeDtypeStruct((rows, 2 * k_cols), F32),
            jax.ShapeDtypeStruct((pad, 2 * k_cols), BF),
            jax.ShapeDtypeStruct((8, width), F32),
        ],
        scratch_shapes=[
            pltpu.VMEM((pad + rows, k_cols), BF),
            pltpu.VMEM((pad + rows, k_cols), BF),
            pltpu.VMEM((pad + rows, k_cols), F32),
            pltpu.VMEM((pad + rows, k_cols), F32),
            pltpu.VMEM((rows, q_cols), BF),
        ],
        compiler_params=PARAMS,
        cost_estimate=pl.CostEstimate(
            flops=2 * rows * q_cols * (width + 5 * (pad + rows)), bytes_accessed=30 * rows * width, transcendentals=0
        ),
    )(
        grad_normed_mlp, cotangent, middle, branch, d_gains, w_o,
        queries, halo, key_value, query_ids, key_ids, log_total,
    )


def project_backward_kernel(
    shard_rows, core, grad_queries, grad_key_value, returned, query_raw, key_raw, cosine, sine,
    h_gains, normed, own, other, grad_middle, tokens, d_gains, terms, mixed_terms,
    grad_tokens, mine, sent,
):
    width = tokens.shape[1]
    k_cols = key_raw.shape[1]
    half = query_raw.shape[1] // 2
    first_is_own = core[0] == 0
    cos, sin = cosine[...], sine[...]
    query_terms = jnp.zeros((1, k_cols), F32)
    parts = []
    for head in range(2 * half // k_cols):
        at = slice(head * k_cols, (head + 1) * k_cols)
        raw = query_raw[:, at]
        grad = turn_backward(grad_queries[:, at], cos, sin)
        grad, term = rms_backward(raw, rms_scale(raw), h_gains[4:5], grad)
        query_terms = query_terms + term
        parts.append(grad.astype(BF))
    total = grad_key_value[...] + returned[...].astype(F32)
    raw = key_raw[...]
    grad = turn_backward(total[:, :k_cols], cos, sin)
    grad, key_terms = rms_backward(raw, rms_scale(raw), h_gains[5:6], grad)
    both = len(parts) // 2
    first = jnp.concatenate(parts[:both] + [grad.astype(BF)], axis=1)
    second = jnp.concatenate(parts[both:] + [total[:, k_cols:].astype(BF)], axis=1)
    grad_own = jnp.where(first_is_own, first, second)
    grad_other = jnp.where(first_is_own, second, first)
    cols = half + k_cols
    grad_normed = by_transpose(grad_own, own[:, :cols]) + by_transpose(grad_other, other[:, :cols])
    values = tokens[...].astype(F32)
    from_attn, in_terms = rms_backward(values, rms_scale(values), d_gains[0:1], grad_normed)
    grad_tokens[...] = (grad_middle[...] + from_attn).astype(BF)
    mine[:, :cols] = over_rows(normed[...], grad_own).astype(BF)
    sent[:, :cols] = over_rows(normed[...], grad_other).astype(BF)
    heads = jnp.concatenate([query_terms, key_terms, jnp.zeros((6, k_cols), F32)], axis=0)
    placed = by_transpose(heads.astype(BF), gain_places(width, k_cols, shard_rows))
    block = jnp.concatenate(
        [in_terms, terms[0:2], mixed_terms[0:1], placed[0:2], jnp.zeros((122, width), F32)], axis=0
    ).T
    mine[:, cols:] = jnp.where(first_is_own, block, 0.0).astype(BF)
    sent[:, cols:] = jnp.where(first_is_own, 0.0, block).astype(BF)


def project_backward(
    core, grad_queries, grad_key_value, returned, query_raw, key_raw, cosine, sine,
    h_gains, normed, own, other, grad_middle, tokens, d_gains, terms, mixed_terms, shard_rows,
):
    rows, width = tokens.shape
    vmem = pl.BlockSpec(memory_space=pltpu.VMEM)
    return pl.pallas_call(
        functools.partial(project_backward_kernel, shard_rows),
        in_specs=[pl.BlockSpec(memory_space=pltpu.SMEM)] + [vmem] * 16,
        out_specs=[vmem] * 3,
        out_shape=[
            jax.ShapeDtypeStruct((rows, width), BF),
            jax.ShapeDtypeStruct(own.shape, BF),
            jax.ShapeDtypeStruct(own.shape, BF),
        ],
        compiler_params=PARAMS,
        cost_estimate=pl.CostEstimate(
            flops=8 * rows * width * own.shape[1], bytes_accessed=30 * rows * width, transcendentals=0
        ),
    )(
        core, grad_queries, grad_key_value, returned, query_raw, key_raw, cosine, sine,
        h_gains, normed, own, other, grad_middle, tokens, d_gains, terms, mixed_terms,
    )


def on_device(
    tokens,
    cotangent,
    doc_ids,
    w_query,
    w_key,
    w_value,
    w_out,
    w_gate,
    w_up,
    w_down,
    gain_attn_in,
    gain_attn_out,
    gain_mlp_in,
    gain_mlp_out,
    gain_query,
    gain_key,
):
    row_count = tokens.shape[1]
    width = tokens.shape[2]
    groups = lax.axis_size("g")
    members = lax.axis_size(PLANE)
    shard_rows = w_query.shape[0]
    head_rows = gain_query.shape[0]
    hidden_all = w_gate.shape[1]
    hidden_own = hidden_all // members
    hidden_pad = -(-hidden_own // 128) * 128
    piece = hidden_own // groups
    q_cols, k_cols = w_query.shape[1], w_key.shape[1]
    attn_scale = HEAD ** (-0.5)

    def gain_columns(d_gains, h_gains):
        columns = list(d_gains) + [
            jnp.pad(h, ((0, 0), (0, shard_rows - head_rows))) for h in h_gains
        ]
        block = jnp.stack(columns, axis=-1)
        return jnp.pad(block, ((0, 0), (0, 0), (0, 128 - len(columns))))

    def spread(weight):
        cut = weight.reshape(shard_rows, 2, groups, members // 2, piece)
        cut = cut.transpose(1, 3, 0, 2, 4).reshape(members, shard_rows, hidden_own)
        return jnp.pad(cut, ((0, 0), (0, 0), (0, hidden_pad - hidden_own)))

    sent = jnp.concatenate([spread(w_gate), spread(w_up)], axis=2)
    sent = lax.all_to_all(sent, PLANE, split_axis=0, concat_axis=0, tiled=True)
    sent = sent.reshape(members * shard_rows, 2 * hidden_pad)
    core = lax.axis_index("c")
    half_cols = q_cols // 2 + k_cols + 128
    gains = gain_columns(
        [g[None] for g in (gain_attn_in, gain_attn_out, gain_mlp_in, gain_mlp_out)],
        [gain_query[None], gain_key[None]],
    )
    halves = jnp.stack(
        [
            jnp.concatenate([w_query[:, : q_cols // 2], w_key, gains[0]], axis=1),
            jnp.concatenate([w_query[:, q_cols // 2 :], w_value, jnp.zeros_like(gains[0])], axis=1),
        ]
    )
    mine = lax.dynamic_index_in_dim(halves, core, 0, keepdims=False)
    other = lax.dynamic_index_in_dim(halves, 1 - core, 0, keepdims=False)
    mine = in_order(mine, swap(other, "c"), core).reshape(2 * shard_rows, half_cols)
    mine, sent = lax.optimization_barrier((group_gather(mine), sent))
    mine = plane_weights(mine).reshape(width, half_cols)
    other = swap(mine, "c")

    down = lax.all_gather(jnp.concatenate([w_down, w_out]), "g", axis=0)
    w_o = plane_weights(down[:, w_down.shape[0] :])
    down = down[:, : w_down.shape[0]].reshape(-1, width)
    down = jnp.pad(down, ((0, hidden_pad - hidden_own), (0, 0)))
    w_o = in_order(w_o, swap(w_o, "c"), core).transpose(1, 2, 3, 0, 4, 5).reshape(q_cols, width)

    both = lax.all_gather(sent, "g", axis=0)
    both = both.reshape(groups, 2, members // 2 * shard_rows, 2 * hidden_pad)
    gate_up = both.transpose(1, 0, 2, 3).reshape(width, 2 * hidden_pad)

    seq_place = lax.axis_index(("g", "y", "c"))
    seq_size = lax.axis_size(("g", "y", "c"))
    first_row = seq_place * row_count
    ids_all = doc_ids[0]
    ids_own = lax.dynamic_slice_in_dim(ids_all, first_row, row_count, 0)
    ids_prev = lax.dynamic_slice_in_dim(
        ids_all, jnp.maximum(first_row - row_count, 0), row_count, 0
    )
    ids_prev = jnp.where(seq_place > 0, ids_prev, -1)
    ids_pad = jnp.concatenate([ids_prev, ids_own])
    query_ids, key_ids = ids_own[:, None], ids_pad[None]
    cosine_table, sine_table = rope_tables(first_row, row_count, HEAD)
    places = jnp.full((1,), core, jnp.int32)
    layer_in, grad_out = tokens[0], cotangent[0]

    normed, query_raw, key_raw, queries, key_value, d_gains, h_gains = project(
        places, layer_in, mine, other, cosine_table, sine_table, shard_rows, q_cols, k_cols
    )
    halo = lax.ppermute(key_value, ("g", "y", "c"), [(i, i + 1) for i in range(seq_size - 1)])
    attended, log_total, branch, middle, normed_mlp = attend(
        queries, halo, key_value, query_ids, key_ids, w_o, layer_in, d_gains, attn_scale
    )

    half = row_count // 2
    from_x, from_y = swap(normed_mlp, "x"), swap(normed_mlp, "y")
    normed_far = jnp.concatenate([swap(from_x[:half], "y"), swap(from_y[half:], "x")])
    normed_near = jnp.concatenate([from_x, from_y])
    normed_all = [with_core(part) for part in (normed_mlp, normed_near, normed_far)]
    far_result = mlp_forward(normed_all[2], gate_up, down, normed_all[2])
    far_sum = core_sum(far_result[3]).astype(BF)
    near_result = mlp_forward(normed_all[1], gate_up, down, far_sum)
    to_x, to_y = sum_near(near_result[3], *send_far(far_sum))
    own_result = mlp_forward(normed_all[0], gate_up, down, to_x)
    mixed = sum_own(own_result[3], to_x, to_y)
    layer_out = middle + norm_gain(mixed, d_gains[3:4])

    _, pullback = jax.vjp(norm_gain, mixed, d_gains[3:4])
    grad_mixed, mixed_terms = pullback(grad_out.astype(F32))
    grad_mixed = grad_mixed.astype(BF)
    from_x, from_y = swap(grad_mixed, "x"), swap(grad_mixed, "y")
    grad_own = with_core(grad_mixed)
    own_grads = mlp_backward(grad_own, own_result[1], own_result[2], gate_up, down, down)
    from_x, from_y = lax.optimization_barrier((from_x, from_y, own_grads[1]))[:2]
    grad_far = with_core(jnp.concatenate([swap(from_x[:half], "y"), swap(from_y[half:], "x")]))
    grad_near = with_core(jnp.concatenate([from_x, from_y]))
    grad_down_terms = down_terms(
        [r[0] for r in (own_result, near_result, far_result)],
        [grad_own, grad_near, grad_far],
        hidden_own,
    )
    grad_down = lax.psum_scatter(grad_down_terms, "g", scatter_dimension=0, tiled=True)
    far_grads = mlp_backward(
        grad_far, far_result[1], far_result[2], gate_up, down, grad_down_terms
    )
    far_sum = core_sum(far_grads[1]).astype(BF)
    near_grads = mlp_backward(grad_near, near_result[1], near_result[2], gate_up, down, far_sum)
    to_x, to_y = sum_near(near_grads[1], *send_far(far_sum))
    gate_up_terms = gate_terms(
        normed_all, [g[0] for g in (own_grads, near_grads, far_grads)], groups, to_x
    )
    grad_normed_mlp = sum_own(own_grads[1], to_x, to_y)
    grad_normed_mlp = after(grad_normed_mlp, gate_up_terms, grad_down)
    term = gate_up_terms.reshape(groups * members * shard_rows, 2 * hidden_pad)
    gate_up_share = lax.psum_scatter(after(term, grad_down), "g", scatter_dimension=0, tiled=True)
    term = gate_up_share.reshape(members, shard_rows, 2 * hidden_pad)
    term = lax.all_to_all(term, PLANE, split_axis=0, concat_axis=0, tiled=True)

    def collect(cut):
        cut = cut[:, :, :hidden_own].reshape(2, members // 2, shard_rows, groups, piece)
        return cut.transpose(2, 0, 3, 1, 4).reshape(shard_rows, hidden_all).astype(F32)

    grad_w_gate = collect(term[:, :, :hidden_pad])
    grad_w_up = collect(term[:, :, hidden_pad:])

    grad_middle, grad_branch, grad_queries, grad_key_value, returned, terms = attend_backward(
        grad_normed_mlp, grad_out, middle, branch, d_gains, w_o,
        queries, halo, key_value, query_ids, key_ids, log_total, attn_scale,
    )
    returned = lax.ppermute(returned, ("g", "y", "c"), [(i + 1, i) for i in range(seq_size - 1)])
    out_terms = over_rows(attended, grad_branch).astype(BF)
    out_terms = out_terms.reshape(2, groups, 2, 2, w_out.shape[0], width)
    out_terms = plane_terms(fold(out_terms, "c", 3))
    grad_in, mine, sent = project_backward(
        places, grad_queries, grad_key_value, returned, query_raw, key_raw,
        cosine_table, sine_table, h_gains, normed, mine, other,
        grad_middle, layer_in, d_gains, terms, mixed_terms, shard_rows,
    )
    mine = (mine.astype(F32) + swap(sent, "c").astype(F32)).astype(BF)
    qkv_terms = plane_terms(mine.reshape(2, groups, 2, 2 * shard_rows, half_cols))
    qkv_terms = qkv_terms.reshape(groups, -1, width)
    share = jnp.concatenate([out_terms, qkv_terms], axis=1)
    share = jnp.pad(share, ((0, 0), (0, -share.shape[1] % 32), (0, 0))).reshape(-1, width)
    share = lax.psum_scatter(after(share, gate_up_share), "g", scatter_dimension=0, tiled=True)
    grad_w_out = share[: w_out.shape[0]].astype(F32)
    qkv_rows = qkv_terms.shape[1]
    share = share[w_out.shape[0] :][:qkv_rows].reshape(2, shard_rows, half_cols)
    mine = lax.dynamic_index_in_dim(share, core, 0, keepdims=False)
    other = lax.dynamic_index_in_dim(share, 1 - core, 0, keepdims=False)
    first, second = in_order(mine, swap(other, "c"), core).astype(F32)
    half = q_cols // 2
    d_terms = first[:, half + k_cols :]
    return (
        layer_out.astype(BF)[None],
        grad_in[None],
        jnp.concatenate([first[:, :half], second[:, :half]], axis=1),
        first[:, half : half + k_cols],
        second[:, half : half + k_cols],
        grad_w_out,
        grad_w_gate,
        grad_w_up,
        grad_down.astype(F32),
        d_terms[:, 0],
        d_terms[:, 1],
        d_terms[:, 2],
        d_terms[:, 3],
        d_terms[:head_rows, 4],
        d_terms[:head_rows, 5],
    )


def solution(mesh):
    batch, seq = mesh.devices.shape
    fine = Mesh(mesh.devices.reshape(batch, seq // 4, 2, 2), ALL)
    rows = ("g", "y", "c")
    return jax.shard_map(
        on_device,
        mesh=fine,
        in_specs=(P("x", rows, None),) * 2
        + (P("x", None),)
        + (P(ALL, None),) * 7
        + (P(ALL),) * 6,
        out_specs=(P("x", rows, None),) * 2 + (P(ALL, None),) * 7 + (P(ALL),) * 6,
        check_vma=False,
    )
```

```python
import functools

import jax
import jax.numpy as jnp
from jax import lax
from jax.experimental import pallas as pl
from jax.experimental.pallas import tpu as pltpu
from jax.sharding import Mesh
from jax.sharding import PartitionSpec as P

HEAD = 256
WINDOW = 512
EPSILON = 1e-06
ROPE_BASE = 10000.0
ALL = ("x", "g", "y", "c")
PLANE = ("x", "y", "c")
BF = jnp.bfloat16
F32 = jnp.float32


def norm_gain(values, gain_vec):
    return (
        values * lax.rsqrt(jnp.mean(values * values, axis=-1, keepdims=True) + EPSILON) * gain_vec
    )


def rope_tables(first_row, row_count, head_size):
    places = (first_row + jnp.arange(row_count, dtype=jnp.int32)).astype(F32)
    frequency = ROPE_BASE ** (-(jnp.arange(head_size // 2, dtype=F32) * 2.0) / head_size)
    angles = places[:, None] * frequency[None, :]
    return (jnp.cos(angles), jnp.sin(angles))


def matmul(left_side, right_side):
    return jnp.dot(left_side, right_side, preferred_element_type=F32)


def over_rows(left_side, right_side):
    return lax.dot_general(
        left_side, right_side, (((0,), (0,)), ((), ())), preferred_element_type=F32
    )


def by_transpose(left_side, right_side):
    return lax.dot_general(
        left_side, right_side, (((1,), (1,)), ((), ())), preferred_element_type=F32
    )


def swap(array, axis):
    return lax.ppermute(array, axis, [(0, 1), (1, 0)])


GELU_A = 0.7978845608028654
GELU_B = 0.044715
TILE = 512
PARAMS = pltpu.CompilerParams(vmem_limit_bytes=58 << 20)


def whole_block(shape):
    return pl.BlockSpec(shape, lambda i: (0,) * len(shape), pipeline_mode=pl.Buffered(1))


def row_block(rows, columns):
    return pl.BlockSpec((rows, columns), lambda i: (i, 0))


def mlp_forward_kernel(normed, gate_up, down, _, hidden, gelu, slope, mixed):
    own = down.shape[0]
    raw = matmul(normed[...], gate_up[...])
    gate_raw, up_raw = raw[:, :own], raw[:, own:]
    square = gate_raw * gate_raw
    bend = jnp.tanh(GELU_A * (gate_raw + GELU_B * square * gate_raw))
    half = 0.5 + 0.5 * bend
    active = gate_raw * half
    turn = 0.5 * gate_raw * (1.0 - bend * bend) * (GELU_A * (1.0 + 3.0 * GELU_B * square))
    low = (active * up_raw).astype(BF)
    hidden[...] = low
    gelu[...] = active.astype(BF)
    slope[...] = ((half + turn) * up_raw).astype(BF)
    mixed[...] = matmul(low, down[...]).astype(BF)


def mlp_forward(normed, gate_up, down, earlier):
    rows, width = normed.shape
    own = down.shape[0]
    flat = jax.ShapeDtypeStruct((rows, own), BF)
    return pl.pallas_call(
        mlp_forward_kernel,
        grid=(rows // TILE,),
        in_specs=[
            row_block(TILE, width),
            whole_block(gate_up.shape),
            whole_block(down.shape),
            pl.BlockSpec(memory_space=pl.ANY),
        ],
        out_specs=[row_block(TILE, own)] * 3 + [row_block(TILE, width)],
        out_shape=[flat, flat, flat, jax.ShapeDtypeStruct((rows, width), BF)],
        compiler_params=PARAMS,
        cost_estimate=pl.CostEstimate(
            flops=6 * rows * width * own, bytes_accessed=rows * (4 * width + 6 * own), transcendentals=0
        ),
    )(normed, gate_up, down, earlier)


def mlp_backward_kernel(grad_mixed, gelu, slope, gate_up, down, _, grad_raw, grad_normed):
    own = down.shape[0]
    grad_hidden = by_transpose(grad_mixed[...], down[...])
    grad_gate = (grad_hidden * slope[...].astype(F32)).astype(BF)
    grad_up = (grad_hidden * gelu[...].astype(F32)).astype(BF)
    grad_raw[:, :own] = grad_gate
    grad_raw[:, own:] = grad_up
    grad_normed[...] = (
        by_transpose(grad_gate, gate_up[:, :own]) + by_transpose(grad_up, gate_up[:, own:])
    ).astype(BF)


def mlp_backward(grad_mixed, gelu, slope, gate_up, down, earlier):
    rows, width = grad_mixed.shape
    own = down.shape[0]
    return pl.pallas_call(
        mlp_backward_kernel,
        grid=(rows // TILE,),
        in_specs=[
            row_block(TILE, width),
            row_block(TILE, own),
            row_block(TILE, own),
            whole_block(gate_up.shape),
            whole_block(down.shape),
            pl.BlockSpec(memory_space=pl.ANY),
        ],
        out_specs=[row_block(TILE, 2 * own), row_block(TILE, width)],
        out_shape=[
            jax.ShapeDtypeStruct((rows, 2 * own), BF),
            jax.ShapeDtypeStruct((rows, width), BF),
        ],
        compiler_params=PARAMS,
        cost_estimate=pl.CostEstimate(
            flops=6 * rows * width * own, bytes_accessed=rows * (4 * width + 8 * own), transcendentals=0
        ),
    )(grad_mixed, gelu, slope, gate_up, down, earlier)


def down_terms_kernel(*refs):
    *ins, out = refs
    half = len(ins) // 2
    total = over_rows(ins[0][...], ins[half][...])
    for left, right in zip(ins[1:half], ins[half + 1 :]):
        total = total + over_rows(left[...], right[...])
    out[...] = total.astype(BF)


def down_terms(hidden, grad_mixed, keep):
    own, width = hidden[0].shape[1], grad_mixed[0].shape[1]
    rows = sum(part.shape[0] for part in hidden)
    return pl.pallas_call(
        down_terms_kernel,
        grid=(own // 128,),
        in_specs=[pl.BlockSpec((part.shape[0], 128), lambda i: (0, i)) for part in hidden]
        + [whole_block(part.shape) for part in grad_mixed],
        out_specs=row_block(128, width),
        out_shape=jax.ShapeDtypeStruct((keep, width), BF),
        compiler_params=PARAMS,
        cost_estimate=pl.CostEstimate(
            flops=2 * rows * width * own, bytes_accessed=2 * rows * (width + own), transcendentals=0
        ),
    )(*hidden, *grad_mixed)


def gate_terms_kernel(*refs):
    *ins, _, out = refs
    half = len(ins) // 2
    total = over_rows(ins[0][...], ins[half][...])
    for left, right in zip(ins[1:half], ins[half + 1 :]):
        total = total + over_rows(left[...], right[...])
    total = total.astype(BF)
    groups, sides, rows, _ = out.shape
    for side in range(sides):
        for group in range(groups):
            first = (side * groups + group) * rows
            out[group, side] = total[first : first + rows]


def gate_terms(normed, grad_raw, groups, earlier):
    width, both = normed[0].shape[1], grad_raw[0].shape[1]
    rows = sum(part.shape[0] for part in normed)
    shape = (groups, 2, width // (2 * groups))
    return pl.pallas_call(
        gate_terms_kernel,
        grid=(both // 256,),
        in_specs=[whole_block(part.shape) for part in normed]
        + [pl.BlockSpec((part.shape[0], 256), lambda i: (0, i)) for part in grad_raw]
        + [pl.BlockSpec(memory_space=pl.ANY)],
        out_specs=pl.BlockSpec(shape + (256,), lambda i: (0, 0, 0, i)),
        out_shape=jax.ShapeDtypeStruct(shape + (both,), BF),
        compiler_params=PARAMS,
        cost_estimate=pl.CostEstimate(
            flops=2 * rows * width * both, bytes_accessed=2 * rows * (width + both), transcendentals=0
        ),
    )(*normed, *grad_raw, earlier)


def after(value, *earlier):
    return lax.optimization_barrier((value, *earlier))[0]


def with_core(part):
    return jnp.concatenate([part, swap(part, "c")])


def core_sum(part):
    half = part.shape[0] // 2
    return part[:half].astype(F32) + swap(part[half:], "c").astype(F32)


def send_far(far):
    half = far.shape[0] // 2
    return swap(far[:half], "y"), swap(far[half:], "x")


def sum_near(near, top, low):
    near = core_sum(near)
    rows = near.shape[0] // 2
    half = rows // 2
    to_x = jnp.concatenate([near[:half] + top, near[half:rows]]).astype(BF)
    to_y = jnp.concatenate([near[rows : rows + half], near[rows + half :] + low]).astype(BF)
    return to_x, to_y


def sum_own(own, to_x, to_y):
    return core_sum(own) + swap(to_x, "x").astype(F32) + swap(to_y, "y").astype(F32)


def in_order(own, other, place):
    both = jnp.concatenate([own[None], other[None], own[None]])
    return lax.dynamic_slice_in_dim(both, place, 2, 0)


def group_gather(own):
    size = lax.axis_size("g")
    parts = [own] + [
        lax.ppermute(own, "g", [((i + k) % size, i) for i in range(size)]) for k in range(1, size)
    ]
    both = jnp.stack(parts + parts[:-1])
    place = lax.axis_index("g")
    return lax.dynamic_slice_in_dim(both, lax.rem(size - place, size), size, 0)


def plane_weights(blocks):
    x, y = lax.axis_index("x"), lax.axis_index("y")
    half = blocks.shape[0] // 2
    first, second = blocks[:half], blocks[half:]
    first = in_order(first, swap(first, "x"), x)
    second = in_order(second, swap(second, "y"), y)
    first = in_order(first, swap(first, "y"), y)
    second = in_order(second, swap(second, "x"), x)
    first = first.transpose(1, 2, 0, 3, 4)
    second = second.transpose(0, 2, 1, 3, 4)
    return jnp.concatenate([first, second], axis=1)


def group_terms(term):
    size = lax.axis_size("g")
    place = lax.axis_index("g")
    total = lax.dynamic_index_in_dim(term, place, 0, keepdims=False).astype(F32)
    for k in range(1, size):
        chunk = lax.dynamic_index_in_dim(term, lax.rem(place + k, size), 0, keepdims=False)
        pairs = [(i, (i + k) % size) for i in range(size)]
        total = total + lax.ppermute(chunk, "g", pairs).astype(F32)
    return total


def fold(term, axis, dim):
    place = lax.axis_index(axis)
    mine = lax.dynamic_index_in_dim(term, place, dim, keepdims=False)
    other = lax.dynamic_index_in_dim(term, 1 - place, dim, keepdims=False)
    return (mine.astype(F32) + swap(other.astype(BF), axis).astype(F32)).astype(BF)


def plane_terms(term):
    half = term.shape[1] // 2
    first = fold(fold(term[:, :half], "x", 0), "y", 1)
    second = fold(fold(term[:, half:], "y", 2), "x", 0)
    return jnp.concatenate([first, second])


def rms_scale(values):
    return lax.rsqrt(jnp.mean(values * values, axis=-1, keepdims=True) + EPSILON)


def rms_backward(values, scale, gain, grad):
    weighted = grad * gain
    inner = jnp.mean(weighted * values, axis=-1, keepdims=True)
    terms = jnp.sum(grad * values * scale, axis=0, keepdims=True)
    return weighted * scale - values * (scale * scale * scale * inner), terms


def turn_forward(values, cosine, sine):
    half = cosine.shape[1]
    low, high = values[:, :half], values[:, half:]
    return jnp.concatenate([low * cosine - high * sine, high * cosine + low * sine], axis=1)


def turn_backward(grad, cosine, sine):
    half = cosine.shape[1]
    low, high = grad[:, :half], grad[:, half:]
    return jnp.concatenate([low * cosine + high * sine, high * cosine - low * sine], axis=1)


def gain_places(width, columns, shard_rows):
    heads = columns // (width // shard_rows)
    row = lax.broadcasted_iota(jnp.int32, (width, columns), 0)
    column = lax.broadcasted_iota(jnp.int32, (width, columns), 1)
    place = (column // heads) * shard_rows + lax.rem(column, heads)
    return jnp.where(row == place, 1.0, 0.0).astype(BF)


def project_kernel(
    shard_rows, core, tokens, earlier, own, other, cosine, sine,
    normed, normed_earlier, query_raw, key_raw, queries, keys, values, d_gains, h_gains,
):
    rows, width = tokens.shape
    pad, k_cols = earlier.shape[0], key_raw.shape[1]
    half = query_raw.shape[1] // 2
    first_is_own = core[0] == 0
    block = jnp.where(
        first_is_own, own[:, half + k_cols :].astype(F32), other[:, half + k_cols :].astype(F32)
    )
    flat = block.T[:8]
    d_gains[...] = flat
    chosen = matmul(flat.astype(BF), gain_places(width, k_cols, shard_rows))
    h_gains[...] = chosen
    before = earlier[...].astype(F32)
    low_before = (before * rms_scale(before) * flat[0:1]).astype(BF)
    normed_earlier[...] = low_before
    inputs = tokens[...].astype(F32)
    low = (inputs * rms_scale(inputs) * flat[0:1]).astype(BF)
    normed[...] = low
    raw_own = matmul(low, own[:, : half + k_cols])
    raw_other = matmul(low, other[:, : half + k_cols])
    before_own = matmul(low_before, own[:, half : half + k_cols])
    before_other = matmul(low_before, other[:, half : half + k_cols])
    first = jnp.where(first_is_own, raw_own, raw_other)
    second = jnp.where(first_is_own, raw_other, raw_own)
    raw_query = jnp.concatenate([first[:, :half], second[:, :half]], axis=1)
    query_raw[...] = raw_query
    values[:pad] = jnp.where(first_is_own, before_other, before_own).astype(BF)
    values[pad:] = second[:, half:].astype(BF)
    raw_before = jnp.where(first_is_own, before_own, before_other)
    for raw, at in ((raw_before, slice(0, pad)), (first[:, half:], slice(pad, pad + rows))):
        key_raw[at] = raw
        part = raw * rms_scale(raw) * chosen[5:6]
        keys[at] = turn_forward(part, cosine[at], sine[at]).astype(BF)
    cos, sin = cosine[pad:], sine[pad:]
    for head in range(2 * half // k_cols):
        at = slice(head * k_cols, (head + 1) * k_cols)
        part = raw_query[:, at]
        part = part * rms_scale(part) * chosen[4:5]
        queries[:, at] = turn_forward(part, cos, sin).astype(BF)


def project(core, tokens, earlier, own, other, cosine, sine, shard_rows, q_cols, k_cols):
    rows, width = tokens.shape
    seen = rows + earlier.shape[0]
    vmem = pl.BlockSpec(memory_space=pltpu.VMEM)
    return pl.pallas_call(
        functools.partial(project_kernel, shard_rows),
        in_specs=[pl.BlockSpec(memory_space=pltpu.SMEM)] + [vmem] * 6,
        out_specs=[vmem] * 9,
        out_shape=[
            jax.ShapeDtypeStruct((rows, width), BF),
            jax.ShapeDtypeStruct(earlier.shape, BF),
            jax.ShapeDtypeStruct((rows, q_cols), F32),
            jax.ShapeDtypeStruct((seen, k_cols), F32),
            jax.ShapeDtypeStruct((rows, q_cols), BF),
            jax.ShapeDtypeStruct((seen, k_cols), BF),
            jax.ShapeDtypeStruct((seen, k_cols), BF),
            jax.ShapeDtypeStruct((8, width), F32),
            jax.ShapeDtypeStruct((8, k_cols), F32),
        ],
        compiler_params=PARAMS,
        cost_estimate=pl.CostEstimate(
            flops=2 * rows * width * (q_cols + 4 * k_cols), bytes_accessed=16 * rows * width, transcendentals=0
        ),
    )(core, tokens, earlier, own, other, cosine, sine)


def tile_mask(first, rows, first_key, keys, query_ids, key_ids, pad):
    query_place = pad + first + lax.broadcasted_iota(jnp.int32, (rows, keys), 0)
    key_place = first_key + lax.broadcasted_iota(jnp.int32, (rows, keys), 1)
    distance = query_place - key_place
    same_doc = query_ids[first : first + rows, :] == key_ids[:, first_key : first_key + keys]
    return (distance >= 0) & (distance < WINDOW) & same_doc


def attend_kernel(
    scale, queries, keys, values, query_ids, key_ids, w_o, tokens, d_gains,
    attended, log_total, branch, middle, normed_mlp,
):
    rows, q_cols = queries.shape
    pad, k_cols = keys.shape[0] - rows, keys.shape[1]
    tile = rows // 2
    span = pad + tile
    lane = lax.broadcasted_iota(jnp.int32, (tile, 128), 1)
    for first in (0, tile):
        at = slice(first, first + tile)
        seen = slice(first, first + span)
        allowed = tile_mask(first, tile, first, span, query_ids, key_ids, pad)
        logs = jnp.zeros((tile, 128), F32)
        for head in range(q_cols // k_cols):
            columns = slice(head * k_cols, (head + 1) * k_cols)
            scores = by_transpose(queries[at, columns], keys[seen]) * scale
            scores = jnp.where(allowed, scores, -1e30)
            row_max = jnp.max(scores, axis=-1, keepdims=True)
            weights = jnp.exp(scores - row_max)
            row_total = jnp.sum(weights, axis=-1, keepdims=True)
            probabilities = (weights * (1.0 / row_total)).astype(BF)
            attended[at, columns] = matmul(probabilities, values[seen]).astype(BF)
            logs = jnp.where(lane == head, row_max + jnp.log(row_total), logs)
        log_total[at] = logs
    out = matmul(attended[...], w_o[...])
    branch[...] = out
    total = tokens[...].astype(F32) + out * rms_scale(out) * d_gains[1:2]
    middle[...] = total
    normed_mlp[...] = (total * rms_scale(total) * d_gains[2:3]).astype(BF)


def attend(queries, keys, values, query_ids, key_ids, w_o, tokens, d_gains, scale):
    rows, q_cols = queries.shape
    width = tokens.shape[1]
    vmem = pl.BlockSpec(memory_space=pltpu.VMEM)
    return pl.pallas_call(
        functools.partial(attend_kernel, scale),
        in_specs=[vmem] * 8,
        out_specs=[vmem] * 5,
        out_shape=[
            jax.ShapeDtypeStruct((rows, q_cols), BF),
            jax.ShapeDtypeStruct((rows, 128), F32),
            jax.ShapeDtypeStruct((rows, width), F32),
            jax.ShapeDtypeStruct((rows, width), F32),
            jax.ShapeDtypeStruct((rows, width), BF),
        ],
        compiler_params=PARAMS,
        cost_estimate=pl.CostEstimate(
            flops=2 * rows * q_cols * (width + 2 * keys.shape[0]), bytes_accessed=20 * rows * width, transcendentals=0
        ),
    )(queries, keys, values, query_ids, key_ids, w_o, tokens, d_gains)


def attend_backward_kernel(
    scale, grad_normed_mlp, cotangent, middle, branch, d_gains, w_o,
    queries, keys, values, query_ids, key_ids, log_total,
    grad_middle, grad_branch, grad_queries, grad_keys, grad_values, terms, grad_attended,
):
    rows, q_cols = queries.shape
    pad, k_cols = keys.shape[0] - rows, keys.shape[1]
    total = middle[...]
    from_mlp, mlp_terms = rms_backward(total, rms_scale(total), d_gains[2:3], grad_normed_mlp[...])
    grad_total = cotangent[...].astype(F32) + from_mlp
    grad_middle[...] = grad_total
    out = branch[...]
    grad_out, out_terms = rms_backward(out, rms_scale(out), d_gains[1:2], grad_total)
    low = grad_out.astype(BF)
    grad_branch[...] = low
    terms[...] = jnp.concatenate([out_terms, mlp_terms, jnp.zeros((6, out.shape[1]), F32)], axis=0)
    grad_attended[...] = by_transpose(low, w_o[...]).astype(BF)
    grad_keys[...] = jnp.zeros_like(grad_keys)
    grad_values[...] = jnp.zeros_like(grad_values)
    tile = rows // 2
    span = pad + tile
    for first in (0, tile):
        at = slice(first, first + tile)
        seen = slice(first, first + span)
        allowed = tile_mask(first, tile, first, span, query_ids, key_ids, pad)
        key_total = jnp.zeros((span, k_cols), F32)
        value_total = jnp.zeros((span, k_cols), F32)
        for head in range(q_cols // k_cols):
            columns = slice(head * k_cols, (head + 1) * k_cols)
            query = queries[at, columns]
            grad = grad_attended[at, columns]
            scores = by_transpose(query, keys[seen]) * scale
            probabilities = jnp.where(
                allowed, jnp.exp(scores - log_total[at, head : head + 1]), 0.0
            )
            grad_prob = by_transpose(grad, values[seen])
            inner = jnp.sum(probabilities * grad_prob, axis=-1, keepdims=True)
            grad_score = (probabilities * (grad_prob - inner)).astype(BF)
            grad_queries[at, columns] = matmul(grad_score, keys[seen]) * scale
            key_total = key_total + over_rows(grad_score, query)
            value_total = value_total + over_rows(probabilities.astype(BF), grad)
        grad_keys[seen] = grad_keys[seen] + key_total * scale
        grad_values[seen] = grad_values[seen] + value_total


def attend_backward(
    grad_normed_mlp, cotangent, middle, branch, d_gains, w_o,
    queries, keys, values, query_ids, key_ids, log_total, scale,
):
    rows, q_cols = queries.shape
    width = middle.shape[1]
    vmem = pl.BlockSpec(memory_space=pltpu.VMEM)
    return pl.pallas_call(
        functools.partial(attend_backward_kernel, scale),
        in_specs=[vmem] * 12,
        out_specs=[vmem] * 6,
        out_shape=[
            jax.ShapeDtypeStruct((rows, width), F32),
            jax.ShapeDtypeStruct((rows, width), BF),
            jax.ShapeDtypeStruct((rows, q_cols), F32),
            jax.ShapeDtypeStruct(keys.shape, F32),
            jax.ShapeDtypeStruct(keys.shape, F32),
            jax.ShapeDtypeStruct((8, width), F32),
        ],
        scratch_shapes=[pltpu.VMEM((rows, q_cols), BF)],
        compiler_params=PARAMS,
        cost_estimate=pl.CostEstimate(
            flops=2 * rows * q_cols * (width + 5 * keys.shape[0]), bytes_accessed=30 * rows * width, transcendentals=0
        ),
    )(
        grad_normed_mlp, cotangent, middle, branch, d_gains, w_o,
        queries, keys, values, query_ids, key_ids, log_total,
    )


def project_backward_kernel(
    shard_rows, core, grad_queries, grad_keys, grad_values, query_raw, key_raw, cosine, sine,
    h_gains, normed, normed_earlier, own, other, tokens, earlier, d_gains, terms, mixed_terms,
    grad_normed, returned, mine, sent,
):
    rows, width = tokens.shape
    pad, k_cols = earlier.shape[0], key_raw.shape[1]
    half = query_raw.shape[1] // 2
    cols = half + k_cols
    first_is_own = core[0] == 0
    cos, sin = cosine[pad:], sine[pad:]
    query_terms = jnp.zeros((1, k_cols), F32)
    parts = []
    for head in range(2 * half // k_cols):
        at = slice(head * k_cols, (head + 1) * k_cols)
        raw = query_raw[:, at]
        grad = turn_backward(grad_queries[:, at], cos, sin)
        grad, term = rms_backward(raw, rms_scale(raw), h_gains[4:5], grad)
        query_terms = query_terms + term
        parts.append(grad.astype(BF))
    raw = key_raw[...]
    grad = turn_backward(grad_keys[...], cosine[...], sine[...])
    grad, key_terms = rms_backward(raw, rms_scale(raw), h_gains[5:6], grad)
    grad_key, grad_value = grad.astype(BF), grad_values[...].astype(BF)
    returned[:, :k_cols] = grad_key[:pad]
    returned[:, k_cols:] = grad_value[:pad]
    kv_own = jnp.where(first_is_own, grad_key, grad_value)
    kv_other = jnp.where(first_is_own, grad_value, grad_key)
    both = len(parts) // 2
    first = jnp.concatenate(parts[:both], axis=1)
    second = jnp.concatenate(parts[both:], axis=1)
    q_own = jnp.where(first_is_own, first, second)
    q_other = jnp.where(first_is_own, second, first)
    grad_own = jnp.concatenate([q_own, kv_own[pad:]], axis=1)
    grad_other = jnp.concatenate([q_other, kv_other[pad:]], axis=1)
    total = by_transpose(grad_own, own[:, :cols]) + by_transpose(grad_other, other[:, :cols])
    grad_normed[...] = total
    values = tokens[...].astype(F32)
    in_terms = jnp.sum(total * values * rms_scale(values), axis=0, keepdims=True)
    total = by_transpose(kv_own[:pad], own[:, half:cols])
    total = total + by_transpose(kv_other[:pad], other[:, half:cols])
    values = earlier[...].astype(F32)
    in_terms = in_terms + jnp.sum(total * values * rms_scale(values), axis=0, keepdims=True)
    low, low_before = normed[...], normed_earlier[...]
    for out, query, key_value in ((mine, q_own, kv_own), (sent, q_other, kv_other)):
        out[:, :half] = over_rows(low, query).astype(BF)
        out[:, half:cols] = (
            over_rows(low, key_value[pad:]) + over_rows(low_before, key_value[:pad])
        ).astype(BF)
    heads = jnp.concatenate([query_terms, key_terms, jnp.zeros((6, k_cols), F32)], axis=0)
    placed = by_transpose(heads.astype(BF), gain_places(width, k_cols, shard_rows))
    block = jnp.concatenate(
        [in_terms, terms[0:2], mixed_terms[0:1], placed[0:2], jnp.zeros((122, width), F32)], axis=0
    ).T
    mine[:, cols:] = jnp.where(first_is_own, block, 0.0).astype(BF)
    sent[:, cols:] = jnp.where(first_is_own, 0.0, block).astype(BF)


def project_backward(
    core, grad_queries, grad_keys, grad_values, query_raw, key_raw, cosine, sine,
    h_gains, normed, normed_earlier, own, other, tokens, earlier, d_gains, terms, mixed_terms,
    shard_rows,
):
    rows, width = tokens.shape
    pad, k_cols = earlier.shape[0], key_raw.shape[1]
    vmem = pl.BlockSpec(memory_space=pltpu.VMEM)
    return pl.pallas_call(
        functools.partial(project_backward_kernel, shard_rows),
        in_specs=[pl.BlockSpec(memory_space=pltpu.SMEM)] + [vmem] * 17,
        out_specs=[vmem] * 4,
        out_shape=[
            jax.ShapeDtypeStruct((rows, width), F32),
            jax.ShapeDtypeStruct((pad, 2 * k_cols), BF),
            jax.ShapeDtypeStruct(own.shape, BF),
            jax.ShapeDtypeStruct(own.shape, BF),
        ],
        compiler_params=PARAMS,
        cost_estimate=pl.CostEstimate(
            flops=9 * rows * width * own.shape[1], bytes_accessed=30 * rows * width, transcendentals=0
        ),
    )(
        core, grad_queries, grad_keys, grad_values, query_raw, key_raw, cosine, sine,
        h_gains, normed, normed_earlier, own, other, tokens, earlier, d_gains, terms, mixed_terms,
    )


def grad_tokens_kernel(core, returned, grad_normed, own, other, tokens, d_gains, grad_middle, out):
    k_cols = returned.shape[1] // 2
    cols = own.shape[1] - 128
    half = cols - k_cols
    first_is_own = core[0] == 0
    grad_key, grad_value = returned[:, :k_cols], returned[:, k_cols:]
    kv_own = jnp.where(first_is_own, grad_key, grad_value)
    kv_other = jnp.where(first_is_own, grad_value, grad_key)
    total = grad_normed[...] + by_transpose(kv_own, own[:, half:cols])
    total = total + by_transpose(kv_other, other[:, half:cols])
    values = tokens[...].astype(F32)
    from_attn, _ = rms_backward(values, rms_scale(values), d_gains[0:1], total)
    out[...] = (grad_middle[...] + from_attn).astype(BF)


def grad_tokens(core, returned, grad_normed, own, other, tokens, d_gains, grad_middle):
    vmem = pl.BlockSpec(memory_space=pltpu.VMEM)
    return pl.pallas_call(
        grad_tokens_kernel,
        in_specs=[pl.BlockSpec(memory_space=pltpu.SMEM)] + [vmem] * 7,
        out_specs=vmem,
        out_shape=jax.ShapeDtypeStruct(tokens.shape, BF),
        compiler_params=PARAMS,
        cost_estimate=pl.CostEstimate(
            flops=2 * tokens.size * returned.shape[1], bytes_accessed=12 * tokens.size, transcendentals=0
        ),
    )(core, returned, grad_normed, own, other, tokens, d_gains, grad_middle)


def on_device(
    tokens,
    cotangent,
    doc_ids,
    w_query,
    w_key,
    w_value,
    w_out,
    w_gate,
    w_up,
    w_down,
    gain_attn_in,
    gain_attn_out,
    gain_mlp_in,
    gain_mlp_out,
    gain_query,
    gain_key,
):
    row_count = tokens.shape[1]
    width = tokens.shape[2]
    groups = lax.axis_size("g")
    members = lax.axis_size(PLANE)
    shard_rows = w_query.shape[0]
    head_rows = gain_query.shape[0]
    hidden_all = w_gate.shape[1]
    hidden_own = hidden_all // members
    hidden_pad = -(-hidden_own // 128) * 128
    piece = hidden_own // groups
    q_cols, k_cols = w_query.shape[1], w_key.shape[1]
    attn_scale = HEAD ** (-0.5)

    def gain_columns(d_gains, h_gains):
        columns = list(d_gains) + [
            jnp.pad(h, ((0, 0), (0, shard_rows - head_rows))) for h in h_gains
        ]
        block = jnp.stack(columns, axis=-1)
        return jnp.pad(block, ((0, 0), (0, 0), (0, 128 - len(columns))))

    seq_place = lax.axis_index(("g", "y", "c"))
    seq_size = lax.axis_size(("g", "y", "c"))
    before = lax.ppermute(tokens[0], ("g", "y", "c"), [(i, i + 1) for i in range(seq_size - 1)])

    def spread(weight):
        cut = weight.reshape(shard_rows, 2, groups, members // 2, piece)
        cut = cut.transpose(1, 3, 0, 2, 4).reshape(members, shard_rows, hidden_own)
        return jnp.pad(cut, ((0, 0), (0, 0), (0, hidden_pad - hidden_own)))

    sent = jnp.concatenate([spread(w_gate), spread(w_up)], axis=2)
    core = lax.axis_index("c")
    half_cols = q_cols // 2 + k_cols + 128
    gains = gain_columns(
        [g[None] for g in (gain_attn_in, gain_attn_out, gain_mlp_in, gain_mlp_out)],
        [gain_query[None], gain_key[None]],
    )
    halves = jnp.stack(
        [
            jnp.concatenate([w_query[:, : q_cols // 2], w_key, gains[0]], axis=1),
            jnp.concatenate([w_query[:, q_cols // 2 :], w_value, jnp.zeros_like(gains[0])], axis=1),
        ]
    )
    mine = lax.dynamic_index_in_dim(halves, core, 0, keepdims=False)
    other = lax.dynamic_index_in_dim(halves, 1 - core, 0, keepdims=False)
    mine = in_order(mine, swap(other, "c"), core).reshape(2 * shard_rows, half_cols)
    mine, before, sent = lax.optimization_barrier((mine, before, sent))
    sent = lax.all_to_all(sent, PLANE, split_axis=0, concat_axis=0, tiled=True)
    sent = sent.reshape(members * shard_rows, 2 * hidden_pad)
    mine, sent = lax.optimization_barrier((group_gather(mine), sent))
    mine = plane_weights(mine).reshape(width, half_cols)
    other = swap(mine, "c")

    down = lax.all_gather(jnp.concatenate([w_down, w_out]), "g", axis=0)
    w_o = down[:, w_down.shape[0] :]
    down = down[:, : w_down.shape[0]].reshape(-1, width)
    down = jnp.pad(down, ((0, hidden_pad - hidden_own), (0, 0)))

    both = lax.all_gather(sent, "g", axis=0)
    both = both.reshape(groups, 2, members // 2 * shard_rows, 2 * hidden_pad)
    gate_up = both.transpose(1, 0, 2, 3).reshape(width, 2 * hidden_pad)

    first_row = seq_place * row_count
    ids_all = doc_ids[0]
    ids_own = lax.dynamic_slice_in_dim(ids_all, first_row, row_count, 0)
    ids_prev = lax.dynamic_slice_in_dim(
        ids_all, jnp.maximum(first_row - row_count, 0), row_count, 0
    )
    ids_prev = jnp.where(seq_place > 0, ids_prev, -1)
    ids_pad = jnp.concatenate([ids_prev, ids_own])
    query_ids, key_ids = ids_own[:, None], ids_pad[None]
    cosine_table, sine_table = rope_tables(first_row - row_count, 2 * row_count, HEAD)
    places = jnp.full((1,), core, jnp.int32)
    layer_in, grad_out = tokens[0], cotangent[0]

    normed, normed_before, query_raw, key_raw, queries, keys, values, d_gains, h_gains = project(
        places, layer_in, before, mine, other, cosine_table, sine_table, shard_rows, q_cols, k_cols
    )
    w_o = plane_weights(after(w_o, keys))
    w_o = in_order(w_o, swap(w_o, "c"), core).transpose(1, 2, 3, 0, 4, 5).reshape(q_cols, width)
    attended, log_total, branch, middle, normed_mlp = attend(
        queries, keys, values, query_ids, key_ids, w_o, layer_in, d_gains, attn_scale
    )

    half = row_count // 2
    from_x, from_y = swap(normed_mlp, "x"), swap(normed_mlp, "y")
    normed_far = jnp.concatenate([swap(from_x[:half], "y"), swap(from_y[half:], "x")])
    normed_near = jnp.concatenate([from_x, from_y])
    normed_all = [with_core(part) for part in (normed_mlp, normed_near, normed_far)]
    far_result = mlp_forward(normed_all[2], gate_up, down, normed_all[2])
    far_sum = core_sum(far_result[3]).astype(BF)
    near_result = mlp_forward(normed_all[1], gate_up, down, far_sum)
    to_x, to_y = sum_near(*lax.optimization_barrier((near_result[3], *send_far(far_sum))))
    own_result = mlp_forward(normed_all[0], gate_up, down, to_x)
    mixed = sum_own(own_result[3], to_x, to_y)
    layer_out = middle + norm_gain(mixed, d_gains[3:4])

    _, pullback = jax.vjp(norm_gain, mixed, d_gains[3:4])
    grad_mixed, mixed_terms = pullback(grad_out.astype(F32))
    grad_mixed = grad_mixed.astype(BF)
    from_x, from_y = swap(grad_mixed, "x"), swap(grad_mixed, "y")
    grad_own = with_core(grad_mixed)
    own_grads = mlp_backward(grad_own, own_result[1], own_result[2], gate_up, down, down)
    from_x, from_y = lax.optimization_barrier((from_x, from_y, own_grads[1]))[:2]
    grad_far = with_core(jnp.concatenate([swap(from_x[:half], "y"), swap(from_y[half:], "x")]))
    grad_near = with_core(jnp.concatenate([from_x, from_y]))
    grad_down_terms = down_terms(
        [r[0] for r in (own_result, near_result, far_result)],
        [grad_own, grad_near, grad_far],
        hidden_own,
    )
    grad_down = group_terms(grad_down_terms.reshape(groups, -1, width))
    far_grads = mlp_backward(
        grad_far, far_result[1], far_result[2], gate_up, down, grad_down_terms
    )
    far_sum = core_sum(far_grads[1]).astype(BF)
    near_grads = mlp_backward(grad_near, near_result[1], near_result[2], gate_up, down, far_sum)
    to_x, to_y = sum_near(*lax.optimization_barrier((near_grads[1], *send_far(far_sum))))
    gate_up_terms = gate_terms(
        normed_all, [g[0] for g in (own_grads, near_grads, far_grads)], groups, to_x
    )
    grad_normed_mlp = sum_own(own_grads[1], to_x, to_y)
    grad_normed_mlp = after(grad_normed_mlp, gate_up_terms)
    term = gate_up_terms.reshape(groups * members * shard_rows, 2 * hidden_pad)
    gate_up_share = lax.psum_scatter(term, "g", scatter_dimension=0, tiled=True)
    term = gate_up_share.reshape(members, shard_rows, 2 * hidden_pad)
    term = lax.all_to_all(term, PLANE, split_axis=0, concat_axis=0, tiled=True)

    def collect(cut):
        cut = cut[:, :, :hidden_own].reshape(2, members // 2, shard_rows, groups, piece)
        return cut.transpose(2, 0, 3, 1, 4).reshape(shard_rows, hidden_all).astype(F32)

    grad_w_gate = collect(term[:, :, :hidden_pad])
    grad_w_up = collect(term[:, :, hidden_pad:])

    grad_middle, grad_branch, grad_queries, grad_keys, grad_values, terms = attend_backward(
        grad_normed_mlp, grad_out, middle, branch, d_gains, w_o,
        queries, keys, values, query_ids, key_ids, log_total, attn_scale,
    )
    out_terms = over_rows(attended, grad_branch).astype(BF)
    out_terms = out_terms.reshape(2, groups, 2, 2, w_out.shape[0], width)
    out_terms = plane_terms(fold(out_terms, "c", 3))
    own_weights, other_weights = mine, other
    grad_normed, returned, mine, sent = project_backward(
        places, after(grad_queries, grad_down), grad_keys, grad_values, query_raw, key_raw,
        cosine_table, sine_table, h_gains, normed, normed_before, own_weights, other_weights,
        layer_in, before, d_gains, terms, mixed_terms, shard_rows,
    )
    returned = lax.ppermute(returned, ("g", "y", "c"), [(i + 1, i) for i in range(seq_size - 1)])
    grad_in = grad_tokens(
        places, returned, grad_normed, own_weights, other_weights, layer_in, d_gains, grad_middle
    )
    mine = (mine.astype(F32) + swap(sent, "c").astype(F32)).astype(BF)
    qkv_terms = plane_terms(mine.reshape(2, groups, 2, 2 * shard_rows, half_cols))
    qkv_terms = qkv_terms.reshape(groups, -1, width)
    share = jnp.concatenate([out_terms, qkv_terms], axis=1)
    share = group_terms(after(share, gate_up_share))
    grad_w_out = share[: w_out.shape[0]]
    share = share[w_out.shape[0] :].astype(BF).reshape(2, shard_rows, half_cols)
    mine = lax.dynamic_index_in_dim(share, core, 0, keepdims=False)
    other = lax.dynamic_index_in_dim(share, 1 - core, 0, keepdims=False)
    first, second = in_order(mine, swap(other, "c"), core).astype(F32)
    half = q_cols // 2
    d_terms = first[:, half + k_cols :]
    return (
        layer_out.astype(BF)[None],
        grad_in[None],
        jnp.concatenate([first[:, :half], second[:, :half]], axis=1),
        first[:, half : half + k_cols],
        second[:, half : half + k_cols],
        grad_w_out,
        grad_w_gate,
        grad_w_up,
        grad_down,
        d_terms[:, 0],
        d_terms[:, 1],
        d_terms[:, 2],
        d_terms[:, 3],
        d_terms[:head_rows, 4],
        d_terms[:head_rows, 5],
    )


def solution(mesh):
    batch, seq = mesh.devices.shape
    fine = Mesh(mesh.devices.reshape(batch, seq // 4, 2, 2), ALL)
    rows = ("g", "y", "c")
    return jax.shard_map(
        on_device,
        mesh=fine,
        in_specs=(P("x", rows, None),) * 2
        + (P("x", None),)
        + (P(ALL, None),) * 7
        + (P(ALL),) * 6,
        out_specs=(P("x", rows, None),) * 2 + (P(ALL, None),) * 7 + (P(ALL),) * 6,
        check_vma=False,
    )
```

```python
import functools

import jax
import jax.numpy as jnp
from jax import lax
from jax.experimental import pallas as pl
from jax.experimental.pallas import tpu as pltpu
from jax.sharding import Mesh
from jax.sharding import PartitionSpec as P

HEAD = 256
WINDOW = 512
EPSILON = 1e-06
ROPE_BASE = 10000.0
ALL = ("x", "g", "y", "c")
PLANE = ("x", "y", "c")
BF = jnp.bfloat16
F32 = jnp.float32


def norm_gain(values, gain_vec):
    return (
        values * lax.rsqrt(jnp.mean(values * values, axis=-1, keepdims=True) + EPSILON) * gain_vec
    )


def rope_tables(first_row, row_count, head_size):
    places = (first_row + jnp.arange(row_count, dtype=jnp.int32)).astype(F32)
    frequency = ROPE_BASE ** (-(jnp.arange(head_size // 2, dtype=F32) * 2.0) / head_size)
    angles = places[:, None] * frequency[None, :]
    return (jnp.cos(angles), jnp.sin(angles))


def matmul(left_side, right_side):
    return jnp.dot(left_side, right_side, preferred_element_type=F32)


def over_rows(left_side, right_side):
    return lax.dot_general(
        left_side, right_side, (((0,), (0,)), ((), ())), preferred_element_type=F32
    )


def by_transpose(left_side, right_side):
    return lax.dot_general(
        left_side, right_side, (((1,), (1,)), ((), ())), preferred_element_type=F32
    )


def swap(array, axis):
    return lax.ppermute(array, axis, [(0, 1), (1, 0)])


GELU_A = 0.7978845608028654
GELU_B = 0.044715
STEP = 256
PARAMS = pltpu.CompilerParams(vmem_limit_bytes=58 << 20)


def whole_block(shape):
    return pl.BlockSpec(shape, lambda i: (0,) * len(shape), pipeline_mode=pl.Buffered(1))


def row_block(rows, columns):
    return pl.BlockSpec((rows, columns), lambda i: (i, 0))


def place_weights(blocks, out, sems):
    groups, sides, rows, _ = blocks.shape
    copies = []
    for side in range(sides):
        for group in range(groups):
            at = side * groups + group
            copies.append(
                pltpu.make_async_copy(
                    blocks.at[group, side], out.at[pl.ds(at * rows, rows)], sems.at[at]
                )
            )
    return copies


def fetch_tile(tiles, step, buffer, sems):
    for at, tile in enumerate(tiles):

        @pl.when(step == at)
        def _():
            pltpu.make_async_copy(tile, buffer.at[at % 2], sems.at[at % 2]).start()


def next_tile(tiles, buffer, sems, blocks, gate_up, weight_sems):
    step = pl.program_id(0)

    @pl.when(step == 0)
    def _():
        copies = place_weights(blocks, gate_up, weight_sems)
        for copy in copies:
            copy.start()
        fetch_tile(tiles, step, buffer, sems)
        for copy in copies:
            copy.wait()

    fetch_tile(tiles, step + 1, buffer, sems)
    slot = lax.rem(step, 2)
    pltpu.make_async_copy(tiles[0], buffer.at[slot], sems.at[slot]).wait()
    return buffer[slot]


def store_half(value, mine, other, count):
    step = pl.program_id(0)

    @pl.when(step < count // 2)
    def _():
        mine[...] = value

    @pl.when(step >= count // 2)
    def _():
        other[...] = value


def mlp_forward_kernel(count, *refs):
    tiles, refs = refs[:count], refs[count:]
    blocks, down, _, hidden, gelu, slope, mine, other, buffer, gate_up, sems, weight_sems = refs
    own = down.shape[0]
    raw = matmul(next_tile(tiles, buffer, sems, blocks, gate_up, weight_sems), gate_up[...])
    gate_raw, up_raw = raw[:, :own], raw[:, own:]
    square = gate_raw * gate_raw
    bend = jnp.tanh(GELU_A * (gate_raw + GELU_B * square * gate_raw))
    half = 0.5 + 0.5 * bend
    active = gate_raw * half
    turn = 0.5 * gate_raw * (1.0 - bend * bend) * (GELU_A * (1.0 + 3.0 * GELU_B * square))
    low = (active * up_raw).astype(BF)
    hidden[...] = low
    gelu[...] = active.astype(BF)
    slope[...] = ((half + turn) * up_raw).astype(BF)
    store_half(matmul(low, down[...]).astype(BF), mine, other, count)


def half_blocks(rows, columns, count):
    return [
        pl.BlockSpec((rows, columns), lambda i: (jnp.minimum(i, count // 2 - 1), 0)),
        pl.BlockSpec((rows, columns), lambda i: (jnp.maximum(i - count // 2, 0), 0)),
    ]


def tile_scratch(tiles, blocks):
    return [
        pltpu.VMEM((2,) + tiles[0].shape, BF),
        pltpu.VMEM((tiles[0].shape[1], blocks.shape[3]), BF),
        pltpu.SemaphoreType.DMA((2,)),
        pltpu.SemaphoreType.DMA((blocks.shape[0] * blocks.shape[1],)),
    ]


def mlp_forward(tiles, blocks, down, earlier):
    count = len(tiles)
    rows, width = tiles[0].shape
    own = down.shape[0]
    total = count * rows
    flat = jax.ShapeDtypeStruct((total, own), BF)
    part = jax.ShapeDtypeStruct((total // 2, width), BF)
    anywhere = pl.BlockSpec(memory_space=pl.ANY)
    return pl.pallas_call(
        functools.partial(mlp_forward_kernel, count),
        grid=(count,),
        in_specs=[anywhere] * (count + 1) + [whole_block(down.shape), anywhere],
        out_specs=[row_block(rows, own)] * 3 + half_blocks(rows, width, count),
        out_shape=[flat, flat, flat, part, part],
        scratch_shapes=tile_scratch(tiles, blocks),
        compiler_params=PARAMS,
        cost_estimate=pl.CostEstimate(
            flops=6 * total * width * own, bytes_accessed=total * (4 * width + 6 * own), transcendentals=0
        ),
    )(*tiles, blocks, down, earlier)


def mlp_backward_kernel(count, *refs):
    tiles, refs = refs[:count], refs[count:]
    gelu, slope, blocks, down, _, grad_raw, mine, other, buffer, gate_up, sems, weight_sems = refs
    own = down.shape[0]
    grad_mixed = next_tile(tiles, buffer, sems, blocks, gate_up, weight_sems)
    grad_hidden = by_transpose(grad_mixed, down[...])
    grad_gate = (grad_hidden * slope[...].astype(F32)).astype(BF)
    grad_up = (grad_hidden * gelu[...].astype(F32)).astype(BF)
    grad_raw[:, :own] = grad_gate
    grad_raw[:, own:] = grad_up
    total = by_transpose(grad_gate, gate_up[:, :own]) + by_transpose(grad_up, gate_up[:, own:])
    store_half(total.astype(BF), mine, other, count)


def mlp_backward(tiles, gelu, slope, blocks, down, earlier):
    count = len(tiles)
    rows, width = tiles[0].shape
    own = down.shape[0]
    total = count * rows
    part = jax.ShapeDtypeStruct((total // 2, width), BF)
    anywhere = pl.BlockSpec(memory_space=pl.ANY)
    return pl.pallas_call(
        functools.partial(mlp_backward_kernel, count),
        grid=(count,),
        in_specs=[anywhere] * count
        + [row_block(rows, own)] * 2
        + [anywhere, whole_block(down.shape), anywhere],
        out_specs=[row_block(rows, 2 * own)] + half_blocks(rows, width, count),
        out_shape=[jax.ShapeDtypeStruct((total, 2 * own), BF), part, part],
        scratch_shapes=tile_scratch(tiles, blocks),
        compiler_params=PARAMS,
        cost_estimate=pl.CostEstimate(
            flops=6 * total * width * own, bytes_accessed=total * (4 * width + 8 * own), transcendentals=0
        ),
    )(*tiles, gelu, slope, blocks, down, earlier)


def rows_of(segments, tiles):
    at = 0
    for segment in segments:
        first = 0
        while first < segment.shape[0]:
            rows = tiles[at].shape[0]
            yield segment, first, tiles[at]
            first += rows
            at += 1


def down_terms_kernel(count, *refs):
    *ins, out = refs
    total = None
    for segment, first, tile in rows_of(ins[:count], ins[count:]):
        part = over_rows(segment[first : first + tile.shape[0], :], tile[...])
        total = part if total is None else total + part
    out[...] = total.astype(BF)


def down_terms(hidden, grad_mixed, keep):
    own, width = hidden[0].shape[1], grad_mixed[0].shape[1]
    rows = sum(part.shape[0] for part in hidden)
    return pl.pallas_call(
        functools.partial(down_terms_kernel, len(hidden)),
        grid=(own // 128,),
        in_specs=[pl.BlockSpec((part.shape[0], 128), lambda i: (0, i)) for part in hidden]
        + [whole_block(part.shape) for part in grad_mixed],
        out_specs=row_block(128, width),
        out_shape=jax.ShapeDtypeStruct((keep, width), BF),
        compiler_params=PARAMS,
        cost_estimate=pl.CostEstimate(
            flops=2 * rows * width * own, bytes_accessed=2 * rows * (width + own), transcendentals=0
        ),
    )(*hidden, *grad_mixed)


def gate_terms_kernel(count, *refs):
    *ins, _, out = refs
    total = None
    for segment, first, tile in rows_of(ins[:count], ins[count:]):
        part = over_rows(tile[...], segment[first : first + tile.shape[0], :])
        total = part if total is None else total + part
    total = total.astype(BF)
    groups, sides, rows, _ = out.shape
    for side in range(sides):
        for group in range(groups):
            first = (side * groups + group) * rows
            out[group, side] = total[first : first + rows]


def gate_terms(normed, grad_raw, groups, first, steps, earlier):
    width = normed[0].shape[1]
    rows = sum(part.shape[0] for part in grad_raw)
    shape = (groups, 2, width // (2 * groups))
    columns = steps * STEP
    return pl.pallas_call(
        functools.partial(gate_terms_kernel, len(grad_raw)),
        grid=(steps,),
        in_specs=[
            pl.BlockSpec((part.shape[0], STEP), lambda i: (0, first + i)) for part in grad_raw
        ]
        + [whole_block(part.shape) for part in normed]
        + [pl.BlockSpec(memory_space=pl.ANY)],
        out_specs=pl.BlockSpec(shape + (STEP,), lambda i: (0, 0, 0, i)),
        out_shape=jax.ShapeDtypeStruct(shape + (columns,), BF),
        compiler_params=PARAMS,
        cost_estimate=pl.CostEstimate(
            flops=2 * rows * width * columns, bytes_accessed=2 * rows * (width + columns), transcendentals=0
        ),
    )(*grad_raw, *normed, earlier)


def after(value, *earlier):
    return lax.optimization_barrier((value, *earlier))[0]


def core_sum(mine, other):
    return mine.astype(F32) + swap(other, "c").astype(F32)


def with_core(*tiles):
    return list(tiles) + [swap(tile, "c") for tile in tiles]


def send_far(far):
    half = far.shape[0] // 2
    return swap(far[:half], "y"), swap(far[half:], "x")


def sum_near(mine, other, top, low):
    mine, other, top, low = lax.optimization_barrier((mine, other, top, low))
    near = core_sum(mine, other)
    rows = near.shape[0] // 2
    half = rows // 2
    to_x = jnp.concatenate([near[:half] + top, near[half:rows]]).astype(BF)
    to_y = jnp.concatenate([near[rows : rows + half], near[rows + half :] + low]).astype(BF)
    return to_x, to_y


def sum_own(mine, other, to_x, to_y):
    total = core_sum(mine, other)
    return total + swap(to_x, "x").astype(F32) + swap(to_y, "y").astype(F32)


def in_order(own, other, place):
    both = jnp.concatenate([own[None], other[None], own[None]])
    return lax.dynamic_slice_in_dim(both, place, 2, 0)


def group_gather(own):
    size = lax.axis_size("g")
    parts = [own] + [
        lax.ppermute(own, "g", [((i + k) % size, i) for i in range(size)]) for k in range(1, size)
    ]
    both = jnp.stack(parts + parts[:-1])
    place = lax.axis_index("g")
    return lax.dynamic_slice_in_dim(both, lax.rem(size - place, size), size, 0)


def plane_weights(blocks, *earlier):
    x, y = lax.axis_index("x"), lax.axis_index("y")
    half = blocks.shape[0] // 2
    first, second = blocks[:half], blocks[half:]
    first = in_order(first, swap(first, "x"), x)
    second = in_order(second, swap(second, "y"), y)
    first, second = lax.optimization_barrier((first, second, *earlier))[:2]
    first = in_order(first, swap(first, "y"), y)
    second = in_order(second, swap(second, "x"), x)
    first = first.transpose(1, 2, 0, 3, 4)
    second = second.transpose(0, 2, 1, 3, 4)
    return jnp.concatenate([first, second], axis=1)


def group_terms(term):
    size = lax.axis_size("g")
    place = lax.axis_index("g")
    total = lax.dynamic_index_in_dim(term, place, 0, keepdims=False).astype(F32)
    for k in range(1, size):
        chunk = lax.dynamic_index_in_dim(term, lax.rem(place + k, size), 0, keepdims=False)
        pairs = [(i, (i + k) % size) for i in range(size)]
        total = total + lax.ppermute(chunk, "g", pairs).astype(F32)
    return total


def fold(term, axis, dim):
    place = lax.axis_index(axis)
    mine = lax.dynamic_index_in_dim(term, place, dim, keepdims=False)
    other = lax.dynamic_index_in_dim(term, 1 - place, dim, keepdims=False)
    return (mine.astype(F32) + swap(other.astype(BF), axis).astype(F32)).astype(BF)


def plane_terms(term):
    half = term.shape[1] // 2
    first = fold(fold(term[:, :half], "x", 0), "y", 1)
    second = fold(fold(term[:, half:], "y", 2), "x", 0)
    return jnp.concatenate([first, second])


def rms_scale(values):
    return lax.rsqrt(jnp.mean(values * values, axis=-1, keepdims=True) + EPSILON)


def rms_backward(values, scale, gain, grad):
    weighted = grad * gain
    inner = jnp.mean(weighted * values, axis=-1, keepdims=True)
    terms = jnp.sum(grad * values * scale, axis=0, keepdims=True)
    return weighted * scale - values * (scale * scale * scale * inner), terms


def turn_forward(values, cosine, sine):
    half = cosine.shape[1]
    low, high = values[:, :half], values[:, half:]
    return jnp.concatenate([low * cosine - high * sine, high * cosine + low * sine], axis=1)


def turn_backward(grad, cosine, sine):
    half = cosine.shape[1]
    low, high = grad[:, :half], grad[:, half:]
    return jnp.concatenate([low * cosine + high * sine, high * cosine - low * sine], axis=1)


def gain_places(width, columns, shard_rows):
    heads = columns // (width // shard_rows)
    row = lax.broadcasted_iota(jnp.int32, (width, columns), 0)
    column = lax.broadcasted_iota(jnp.int32, (width, columns), 1)
    place = (column // heads) * shard_rows + lax.rem(column, heads)
    return jnp.where(row == place, 1.0, 0.0).astype(BF)


def project_kernel(
    shard_rows, core, tokens, earlier, own, other, cosine, sine,
    normed, normed_earlier, query_raw, key_raw, queries, keys, values, d_gains, h_gains,
):
    rows, width = tokens.shape
    pad, k_cols = earlier.shape[0], key_raw.shape[1]
    half = query_raw.shape[1] // 2
    first_is_own = core[0] == 0
    block = jnp.where(
        first_is_own, own[:, half + k_cols :].astype(F32), other[:, half + k_cols :].astype(F32)
    )
    flat = block.T[:8]
    d_gains[...] = flat
    chosen = matmul(flat.astype(BF), gain_places(width, k_cols, shard_rows))
    h_gains[...] = chosen
    before = earlier[...].astype(F32)
    low_before = (before * rms_scale(before) * flat[0:1]).astype(BF)
    normed_earlier[...] = low_before
    inputs = tokens[...].astype(F32)
    low = (inputs * rms_scale(inputs) * flat[0:1]).astype(BF)
    normed[...] = low
    raw_own = matmul(low, own[:, : half + k_cols])
    raw_other = matmul(low, other[:, : half + k_cols])
    before_own = matmul(low_before, own[:, half : half + k_cols])
    before_other = matmul(low_before, other[:, half : half + k_cols])
    first = jnp.where(first_is_own, raw_own, raw_other)
    second = jnp.where(first_is_own, raw_other, raw_own)
    raw_query = jnp.concatenate([first[:, :half], second[:, :half]], axis=1)
    query_raw[...] = raw_query
    values[:pad] = jnp.where(first_is_own, before_other, before_own).astype(BF)
    values[pad:] = second[:, half:].astype(BF)
    raw_before = jnp.where(first_is_own, before_own, before_other)
    for raw, at in ((raw_before, slice(0, pad)), (first[:, half:], slice(pad, pad + rows))):
        key_raw[at] = raw
        part = raw * rms_scale(raw) * chosen[5:6]
        keys[at] = turn_forward(part, cosine[at], sine[at]).astype(BF)
    cos, sin = cosine[pad:], sine[pad:]
    for head in range(2 * half // k_cols):
        at = slice(head * k_cols, (head + 1) * k_cols)
        part = raw_query[:, at]
        part = part * rms_scale(part) * chosen[4:5]
        queries[:, at] = turn_forward(part, cos, sin).astype(BF)


def project(core, tokens, earlier, own, other, cosine, sine, shard_rows, q_cols, k_cols):
    rows, width = tokens.shape
    seen = rows + earlier.shape[0]
    vmem = pl.BlockSpec(memory_space=pltpu.VMEM)
    return pl.pallas_call(
        functools.partial(project_kernel, shard_rows),
        in_specs=[pl.BlockSpec(memory_space=pltpu.SMEM)] + [vmem] * 6,
        out_specs=[vmem] * 9,
        out_shape=[
            jax.ShapeDtypeStruct((rows, width), BF),
            jax.ShapeDtypeStruct(earlier.shape, BF),
            jax.ShapeDtypeStruct((rows, q_cols), F32),
            jax.ShapeDtypeStruct((seen, k_cols), F32),
            jax.ShapeDtypeStruct((rows, q_cols), BF),
            jax.ShapeDtypeStruct((seen, k_cols), BF),
            jax.ShapeDtypeStruct((seen, k_cols), BF),
            jax.ShapeDtypeStruct((8, width), F32),
            jax.ShapeDtypeStruct((8, k_cols), F32),
        ],
        compiler_params=PARAMS,
        cost_estimate=pl.CostEstimate(
            flops=2 * rows * width * (q_cols + 4 * k_cols), bytes_accessed=16 * rows * width, transcendentals=0
        ),
    )(core, tokens, earlier, own, other, cosine, sine)


def tile_mask(first, rows, first_key, keys, query_ids, key_ids, pad):
    query_place = pad + first + lax.broadcasted_iota(jnp.int32, (rows, keys), 0)
    key_place = first_key + lax.broadcasted_iota(jnp.int32, (rows, keys), 1)
    distance = query_place - key_place
    same_doc = query_ids[first : first + rows, :] == key_ids[:, first_key : first_key + keys]
    return (distance >= 0) & (distance < WINDOW) & same_doc


def attend_kernel(
    scale, queries, keys, values, query_ids, key_ids, w_o, tokens, d_gains,
    attended, log_total, branch, middle, normed_mlp,
):
    rows, q_cols = queries.shape
    pad, k_cols = keys.shape[0] - rows, keys.shape[1]
    tile = rows // 2
    span = pad + tile
    lane = lax.broadcasted_iota(jnp.int32, (tile, 128), 1)
    for first in (0, tile):
        at = slice(first, first + tile)
        seen = slice(first, first + span)
        allowed = tile_mask(first, tile, first, span, query_ids, key_ids, pad)
        logs = jnp.zeros((tile, 128), F32)
        for head in range(q_cols // k_cols):
            columns = slice(head * k_cols, (head + 1) * k_cols)
            scores = by_transpose(queries[at, columns], keys[seen]) * scale
            scores = jnp.where(allowed, scores, -1e30)
            row_max = jnp.max(scores, axis=-1, keepdims=True)
            weights = jnp.exp(scores - row_max)
            row_total = jnp.sum(weights, axis=-1, keepdims=True)
            probabilities = (weights * (1.0 / row_total)).astype(BF)
            attended[at, columns] = matmul(probabilities, values[seen]).astype(BF)
            logs = jnp.where(lane == head, row_max + jnp.log(row_total), logs)
        log_total[at] = logs
    out = matmul(attended[...], w_o[...])
    branch[...] = out
    total = tokens[...].astype(F32) + out * rms_scale(out) * d_gains[1:2]
    middle[...] = total
    normed_mlp[...] = (total * rms_scale(total) * d_gains[2:3]).astype(BF)


def attend(queries, keys, values, query_ids, key_ids, w_o, tokens, d_gains, scale):
    rows, q_cols = queries.shape
    width = tokens.shape[1]
    vmem = pl.BlockSpec(memory_space=pltpu.VMEM)
    return pl.pallas_call(
        functools.partial(attend_kernel, scale),
        in_specs=[vmem] * 8,
        out_specs=[vmem] * 5,
        out_shape=[
            jax.ShapeDtypeStruct((rows, q_cols), BF),
            jax.ShapeDtypeStruct((rows, 128), F32),
            jax.ShapeDtypeStruct((rows, width), F32),
            jax.ShapeDtypeStruct((rows, width), F32),
            jax.ShapeDtypeStruct((rows, width), BF),
        ],
        compiler_params=PARAMS,
        cost_estimate=pl.CostEstimate(
            flops=2 * rows * q_cols * (width + 2 * keys.shape[0]), bytes_accessed=20 * rows * width, transcendentals=0
        ),
    )(queries, keys, values, query_ids, key_ids, w_o, tokens, d_gains)


def attend_backward_kernel(
    scale, grad_normed_mlp, cotangent, middle, branch, d_gains, w_o,
    queries, keys, values, query_ids, key_ids, log_total,
    grad_middle, grad_branch, grad_queries, grad_keys, grad_values, terms, grad_attended,
):
    rows, q_cols = queries.shape
    pad, k_cols = keys.shape[0] - rows, keys.shape[1]
    total = middle[...]
    from_mlp, mlp_terms = rms_backward(total, rms_scale(total), d_gains[2:3], grad_normed_mlp[...])
    grad_total = cotangent[...].astype(F32) + from_mlp
    grad_middle[...] = grad_total
    out = branch[...]
    grad_out, out_terms = rms_backward(out, rms_scale(out), d_gains[1:2], grad_total)
    low = grad_out.astype(BF)
    grad_branch[...] = low
    terms[...] = jnp.concatenate([out_terms, mlp_terms, jnp.zeros((6, out.shape[1]), F32)], axis=0)
    grad_attended[...] = by_transpose(low, w_o[...]).astype(BF)
    grad_keys[...] = jnp.zeros_like(grad_keys)
    grad_values[...] = jnp.zeros_like(grad_values)
    tile = rows // 2
    span = pad + tile
    for first in (0, tile):
        at = slice(first, first + tile)
        seen = slice(first, first + span)
        allowed = tile_mask(first, tile, first, span, query_ids, key_ids, pad)
        key_total = jnp.zeros((span, k_cols), F32)
        value_total = jnp.zeros((span, k_cols), F32)
        for head in range(q_cols // k_cols):
            columns = slice(head * k_cols, (head + 1) * k_cols)
            query = queries[at, columns]
            grad = grad_attended[at, columns]
            scores = by_transpose(query, keys[seen]) * scale
            probabilities = jnp.where(
                allowed, jnp.exp(scores - log_total[at, head : head + 1]), 0.0
            )
            grad_prob = by_transpose(grad, values[seen])
            inner = jnp.sum(probabilities * grad_prob, axis=-1, keepdims=True)
            grad_score = (probabilities * (grad_prob - inner)).astype(BF)
            grad_queries[at, columns] = matmul(grad_score, keys[seen]) * scale
            key_total = key_total + over_rows(grad_score, query)
            value_total = value_total + over_rows(probabilities.astype(BF), grad)
        grad_keys[seen] = grad_keys[seen] + key_total * scale
        grad_values[seen] = grad_values[seen] + value_total


def attend_backward(
    grad_normed_mlp, cotangent, middle, branch, d_gains, w_o,
    queries, keys, values, query_ids, key_ids, log_total, scale,
):
    rows, q_cols = queries.shape
    width = middle.shape[1]
    vmem = pl.BlockSpec(memory_space=pltpu.VMEM)
    return pl.pallas_call(
        functools.partial(attend_backward_kernel, scale),
        in_specs=[vmem] * 12,
        out_specs=[vmem] * 6,
        out_shape=[
            jax.ShapeDtypeStruct((rows, width), F32),
            jax.ShapeDtypeStruct((rows, width), BF),
            jax.ShapeDtypeStruct((rows, q_cols), F32),
            jax.ShapeDtypeStruct(keys.shape, F32),
            jax.ShapeDtypeStruct(keys.shape, F32),
            jax.ShapeDtypeStruct((8, width), F32),
        ],
        scratch_shapes=[pltpu.VMEM((rows, q_cols), BF)],
        compiler_params=PARAMS,
        cost_estimate=pl.CostEstimate(
            flops=2 * rows * q_cols * (width + 5 * keys.shape[0]), bytes_accessed=30 * rows * width, transcendentals=0
        ),
    )(
        grad_normed_mlp, cotangent, middle, branch, d_gains, w_o,
        queries, keys, values, query_ids, key_ids, log_total,
    )


def project_backward_kernel(
    shard_rows, core, grad_queries, grad_keys, grad_values, query_raw, key_raw, cosine, sine,
    h_gains, normed, normed_earlier, own, other, tokens, earlier, d_gains, terms, mixed_terms,
    grad_normed, returned, mine, sent,
):
    rows, width = tokens.shape
    pad, k_cols = earlier.shape[0], key_raw.shape[1]
    half = query_raw.shape[1] // 2
    cols = half + k_cols
    first_is_own = core[0] == 0
    cos, sin = cosine[pad:], sine[pad:]
    query_terms = jnp.zeros((1, k_cols), F32)
    parts = []
    for head in range(2 * half // k_cols):
        at = slice(head * k_cols, (head + 1) * k_cols)
        raw = query_raw[:, at]
        grad = turn_backward(grad_queries[:, at], cos, sin)
        grad, term = rms_backward(raw, rms_scale(raw), h_gains[4:5], grad)
        query_terms = query_terms + term
        parts.append(grad.astype(BF))
    raw = key_raw[...]
    grad = turn_backward(grad_keys[...], cosine[...], sine[...])
    grad, key_terms = rms_backward(raw, rms_scale(raw), h_gains[5:6], grad)
    grad_key, grad_value = grad.astype(BF), grad_values[...].astype(BF)
    returned[:, :k_cols] = grad_key[:pad]
    returned[:, k_cols:] = grad_value[:pad]
    kv_own = jnp.where(first_is_own, grad_key, grad_value)
    kv_other = jnp.where(first_is_own, grad_value, grad_key)
    both = len(parts) // 2
    first = jnp.concatenate(parts[:both], axis=1)
    second = jnp.concatenate(parts[both:], axis=1)
    q_own = jnp.where(first_is_own, first, second)
    q_other = jnp.where(first_is_own, second, first)
    grad_own = jnp.concatenate([q_own, kv_own[pad:]], axis=1)
    grad_other = jnp.concatenate([q_other, kv_other[pad:]], axis=1)
    total = by_transpose(grad_own, own[:, :cols]) + by_transpose(grad_other, other[:, :cols])
    grad_normed[...] = total
    values = tokens[...].astype(F32)
    in_terms = jnp.sum(total * values * rms_scale(values), axis=0, keepdims=True)
    total = by_transpose(kv_own[:pad], own[:, half:cols])
    total = total + by_transpose(kv_other[:pad], other[:, half:cols])
    values = earlier[...].astype(F32)
    in_terms = in_terms + jnp.sum(total * values * rms_scale(values), axis=0, keepdims=True)
    low, low_before = normed[...], normed_earlier[...]
    for out, query, key_value in ((mine, q_own, kv_own), (sent, q_other, kv_other)):
        out[:, :half] = over_rows(low, query).astype(BF)
        out[:, half:cols] = (
            over_rows(low, key_value[pad:]) + over_rows(low_before, key_value[:pad])
        ).astype(BF)
    heads = jnp.concatenate([query_terms, key_terms, jnp.zeros((6, k_cols), F32)], axis=0)
    placed = by_transpose(heads.astype(BF), gain_places(width, k_cols, shard_rows))
    block = jnp.concatenate(
        [in_terms, terms[0:2], mixed_terms[0:1], placed[0:2], jnp.zeros((122, width), F32)], axis=0
    ).T
    mine[:, cols:] = jnp.where(first_is_own, block, 0.0).astype(BF)
    sent[:, cols:] = jnp.where(first_is_own, 0.0, block).astype(BF)


def project_backward(
    core, grad_queries, grad_keys, grad_values, query_raw, key_raw, cosine, sine,
    h_gains, normed, normed_earlier, own, other, tokens, earlier, d_gains, terms, mixed_terms,
    shard_rows,
):
    rows, width = tokens.shape
    pad, k_cols = earlier.shape[0], key_raw.shape[1]
    vmem = pl.BlockSpec(memory_space=pltpu.VMEM)
    return pl.pallas_call(
        functools.partial(project_backward_kernel, shard_rows),
        in_specs=[pl.BlockSpec(memory_space=pltpu.SMEM)] + [vmem] * 17,
        out_specs=[vmem] * 4,
        out_shape=[
            jax.ShapeDtypeStruct((rows, width), F32),
            jax.ShapeDtypeStruct((pad, 2 * k_cols), BF),
            jax.ShapeDtypeStruct(own.shape, BF),
            jax.ShapeDtypeStruct(own.shape, BF),
        ],
        compiler_params=PARAMS,
        cost_estimate=pl.CostEstimate(
            flops=9 * rows * width * own.shape[1], bytes_accessed=30 * rows * width, transcendentals=0
        ),
    )(
        core, grad_queries, grad_keys, grad_values, query_raw, key_raw, cosine, sine,
        h_gains, normed, normed_earlier, own, other, tokens, earlier, d_gains, terms, mixed_terms,
    )


def grad_tokens_kernel(core, returned, grad_normed, own, other, tokens, d_gains, grad_middle, out):
    k_cols = returned.shape[1] // 2
    cols = own.shape[1] - 128
    half = cols - k_cols
    first_is_own = core[0] == 0
    grad_key, grad_value = returned[:, :k_cols], returned[:, k_cols:]
    kv_own = jnp.where(first_is_own, grad_key, grad_value)
    kv_other = jnp.where(first_is_own, grad_value, grad_key)
    total = grad_normed[...] + by_transpose(kv_own, own[:, half:cols])
    total = total + by_transpose(kv_other, other[:, half:cols])
    values = tokens[...].astype(F32)
    from_attn, _ = rms_backward(values, rms_scale(values), d_gains[0:1], total)
    out[...] = (grad_middle[...] + from_attn).astype(BF)


def grad_tokens(core, returned, grad_normed, own, other, tokens, d_gains, grad_middle):
    vmem = pl.BlockSpec(memory_space=pltpu.VMEM)
    return pl.pallas_call(
        grad_tokens_kernel,
        in_specs=[pl.BlockSpec(memory_space=pltpu.SMEM)] + [vmem] * 7,
        out_specs=vmem,
        out_shape=jax.ShapeDtypeStruct(tokens.shape, BF),
        compiler_params=PARAMS,
        cost_estimate=pl.CostEstimate(
            flops=2 * tokens.size * returned.shape[1], bytes_accessed=12 * tokens.size, transcendentals=0
        ),
    )(core, returned, grad_normed, own, other, tokens, d_gains, grad_middle)


def on_device(
    tokens,
    cotangent,
    doc_ids,
    w_query,
    w_key,
    w_value,
    w_out,
    w_gate,
    w_up,
    w_down,
    gain_attn_in,
    gain_attn_out,
    gain_mlp_in,
    gain_mlp_out,
    gain_query,
    gain_key,
):
    row_count = tokens.shape[1]
    width = tokens.shape[2]
    groups = lax.axis_size("g")
    members = lax.axis_size(PLANE)
    shard_rows = w_query.shape[0]
    head_rows = gain_query.shape[0]
    hidden_all = w_gate.shape[1]
    hidden_own = hidden_all // members
    hidden_pad = -(-hidden_own // 128) * 128
    piece = hidden_own // groups
    q_cols, k_cols = w_query.shape[1], w_key.shape[1]
    attn_scale = HEAD ** (-0.5)

    def gain_columns(d_gains, h_gains):
        columns = list(d_gains) + [
            jnp.pad(h, ((0, 0), (0, shard_rows - head_rows))) for h in h_gains
        ]
        block = jnp.stack(columns, axis=-1)
        return jnp.pad(block, ((0, 0), (0, 0), (0, 128 - len(columns))))

    seq_place = lax.axis_index(("g", "y", "c"))
    seq_size = lax.axis_size(("g", "y", "c"))
    before = lax.ppermute(tokens[0], ("g", "y", "c"), [(i, i + 1) for i in range(seq_size - 1)])

    def spread(weight):
        cut = weight.reshape(shard_rows, 2, groups, members // 2, piece)
        cut = cut.transpose(1, 3, 0, 2, 4).reshape(members, shard_rows, hidden_own)
        return jnp.pad(cut, ((0, 0), (0, 0), (0, hidden_pad - hidden_own)))

    sent = jnp.concatenate([spread(w_gate), spread(w_up)], axis=2)
    core = lax.axis_index("c")
    half_cols = q_cols // 2 + k_cols + 128
    gains = gain_columns(
        [g[None] for g in (gain_attn_in, gain_attn_out, gain_mlp_in, gain_mlp_out)],
        [gain_query[None], gain_key[None]],
    )
    halves = jnp.stack(
        [
            jnp.concatenate([w_query[:, : q_cols // 2], w_key, gains[0]], axis=1),
            jnp.concatenate([w_query[:, q_cols // 2 :], w_value, jnp.zeros_like(gains[0])], axis=1),
        ]
    )
    mine = lax.dynamic_index_in_dim(halves, core, 0, keepdims=False)
    other = lax.dynamic_index_in_dim(halves, 1 - core, 0, keepdims=False)
    mine = in_order(mine, swap(other, "c"), core).reshape(2 * shard_rows, half_cols)
    mine, before, sent = lax.optimization_barrier((mine, before, sent))
    sent = lax.all_to_all(sent, PLANE, split_axis=0, concat_axis=0, tiled=True)
    sent = sent.reshape(members * shard_rows, 2 * hidden_pad)
    mine, sent = lax.optimization_barrier((group_gather(mine), sent))
    mine = plane_weights(mine).reshape(width, half_cols)
    other = swap(mine, "c")

    down = lax.all_gather(jnp.concatenate([w_down, w_out]), "g", axis=0)
    w_o = down[:, w_down.shape[0] :]
    down = down[:, : w_down.shape[0]].reshape(-1, width)
    down = jnp.pad(down, ((0, hidden_pad - hidden_own), (0, 0)))

    both = lax.all_gather(sent, "g", axis=0)
    gate_up = both.reshape(groups, 2, members // 2 * shard_rows, 2 * hidden_pad)
    if gate_up.shape[2] % 16:
        gate_up = gate_up.transpose(1, 0, 2, 3).reshape(1, 1, width, 2 * hidden_pad)

    first_row = seq_place * row_count
    ids_all = doc_ids[0]
    ids_own = lax.dynamic_slice_in_dim(ids_all, first_row, row_count, 0)
    ids_prev = lax.dynamic_slice_in_dim(
        ids_all, jnp.maximum(first_row - row_count, 0), row_count, 0
    )
    ids_prev = jnp.where(seq_place > 0, ids_prev, -1)
    ids_pad = jnp.concatenate([ids_prev, ids_own])
    query_ids, key_ids = ids_own[:, None], ids_pad[None]
    cosine_table, sine_table = rope_tables(first_row - row_count, 2 * row_count, HEAD)
    places = jnp.full((1,), core, jnp.int32)
    layer_in, grad_out = tokens[0], cotangent[0]

    normed, normed_before, query_raw, key_raw, queries, keys, values, d_gains, h_gains = project(
        places, layer_in, before, mine, other, cosine_table, sine_table, shard_rows, q_cols, k_cols
    )
    w_o = plane_weights(w_o, keys)
    w_o = in_order(w_o, swap(w_o, "c"), core).transpose(1, 2, 3, 0, 4, 5).reshape(q_cols, width)
    w_o = after(w_o, down)
    attended, log_total, branch, middle, normed_mlp = attend(
        queries, keys, values, query_ids, key_ids, w_o, layer_in, d_gains, attn_scale
    )

    half = row_count // 2
    from_x, from_y = swap(normed_mlp, "x"), swap(normed_mlp, "y")
    normed_own = with_core(normed_mlp)
    normed_near = with_core(from_x, from_y)
    normed_far = with_core(swap(from_x[:half], "y"), swap(from_y[half:], "x"))
    far_result = mlp_forward(normed_far, gate_up, down, normed_own[1])
    far_sum = core_sum(*far_result[3:]).astype(BF)
    near_result = mlp_forward(normed_near, gate_up, down, far_sum)
    to_x, to_y = sum_near(*near_result[3:], *send_far(far_sum))
    own_result = mlp_forward(normed_own, gate_up, down, to_x)
    mixed = sum_own(*own_result[3:], to_x, to_y)
    layer_out = middle + norm_gain(mixed, d_gains[3:4])

    _, pullback = jax.vjp(norm_gain, mixed, d_gains[3:4])
    grad_mixed, mixed_terms = pullback(grad_out.astype(F32))
    grad_mixed = grad_mixed.astype(BF)
    from_x, from_y = swap(grad_mixed, "x"), swap(grad_mixed, "y")
    grad_own = with_core(grad_mixed)
    own_grads = mlp_backward(grad_own, own_result[1], own_result[2], gate_up, down, down)
    from_x, from_y = lax.optimization_barrier((from_x, from_y, own_grads[1]))[:2]
    grad_near = with_core(from_x, from_y)
    grad_far = with_core(swap(from_x[:half], "y"), swap(from_y[half:], "x"))
    grad_down_terms = down_terms(
        [r[0] for r in (own_result, near_result, far_result)],
        grad_own + grad_near + grad_far,
        hidden_own,
    )
    grad_down = group_terms(grad_down_terms.reshape(groups, -1, width))
    far_grads = mlp_backward(
        grad_far, far_result[1], far_result[2], gate_up, down, grad_down_terms
    )
    far_sum = core_sum(*far_grads[1:]).astype(BF)
    near_grads = mlp_backward(grad_near, near_result[1], near_result[2], gate_up, down, far_sum)
    to_x, to_y = sum_near(*near_grads[1:], *send_far(far_sum))
    raw_grads = [g[0] for g in (own_grads, near_grads, far_grads)]
    steps = 2 * hidden_pad // STEP
    first_steps = steps // 2 + steps % 2
    first_terms = gate_terms(
        normed_own + normed_near + normed_far, raw_grads, groups, 0, first_steps, to_x
    )
    second_terms = gate_terms(
        normed_own + normed_near + normed_far,
        raw_grads,
        groups,
        first_steps,
        steps - first_steps,
        first_terms,
    )
    grad_normed_mlp = sum_own(*own_grads[1:], to_x, to_y)
    grad_normed_mlp = after(grad_normed_mlp, second_terms)

    def scatter(term):
        term = term.reshape(groups * members * shard_rows, term.shape[3])
        return lax.psum_scatter(term, "g", scatter_dimension=0, tiled=True)

    def to_owner(term):
        term = term.reshape(members, shard_rows, term.shape[1])
        return lax.all_to_all(term, PLANE, split_axis=0, concat_axis=0, tiled=True)

    first_share = scatter(first_terms)
    second_share = scatter(after(second_terms, first_share))
    first_share = to_owner(first_share)
    term = jnp.concatenate([first_share, to_owner(second_share)], axis=2)

    def collect(cut):
        cut = cut[:, :, :hidden_own].reshape(2, members // 2, shard_rows, groups, piece)
        return cut.transpose(2, 0, 3, 1, 4).reshape(shard_rows, hidden_all).astype(F32)

    grad_w_gate = collect(term[:, :, :hidden_pad])
    grad_w_up = collect(term[:, :, hidden_pad:])

    grad_middle, grad_branch, grad_queries, grad_keys, grad_values, terms = attend_backward(
        grad_normed_mlp, grad_out, middle, branch, d_gains, w_o,
        queries, keys, values, query_ids, key_ids, log_total, attn_scale,
    )
    out_terms = over_rows(attended, grad_branch).astype(BF)
    out_terms = out_terms.reshape(2, groups, 2, 2, w_out.shape[0], width)
    out_terms = plane_terms(fold(out_terms, "c", 3))
    own_weights, other_weights = mine, other
    grad_normed, returned, mine, sent = project_backward(
        places, after(grad_queries, grad_down), grad_keys, grad_values, query_raw, key_raw,
        cosine_table, sine_table, h_gains, normed, normed_before, own_weights, other_weights,
        layer_in, before, d_gains, terms, mixed_terms, shard_rows,
    )
    returned = lax.ppermute(returned, ("g", "y", "c"), [(i + 1, i) for i in range(seq_size - 1)])
    grad_in = grad_tokens(
        places, returned, grad_normed, own_weights, other_weights, layer_in, d_gains, grad_middle
    )
    mine = (mine.astype(F32) + swap(sent, "c").astype(F32)).astype(BF)
    qkv_terms = plane_terms(mine.reshape(2, groups, 2, 2 * shard_rows, half_cols))
    qkv_terms = qkv_terms.reshape(groups, -1, width)
    share = jnp.concatenate([out_terms, qkv_terms], axis=1)
    share = group_terms(after(share, first_share, second_share, grad_in))
    grad_w_out = share[: w_out.shape[0]]
    share = share[w_out.shape[0] :].astype(BF).reshape(2, shard_rows, half_cols)
    mine = lax.dynamic_index_in_dim(share, core, 0, keepdims=False)
    other = lax.dynamic_index_in_dim(share, 1 - core, 0, keepdims=False)
    first, second = in_order(mine, swap(other, "c"), core).astype(F32)
    half = q_cols // 2
    d_terms = first[:, half + k_cols :]
    return (
        layer_out.astype(BF)[None],
        grad_in[None],
        jnp.concatenate([first[:, :half], second[:, :half]], axis=1),
        first[:, half : half + k_cols],
        second[:, half : half + k_cols],
        grad_w_out,
        grad_w_gate,
        grad_w_up,
        grad_down,
        d_terms[:, 0],
        d_terms[:, 1],
        d_terms[:, 2],
        d_terms[:, 3],
        d_terms[:head_rows, 4],
        d_terms[:head_rows, 5],
    )


def solution(mesh):
    batch, seq = mesh.devices.shape
    fine = Mesh(mesh.devices.reshape(batch, seq // 4, 2, 2), ALL)
    rows = ("g", "y", "c")
    return jax.shard_map(
        on_device,
        mesh=fine,
        in_specs=(P("x", rows, None),) * 2
        + (P("x", None),)
        + (P(ALL, None),) * 7
        + (P(ALL),) * 6,
        out_specs=(P("x", rows, None),) * 2 + (P(ALL, None),) * 7 + (P(ALL),) * 6,
        check_vma=False,
    )
```

```python
import functools

import jax
import jax.numpy as jnp
from jax import lax
from jax.experimental import pallas as pl
from jax.experimental.pallas import tpu as pltpu
from jax.sharding import Mesh
from jax.sharding import PartitionSpec as P

HEAD = 256
WINDOW = 512
EPSILON = 1e-06
ROPE_BASE = 10000.0
ALL = ("x", "g", "y", "c")
PLANE = ("x", "y", "c")
BF = jnp.bfloat16
F32 = jnp.float32


def norm_gain(values, gain_vec):
    return (
        values * lax.rsqrt(jnp.mean(values * values, axis=-1, keepdims=True) + EPSILON) * gain_vec
    )


def rope_tables(first_row, row_count, head_size):
    places = (first_row + jnp.arange(row_count, dtype=jnp.int32)).astype(F32)
    frequency = ROPE_BASE ** (-(jnp.arange(head_size // 2, dtype=F32) * 2.0) / head_size)
    angles = places[:, None] * frequency[None, :]
    return (jnp.cos(angles), jnp.sin(angles))


def matmul(left_side, right_side):
    return jnp.dot(left_side, right_side, preferred_element_type=F32)


def over_rows(left_side, right_side):
    return lax.dot_general(
        left_side, right_side, (((0,), (0,)), ((), ())), preferred_element_type=F32
    )


def by_transpose(left_side, right_side):
    return lax.dot_general(
        left_side, right_side, (((1,), (1,)), ((), ())), preferred_element_type=F32
    )


def swap(array, axis):
    return lax.ppermute(array, axis, [(0, 1), (1, 0)])


GELU_A = 0.7978845608028654
GELU_B = 0.044715
TILE = 512
STEP = 256
PARAMS = pltpu.CompilerParams(vmem_limit_bytes=58 << 20)


def whole_block(shape):
    return pl.BlockSpec(shape, lambda i: (0,) * len(shape), pipeline_mode=pl.Buffered(1))


def row_block(rows, columns):
    return pl.BlockSpec((rows, columns), lambda i: (i, 0))


def store_half(value, mine, other):
    step, half = pl.program_id(0), pl.num_programs(0) // 2

    @pl.when(step < half)
    def _():
        mine[...] = value

    @pl.when(step >= half)
    def _():
        other[...] = value


def half_blocks(rows, columns):
    half = rows // TILE // 2
    return [
        pl.BlockSpec((TILE, columns), lambda i: (jnp.minimum(i, half - 1), 0)),
        pl.BlockSpec((TILE, columns), lambda i: (jnp.maximum(i - half, 0), 0)),
    ]


def mlp_forward_kernel(normed, gate_up, down, _, hidden, gelu, slope, mine, other):
    own = down.shape[0]
    raw = matmul(normed[...], gate_up[...])
    gate_raw, up_raw = raw[:, :own], raw[:, own:]
    square = gate_raw * gate_raw
    bend = jnp.tanh(GELU_A * (gate_raw + GELU_B * square * gate_raw))
    half = 0.5 + 0.5 * bend
    active = gate_raw * half
    turn = 0.5 * gate_raw * (1.0 - bend * bend) * (GELU_A * (1.0 + 3.0 * GELU_B * square))
    low = (active * up_raw).astype(BF)
    hidden[...] = low
    gelu[...] = active.astype(BF)
    slope[...] = ((half + turn) * up_raw).astype(BF)
    store_half(matmul(low, down[...]).astype(BF), mine, other)


def mlp_forward(normed, gate_up, down, earlier):
    rows, width = normed.shape
    own = down.shape[0]
    flat = jax.ShapeDtypeStruct((rows, own), BF)
    part = jax.ShapeDtypeStruct((rows // 2, width), BF)
    return pl.pallas_call(
        mlp_forward_kernel,
        grid=(rows // TILE,),
        in_specs=[
            row_block(TILE, width),
            whole_block(gate_up.shape),
            whole_block(down.shape),
            pl.BlockSpec(memory_space=pl.ANY),
        ],
        out_specs=[row_block(TILE, own)] * 3 + half_blocks(rows, width),
        out_shape=[flat, flat, flat, part, part],
        compiler_params=PARAMS,
        cost_estimate=pl.CostEstimate(
            flops=6 * rows * width * own, bytes_accessed=rows * (4 * width + 6 * own), transcendentals=0
        ),
    )(normed, gate_up, down, earlier)


def mlp_backward_kernel(grad_mixed, gelu, slope, gate_up, down, _, grad_raw, mine, other):
    own = down.shape[0]
    grad_hidden = by_transpose(grad_mixed[...], down[...])
    grad_gate = (grad_hidden * slope[...].astype(F32)).astype(BF)
    grad_up = (grad_hidden * gelu[...].astype(F32)).astype(BF)
    grad_raw[:, :own] = grad_gate
    grad_raw[:, own:] = grad_up
    total = by_transpose(grad_gate, gate_up[:, :own]) + by_transpose(grad_up, gate_up[:, own:])
    store_half(total.astype(BF), mine, other)


def mlp_backward(grad_mixed, gelu, slope, gate_up, down, earlier):
    rows, width = grad_mixed.shape
    own = down.shape[0]
    return pl.pallas_call(
        mlp_backward_kernel,
        grid=(rows // TILE,),
        in_specs=[
            row_block(TILE, width),
            row_block(TILE, own),
            row_block(TILE, own),
            whole_block(gate_up.shape),
            whole_block(down.shape),
            pl.BlockSpec(memory_space=pl.ANY),
        ],
        out_specs=[row_block(TILE, 2 * own)] + half_blocks(rows, width),
        out_shape=[
            jax.ShapeDtypeStruct((rows, 2 * own), BF),
            jax.ShapeDtypeStruct((rows // 2, width), BF),
            jax.ShapeDtypeStruct((rows // 2, width), BF),
        ],
        compiler_params=PARAMS,
        cost_estimate=pl.CostEstimate(
            flops=6 * rows * width * own, bytes_accessed=rows * (4 * width + 8 * own), transcendentals=0
        ),
    )(grad_mixed, gelu, slope, gate_up, down, earlier)


def down_terms_kernel(*refs):
    *ins, out = refs
    half = len(ins) // 2
    total = over_rows(ins[0][...], ins[half][...])
    for left, right in zip(ins[1:half], ins[half + 1 :]):
        total = total + over_rows(left[...], right[...])
    out[...] = total.astype(BF)


def down_terms(hidden, grad_mixed, keep):
    own, width = hidden[0].shape[1], grad_mixed[0].shape[1]
    rows = sum(part.shape[0] for part in hidden)
    return pl.pallas_call(
        down_terms_kernel,
        grid=(own // 128,),
        in_specs=[pl.BlockSpec((part.shape[0], 128), lambda i: (0, i)) for part in hidden]
        + [whole_block(part.shape) for part in grad_mixed],
        out_specs=row_block(128, width),
        out_shape=jax.ShapeDtypeStruct((keep, width), BF),
        compiler_params=PARAMS,
        cost_estimate=pl.CostEstimate(
            flops=2 * rows * width * own, bytes_accessed=2 * rows * (width + own), transcendentals=0
        ),
    )(*hidden, *grad_mixed)


def gate_terms_kernel(*refs):
    *ins, _, out = refs
    half = len(ins) // 2
    total = over_rows(ins[0][...], ins[half][...])
    for left, right in zip(ins[1:half], ins[half + 1 :]):
        total = total + over_rows(left[...], right[...])
    total = total.astype(BF)
    groups, sides, rows, _ = out.shape
    for side in range(sides):
        for group in range(groups):
            first = (side * groups + group) * rows
            out[group, side] = total[first : first + rows]


def gate_terms(normed, grad_raw, groups, first, steps, earlier):
    width, both = normed[0].shape[1], steps * STEP
    rows = sum(part.shape[0] for part in normed)
    shape = (groups, 2, width // (2 * groups))
    return pl.pallas_call(
        gate_terms_kernel,
        grid=(steps,),
        in_specs=[whole_block(part.shape) for part in normed]
        + [pl.BlockSpec((part.shape[0], STEP), lambda i: (0, first + i)) for part in grad_raw]
        + [pl.BlockSpec(memory_space=pl.ANY)],
        out_specs=pl.BlockSpec(shape + (STEP,), lambda i: (0, 0, 0, i)),
        out_shape=jax.ShapeDtypeStruct(shape + (both,), BF),
        compiler_params=PARAMS,
        cost_estimate=pl.CostEstimate(
            flops=2 * rows * width * both, bytes_accessed=2 * rows * (width + both), transcendentals=0
        ),
    )(*normed, *grad_raw, earlier)


def after(value, *earlier):
    return lax.optimization_barrier((value, *earlier))[0]


def with_core(part):
    return jnp.concatenate([part, swap(part, "c")])


def core_sum(mine, other):
    return mine.astype(F32) + swap(other, "c").astype(F32)


def send_far(far):
    half = far.shape[0] // 2
    return swap(far[:half], "y"), swap(far[half:], "x")


def sum_near(mine, other, top, low):
    mine, other, top, low = lax.optimization_barrier((mine, other, top, low))
    near = core_sum(mine, other)
    rows = near.shape[0] // 2
    half = rows // 2
    to_x = jnp.concatenate([near[:half] + top, near[half:rows]]).astype(BF)
    to_y = jnp.concatenate([near[rows : rows + half], near[rows + half :] + low]).astype(BF)
    return to_x, to_y


def sum_own(mine, other, to_x, to_y):
    total = core_sum(mine, other)
    return total + swap(to_x, "x").astype(F32) + swap(to_y, "y").astype(F32)


def in_order(own, other, place):
    both = jnp.concatenate([own[None], other[None], own[None]])
    return lax.dynamic_slice_in_dim(both, place, 2, 0)


def group_gather(own):
    size = lax.axis_size("g")
    parts = [own] + [
        lax.ppermute(own, "g", [((i + k) % size, i) for i in range(size)]) for k in range(1, size)
    ]
    both = jnp.stack(parts + parts[:-1])
    place = lax.axis_index("g")
    return lax.dynamic_slice_in_dim(both, lax.rem(size - place, size), size, 0)


def plane_weights(blocks, *earlier):
    x, y = lax.axis_index("x"), lax.axis_index("y")
    half = blocks.shape[0] // 2
    first, second = blocks[:half], blocks[half:]
    first = in_order(first, swap(first, "x"), x)
    second = in_order(second, swap(second, "y"), y)
    first, second = lax.optimization_barrier((first, second, *earlier))[:2]
    first = in_order(first, swap(first, "y"), y)
    second = in_order(second, swap(second, "x"), x)
    first = first.transpose(1, 2, 0, 3, 4)
    second = second.transpose(0, 2, 1, 3, 4)
    return jnp.concatenate([first, second], axis=1)


def group_terms(term):
    size = lax.axis_size("g")
    place = lax.axis_index("g")
    total = lax.dynamic_index_in_dim(term, place, 0, keepdims=False).astype(F32)
    for k in range(1, size):
        chunk = lax.dynamic_index_in_dim(term, lax.rem(place + k, size), 0, keepdims=False)
        pairs = [(i, (i + k) % size) for i in range(size)]
        total = total + lax.ppermute(chunk, "g", pairs).astype(F32)
    return total


def fold(term, axis, dim):
    place = lax.axis_index(axis)
    mine = lax.dynamic_index_in_dim(term, place, dim, keepdims=False)
    other = lax.dynamic_index_in_dim(term, 1 - place, dim, keepdims=False)
    return (mine.astype(F32) + swap(other.astype(BF), axis).astype(F32)).astype(BF)


def plane_terms(term):
    half = term.shape[1] // 2
    first = fold(fold(term[:, :half], "x", 0), "y", 1)
    second = fold(fold(term[:, half:], "y", 2), "x", 0)
    return jnp.concatenate([first, second])


def rms_scale(values):
    return lax.rsqrt(jnp.mean(values * values, axis=-1, keepdims=True) + EPSILON)


def rms_backward(values, scale, gain, grad):
    weighted = grad * gain
    inner = jnp.mean(weighted * values, axis=-1, keepdims=True)
    terms = jnp.sum(grad * values * scale, axis=0, keepdims=True)
    return weighted * scale - values * (scale * scale * scale * inner), terms


def turn_forward(values, cosine, sine):
    half = cosine.shape[1]
    low, high = values[:, :half], values[:, half:]
    return jnp.concatenate([low * cosine - high * sine, high * cosine + low * sine], axis=1)


def turn_backward(grad, cosine, sine):
    half = cosine.shape[1]
    low, high = grad[:, :half], grad[:, half:]
    return jnp.concatenate([low * cosine + high * sine, high * cosine - low * sine], axis=1)


def gain_places(width, columns, shard_rows):
    heads = columns // (width // shard_rows)
    row = lax.broadcasted_iota(jnp.int32, (width, columns), 0)
    column = lax.broadcasted_iota(jnp.int32, (width, columns), 1)
    place = (column // heads) * shard_rows + lax.rem(column, heads)
    return jnp.where(row == place, 1.0, 0.0).astype(BF)


def project_kernel(
    shard_rows, core, tokens, earlier, own, other, cosine, sine,
    normed, normed_earlier, query_raw, key_raw, queries, keys, values, d_gains, h_gains,
):
    rows, width = tokens.shape
    pad, k_cols = earlier.shape[0], key_raw.shape[1]
    half = query_raw.shape[1] // 2
    first_is_own = core[0] == 0
    block = jnp.where(
        first_is_own, own[:, half + k_cols :].astype(F32), other[:, half + k_cols :].astype(F32)
    )
    flat = block.T[:8]
    d_gains[...] = flat
    chosen = matmul(flat.astype(BF), gain_places(width, k_cols, shard_rows))
    h_gains[...] = chosen
    before = earlier[...].astype(F32)
    low_before = (before * rms_scale(before) * flat[0:1]).astype(BF)
    normed_earlier[...] = low_before
    inputs = tokens[...].astype(F32)
    low = (inputs * rms_scale(inputs) * flat[0:1]).astype(BF)
    normed[...] = low
    raw_own = matmul(low, own[:, : half + k_cols])
    raw_other = matmul(low, other[:, : half + k_cols])
    before_own = matmul(low_before, own[:, half : half + k_cols])
    before_other = matmul(low_before, other[:, half : half + k_cols])
    first = jnp.where(first_is_own, raw_own, raw_other)
    second = jnp.where(first_is_own, raw_other, raw_own)
    raw_query = jnp.concatenate([first[:, :half], second[:, :half]], axis=1)
    query_raw[...] = raw_query
    values[:pad] = jnp.where(first_is_own, before_other, before_own).astype(BF)
    values[pad:] = second[:, half:].astype(BF)
    raw_before = jnp.where(first_is_own, before_own, before_other)
    for raw, at in ((raw_before, slice(0, pad)), (first[:, half:], slice(pad, pad + rows))):
        key_raw[at] = raw
        part = raw * rms_scale(raw) * chosen[5:6]
        keys[at] = turn_forward(part, cosine[at], sine[at]).astype(BF)
    cos, sin = cosine[pad:], sine[pad:]
    for head in range(2 * half // k_cols):
        at = slice(head * k_cols, (head + 1) * k_cols)
        part = raw_query[:, at]
        part = part * rms_scale(part) * chosen[4:5]
        queries[:, at] = turn_forward(part, cos, sin).astype(BF)


def project(core, tokens, earlier, own, other, cosine, sine, shard_rows, q_cols, k_cols):
    rows, width = tokens.shape
    seen = rows + earlier.shape[0]
    vmem = pl.BlockSpec(memory_space=pltpu.VMEM)
    return pl.pallas_call(
        functools.partial(project_kernel, shard_rows),
        in_specs=[pl.BlockSpec(memory_space=pltpu.SMEM)] + [vmem] * 6,
        out_specs=[vmem] * 9,
        out_shape=[
            jax.ShapeDtypeStruct((rows, width), BF),
            jax.ShapeDtypeStruct(earlier.shape, BF),
            jax.ShapeDtypeStruct((rows, q_cols), F32),
            jax.ShapeDtypeStruct((seen, k_cols), F32),
            jax.ShapeDtypeStruct((rows, q_cols), BF),
            jax.ShapeDtypeStruct((seen, k_cols), BF),
            jax.ShapeDtypeStruct((seen, k_cols), BF),
            jax.ShapeDtypeStruct((8, width), F32),
            jax.ShapeDtypeStruct((8, k_cols), F32),
        ],
        compiler_params=PARAMS,
        cost_estimate=pl.CostEstimate(
            flops=2 * rows * width * (q_cols + 4 * k_cols), bytes_accessed=16 * rows * width, transcendentals=0
        ),
    )(core, tokens, earlier, own, other, cosine, sine)


def tile_mask(first, rows, first_key, keys, query_ids, key_ids, pad):
    query_place = pad + first + lax.broadcasted_iota(jnp.int32, (rows, keys), 0)
    key_place = first_key + lax.broadcasted_iota(jnp.int32, (rows, keys), 1)
    distance = query_place - key_place
    same_doc = query_ids[first : first + rows, :] == key_ids[:, first_key : first_key + keys]
    return (distance >= 0) & (distance < WINDOW) & same_doc


def attend_kernel(
    scale, queries, keys, values, query_ids, key_ids, w_o, tokens, d_gains,
    attended, log_total, branch, middle, normed_mlp,
):
    rows, q_cols = queries.shape
    pad, k_cols = keys.shape[0] - rows, keys.shape[1]
    tile = rows // 2
    span = pad + tile
    lane = lax.broadcasted_iota(jnp.int32, (tile, 128), 1)
    for first in (0, tile):
        at = slice(first, first + tile)
        seen = slice(first, first + span)
        allowed = tile_mask(first, tile, first, span, query_ids, key_ids, pad)
        logs = jnp.zeros((tile, 128), F32)
        for head in range(q_cols // k_cols):
            columns = slice(head * k_cols, (head + 1) * k_cols)
            scores = by_transpose(queries[at, columns], keys[seen]) * scale
            scores = jnp.where(allowed, scores, -1e30)
            row_max = jnp.max(scores, axis=-1, keepdims=True)
            weights = jnp.exp(scores - row_max)
            row_total = jnp.sum(weights, axis=-1, keepdims=True)
            probabilities = (weights * (1.0 / row_total)).astype(BF)
            attended[at, columns] = matmul(probabilities, values[seen]).astype(BF)
            logs = jnp.where(lane == head, row_max + jnp.log(row_total), logs)
        log_total[at] = logs
    out = matmul(attended[...], w_o[...])
    branch[...] = out
    total = tokens[...].astype(F32) + out * rms_scale(out) * d_gains[1:2]
    middle[...] = total
    normed_mlp[...] = (total * rms_scale(total) * d_gains[2:3]).astype(BF)


def attend(queries, keys, values, query_ids, key_ids, w_o, tokens, d_gains, scale):
    rows, q_cols = queries.shape
    width = tokens.shape[1]
    vmem = pl.BlockSpec(memory_space=pltpu.VMEM)
    return pl.pallas_call(
        functools.partial(attend_kernel, scale),
        in_specs=[vmem] * 8,
        out_specs=[vmem] * 5,
        out_shape=[
            jax.ShapeDtypeStruct((rows, q_cols), BF),
            jax.ShapeDtypeStruct((rows, 128), F32),
            jax.ShapeDtypeStruct((rows, width), F32),
            jax.ShapeDtypeStruct((rows, width), F32),
            jax.ShapeDtypeStruct((rows, width), BF),
        ],
        compiler_params=PARAMS,
        cost_estimate=pl.CostEstimate(
            flops=2 * rows * q_cols * (width + 2 * keys.shape[0]), bytes_accessed=20 * rows * width, transcendentals=0
        ),
    )(queries, keys, values, query_ids, key_ids, w_o, tokens, d_gains)


def attend_backward_kernel(
    scale, grad_normed_mlp, cotangent, middle, branch, d_gains, w_o,
    queries, keys, values, query_ids, key_ids, log_total,
    grad_middle, grad_branch, grad_queries, grad_keys, grad_values, terms, grad_attended,
):
    rows, q_cols = queries.shape
    pad, k_cols = keys.shape[0] - rows, keys.shape[1]
    total = middle[...]
    from_mlp, mlp_terms = rms_backward(total, rms_scale(total), d_gains[2:3], grad_normed_mlp[...])
    grad_total = cotangent[...].astype(F32) + from_mlp
    grad_middle[...] = grad_total
    out = branch[...]
    grad_out, out_terms = rms_backward(out, rms_scale(out), d_gains[1:2], grad_total)
    low = grad_out.astype(BF)
    grad_branch[...] = low
    terms[...] = jnp.concatenate([out_terms, mlp_terms, jnp.zeros((6, out.shape[1]), F32)], axis=0)
    grad_attended[...] = by_transpose(low, w_o[...]).astype(BF)
    grad_keys[...] = jnp.zeros_like(grad_keys)
    grad_values[...] = jnp.zeros_like(grad_values)
    tile = rows // 2
    span = pad + tile
    for first in (0, tile):
        at = slice(first, first + tile)
        seen = slice(first, first + span)
        allowed = tile_mask(first, tile, first, span, query_ids, key_ids, pad)
        key_total = jnp.zeros((span, k_cols), F32)
        value_total = jnp.zeros((span, k_cols), F32)
        for head in range(q_cols // k_cols):
            columns = slice(head * k_cols, (head + 1) * k_cols)
            query = queries[at, columns]
            grad = grad_attended[at, columns]
            scores = by_transpose(query, keys[seen]) * scale
            probabilities = jnp.where(
                allowed, jnp.exp(scores - log_total[at, head : head + 1]), 0.0
            )
            grad_prob = by_transpose(grad, values[seen])
            inner = jnp.sum(probabilities * grad_prob, axis=-1, keepdims=True)
            grad_score = (probabilities * (grad_prob - inner)).astype(BF)
            grad_queries[at, columns] = matmul(grad_score, keys[seen]) * scale
            key_total = key_total + over_rows(grad_score, query)
            value_total = value_total + over_rows(probabilities.astype(BF), grad)
        grad_keys[seen] = grad_keys[seen] + key_total * scale
        grad_values[seen] = grad_values[seen] + value_total


def attend_backward(
    grad_normed_mlp, cotangent, middle, branch, d_gains, w_o,
    queries, keys, values, query_ids, key_ids, log_total, scale,
):
    rows, q_cols = queries.shape
    width = middle.shape[1]
    vmem = pl.BlockSpec(memory_space=pltpu.VMEM)
    return pl.pallas_call(
        functools.partial(attend_backward_kernel, scale),
        in_specs=[vmem] * 12,
        out_specs=[vmem] * 6,
        out_shape=[
            jax.ShapeDtypeStruct((rows, width), F32),
            jax.ShapeDtypeStruct((rows, width), BF),
            jax.ShapeDtypeStruct((rows, q_cols), F32),
            jax.ShapeDtypeStruct(keys.shape, F32),
            jax.ShapeDtypeStruct(keys.shape, F32),
            jax.ShapeDtypeStruct((8, width), F32),
        ],
        scratch_shapes=[pltpu.VMEM((rows, q_cols), BF)],
        compiler_params=PARAMS,
        cost_estimate=pl.CostEstimate(
            flops=2 * rows * q_cols * (width + 5 * keys.shape[0]), bytes_accessed=30 * rows * width, transcendentals=0
        ),
    )(
        grad_normed_mlp, cotangent, middle, branch, d_gains, w_o,
        queries, keys, values, query_ids, key_ids, log_total,
    )


def project_backward_kernel(
    shard_rows, core, grad_queries, grad_keys, grad_values, query_raw, key_raw, cosine, sine,
    h_gains, normed, normed_earlier, own, other, tokens, earlier, d_gains, terms, mixed_terms,
    grad_normed, returned, mine, sent,
):
    rows, width = tokens.shape
    pad, k_cols = earlier.shape[0], key_raw.shape[1]
    half = query_raw.shape[1] // 2
    cols = half + k_cols
    first_is_own = core[0] == 0
    cos, sin = cosine[pad:], sine[pad:]
    query_terms = jnp.zeros((1, k_cols), F32)
    parts = []
    for head in range(2 * half // k_cols):
        at = slice(head * k_cols, (head + 1) * k_cols)
        raw = query_raw[:, at]
        grad = turn_backward(grad_queries[:, at], cos, sin)
        grad, term = rms_backward(raw, rms_scale(raw), h_gains[4:5], grad)
        query_terms = query_terms + term
        parts.append(grad.astype(BF))
    raw = key_raw[...]
    grad = turn_backward(grad_keys[...], cosine[...], sine[...])
    grad, key_terms = rms_backward(raw, rms_scale(raw), h_gains[5:6], grad)
    grad_key, grad_value = grad.astype(BF), grad_values[...].astype(BF)
    returned[:, :k_cols] = grad_key[:pad]
    returned[:, k_cols:] = grad_value[:pad]
    kv_own = jnp.where(first_is_own, grad_key, grad_value)
    kv_other = jnp.where(first_is_own, grad_value, grad_key)
    both = len(parts) // 2
    first = jnp.concatenate(parts[:both], axis=1)
    second = jnp.concatenate(parts[both:], axis=1)
    q_own = jnp.where(first_is_own, first, second)
    q_other = jnp.where(first_is_own, second, first)
    grad_own = jnp.concatenate([q_own, kv_own[pad:]], axis=1)
    grad_other = jnp.concatenate([q_other, kv_other[pad:]], axis=1)
    total = by_transpose(grad_own, own[:, :cols]) + by_transpose(grad_other, other[:, :cols])
    grad_normed[...] = total
    values = tokens[...].astype(F32)
    in_terms = jnp.sum(total * values * rms_scale(values), axis=0, keepdims=True)
    total = by_transpose(kv_own[:pad], own[:, half:cols])
    total = total + by_transpose(kv_other[:pad], other[:, half:cols])
    values = earlier[...].astype(F32)
    in_terms = in_terms + jnp.sum(total * values * rms_scale(values), axis=0, keepdims=True)
    low, low_before = normed[...], normed_earlier[...]
    for out, query, key_value in ((mine, q_own, kv_own), (sent, q_other, kv_other)):
        out[:, :half] = over_rows(low, query).astype(BF)
        out[:, half:cols] = (
            over_rows(low, key_value[pad:]) + over_rows(low_before, key_value[:pad])
        ).astype(BF)
    heads = jnp.concatenate([query_terms, key_terms, jnp.zeros((6, k_cols), F32)], axis=0)
    placed = by_transpose(heads.astype(BF), gain_places(width, k_cols, shard_rows))
    block = jnp.concatenate(
        [in_terms, terms[0:2], mixed_terms[0:1], placed[0:2], jnp.zeros((122, width), F32)], axis=0
    ).T
    mine[:, cols:] = jnp.where(first_is_own, block, 0.0).astype(BF)
    sent[:, cols:] = jnp.where(first_is_own, 0.0, block).astype(BF)


def project_backward(
    core, grad_queries, grad_keys, grad_values, query_raw, key_raw, cosine, sine,
    h_gains, normed, normed_earlier, own, other, tokens, earlier, d_gains, terms, mixed_terms,
    shard_rows,
):
    rows, width = tokens.shape
    pad, k_cols = earlier.shape[0], key_raw.shape[1]
    vmem = pl.BlockSpec(memory_space=pltpu.VMEM)
    return pl.pallas_call(
        functools.partial(project_backward_kernel, shard_rows),
        in_specs=[pl.BlockSpec(memory_space=pltpu.SMEM)] + [vmem] * 17,
        out_specs=[vmem] * 4,
        out_shape=[
            jax.ShapeDtypeStruct((rows, width), F32),
            jax.ShapeDtypeStruct((pad, 2 * k_cols), BF),
            jax.ShapeDtypeStruct(own.shape, BF),
            jax.ShapeDtypeStruct(own.shape, BF),
        ],
        compiler_params=PARAMS,
        cost_estimate=pl.CostEstimate(
            flops=9 * rows * width * own.shape[1], bytes_accessed=30 * rows * width, transcendentals=0
        ),
    )(
        core, grad_queries, grad_keys, grad_values, query_raw, key_raw, cosine, sine,
        h_gains, normed, normed_earlier, own, other, tokens, earlier, d_gains, terms, mixed_terms,
    )


def grad_tokens_kernel(core, returned, grad_normed, own, other, tokens, d_gains, grad_middle, out):
    k_cols = returned.shape[1] // 2
    cols = own.shape[1] - 128
    half = cols - k_cols
    first_is_own = core[0] == 0
    grad_key, grad_value = returned[:, :k_cols], returned[:, k_cols:]
    kv_own = jnp.where(first_is_own, grad_key, grad_value)
    kv_other = jnp.where(first_is_own, grad_value, grad_key)
    total = grad_normed[...] + by_transpose(kv_own, own[:, half:cols])
    total = total + by_transpose(kv_other, other[:, half:cols])
    values = tokens[...].astype(F32)
    from_attn, _ = rms_backward(values, rms_scale(values), d_gains[0:1], total)
    out[...] = (grad_middle[...] + from_attn).astype(BF)


def grad_tokens(core, returned, grad_normed, own, other, tokens, d_gains, grad_middle):
    vmem = pl.BlockSpec(memory_space=pltpu.VMEM)
    return pl.pallas_call(
        grad_tokens_kernel,
        in_specs=[pl.BlockSpec(memory_space=pltpu.SMEM)] + [vmem] * 7,
        out_specs=vmem,
        out_shape=jax.ShapeDtypeStruct(tokens.shape, BF),
        compiler_params=PARAMS,
        cost_estimate=pl.CostEstimate(
            flops=2 * tokens.size * returned.shape[1], bytes_accessed=12 * tokens.size, transcendentals=0
        ),
    )(core, returned, grad_normed, own, other, tokens, d_gains, grad_middle)


def on_device(
    tokens,
    cotangent,
    doc_ids,
    w_query,
    w_key,
    w_value,
    w_out,
    w_gate,
    w_up,
    w_down,
    gain_attn_in,
    gain_attn_out,
    gain_mlp_in,
    gain_mlp_out,
    gain_query,
    gain_key,
):
    row_count = tokens.shape[1]
    width = tokens.shape[2]
    groups = lax.axis_size("g")
    members = lax.axis_size(PLANE)
    shard_rows = w_query.shape[0]
    head_rows = gain_query.shape[0]
    hidden_all = w_gate.shape[1]
    hidden_own = hidden_all // members
    hidden_pad = -(-hidden_own // 128) * 128
    piece = hidden_own // groups
    q_cols, k_cols = w_query.shape[1], w_key.shape[1]
    attn_scale = HEAD ** (-0.5)

    def gain_columns(d_gains, h_gains):
        columns = list(d_gains) + [
            jnp.pad(h, ((0, 0), (0, shard_rows - head_rows))) for h in h_gains
        ]
        block = jnp.stack(columns, axis=-1)
        return jnp.pad(block, ((0, 0), (0, 0), (0, 128 - len(columns))))

    seq_place = lax.axis_index(("g", "y", "c"))
    seq_size = lax.axis_size(("g", "y", "c"))
    before = lax.ppermute(tokens[0], ("g", "y", "c"), [(i, i + 1) for i in range(seq_size - 1)])

    def spread(weight):
        cut = weight.reshape(shard_rows, 2, groups, members // 2, piece)
        cut = cut.transpose(1, 3, 0, 2, 4).reshape(members, shard_rows, hidden_own)
        return jnp.pad(cut, ((0, 0), (0, 0), (0, hidden_pad - hidden_own)))

    sent = jnp.concatenate([spread(w_gate), spread(w_up)], axis=2)
    core = lax.axis_index("c")
    half_cols = q_cols // 2 + k_cols + 128
    gains = gain_columns(
        [g[None] for g in (gain_attn_in, gain_attn_out, gain_mlp_in, gain_mlp_out)],
        [gain_query[None], gain_key[None]],
    )
    halves = jnp.stack(
        [
            jnp.concatenate([w_query[:, : q_cols // 2], w_key, gains[0]], axis=1),
            jnp.concatenate([w_query[:, q_cols // 2 :], w_value, jnp.zeros_like(gains[0])], axis=1),
        ]
    )
    mine = lax.dynamic_index_in_dim(halves, core, 0, keepdims=False)
    other = lax.dynamic_index_in_dim(halves, 1 - core, 0, keepdims=False)
    mine = in_order(mine, swap(other, "c"), core).reshape(2 * shard_rows, half_cols)
    mine, before, sent = lax.optimization_barrier((mine, before, sent))
    sent = lax.all_to_all(sent, PLANE, split_axis=0, concat_axis=0, tiled=True)
    sent = sent.reshape(members * shard_rows, 2 * hidden_pad)
    mine, sent = lax.optimization_barrier((group_gather(mine), sent))
    mine = plane_weights(mine).reshape(width, half_cols)
    other = swap(mine, "c")

    down = lax.all_gather(jnp.concatenate([w_down, w_out]), "g", axis=0)
    w_o = down[:, w_down.shape[0] :]
    down = down[:, : w_down.shape[0]].reshape(-1, width)
    down = jnp.pad(down, ((0, hidden_pad - hidden_own), (0, 0)))

    both = lax.all_gather(sent, "g", axis=0)
    both = both.reshape(groups, 2, members // 2 * shard_rows, 2 * hidden_pad)
    gate_up = both.transpose(1, 0, 2, 3).reshape(width, 2 * hidden_pad)

    first_row = seq_place * row_count
    ids_all = doc_ids[0]
    ids_own = lax.dynamic_slice_in_dim(ids_all, first_row, row_count, 0)
    ids_prev = lax.dynamic_slice_in_dim(
        ids_all, jnp.maximum(first_row - row_count, 0), row_count, 0
    )
    ids_prev = jnp.where(seq_place > 0, ids_prev, -1)
    ids_pad = jnp.concatenate([ids_prev, ids_own])
    query_ids, key_ids = ids_own[:, None], ids_pad[None]
    cosine_table, sine_table = rope_tables(first_row - row_count, 2 * row_count, HEAD)
    places = jnp.full((1,), core, jnp.int32)
    layer_in, grad_out = tokens[0], cotangent[0]

    normed, normed_before, query_raw, key_raw, queries, keys, values, d_gains, h_gains = project(
        places, layer_in, before, mine, other, cosine_table, sine_table, shard_rows, q_cols, k_cols
    )
    w_o = plane_weights(w_o, keys)
    w_o = in_order(w_o, swap(w_o, "c"), core).transpose(1, 2, 3, 0, 4, 5).reshape(q_cols, width)
    w_o = after(w_o, down)
    attended, log_total, branch, middle, normed_mlp = attend(
        queries, keys, values, query_ids, key_ids, w_o, layer_in, d_gains, attn_scale
    )

    half = row_count // 2
    from_x, from_y = swap(normed_mlp, "x"), swap(normed_mlp, "y")
    normed_far = jnp.concatenate([swap(from_x[:half], "y"), swap(from_y[half:], "x")])
    normed_near = jnp.concatenate([from_x, from_y])
    normed_far, gate_up = lax.optimization_barrier((normed_far, gate_up))
    normed_all = [with_core(part) for part in (normed_mlp, normed_near, normed_far)]
    far_result = mlp_forward(normed_all[2], gate_up, down, normed_all[0])
    far_sum = core_sum(*far_result[3:]).astype(BF)
    near_result = mlp_forward(normed_all[1], gate_up, down, far_sum)
    to_x, to_y = sum_near(*near_result[3:], *send_far(far_sum))
    own_result = mlp_forward(normed_all[0], gate_up, down, to_x)
    mixed = sum_own(*own_result[3:], to_x, to_y)
    layer_out = middle + norm_gain(mixed, d_gains[3:4])

    _, pullback = jax.vjp(norm_gain, mixed, d_gains[3:4])
    grad_mixed, mixed_terms = pullback(grad_out.astype(F32))
    grad_mixed = grad_mixed.astype(BF)
    from_x, from_y = swap(grad_mixed, "x"), swap(grad_mixed, "y")
    grad_own = with_core(grad_mixed)
    own_grads = mlp_backward(grad_own, own_result[1], own_result[2], gate_up, down, down)
    from_x, from_y = lax.optimization_barrier((from_x, from_y, own_grads[1]))[:2]
    grad_far = with_core(jnp.concatenate([swap(from_x[:half], "y"), swap(from_y[half:], "x")]))
    grad_near = with_core(jnp.concatenate([from_x, from_y]))
    grad_down_terms = down_terms(
        [r[0] for r in (own_result, near_result, far_result)],
        [grad_own, grad_near, grad_far],
        hidden_own,
    )
    grad_down = group_terms(grad_down_terms.reshape(groups, -1, width))
    far_grads = mlp_backward(
        grad_far, far_result[1], far_result[2], gate_up, down, grad_down_terms
    )
    far_sum = core_sum(*far_grads[1:]).astype(BF)
    near_grads = mlp_backward(grad_near, near_result[1], near_result[2], gate_up, down, far_sum)
    to_x, to_y = sum_near(*near_grads[1:], *send_far(far_sum))
    raw_grads = [g[0] for g in (own_grads, near_grads, far_grads)]
    gate_up_terms = gate_terms(normed_all, raw_grads, groups, 0, 2 * hidden_pad // STEP, to_x)
    grad_normed_mlp = sum_own(*own_grads[1:], to_x, to_y)
    grad_normed_mlp = after(grad_normed_mlp, gate_up_terms)
    term = gate_up_terms.reshape(groups * members * shard_rows, 2 * hidden_pad)
    term = lax.psum_scatter(term, "g", scatter_dimension=0, tiled=True)
    gate_up_share = term.reshape(members, shard_rows, 2 * hidden_pad)
    term = lax.all_to_all(gate_up_share, PLANE, split_axis=0, concat_axis=0, tiled=True)

    def collect(cut):
        cut = cut[:, :, :hidden_own].reshape(2, members // 2, shard_rows, groups, piece)
        return cut.transpose(2, 0, 3, 1, 4).reshape(shard_rows, hidden_all).astype(F32)

    grad_w_gate = collect(term[:, :, :hidden_pad])
    grad_w_up = collect(term[:, :, hidden_pad:])

    grad_middle, grad_branch, grad_queries, grad_keys, grad_values, terms = attend_backward(
        grad_normed_mlp, grad_out, middle, branch, d_gains, w_o,
        queries, keys, values, query_ids, key_ids, log_total, attn_scale,
    )
    out_terms = over_rows(attended, grad_branch).astype(BF)
    out_terms = out_terms.reshape(2, groups, 2, 2, w_out.shape[0], width)
    out_terms = plane_terms(fold(out_terms, "c", 3))
    own_weights, other_weights = mine, other
    grad_normed, returned, mine, sent = project_backward(
        places, after(grad_queries, grad_down), grad_keys, grad_values, query_raw, key_raw,
        cosine_table, sine_table, h_gains, normed, normed_before, own_weights, other_weights,
        layer_in, before, d_gains, terms, mixed_terms, shard_rows,
    )
    returned = lax.ppermute(returned, ("g", "y", "c"), [(i + 1, i) for i in range(seq_size - 1)])
    grad_in = grad_tokens(
        places, returned, grad_normed, own_weights, other_weights, layer_in, d_gains, grad_middle
    )
    mine = (mine.astype(F32) + swap(sent, "c").astype(F32)).astype(BF)
    qkv_terms = plane_terms(mine.reshape(2, groups, 2, 2 * shard_rows, half_cols))
    qkv_terms = qkv_terms.reshape(groups, -1, width)
    share = jnp.concatenate([out_terms, qkv_terms], axis=1)
    share = group_terms(after(share, gate_up_share))
    grad_w_out = share[: w_out.shape[0]]
    share = share[w_out.shape[0] :].astype(BF).reshape(2, shard_rows, half_cols)
    mine = lax.dynamic_index_in_dim(share, core, 0, keepdims=False)
    other = lax.dynamic_index_in_dim(share, 1 - core, 0, keepdims=False)
    first, second = in_order(mine, swap(other, "c"), core).astype(F32)
    half = q_cols // 2
    d_terms = first[:, half + k_cols :]
    return (
        layer_out.astype(BF)[None],
        grad_in[None],
        jnp.concatenate([first[:, :half], second[:, :half]], axis=1),
        first[:, half : half + k_cols],
        second[:, half : half + k_cols],
        grad_w_out,
        grad_w_gate,
        grad_w_up,
        grad_down,
        d_terms[:, 0],
        d_terms[:, 1],
        d_terms[:, 2],
        d_terms[:, 3],
        d_terms[:head_rows, 4],
        d_terms[:head_rows, 5],
    )


def solution(mesh):
    batch, seq = mesh.devices.shape
    fine = Mesh(mesh.devices.reshape(batch, seq // 4, 2, 2), ALL)
    rows = ("g", "y", "c")
    return jax.shard_map(
        on_device,
        mesh=fine,
        in_specs=(P("x", rows, None),) * 2
        + (P("x", None),)
        + (P(ALL, None),) * 7
        + (P(ALL),) * 6,
        out_specs=(P("x", rows, None),) * 2 + (P(ALL, None),) * 7 + (P(ALL),) * 6,
        check_vma=False,
    )
```

```python
import functools

import jax
import jax.numpy as jnp
from jax import lax
from jax.experimental import pallas as pl
from jax.experimental.pallas import tpu as pltpu
from jax.sharding import Mesh
from jax.sharding import PartitionSpec as P

HEAD = 256
WINDOW = 512
EPSILON = 1e-06
ROPE_BASE = 10000.0
ALL = ("x", "g", "y", "c")
PLANE = ("x", "y", "c")
BF = jnp.bfloat16
F32 = jnp.float32


def norm_gain(values, gain_vec):
    return (
        values * lax.rsqrt(jnp.mean(values * values, axis=-1, keepdims=True) + EPSILON) * gain_vec
    )


def rope_tables(first_row, row_count, head_size):
    places = (first_row + jnp.arange(row_count, dtype=jnp.int32)).astype(F32)
    frequency = ROPE_BASE ** (-(jnp.arange(head_size // 2, dtype=F32) * 2.0) / head_size)
    angles = places[:, None] * frequency[None, :]
    return (jnp.cos(angles), jnp.sin(angles))


def matmul(left_side, right_side):
    return jnp.dot(left_side, right_side, preferred_element_type=F32)


def over_rows(left_side, right_side):
    return lax.dot_general(
        left_side, right_side, (((0,), (0,)), ((), ())), preferred_element_type=F32
    )


def by_transpose(left_side, right_side):
    return lax.dot_general(
        left_side, right_side, (((1,), (1,)), ((), ())), preferred_element_type=F32
    )


def swap(array, axis):
    return lax.ppermute(array, axis, [(0, 1), (1, 0)])


GELU_A = 0.7978845608028654
GELU_B = 0.044715
TILE = 512
PARAMS = pltpu.CompilerParams(vmem_limit_bytes=58 << 20)


def whole_block(shape):
    return pl.BlockSpec(shape, lambda i: (0,) * len(shape), pipeline_mode=pl.Buffered(1))


def row_block(rows, columns):
    return pl.BlockSpec((rows, columns), lambda i: (i, 0))


def mlp_forward_kernel(normed, gate_up, down, _, hidden, gelu, slope, mixed):
    own = down.shape[0]
    raw = matmul(normed[...], gate_up[...])
    gate_raw, up_raw = raw[:, :own], raw[:, own:]
    square = gate_raw * gate_raw
    bend = jnp.tanh(GELU_A * (gate_raw + GELU_B * square * gate_raw))
    half = 0.5 + 0.5 * bend
    active = gate_raw * half
    turn = 0.5 * gate_raw * (1.0 - bend * bend) * (GELU_A * (1.0 + 3.0 * GELU_B * square))
    low = (active * up_raw).astype(BF)
    hidden[...] = low
    gelu[...] = active.astype(BF)
    slope[...] = ((half + turn) * up_raw).astype(BF)
    mixed[...] = matmul(low, down[...]).astype(BF)


def mlp_forward(normed, gate_up, down, earlier):
    rows, width = normed.shape
    own = down.shape[0]
    flat = jax.ShapeDtypeStruct((rows, own), BF)
    return pl.pallas_call(
        mlp_forward_kernel,
        grid=(rows // TILE,),
        in_specs=[
            row_block(TILE, width),
            whole_block(gate_up.shape),
            whole_block(down.shape),
            pl.BlockSpec(memory_space=pl.ANY),
        ],
        out_specs=[row_block(TILE, own)] * 3 + [row_block(TILE, width)],
        out_shape=[flat, flat, flat, jax.ShapeDtypeStruct((rows, width), BF)],
        compiler_params=PARAMS,
        cost_estimate=pl.CostEstimate(
            flops=6 * rows * width * own, bytes_accessed=rows * (4 * width + 6 * own), transcendentals=0
        ),
    )(normed, gate_up, down, earlier)


def mlp_backward_kernel(grad_mixed, gelu, slope, gate_up, down, _, grad_raw, grad_normed):
    own = down.shape[0]
    grad_hidden = by_transpose(grad_mixed[...], down[...])
    grad_gate = (grad_hidden * slope[...].astype(F32)).astype(BF)
    grad_up = (grad_hidden * gelu[...].astype(F32)).astype(BF)
    grad_raw[:, :own] = grad_gate
    grad_raw[:, own:] = grad_up
    grad_normed[...] = (
        by_transpose(grad_gate, gate_up[:, :own]) + by_transpose(grad_up, gate_up[:, own:])
    ).astype(BF)


def mlp_backward(grad_mixed, gelu, slope, gate_up, down, earlier):
    rows, width = grad_mixed.shape
    own = down.shape[0]
    return pl.pallas_call(
        mlp_backward_kernel,
        grid=(rows // TILE,),
        in_specs=[
            row_block(TILE, width),
            row_block(TILE, own),
            row_block(TILE, own),
            whole_block(gate_up.shape),
            whole_block(down.shape),
            pl.BlockSpec(memory_space=pl.ANY),
        ],
        out_specs=[row_block(TILE, 2 * own), row_block(TILE, width)],
        out_shape=[
            jax.ShapeDtypeStruct((rows, 2 * own), BF),
            jax.ShapeDtypeStruct((rows, width), BF),
        ],
        compiler_params=PARAMS,
        cost_estimate=pl.CostEstimate(
            flops=6 * rows * width * own, bytes_accessed=rows * (4 * width + 8 * own), transcendentals=0
        ),
    )(grad_mixed, gelu, slope, gate_up, down, earlier)


def down_terms_kernel(*refs):
    *ins, out = refs
    half = len(ins) // 2
    total = over_rows(ins[0][...], ins[half][...])
    for left, right in zip(ins[1:half], ins[half + 1 :]):
        total = total + over_rows(left[...], right[...])
    out[...] = total.astype(BF)


def down_terms(hidden, grad_mixed, keep):
    own, width = hidden[0].shape[1], grad_mixed[0].shape[1]
    rows = sum(part.shape[0] for part in hidden)
    return pl.pallas_call(
        down_terms_kernel,
        grid=(own // 128,),
        in_specs=[pl.BlockSpec((part.shape[0], 128), lambda i: (0, i)) for part in hidden]
        + [whole_block(part.shape) for part in grad_mixed],
        out_specs=row_block(128, width),
        out_shape=jax.ShapeDtypeStruct((keep, width), BF),
        compiler_params=PARAMS,
        cost_estimate=pl.CostEstimate(
            flops=2 * rows * width * own, bytes_accessed=2 * rows * (width + own), transcendentals=0
        ),
    )(*hidden, *grad_mixed)


def gate_terms_kernel(*refs):
    *ins, _, out = refs
    half = len(ins) // 2
    total = over_rows(ins[0][...], ins[half][...])
    for left, right in zip(ins[1:half], ins[half + 1 :]):
        total = total + over_rows(left[...], right[...])
    total = total.astype(BF)
    groups, sides, rows, _ = out.shape
    for side in range(sides):
        for group in range(groups):
            first = (side * groups + group) * rows
            out[group, side] = total[first : first + rows]


def gate_terms(normed, grad_raw, groups, earlier):
    width, both = normed[0].shape[1], grad_raw[0].shape[1]
    rows = sum(part.shape[0] for part in normed)
    shape = (groups, 2, width // (2 * groups))
    return pl.pallas_call(
        gate_terms_kernel,
        grid=(both // 256,),
        in_specs=[whole_block(part.shape) for part in normed]
        + [pl.BlockSpec((part.shape[0], 256), lambda i: (0, i)) for part in grad_raw]
        + [pl.BlockSpec(memory_space=pl.ANY)],
        out_specs=pl.BlockSpec(shape + (256,), lambda i: (0, 0, 0, i)),
        out_shape=jax.ShapeDtypeStruct(shape + (both,), BF),
        compiler_params=PARAMS,
        cost_estimate=pl.CostEstimate(
            flops=2 * rows * width * both, bytes_accessed=2 * rows * (width + both), transcendentals=0
        ),
    )(*normed, *grad_raw, earlier)


def after(value, *earlier):
    return lax.optimization_barrier((value, *earlier))[0]


def with_core(part):
    return jnp.concatenate([part, swap(part, "c")])


def core_sum(part):
    half = part.shape[0] // 2
    return part[:half].astype(F32) + swap(part[half:], "c").astype(F32)


def send_far(far):
    half = far.shape[0] // 2
    return swap(far[:half], "y"), swap(far[half:], "x")


def sum_near(near, top, low):
    near = core_sum(near)
    rows = near.shape[0] // 2
    half = rows // 2
    to_x = jnp.concatenate([near[:half] + top, near[half:rows]]).astype(BF)
    to_y = jnp.concatenate([near[rows : rows + half], near[rows + half :] + low]).astype(BF)
    return to_x, to_y


def sum_own(own, to_x, to_y):
    return core_sum(own) + swap(to_x, "x").astype(F32) + swap(to_y, "y").astype(F32)


def in_order(own, other, place):
    both = jnp.concatenate([own[None], other[None], own[None]])
    return lax.dynamic_slice_in_dim(both, place, 2, 0)


def group_gather(own):
    size = lax.axis_size("g")
    parts = [own] + [
        lax.ppermute(own, "g", [((i + k) % size, i) for i in range(size)]) for k in range(1, size)
    ]
    both = jnp.stack(parts + parts[:-1])
    place = lax.axis_index("g")
    return lax.dynamic_slice_in_dim(both, lax.rem(size - place, size), size, 0)


def plane_near(blocks):
    half = blocks.shape[0] // 2
    first, second = blocks[:half], blocks[half:]
    first = in_order(first, swap(first, "x"), lax.axis_index("x"))
    second = in_order(second, swap(second, "y"), lax.axis_index("y"))
    return first, second


def plane_far(first, second):
    first = in_order(first, swap(first, "y"), lax.axis_index("y"))
    second = in_order(second, swap(second, "x"), lax.axis_index("x"))
    first = first.transpose(1, 2, 0, 3, 4)
    second = second.transpose(0, 2, 1, 3, 4)
    return jnp.concatenate([first, second], axis=1)


def group_terms(term):
    size = lax.axis_size("g")
    place = lax.axis_index("g")
    total = lax.dynamic_index_in_dim(term, place, 0, keepdims=False).astype(F32)
    for k in range(1, size):
        chunk = lax.dynamic_index_in_dim(term, lax.rem(place + k, size), 0, keepdims=False)
        pairs = [(i, (i + k) % size) for i in range(size)]
        total = total + lax.ppermute(chunk, "g", pairs).astype(F32)
    return total


def fold(term, axis, dim):
    place = lax.axis_index(axis)
    mine = lax.dynamic_index_in_dim(term, place, dim, keepdims=False)
    other = lax.dynamic_index_in_dim(term, 1 - place, dim, keepdims=False)
    return (mine.astype(F32) + swap(other.astype(BF), axis).astype(F32)).astype(BF)


def plane_terms(term):
    half = term.shape[1] // 2
    first = fold(fold(term[:, :half], "x", 0), "y", 1)
    second = fold(fold(term[:, half:], "y", 2), "x", 0)
    return jnp.concatenate([first, second])


def rms_scale(values):
    return lax.rsqrt(jnp.mean(values * values, axis=-1, keepdims=True) + EPSILON)


def rms_backward(values, scale, gain, grad):
    weighted = grad * gain
    inner = jnp.mean(weighted * values, axis=-1, keepdims=True)
    terms = jnp.sum(grad * values * scale, axis=0, keepdims=True)
    return weighted * scale - values * (scale * scale * scale * inner), terms


def turn_forward(values, cosine, sine):
    half = cosine.shape[1]
    low, high = values[:, :half], values[:, half:]
    return jnp.concatenate([low * cosine - high * sine, high * cosine + low * sine], axis=1)


def turn_backward(grad, cosine, sine):
    half = cosine.shape[1]
    low, high = grad[:, :half], grad[:, half:]
    return jnp.concatenate([low * cosine + high * sine, high * cosine - low * sine], axis=1)


def gain_places(width, columns, shard_rows):
    heads = columns // (width // shard_rows)
    row = lax.broadcasted_iota(jnp.int32, (width, columns), 0)
    column = lax.broadcasted_iota(jnp.int32, (width, columns), 1)
    place = (column // heads) * shard_rows + lax.rem(column, heads)
    return jnp.where(row == place, 1.0, 0.0).astype(BF)


def project_kernel(
    shard_rows, core, tokens, earlier, own, other, cosine, sine,
    normed, normed_earlier, query_raw, key_raw, queries, keys, values, d_gains, h_gains,
):
    rows, width = tokens.shape
    pad, k_cols = earlier.shape[0], key_raw.shape[1]
    half = query_raw.shape[1] // 2
    first_is_own = core[0] == 0
    block = jnp.where(
        first_is_own, own[:, half + k_cols :].astype(F32), other[:, half + k_cols :].astype(F32)
    )
    flat = block.T[:8]
    d_gains[...] = flat
    chosen = matmul(flat.astype(BF), gain_places(width, k_cols, shard_rows))
    h_gains[...] = chosen
    before = earlier[...].astype(F32)
    low_before = (before * rms_scale(before) * flat[0:1]).astype(BF)
    normed_earlier[...] = low_before
    inputs = tokens[...].astype(F32)
    low = (inputs * rms_scale(inputs) * flat[0:1]).astype(BF)
    normed[...] = low
    raw_own = matmul(low, own[:, : half + k_cols])
    raw_other = matmul(low, other[:, : half + k_cols])
    before_own = matmul(low_before, own[:, half : half + k_cols])
    before_other = matmul(low_before, other[:, half : half + k_cols])
    first = jnp.where(first_is_own, raw_own, raw_other)
    second = jnp.where(first_is_own, raw_other, raw_own)
    raw_query = jnp.concatenate([first[:, :half], second[:, :half]], axis=1)
    query_raw[...] = raw_query
    values[:pad] = jnp.where(first_is_own, before_other, before_own).astype(BF)
    values[pad:] = second[:, half:].astype(BF)
    raw_before = jnp.where(first_is_own, before_own, before_other)
    for raw, at in ((raw_before, slice(0, pad)), (first[:, half:], slice(pad, pad + rows))):
        key_raw[at] = raw
        part = raw * rms_scale(raw) * chosen[5:6]
        keys[at] = turn_forward(part, cosine[at], sine[at]).astype(BF)
    cos, sin = cosine[pad:], sine[pad:]
    for head in range(2 * half // k_cols):
        at = slice(head * k_cols, (head + 1) * k_cols)
        part = raw_query[:, at]
        part = part * rms_scale(part) * chosen[4:5]
        queries[:, at] = turn_forward(part, cos, sin).astype(BF)


def project(core, tokens, earlier, own, other, cosine, sine, shard_rows, q_cols, k_cols):
    rows, width = tokens.shape
    seen = rows + earlier.shape[0]
    vmem = pl.BlockSpec(memory_space=pltpu.VMEM)
    return pl.pallas_call(
        functools.partial(project_kernel, shard_rows),
        in_specs=[pl.BlockSpec(memory_space=pltpu.SMEM)] + [vmem] * 6,
        out_specs=[vmem] * 9,
        out_shape=[
            jax.ShapeDtypeStruct((rows, width), BF),
            jax.ShapeDtypeStruct(earlier.shape, BF),
            jax.ShapeDtypeStruct((rows, q_cols), F32),
            jax.ShapeDtypeStruct((seen, k_cols), F32),
            jax.ShapeDtypeStruct((rows, q_cols), BF),
            jax.ShapeDtypeStruct((seen, k_cols), BF),
            jax.ShapeDtypeStruct((seen, k_cols), BF),
            jax.ShapeDtypeStruct((8, width), F32),
            jax.ShapeDtypeStruct((8, k_cols), F32),
        ],
        compiler_params=PARAMS,
        cost_estimate=pl.CostEstimate(
            flops=2 * rows * width * (q_cols + 4 * k_cols), bytes_accessed=16 * rows * width, transcendentals=0
        ),
    )(core, tokens, earlier, own, other, cosine, sine)


def tile_mask(first, rows, first_key, keys, query_ids, key_ids, pad):
    query_place = pad + first + lax.broadcasted_iota(jnp.int32, (rows, keys), 0)
    key_place = first_key + lax.broadcasted_iota(jnp.int32, (rows, keys), 1)
    distance = query_place - key_place
    same_doc = query_ids[first : first + rows, :] == key_ids[:, first_key : first_key + keys]
    return (distance >= 0) & (distance < WINDOW) & same_doc


def attend_kernel(
    scale, queries, keys, values, query_ids, key_ids, w_o, tokens, d_gains,
    attended, log_total, branch, middle, normed_mlp,
):
    rows, q_cols = queries.shape
    pad, k_cols = keys.shape[0] - rows, keys.shape[1]
    tile = rows // 2
    span = pad + tile
    lane = lax.broadcasted_iota(jnp.int32, (tile, 128), 1)
    for first in (0, tile):
        at = slice(first, first + tile)
        seen = slice(first, first + span)
        allowed = tile_mask(first, tile, first, span, query_ids, key_ids, pad)
        logs = jnp.zeros((tile, 128), F32)
        for head in range(q_cols // k_cols):
            columns = slice(head * k_cols, (head + 1) * k_cols)
            scores = by_transpose(queries[at, columns], keys[seen]) * scale
            scores = jnp.where(allowed, scores, -1e30)
            row_max = jnp.max(scores, axis=-1, keepdims=True)
            weights = jnp.exp(scores - row_max)
            row_total = jnp.sum(weights, axis=-1, keepdims=True)
            probabilities = (weights * (1.0 / row_total)).astype(BF)
            attended[at, columns] = matmul(probabilities, values[seen]).astype(BF)
            logs = jnp.where(lane == head, row_max + jnp.log(row_total), logs)
        log_total[at] = logs
    out = matmul(attended[...], w_o[...])
    branch[...] = out
    total = tokens[...].astype(F32) + out * rms_scale(out) * d_gains[1:2]
    middle[...] = total
    normed_mlp[...] = (total * rms_scale(total) * d_gains[2:3]).astype(BF)


def attend(queries, keys, values, query_ids, key_ids, w_o, tokens, d_gains, scale):
    rows, q_cols = queries.shape
    width = tokens.shape[1]
    vmem = pl.BlockSpec(memory_space=pltpu.VMEM)
    return pl.pallas_call(
        functools.partial(attend_kernel, scale),
        in_specs=[vmem] * 8,
        out_specs=[vmem] * 5,
        out_shape=[
            jax.ShapeDtypeStruct((rows, q_cols), BF),
            jax.ShapeDtypeStruct((rows, 128), F32),
            jax.ShapeDtypeStruct((rows, width), F32),
            jax.ShapeDtypeStruct((rows, width), F32),
            jax.ShapeDtypeStruct((rows, width), BF),
        ],
        compiler_params=PARAMS,
        cost_estimate=pl.CostEstimate(
            flops=2 * rows * q_cols * (width + 2 * keys.shape[0]), bytes_accessed=20 * rows * width, transcendentals=0
        ),
    )(queries, keys, values, query_ids, key_ids, w_o, tokens, d_gains)


def attend_backward_kernel(
    scale, grad_normed_mlp, cotangent, middle, branch, d_gains, w_o,
    queries, keys, values, query_ids, key_ids, log_total,
    grad_middle, grad_branch, grad_queries, grad_keys, grad_values, terms, grad_attended,
):
    rows, q_cols = queries.shape
    pad, k_cols = keys.shape[0] - rows, keys.shape[1]
    total = middle[...]
    from_mlp, mlp_terms = rms_backward(total, rms_scale(total), d_gains[2:3], grad_normed_mlp[...])
    grad_total = cotangent[...].astype(F32) + from_mlp
    grad_middle[...] = grad_total
    out = branch[...]
    grad_out, out_terms = rms_backward(out, rms_scale(out), d_gains[1:2], grad_total)
    low = grad_out.astype(BF)
    grad_branch[...] = low
    terms[...] = jnp.concatenate([out_terms, mlp_terms, jnp.zeros((6, out.shape[1]), F32)], axis=0)
    grad_attended[...] = by_transpose(low, w_o[...]).astype(BF)
    grad_keys[...] = jnp.zeros_like(grad_keys)
    grad_values[...] = jnp.zeros_like(grad_values)
    tile = rows // 2
    span = pad + tile
    for first in (0, tile):
        at = slice(first, first + tile)
        seen = slice(first, first + span)
        allowed = tile_mask(first, tile, first, span, query_ids, key_ids, pad)
        key_total = jnp.zeros((span, k_cols), F32)
        value_total = jnp.zeros((span, k_cols), F32)
        for head in range(q_cols // k_cols):
            columns = slice(head * k_cols, (head + 1) * k_cols)
            query = queries[at, columns]
            grad = grad_attended[at, columns]
            scores = by_transpose(query, keys[seen]) * scale
            probabilities = jnp.where(
                allowed, jnp.exp(scores - log_total[at, head : head + 1]), 0.0
            )
            grad_prob = by_transpose(grad, values[seen])
            inner = jnp.sum(probabilities * grad_prob, axis=-1, keepdims=True)
            grad_score = (probabilities * (grad_prob - inner)).astype(BF)
            grad_queries[at, columns] = matmul(grad_score, keys[seen]) * scale
            key_total = key_total + over_rows(grad_score, query)
            value_total = value_total + over_rows(probabilities.astype(BF), grad)
        grad_keys[seen] = grad_keys[seen] + key_total * scale
        grad_values[seen] = grad_values[seen] + value_total


def attend_backward(
    grad_normed_mlp, cotangent, middle, branch, d_gains, w_o,
    queries, keys, values, query_ids, key_ids, log_total, scale,
):
    rows, q_cols = queries.shape
    width = middle.shape[1]
    vmem = pl.BlockSpec(memory_space=pltpu.VMEM)
    return pl.pallas_call(
        functools.partial(attend_backward_kernel, scale),
        in_specs=[vmem] * 12,
        out_specs=[vmem] * 6,
        out_shape=[
            jax.ShapeDtypeStruct((rows, width), F32),
            jax.ShapeDtypeStruct((rows, width), BF),
            jax.ShapeDtypeStruct((rows, q_cols), F32),
            jax.ShapeDtypeStruct(keys.shape, F32),
            jax.ShapeDtypeStruct(keys.shape, F32),
            jax.ShapeDtypeStruct((8, width), F32),
        ],
        scratch_shapes=[pltpu.VMEM((rows, q_cols), BF)],
        compiler_params=PARAMS,
        cost_estimate=pl.CostEstimate(
            flops=2 * rows * q_cols * (width + 5 * keys.shape[0]), bytes_accessed=30 * rows * width, transcendentals=0
        ),
    )(
        grad_normed_mlp, cotangent, middle, branch, d_gains, w_o,
        queries, keys, values, query_ids, key_ids, log_total,
    )


def project_backward_kernel(
    shard_rows, core, grad_queries, grad_keys, grad_values, query_raw, key_raw, cosine, sine,
    h_gains, normed, normed_earlier, own, other, tokens, earlier, d_gains, terms, mixed_terms,
    grad_normed, returned, mine, sent,
):
    rows, width = tokens.shape
    pad, k_cols = earlier.shape[0], key_raw.shape[1]
    half = query_raw.shape[1] // 2
    cols = half + k_cols
    first_is_own = core[0] == 0
    cos, sin = cosine[pad:], sine[pad:]
    query_terms = jnp.zeros((1, k_cols), F32)
    parts = []
    for head in range(2 * half // k_cols):
        at = slice(head * k_cols, (head + 1) * k_cols)
        raw = query_raw[:, at]
        grad = turn_backward(grad_queries[:, at], cos, sin)
        grad, term = rms_backward(raw, rms_scale(raw), h_gains[4:5], grad)
        query_terms = query_terms + term
        parts.append(grad.astype(BF))
    raw = key_raw[...]
    grad = turn_backward(grad_keys[...], cosine[...], sine[...])
    grad, key_terms = rms_backward(raw, rms_scale(raw), h_gains[5:6], grad)
    grad_key, grad_value = grad.astype(BF), grad_values[...].astype(BF)
    returned[:, :k_cols] = grad_key[:pad]
    returned[:, k_cols:] = grad_value[:pad]
    kv_own = jnp.where(first_is_own, grad_key, grad_value)
    kv_other = jnp.where(first_is_own, grad_value, grad_key)
    both = len(parts) // 2
    first = jnp.concatenate(parts[:both], axis=1)
    second = jnp.concatenate(parts[both:], axis=1)
    q_own = jnp.where(first_is_own, first, second)
    q_other = jnp.where(first_is_own, second, first)
    grad_own = jnp.concatenate([q_own, kv_own[pad:]], axis=1)
    grad_other = jnp.concatenate([q_other, kv_other[pad:]], axis=1)
    total = by_transpose(grad_own, own[:, :cols]) + by_transpose(grad_other, other[:, :cols])
    grad_normed[...] = total
    values = tokens[...].astype(F32)
    in_terms = jnp.sum(total * values * rms_scale(values), axis=0, keepdims=True)
    total = by_transpose(kv_own[:pad], own[:, half:cols])
    total = total + by_transpose(kv_other[:pad], other[:, half:cols])
    values = earlier[...].astype(F32)
    in_terms = in_terms + jnp.sum(total * values * rms_scale(values), axis=0, keepdims=True)
    low, low_before = normed[...], normed_earlier[...]
    for out, query, key_value in ((mine, q_own, kv_own), (sent, q_other, kv_other)):
        out[:, :half] = over_rows(low, query).astype(BF)
        out[:, half:cols] = (
            over_rows(low, key_value[pad:]) + over_rows(low_before, key_value[:pad])
        ).astype(BF)
    heads = jnp.concatenate([query_terms, key_terms, jnp.zeros((6, k_cols), F32)], axis=0)
    placed = by_transpose(heads.astype(BF), gain_places(width, k_cols, shard_rows))
    block = jnp.concatenate(
        [in_terms, terms[0:2], mixed_terms[0:1], placed[0:2], jnp.zeros((122, width), F32)], axis=0
    ).T
    mine[:, cols:] = jnp.where(first_is_own, block, 0.0).astype(BF)
    sent[:, cols:] = jnp.where(first_is_own, 0.0, block).astype(BF)


def project_backward(
    core, grad_queries, grad_keys, grad_values, query_raw, key_raw, cosine, sine,
    h_gains, normed, normed_earlier, own, other, tokens, earlier, d_gains, terms, mixed_terms,
    shard_rows,
):
    rows, width = tokens.shape
    pad, k_cols = earlier.shape[0], key_raw.shape[1]
    vmem = pl.BlockSpec(memory_space=pltpu.VMEM)
    return pl.pallas_call(
        functools.partial(project_backward_kernel, shard_rows),
        in_specs=[pl.BlockSpec(memory_space=pltpu.SMEM)] + [vmem] * 17,
        out_specs=[vmem] * 4,
        out_shape=[
            jax.ShapeDtypeStruct((rows, width), F32),
            jax.ShapeDtypeStruct((pad, 2 * k_cols), BF),
            jax.ShapeDtypeStruct(own.shape, BF),
            jax.ShapeDtypeStruct(own.shape, BF),
        ],
        compiler_params=PARAMS,
        cost_estimate=pl.CostEstimate(
            flops=9 * rows * width * own.shape[1], bytes_accessed=30 * rows * width, transcendentals=0
        ),
    )(
        core, grad_queries, grad_keys, grad_values, query_raw, key_raw, cosine, sine,
        h_gains, normed, normed_earlier, own, other, tokens, earlier, d_gains, terms, mixed_terms,
    )


def grad_tokens_kernel(core, returned, grad_normed, own, other, tokens, d_gains, grad_middle, out):
    k_cols = returned.shape[1] // 2
    cols = own.shape[1] - 128
    half = cols - k_cols
    first_is_own = core[0] == 0
    grad_key, grad_value = returned[:, :k_cols], returned[:, k_cols:]
    kv_own = jnp.where(first_is_own, grad_key, grad_value)
    kv_other = jnp.where(first_is_own, grad_value, grad_key)
    total = grad_normed[...] + by_transpose(kv_own, own[:, half:cols])
    total = total + by_transpose(kv_other, other[:, half:cols])
    values = tokens[...].astype(F32)
    from_attn, _ = rms_backward(values, rms_scale(values), d_gains[0:1], total)
    out[...] = (grad_middle[...] + from_attn).astype(BF)


def grad_tokens(core, returned, grad_normed, own, other, tokens, d_gains, grad_middle):
    vmem = pl.BlockSpec(memory_space=pltpu.VMEM)
    return pl.pallas_call(
        grad_tokens_kernel,
        in_specs=[pl.BlockSpec(memory_space=pltpu.SMEM)] + [vmem] * 7,
        out_specs=vmem,
        out_shape=jax.ShapeDtypeStruct(tokens.shape, BF),
        compiler_params=PARAMS,
        cost_estimate=pl.CostEstimate(
            flops=2 * tokens.size * returned.shape[1], bytes_accessed=12 * tokens.size, transcendentals=0
        ),
    )(core, returned, grad_normed, own, other, tokens, d_gains, grad_middle)


def owner_rows_kernel(groups, piece, term, gate, up):
    sides, lanes = term.shape[0] // 2, term.shape[2] // 2
    for out, first in ((gate, 0), (up, lanes)):
        parts = []
        for side in range(2):
            rows = [
                term[side * sides + member, :, first : first + lanes].astype(F32)
                for member in range(sides)
            ]
            for group in range(groups):
                parts += [row[:, group * piece : (group + 1) * piece] for row in rows]
        out[...] = jnp.concatenate(parts, axis=1)


def owner_rows(term, groups, piece):
    vmem = pl.BlockSpec(memory_space=pltpu.VMEM)
    shape = jax.ShapeDtypeStruct((term.shape[1], term.shape[0] * groups * piece), F32)
    return pl.pallas_call(
        functools.partial(owner_rows_kernel, groups, piece),
        in_specs=[vmem],
        out_specs=[vmem, vmem],
        out_shape=[shape, shape],
        compiler_params=PARAMS,
        cost_estimate=pl.CostEstimate(
            flops=term.size, bytes_accessed=6 * term.size, transcendentals=0
        ),
    )(term)


def on_device(
    tokens,
    cotangent,
    doc_ids,
    w_query,
    w_key,
    w_value,
    w_out,
    w_gate,
    w_up,
    w_down,
    gain_attn_in,
    gain_attn_out,
    gain_mlp_in,
    gain_mlp_out,
    gain_query,
    gain_key,
):
    row_count = tokens.shape[1]
    width = tokens.shape[2]
    groups = lax.axis_size("g")
    members = lax.axis_size(PLANE)
    shard_rows = w_query.shape[0]
    head_rows = gain_query.shape[0]
    hidden_all = w_gate.shape[1]
    hidden_own = hidden_all // members
    hidden_pad = -(-hidden_own // 128) * 128
    piece = hidden_own // groups
    q_cols, k_cols = w_query.shape[1], w_key.shape[1]
    attn_scale = HEAD ** (-0.5)

    def gain_columns(d_gains, h_gains):
        columns = list(d_gains) + [
            jnp.pad(h, ((0, 0), (0, shard_rows - head_rows))) for h in h_gains
        ]
        block = jnp.stack(columns, axis=-1)
        return jnp.pad(block, ((0, 0), (0, 0), (0, 128 - len(columns))))

    seq_place = lax.axis_index(("g", "y", "c"))
    seq_size = lax.axis_size(("g", "y", "c"))
    before = lax.ppermute(tokens[0], ("g", "y", "c"), [(i, i + 1) for i in range(seq_size - 1)])

    def spread(weight):
        cut = weight.reshape(shard_rows, 2, groups, members // 2, piece)
        cut = cut.transpose(1, 3, 0, 2, 4).reshape(members, shard_rows, hidden_own)
        return jnp.pad(cut, ((0, 0), (0, 0), (0, hidden_pad - hidden_own)))

    sent = jnp.concatenate([spread(w_gate), spread(w_up)], axis=2)
    core = lax.axis_index("c")
    half_cols = q_cols // 2 + k_cols + 128
    gains = gain_columns(
        [g[None] for g in (gain_attn_in, gain_attn_out, gain_mlp_in, gain_mlp_out)],
        [gain_query[None], gain_key[None]],
    )
    halves = jnp.stack(
        [
            jnp.concatenate([w_query[:, : q_cols // 2], w_key, gains[0]], axis=1),
            jnp.concatenate([w_query[:, q_cols // 2 :], w_value, jnp.zeros_like(gains[0])], axis=1),
        ]
    )
    mine = lax.dynamic_index_in_dim(halves, core, 0, keepdims=False)
    other = lax.dynamic_index_in_dim(halves, 1 - core, 0, keepdims=False)
    mine = in_order(mine, swap(other, "c"), core).reshape(2 * shard_rows, half_cols)
    mine, before, sent = lax.optimization_barrier((mine, before, sent))
    sent = lax.all_to_all(sent, PLANE, split_axis=0, concat_axis=0, tiled=True)
    sent = sent.reshape(members * shard_rows, 2 * hidden_pad)
    w_o = group_gather(after(w_out, mine))
    mine, sent = lax.optimization_barrier((group_gather(mine), sent))
    near, w_o = lax.optimization_barrier((plane_near(mine), w_o))
    w_o = plane_near(w_o)
    mine, w_o = lax.optimization_barrier((plane_far(*near), w_o))
    mine = mine.reshape(width, half_cols)
    w_o = plane_far(*w_o)
    other = swap(mine, "c")

    down = lax.all_gather(w_down, "g", axis=0, tiled=True)
    down = jnp.pad(down, ((0, hidden_pad - hidden_own), (0, 0)))

    both = lax.all_gather(sent, "g", axis=0)
    both = both.reshape(groups, 2, members // 2 * shard_rows, 2 * hidden_pad)
    gate_up = both.transpose(1, 0, 2, 3).reshape(width, 2 * hidden_pad)

    first_row = seq_place * row_count
    ids_all = doc_ids[0]
    ids_own = lax.dynamic_slice_in_dim(ids_all, first_row, row_count, 0)
    ids_prev = lax.dynamic_slice_in_dim(
        ids_all, jnp.maximum(first_row - row_count, 0), row_count, 0
    )
    ids_prev = jnp.where(seq_place > 0, ids_prev, -1)
    ids_pad = jnp.concatenate([ids_prev, ids_own])
    query_ids, key_ids = ids_own[:, None], ids_pad[None]
    cosine_table, sine_table = rope_tables(first_row - row_count, 2 * row_count, HEAD)
    places = jnp.full((1,), core, jnp.int32)
    layer_in, grad_out = tokens[0], cotangent[0]

    normed, normed_before, query_raw, key_raw, queries, keys, values, d_gains, h_gains = project(
        places, layer_in, before, mine, other, cosine_table, sine_table, shard_rows, q_cols, k_cols
    )
    w_o = after(w_o, keys)
    w_o = in_order(w_o, swap(w_o, "c"), core).transpose(1, 2, 3, 0, 4, 5).reshape(q_cols, width)
    attended, log_total, branch, middle, normed_mlp = attend(
        queries, keys, values, query_ids, key_ids, w_o, layer_in, d_gains, attn_scale
    )

    half = row_count // 2
    from_x, from_y = swap(normed_mlp, "x"), swap(normed_mlp, "y")
    normed_far = jnp.concatenate([swap(from_x[:half], "y"), swap(from_y[half:], "x")])
    normed_near = jnp.concatenate([from_x, from_y])
    normed_all = [with_core(part) for part in (normed_mlp, normed_near, normed_far)]
    far_result = mlp_forward(normed_all[2], gate_up, down, normed_all[2])
    far_sum = core_sum(far_result[3]).astype(BF)
    near_result = mlp_forward(normed_all[1], gate_up, down, far_sum)
    to_x, to_y = sum_near(*lax.optimization_barrier((near_result[3], *send_far(far_sum))))
    own_result = mlp_forward(normed_all[0], gate_up, down, to_x)
    mixed = sum_own(own_result[3], to_x, to_y)
    layer_out = middle + norm_gain(mixed, d_gains[3:4])

    _, pullback = jax.vjp(norm_gain, mixed, d_gains[3:4])
    grad_mixed, mixed_terms = pullback(grad_out.astype(F32))
    grad_mixed = grad_mixed.astype(BF)
    from_x, from_y = swap(grad_mixed, "x"), swap(grad_mixed, "y")
    grad_own = with_core(grad_mixed)
    own_grads = mlp_backward(grad_own, own_result[1], own_result[2], gate_up, down, down)
    from_x, from_y = lax.optimization_barrier((from_x, from_y, own_grads[1]))[:2]
    grad_far = with_core(jnp.concatenate([swap(from_x[:half], "y"), swap(from_y[half:], "x")]))
    grad_near = with_core(jnp.concatenate([from_x, from_y]))
    grad_down_terms = down_terms(
        [r[0] for r in (own_result, near_result, far_result)],
        [grad_own, grad_near, grad_far],
        hidden_own,
    )
    grad_down = group_terms(grad_down_terms.reshape(groups, -1, width))
    far_grads = mlp_backward(
        grad_far, far_result[1], far_result[2], gate_up, down, grad_down_terms
    )
    far_sum = core_sum(far_grads[1]).astype(BF)
    near_grads = mlp_backward(grad_near, near_result[1], near_result[2], gate_up, down, far_sum)
    to_x, to_y = sum_near(*lax.optimization_barrier((near_grads[1], *send_far(far_sum))))
    gate_up_terms = gate_terms(
        normed_all, [g[0] for g in (own_grads, near_grads, far_grads)], groups, to_x
    )
    grad_normed_mlp = sum_own(own_grads[1], to_x, to_y)
    grad_normed_mlp = after(grad_normed_mlp, gate_up_terms)
    term = gate_up_terms.reshape(groups * members * shard_rows, 2 * hidden_pad)
    gate_up_share = lax.psum_scatter(term, "g", scatter_dimension=0, tiled=True)
    gate_up_share = gate_up_share.reshape(members, shard_rows, 2 * hidden_pad)
    term = lax.all_to_all(gate_up_share, PLANE, split_axis=0, concat_axis=0, tiled=True)

    grad_w_gate, grad_w_up = owner_rows(term, groups, piece)

    grad_middle, grad_branch, grad_queries, grad_keys, grad_values, terms = attend_backward(
        grad_normed_mlp, grad_out, middle, branch, d_gains, w_o,
        queries, keys, values, query_ids, key_ids, log_total, attn_scale,
    )
    out_terms = over_rows(attended, grad_branch).astype(BF)
    out_terms = out_terms.reshape(2, groups, 2, 2, w_out.shape[0], width)
    out_terms = plane_terms(fold(out_terms, "c", 3))
    own_weights, other_weights = mine, other
    grad_normed, returned, mine, sent = project_backward(
        places, after(grad_queries, grad_down), grad_keys, grad_values, query_raw, key_raw,
        cosine_table, sine_table, h_gains, normed, normed_before, own_weights, other_weights,
        layer_in, before, d_gains, terms, mixed_terms, shard_rows,
    )
    returned = lax.ppermute(returned, ("g", "y", "c"), [(i + 1, i) for i in range(seq_size - 1)])
    grad_in = grad_tokens(
        places, returned, grad_normed, own_weights, other_weights, layer_in, d_gains, grad_middle
    )
    mine = (mine.astype(F32) + swap(sent, "c").astype(F32)).astype(BF)
    qkv_terms = plane_terms(mine.reshape(2, groups, 2, 2 * shard_rows, half_cols))
    qkv_terms = qkv_terms.reshape(groups, -1, width)
    share = jnp.concatenate([out_terms, qkv_terms], axis=1)
    share = group_terms(after(share, gate_up_share))
    grad_w_out = share[: w_out.shape[0]]
    share = share[w_out.shape[0] :].astype(BF).reshape(2, shard_rows, half_cols)
    mine = lax.dynamic_index_in_dim(share, core, 0, keepdims=False)
    other = lax.dynamic_index_in_dim(share, 1 - core, 0, keepdims=False)
    first, second = in_order(mine, swap(other, "c"), core).astype(F32)
    half = q_cols // 2
    d_terms = first[:, half + k_cols :]
    return (
        layer_out.astype(BF)[None],
        grad_in[None],
        jnp.concatenate([first[:, :half], second[:, :half]], axis=1),
        first[:, half : half + k_cols],
        second[:, half : half + k_cols],
        grad_w_out,
        grad_w_gate,
        grad_w_up,
        grad_down,
        d_terms[:, 0],
        d_terms[:, 1],
        d_terms[:, 2],
        d_terms[:, 3],
        d_terms[:head_rows, 4],
        d_terms[:head_rows, 5],
    )


def solution(mesh):
    batch, seq = mesh.devices.shape
    fine = Mesh(mesh.devices.reshape(batch, seq // 4, 2, 2), ALL)
    rows = ("g", "y", "c")
    return jax.shard_map(
        on_device,
        mesh=fine,
        in_specs=(P("x", rows, None),) * 2
        + (P("x", None),)
        + (P(ALL, None),) * 7
        + (P(ALL),) * 6,
        out_specs=(P("x", rows, None),) * 2 + (P(ALL, None),) * 7 + (P(ALL),) * 6,
        check_vma=False,
    )
```

```python
import functools

import jax
import jax.numpy as jnp
from jax import lax
from jax.experimental import pallas as pl
from jax.experimental.pallas import tpu as pltpu
from jax.sharding import Mesh
from jax.sharding import PartitionSpec as P

HEAD = 256
WINDOW = 512
EPSILON = 1e-06
ROPE_BASE = 10000.0
ALL = ("x", "g", "y", "c")
PLANE = ("x", "y", "c")
BF = jnp.bfloat16
F32 = jnp.float32


def norm_gain(values, gain_vec):
    return (
        values * lax.rsqrt(jnp.mean(values * values, axis=-1, keepdims=True) + EPSILON) * gain_vec
    )


def rope_tables(first_row, row_count, head_size):
    places = (first_row + jnp.arange(row_count, dtype=jnp.int32)).astype(F32)
    frequency = ROPE_BASE ** (-(jnp.arange(head_size // 2, dtype=F32) * 2.0) / head_size)
    angles = places[:, None] * frequency[None, :]
    return (jnp.cos(angles), jnp.sin(angles))


def matmul(left_side, right_side):
    return jnp.dot(left_side, right_side, preferred_element_type=F32)


def over_rows(left_side, right_side):
    return lax.dot_general(
        left_side, right_side, (((0,), (0,)), ((), ())), preferred_element_type=F32
    )


def by_transpose(left_side, right_side):
    return lax.dot_general(
        left_side, right_side, (((1,), (1,)), ((), ())), preferred_element_type=F32
    )


def swap(array, axis):
    return lax.ppermute(array, axis, [(0, 1), (1, 0)])


GELU_A = 0.7978845608028654
GELU_B = 0.044715
TILE = 512
PARAMS = pltpu.CompilerParams(vmem_limit_bytes=58 << 20)


def whole_block(shape):
    return pl.BlockSpec(shape, lambda i: (0,) * len(shape), pipeline_mode=pl.Buffered(1))


def row_block(rows, columns):
    return pl.BlockSpec((rows, columns), lambda i: (i, 0))


def mlp_forward_kernel(normed, gate_up, down, _, hidden, gelu, slope, mixed):
    own = down.shape[0]
    raw = matmul(normed[...], gate_up[...])
    gate_raw, up_raw = raw[:, :own], raw[:, own:]
    square = gate_raw * gate_raw
    bend = jnp.tanh(GELU_A * (gate_raw + GELU_B * square * gate_raw))
    half = 0.5 + 0.5 * bend
    active = gate_raw * half
    turn = 0.5 * gate_raw * (1.0 - bend * bend) * (GELU_A * (1.0 + 3.0 * GELU_B * square))
    low = (active * up_raw).astype(BF)
    hidden[...] = low
    gelu[...] = active.astype(BF)
    slope[...] = ((half + turn) * up_raw).astype(BF)
    mixed[...] = matmul(low, down[...]).astype(BF)


def mlp_forward(normed, gate_up, down, earlier):
    rows, width = normed.shape
    own = down.shape[0]
    flat = jax.ShapeDtypeStruct((rows, own), BF)
    return pl.pallas_call(
        mlp_forward_kernel,
        grid=(rows // TILE,),
        in_specs=[
            row_block(TILE, width),
            whole_block(gate_up.shape),
            whole_block(down.shape),
            pl.BlockSpec(memory_space=pl.ANY),
        ],
        out_specs=[row_block(TILE, own)] * 3 + [row_block(TILE, width)],
        out_shape=[flat, flat, flat, jax.ShapeDtypeStruct((rows, width), BF)],
        compiler_params=PARAMS,
        cost_estimate=pl.CostEstimate(
            flops=6 * rows * width * own, bytes_accessed=rows * (4 * width + 6 * own), transcendentals=0
        ),
    )(normed, gate_up, down, earlier)


def mlp_backward_kernel(grad_mixed, gelu, slope, gate_up, down, _, grad_raw, grad_normed):
    own = down.shape[0]
    grad_hidden = by_transpose(grad_mixed[...], down[...])
    grad_gate = (grad_hidden * slope[...].astype(F32)).astype(BF)
    grad_up = (grad_hidden * gelu[...].astype(F32)).astype(BF)
    grad_raw[:, :own] = grad_gate
    grad_raw[:, own:] = grad_up
    grad_normed[...] = (
        by_transpose(grad_gate, gate_up[:, :own]) + by_transpose(grad_up, gate_up[:, own:])
    ).astype(BF)


def mlp_backward(grad_mixed, gelu, slope, gate_up, down, earlier):
    rows, width = grad_mixed.shape
    own = down.shape[0]
    return pl.pallas_call(
        mlp_backward_kernel,
        grid=(rows // TILE,),
        in_specs=[
            row_block(TILE, width),
            row_block(TILE, own),
            row_block(TILE, own),
            whole_block(gate_up.shape),
            whole_block(down.shape),
            pl.BlockSpec(memory_space=pl.ANY),
        ],
        out_specs=[row_block(TILE, 2 * own), row_block(TILE, width)],
        out_shape=[
            jax.ShapeDtypeStruct((rows, 2 * own), BF),
            jax.ShapeDtypeStruct((rows, width), BF),
        ],
        compiler_params=PARAMS,
        cost_estimate=pl.CostEstimate(
            flops=6 * rows * width * own, bytes_accessed=rows * (4 * width + 8 * own), transcendentals=0
        ),
    )(grad_mixed, gelu, slope, gate_up, down, earlier)


def down_terms_kernel(*refs):
    *ins, out = refs
    half = len(ins) // 2
    total = over_rows(ins[0][...], ins[half][...])
    for left, right in zip(ins[1:half], ins[half + 1 :]):
        total = total + over_rows(left[...], right[...])
    out[...] = total.astype(BF)


def down_terms(hidden, grad_mixed, keep):
    own, width = hidden[0].shape[1], grad_mixed[0].shape[1]
    rows = sum(part.shape[0] for part in hidden)
    return pl.pallas_call(
        down_terms_kernel,
        grid=(own // 128,),
        in_specs=[pl.BlockSpec((part.shape[0], 128), lambda i: (0, i)) for part in hidden]
        + [whole_block(part.shape) for part in grad_mixed],
        out_specs=row_block(128, width),
        out_shape=jax.ShapeDtypeStruct((keep, width), BF),
        compiler_params=PARAMS,
        cost_estimate=pl.CostEstimate(
            flops=2 * rows * width * own, bytes_accessed=2 * rows * (width + own), transcendentals=0
        ),
    )(*hidden, *grad_mixed)


def gate_terms_kernel(*refs):
    *ins, _, out = refs
    half = len(ins) // 2
    total = over_rows(ins[0][...], ins[half][...])
    for left, right in zip(ins[1:half], ins[half + 1 :]):
        total = total + over_rows(left[...], right[...])
    total = total.astype(BF)
    groups, sides, rows, _ = out.shape
    for side in range(sides):
        for group in range(groups):
            first = (side * groups + group) * rows
            out[group, side] = total[first : first + rows]


def gate_terms(normed, grad_raw, groups, earlier):
    width, both = normed[0].shape[1], grad_raw[0].shape[1]
    rows = sum(part.shape[0] for part in normed)
    shape = (groups, 2, width // (2 * groups))
    return pl.pallas_call(
        gate_terms_kernel,
        grid=(both // 256,),
        in_specs=[whole_block(part.shape) for part in normed]
        + [pl.BlockSpec((part.shape[0], 256), lambda i: (0, i)) for part in grad_raw]
        + [pl.BlockSpec(memory_space=pl.ANY)],
        out_specs=pl.BlockSpec(shape + (256,), lambda i: (0, 0, 0, i)),
        out_shape=jax.ShapeDtypeStruct(shape + (both,), BF),
        compiler_params=PARAMS,
        cost_estimate=pl.CostEstimate(
            flops=2 * rows * width * both, bytes_accessed=2 * rows * (width + both), transcendentals=0
        ),
    )(*normed, *grad_raw, earlier)


def after(value, *earlier):
    return lax.optimization_barrier((value, *earlier))[0]


def with_core(part):
    return jnp.concatenate([part, swap(part, "c")])


def core_sum(part):
    half = part.shape[0] // 2
    return part[:half].astype(F32) + swap(part[half:], "c").astype(F32)


def send_far(far):
    half = far.shape[0] // 2
    return swap(far[:half], "y"), swap(far[half:], "x")


def sum_near(near, top, low):
    near = core_sum(near)
    rows = near.shape[0] // 2
    half = rows // 2
    to_x = jnp.concatenate([near[:half] + top, near[half:rows]]).astype(BF)
    to_y = jnp.concatenate([near[rows : rows + half], near[rows + half :] + low]).astype(BF)
    return to_x, to_y


def sum_own(own, to_x, to_y):
    return core_sum(own) + swap(to_x, "x").astype(F32) + swap(to_y, "y").astype(F32)


def in_order(own, other, place):
    both = jnp.concatenate([own[None], other[None], own[None]])
    return lax.dynamic_slice_in_dim(both, place, 2, 0)


def group_gather(own):
    size = lax.axis_size("g")
    parts = [own] + [
        lax.ppermute(own, "g", [((i + k) % size, i) for i in range(size)]) for k in range(1, size)
    ]
    both = jnp.stack(parts + parts[:-1])
    place = lax.axis_index("g")
    return lax.dynamic_slice_in_dim(both, lax.rem(size - place, size), size, 0)


def plane_start(blocks):
    half = blocks.shape[0] // 2
    return swap(blocks[:half], "x"), swap(blocks[half:], "y")


def plane_weights(blocks, from_x, from_y):
    x, y = lax.axis_index("x"), lax.axis_index("y")
    half = blocks.shape[0] // 2
    first = in_order(blocks[:half], from_x, x)
    second = in_order(blocks[half:], from_y, y)
    first = in_order(first, swap(first, "y"), y)
    second = in_order(second, swap(second, "x"), x)
    first = first.transpose(1, 2, 0, 3, 4)
    second = second.transpose(0, 2, 1, 3, 4)
    return jnp.concatenate([first, second], axis=1)


def group_terms(term):
    size = lax.axis_size("g")
    place = lax.axis_index("g")
    total = lax.dynamic_index_in_dim(term, place, 0, keepdims=False).astype(F32)
    for k in range(1, size):
        chunk = lax.dynamic_index_in_dim(term, lax.rem(place + k, size), 0, keepdims=False)
        pairs = [(i, (i + k) % size) for i in range(size)]
        total = total + lax.ppermute(chunk, "g", pairs).astype(F32)
    return total


def fold(term, axis, dim):
    place = lax.axis_index(axis)
    mine = lax.dynamic_index_in_dim(term, place, dim, keepdims=False)
    other = lax.dynamic_index_in_dim(term, 1 - place, dim, keepdims=False)
    return (mine.astype(F32) + swap(other.astype(BF), axis).astype(F32)).astype(BF)


def plane_terms(term):
    half = term.shape[1] // 2
    first = fold(fold(term[:, :half], "x", 0), "y", 1)
    second = fold(fold(term[:, half:], "y", 2), "x", 0)
    return jnp.concatenate([first, second])


def rms_scale(values):
    return lax.rsqrt(jnp.mean(values * values, axis=-1, keepdims=True) + EPSILON)


def rms_backward(values, scale, gain, grad):
    weighted = grad * gain
    inner = jnp.mean(weighted * values, axis=-1, keepdims=True)
    terms = jnp.sum(grad * values * scale, axis=0, keepdims=True)
    return weighted * scale - values * (scale * scale * scale * inner), terms


def turn_forward(values, cosine, sine):
    half = cosine.shape[1]
    low, high = values[:, :half], values[:, half:]
    return jnp.concatenate([low * cosine - high * sine, high * cosine + low * sine], axis=1)


def turn_backward(grad, cosine, sine):
    half = cosine.shape[1]
    low, high = grad[:, :half], grad[:, half:]
    return jnp.concatenate([low * cosine + high * sine, high * cosine - low * sine], axis=1)


def gain_places(width, columns, shard_rows):
    heads = columns // (width // shard_rows)
    row = lax.broadcasted_iota(jnp.int32, (width, columns), 0)
    column = lax.broadcasted_iota(jnp.int32, (width, columns), 1)
    place = (column // heads) * shard_rows + lax.rem(column, heads)
    return jnp.where(row == place, 1.0, 0.0).astype(BF)


def project_kernel(
    shard_rows, core, tokens, earlier, own, other, cosine, sine,
    normed, normed_earlier, query_raw, key_raw, queries, keys, values, d_gains, h_gains,
):
    rows, width = tokens.shape
    pad, k_cols = earlier.shape[0], key_raw.shape[1]
    half = query_raw.shape[1] // 2
    first_is_own = core[0] == 0
    block = jnp.where(
        first_is_own, own[:, half + k_cols :].astype(F32), other[:, half + k_cols :].astype(F32)
    )
    flat = block.T[:8]
    d_gains[...] = flat
    chosen = matmul(flat.astype(BF), gain_places(width, k_cols, shard_rows))
    h_gains[...] = chosen
    before = earlier[...].astype(F32)
    low_before = (before * rms_scale(before) * flat[0:1]).astype(BF)
    normed_earlier[...] = low_before
    inputs = tokens[...].astype(F32)
    low = (inputs * rms_scale(inputs) * flat[0:1]).astype(BF)
    normed[...] = low
    raw_own = matmul(low, own[:, : half + k_cols])
    raw_other = matmul(low, other[:, : half + k_cols])
    before_own = matmul(low_before, own[:, half : half + k_cols])
    before_other = matmul(low_before, other[:, half : half + k_cols])
    first = jnp.where(first_is_own, raw_own, raw_other)
    second = jnp.where(first_is_own, raw_other, raw_own)
    raw_query = jnp.concatenate([first[:, :half], second[:, :half]], axis=1)
    query_raw[...] = raw_query
    values[:pad] = jnp.where(first_is_own, before_other, before_own).astype(BF)
    values[pad:] = second[:, half:].astype(BF)
    raw_before = jnp.where(first_is_own, before_own, before_other)
    for raw, at in ((raw_before, slice(0, pad)), (first[:, half:], slice(pad, pad + rows))):
        key_raw[at] = raw
        part = raw * rms_scale(raw) * chosen[5:6]
        keys[at] = turn_forward(part, cosine[at], sine[at]).astype(BF)
    cos, sin = cosine[pad:], sine[pad:]
    for head in range(2 * half // k_cols):
        at = slice(head * k_cols, (head + 1) * k_cols)
        part = raw_query[:, at]
        part = part * rms_scale(part) * chosen[4:5]
        queries[:, at] = turn_forward(part, cos, sin).astype(BF)


def project(core, tokens, earlier, own, other, cosine, sine, shard_rows, q_cols, k_cols):
    rows, width = tokens.shape
    seen = rows + earlier.shape[0]
    vmem = pl.BlockSpec(memory_space=pltpu.VMEM)
    return pl.pallas_call(
        functools.partial(project_kernel, shard_rows),
        in_specs=[pl.BlockSpec(memory_space=pltpu.SMEM)] + [vmem] * 6,
        out_specs=[vmem] * 9,
        out_shape=[
            jax.ShapeDtypeStruct((rows, width), BF),
            jax.ShapeDtypeStruct(earlier.shape, BF),
            jax.ShapeDtypeStruct((rows, q_cols), F32),
            jax.ShapeDtypeStruct((seen, k_cols), F32),
            jax.ShapeDtypeStruct((rows, q_cols), BF),
            jax.ShapeDtypeStruct((seen, k_cols), BF),
            jax.ShapeDtypeStruct((seen, k_cols), BF),
            jax.ShapeDtypeStruct((8, width), F32),
            jax.ShapeDtypeStruct((8, k_cols), F32),
        ],
        compiler_params=PARAMS,
        cost_estimate=pl.CostEstimate(
            flops=2 * rows * width * (q_cols + 4 * k_cols), bytes_accessed=16 * rows * width, transcendentals=0
        ),
    )(core, tokens, earlier, own, other, cosine, sine)


def tile_mask(first, rows, first_key, keys, query_ids, key_ids, pad):
    query_place = pad + first + lax.broadcasted_iota(jnp.int32, (rows, keys), 0)
    key_place = first_key + lax.broadcasted_iota(jnp.int32, (rows, keys), 1)
    distance = query_place - key_place
    same_doc = query_ids[first : first + rows, :] == key_ids[:, first_key : first_key + keys]
    return (distance >= 0) & (distance < WINDOW) & same_doc


def attend_kernel(
    scale, queries, keys, values, query_ids, key_ids, w_o, tokens, d_gains,
    attended, log_total, branch, middle, normed_mlp,
):
    rows, q_cols = queries.shape
    pad, k_cols = keys.shape[0] - rows, keys.shape[1]
    tile = rows // 2
    span = pad + tile
    lane = lax.broadcasted_iota(jnp.int32, (tile, 128), 1)
    for first in (0, tile):
        at = slice(first, first + tile)
        seen = slice(first, first + span)
        allowed = tile_mask(first, tile, first, span, query_ids, key_ids, pad)
        logs = jnp.zeros((tile, 128), F32)
        for head in range(q_cols // k_cols):
            columns = slice(head * k_cols, (head + 1) * k_cols)
            scores = by_transpose(queries[at, columns], keys[seen]) * scale
            scores = jnp.where(allowed, scores, -1e30)
            row_max = jnp.max(scores, axis=-1, keepdims=True)
            weights = jnp.exp(scores - row_max)
            row_total = jnp.sum(weights, axis=-1, keepdims=True)
            probabilities = (weights * (1.0 / row_total)).astype(BF)
            attended[at, columns] = matmul(probabilities, values[seen]).astype(BF)
            logs = jnp.where(lane == head, row_max + jnp.log(row_total), logs)
        log_total[at] = logs
    out = matmul(attended[...], w_o[...])
    branch[...] = out
    total = tokens[...].astype(F32) + out * rms_scale(out) * d_gains[1:2]
    middle[...] = total
    normed_mlp[...] = (total * rms_scale(total) * d_gains[2:3]).astype(BF)


def attend(queries, keys, values, query_ids, key_ids, w_o, tokens, d_gains, scale):
    rows, q_cols = queries.shape
    width = tokens.shape[1]
    vmem = pl.BlockSpec(memory_space=pltpu.VMEM)
    return pl.pallas_call(
        functools.partial(attend_kernel, scale),
        in_specs=[vmem] * 8,
        out_specs=[vmem] * 5,
        out_shape=[
            jax.ShapeDtypeStruct((rows, q_cols), BF),
            jax.ShapeDtypeStruct((rows, 128), F32),
            jax.ShapeDtypeStruct((rows, width), F32),
            jax.ShapeDtypeStruct((rows, width), F32),
            jax.ShapeDtypeStruct((rows, width), BF),
        ],
        compiler_params=PARAMS,
        cost_estimate=pl.CostEstimate(
            flops=2 * rows * q_cols * (width + 2 * keys.shape[0]), bytes_accessed=20 * rows * width, transcendentals=0
        ),
    )(queries, keys, values, query_ids, key_ids, w_o, tokens, d_gains)


def attend_backward_kernel(
    scale, grad_normed_mlp, cotangent, middle, branch, d_gains, w_o,
    queries, keys, values, query_ids, key_ids, log_total,
    grad_middle, grad_branch, grad_queries, grad_keys, grad_values, terms, grad_attended,
):
    rows, q_cols = queries.shape
    pad, k_cols = keys.shape[0] - rows, keys.shape[1]
    total = middle[...]
    from_mlp, mlp_terms = rms_backward(total, rms_scale(total), d_gains[2:3], grad_normed_mlp[...])
    grad_total = cotangent[...].astype(F32) + from_mlp
    grad_middle[...] = grad_total
    out = branch[...]
    grad_out, out_terms = rms_backward(out, rms_scale(out), d_gains[1:2], grad_total)
    low = grad_out.astype(BF)
    grad_branch[...] = low
    terms[...] = jnp.concatenate([out_terms, mlp_terms, jnp.zeros((6, out.shape[1]), F32)], axis=0)
    grad_attended[...] = by_transpose(low, w_o[...]).astype(BF)
    grad_keys[...] = jnp.zeros_like(grad_keys)
    grad_values[...] = jnp.zeros_like(grad_values)
    tile = rows // 2
    span = pad + tile
    for first in (0, tile):
        at = slice(first, first + tile)
        seen = slice(first, first + span)
        allowed = tile_mask(first, tile, first, span, query_ids, key_ids, pad)
        key_total = jnp.zeros((span, k_cols), F32)
        value_total = jnp.zeros((span, k_cols), F32)
        for head in range(q_cols // k_cols):
            columns = slice(head * k_cols, (head + 1) * k_cols)
            query = queries[at, columns]
            grad = grad_attended[at, columns]
            scores = by_transpose(query, keys[seen]) * scale
            probabilities = jnp.where(
                allowed, jnp.exp(scores - log_total[at, head : head + 1]), 0.0
            )
            grad_prob = by_transpose(grad, values[seen])
            inner = jnp.sum(probabilities * grad_prob, axis=-1, keepdims=True)
            grad_score = (probabilities * (grad_prob - inner)).astype(BF)
            grad_queries[at, columns] = matmul(grad_score, keys[seen]) * scale
            key_total = key_total + over_rows(grad_score, query)
            value_total = value_total + over_rows(probabilities.astype(BF), grad)
        grad_keys[seen] = grad_keys[seen] + key_total * scale
        grad_values[seen] = grad_values[seen] + value_total


def attend_backward(
    grad_normed_mlp, cotangent, middle, branch, d_gains, w_o,
    queries, keys, values, query_ids, key_ids, log_total, scale,
):
    rows, q_cols = queries.shape
    width = middle.shape[1]
    vmem = pl.BlockSpec(memory_space=pltpu.VMEM)
    return pl.pallas_call(
        functools.partial(attend_backward_kernel, scale),
        in_specs=[vmem] * 12,
        out_specs=[vmem] * 6,
        out_shape=[
            jax.ShapeDtypeStruct((rows, width), F32),
            jax.ShapeDtypeStruct((rows, width), BF),
            jax.ShapeDtypeStruct((rows, q_cols), F32),
            jax.ShapeDtypeStruct(keys.shape, F32),
            jax.ShapeDtypeStruct(keys.shape, F32),
            jax.ShapeDtypeStruct((8, width), F32),
        ],
        scratch_shapes=[pltpu.VMEM((rows, q_cols), BF)],
        compiler_params=PARAMS,
        cost_estimate=pl.CostEstimate(
            flops=2 * rows * q_cols * (width + 5 * keys.shape[0]), bytes_accessed=30 * rows * width, transcendentals=0
        ),
    )(
        grad_normed_mlp, cotangent, middle, branch, d_gains, w_o,
        queries, keys, values, query_ids, key_ids, log_total,
    )


def project_backward_kernel(
    shard_rows, core, grad_queries, grad_keys, grad_values, query_raw, key_raw, cosine, sine,
    h_gains, normed, normed_earlier, own, other, tokens, earlier, d_gains, terms, mixed_terms,
    grad_normed, returned, mine, sent,
):
    rows, width = tokens.shape
    pad, k_cols = earlier.shape[0], key_raw.shape[1]
    half = query_raw.shape[1] // 2
    cols = half + k_cols
    first_is_own = core[0] == 0
    cos, sin = cosine[pad:], sine[pad:]
    query_terms = jnp.zeros((1, k_cols), F32)
    parts = []
    for head in range(2 * half // k_cols):
        at = slice(head * k_cols, (head + 1) * k_cols)
        raw = query_raw[:, at]
        grad = turn_backward(grad_queries[:, at], cos, sin)
        grad, term = rms_backward(raw, rms_scale(raw), h_gains[4:5], grad)
        query_terms = query_terms + term
        parts.append(grad.astype(BF))
    raw = key_raw[...]
    grad = turn_backward(grad_keys[...], cosine[...], sine[...])
    grad, key_terms = rms_backward(raw, rms_scale(raw), h_gains[5:6], grad)
    grad_key, grad_value = grad.astype(BF), grad_values[...].astype(BF)
    returned[:, :k_cols] = grad_key[:pad]
    returned[:, k_cols:] = grad_value[:pad]
    kv_own = jnp.where(first_is_own, grad_key, grad_value)
    kv_other = jnp.where(first_is_own, grad_value, grad_key)
    both = len(parts) // 2
    first = jnp.concatenate(parts[:both], axis=1)
    second = jnp.concatenate(parts[both:], axis=1)
    q_own = jnp.where(first_is_own, first, second)
    q_other = jnp.where(first_is_own, second, first)
    grad_own = jnp.concatenate([q_own, kv_own[pad:]], axis=1)
    grad_other = jnp.concatenate([q_other, kv_other[pad:]], axis=1)
    total = by_transpose(grad_own, own[:, :cols]) + by_transpose(grad_other, other[:, :cols])
    grad_normed[...] = total
    values = tokens[...].astype(F32)
    in_terms = jnp.sum(total * values * rms_scale(values), axis=0, keepdims=True)
    total = by_transpose(kv_own[:pad], own[:, half:cols])
    total = total + by_transpose(kv_other[:pad], other[:, half:cols])
    values = earlier[...].astype(F32)
    in_terms = in_terms + jnp.sum(total * values * rms_scale(values), axis=0, keepdims=True)
    low, low_before = normed[...], normed_earlier[...]
    for out, query, key_value in ((mine, q_own, kv_own), (sent, q_other, kv_other)):
        out[:, :half] = over_rows(low, query).astype(BF)
        out[:, half:cols] = (
            over_rows(low, key_value[pad:]) + over_rows(low_before, key_value[:pad])
        ).astype(BF)
    heads = jnp.concatenate([query_terms, key_terms, jnp.zeros((6, k_cols), F32)], axis=0)
    placed = by_transpose(heads.astype(BF), gain_places(width, k_cols, shard_rows))
    block = jnp.concatenate(
        [in_terms, terms[0:2], mixed_terms[0:1], placed[0:2], jnp.zeros((122, width), F32)], axis=0
    ).T
    mine[:, cols:] = jnp.where(first_is_own, block, 0.0).astype(BF)
    sent[:, cols:] = jnp.where(first_is_own, 0.0, block).astype(BF)


def project_backward(
    core, grad_queries, grad_keys, grad_values, query_raw, key_raw, cosine, sine,
    h_gains, normed, normed_earlier, own, other, tokens, earlier, d_gains, terms, mixed_terms,
    shard_rows,
):
    rows, width = tokens.shape
    pad, k_cols = earlier.shape[0], key_raw.shape[1]
    vmem = pl.BlockSpec(memory_space=pltpu.VMEM)
    return pl.pallas_call(
        functools.partial(project_backward_kernel, shard_rows),
        in_specs=[pl.BlockSpec(memory_space=pltpu.SMEM)] + [vmem] * 17,
        out_specs=[vmem] * 4,
        out_shape=[
            jax.ShapeDtypeStruct((rows, width), F32),
            jax.ShapeDtypeStruct((pad, 2 * k_cols), BF),
            jax.ShapeDtypeStruct(own.shape, BF),
            jax.ShapeDtypeStruct(own.shape, BF),
        ],
        compiler_params=PARAMS,
        cost_estimate=pl.CostEstimate(
            flops=9 * rows * width * own.shape[1], bytes_accessed=30 * rows * width, transcendentals=0
        ),
    )(
        core, grad_queries, grad_keys, grad_values, query_raw, key_raw, cosine, sine,
        h_gains, normed, normed_earlier, own, other, tokens, earlier, d_gains, terms, mixed_terms,
    )


def grad_tokens_kernel(core, returned, grad_normed, own, other, tokens, d_gains, grad_middle, out):
    k_cols = returned.shape[1] // 2
    cols = own.shape[1] - 128
    half = cols - k_cols
    first_is_own = core[0] == 0
    grad_key, grad_value = returned[:, :k_cols], returned[:, k_cols:]
    kv_own = jnp.where(first_is_own, grad_key, grad_value)
    kv_other = jnp.where(first_is_own, grad_value, grad_key)
    total = grad_normed[...] + by_transpose(kv_own, own[:, half:cols])
    total = total + by_transpose(kv_other, other[:, half:cols])
    values = tokens[...].astype(F32)
    from_attn, _ = rms_backward(values, rms_scale(values), d_gains[0:1], total)
    out[...] = (grad_middle[...] + from_attn).astype(BF)


def grad_tokens(core, returned, grad_normed, own, other, tokens, d_gains, grad_middle):
    vmem = pl.BlockSpec(memory_space=pltpu.VMEM)
    return pl.pallas_call(
        grad_tokens_kernel,
        in_specs=[pl.BlockSpec(memory_space=pltpu.SMEM)] + [vmem] * 7,
        out_specs=vmem,
        out_shape=jax.ShapeDtypeStruct(tokens.shape, BF),
        compiler_params=PARAMS,
        cost_estimate=pl.CostEstimate(
            flops=2 * tokens.size * returned.shape[1], bytes_accessed=12 * tokens.size, transcendentals=0
        ),
    )(core, returned, grad_normed, own, other, tokens, d_gains, grad_middle)


def owner_rows_kernel(groups, piece, term, gate, up):
    sides, lanes = term.shape[0] // 2, term.shape[2] // 2
    for out, first in ((gate, 0), (up, lanes)):
        parts = []
        for side in range(2):
            rows = [
                term[side * sides + member, :, first : first + lanes].astype(F32)
                for member in range(sides)
            ]
            for group in range(groups):
                parts += [row[:, group * piece : (group + 1) * piece] for row in rows]
        out[...] = jnp.concatenate(parts, axis=1)


def owner_rows(term, groups, piece):
    vmem = pl.BlockSpec(memory_space=pltpu.VMEM)
    shape = jax.ShapeDtypeStruct((term.shape[1], term.shape[0] * groups * piece), F32)
    return pl.pallas_call(
        functools.partial(owner_rows_kernel, groups, piece),
        in_specs=[vmem],
        out_specs=[vmem, vmem],
        out_shape=[shape, shape],
        compiler_params=PARAMS,
        cost_estimate=pl.CostEstimate(
            flops=term.size, bytes_accessed=6 * term.size, transcendentals=0
        ),
    )(term)


def on_device(
    tokens,
    cotangent,
    doc_ids,
    w_query,
    w_key,
    w_value,
    w_out,
    w_gate,
    w_up,
    w_down,
    gain_attn_in,
    gain_attn_out,
    gain_mlp_in,
    gain_mlp_out,
    gain_query,
    gain_key,
):
    row_count = tokens.shape[1]
    width = tokens.shape[2]
    groups = lax.axis_size("g")
    members = lax.axis_size(PLANE)
    shard_rows = w_query.shape[0]
    head_rows = gain_query.shape[0]
    hidden_all = w_gate.shape[1]
    hidden_own = hidden_all // members
    hidden_pad = -(-hidden_own // 128) * 128
    piece = hidden_own // groups
    q_cols, k_cols = w_query.shape[1], w_key.shape[1]
    attn_scale = HEAD ** (-0.5)

    def gain_columns(d_gains, h_gains):
        columns = list(d_gains) + [
            jnp.pad(h, ((0, 0), (0, shard_rows - head_rows))) for h in h_gains
        ]
        block = jnp.stack(columns, axis=-1)
        return jnp.pad(block, ((0, 0), (0, 0), (0, 128 - len(columns))))

    seq_place = lax.axis_index(("g", "y", "c"))
    seq_size = lax.axis_size(("g", "y", "c"))
    before = lax.ppermute(tokens[0], ("g", "y", "c"), [(i, i + 1) for i in range(seq_size - 1)])

    def spread(weight):
        cut = weight.reshape(shard_rows, 2, groups, members // 2, piece)
        cut = cut.transpose(1, 3, 0, 2, 4).reshape(members, shard_rows, hidden_own)
        return jnp.pad(cut, ((0, 0), (0, 0), (0, hidden_pad - hidden_own)))

    sent = jnp.concatenate([spread(w_gate), spread(w_up)], axis=2)
    core = lax.axis_index("c")
    half_cols = q_cols // 2 + k_cols + 128
    gains = gain_columns(
        [g[None] for g in (gain_attn_in, gain_attn_out, gain_mlp_in, gain_mlp_out)],
        [gain_query[None], gain_key[None]],
    )
    halves = jnp.stack(
        [
            jnp.concatenate([w_query[:, : q_cols // 2], w_key, gains[0]], axis=1),
            jnp.concatenate([w_query[:, q_cols // 2 :], w_value, jnp.zeros_like(gains[0])], axis=1),
        ]
    )
    mine = lax.dynamic_index_in_dim(halves, core, 0, keepdims=False)
    other = lax.dynamic_index_in_dim(halves, 1 - core, 0, keepdims=False)
    mine = in_order(mine, swap(other, "c"), core).reshape(2 * shard_rows, half_cols)
    mine, before, sent = lax.optimization_barrier((mine, before, sent))
    sent = lax.all_to_all(sent, PLANE, split_axis=0, concat_axis=0, tiled=True)
    sent = sent.reshape(members * shard_rows, 2 * hidden_pad)
    mine, sent = lax.optimization_barrier((group_gather(mine), sent))
    mine = plane_weights(mine, *plane_start(mine)).reshape(width, half_cols)
    other = swap(mine, "c")

    down = lax.all_gather(jnp.concatenate([w_down, w_out]), "g", axis=0)
    w_o = down[:, w_down.shape[0] :]
    down = down[:, : w_down.shape[0]].reshape(-1, width)
    down = jnp.pad(down, ((0, hidden_pad - hidden_own), (0, 0)))

    both = lax.all_gather(sent, "g", axis=0)
    both = both.reshape(groups, 2, members // 2 * shard_rows, 2 * hidden_pad)
    gate_up = both.transpose(1, 0, 2, 3).reshape(width, 2 * hidden_pad)

    first_row = seq_place * row_count
    ids_all = doc_ids[0]
    ids_own = lax.dynamic_slice_in_dim(ids_all, first_row, row_count, 0)
    ids_prev = lax.dynamic_slice_in_dim(
        ids_all, jnp.maximum(first_row - row_count, 0), row_count, 0
    )
    ids_prev = jnp.where(seq_place > 0, ids_prev, -1)
    ids_pad = jnp.concatenate([ids_prev, ids_own])
    query_ids, key_ids = ids_own[:, None], ids_pad[None]
    cosine_table, sine_table = rope_tables(first_row - row_count, 2 * row_count, HEAD)
    places = jnp.full((1,), core, jnp.int32)
    layer_in, grad_out = tokens[0], cotangent[0]

    normed, normed_before, query_raw, key_raw, queries, keys, values, d_gains, h_gains = project(
        places, layer_in, before, mine, other, cosine_table, sine_table, shard_rows, q_cols, k_cols
    )
    w_o = plane_weights(*lax.optimization_barrier((w_o, *plane_start(w_o), keys))[:3])
    w_o = in_order(w_o, swap(w_o, "c"), core).transpose(1, 2, 3, 0, 4, 5).reshape(q_cols, width)
    attended, log_total, branch, middle, normed_mlp = attend(
        queries, keys, values, query_ids, key_ids, w_o, layer_in, d_gains, attn_scale
    )

    half = row_count // 2
    from_x, from_y = swap(normed_mlp, "x"), swap(normed_mlp, "y")
    normed_far = jnp.concatenate([swap(from_x[:half], "y"), swap(from_y[half:], "x")])
    normed_near = jnp.concatenate([from_x, from_y])
    normed_all = [with_core(part) for part in (normed_mlp, normed_near, normed_far)]
    far_result = mlp_forward(normed_all[2], gate_up, down, normed_all[2])
    far_sum = core_sum(far_result[3]).astype(BF)
    near_result = mlp_forward(normed_all[1], gate_up, down, far_sum)
    to_x, to_y = sum_near(*lax.optimization_barrier((near_result[3], *send_far(far_sum))))
    own_result = mlp_forward(normed_all[0], gate_up, down, to_x)
    mixed = sum_own(own_result[3], to_x, to_y)
    layer_out = middle + norm_gain(mixed, d_gains[3:4])

    _, pullback = jax.vjp(norm_gain, mixed, d_gains[3:4])
    grad_mixed, mixed_terms = pullback(grad_out.astype(F32))
    grad_mixed = grad_mixed.astype(BF)
    from_x, from_y = swap(grad_mixed, "x"), swap(grad_mixed, "y")
    grad_own = with_core(grad_mixed)
    own_grads = mlp_backward(grad_own, own_result[1], own_result[2], gate_up, down, down)
    from_x, from_y = lax.optimization_barrier((from_x, from_y, own_grads[1]))[:2]
    grad_far = with_core(jnp.concatenate([swap(from_x[:half], "y"), swap(from_y[half:], "x")]))
    grad_near = with_core(jnp.concatenate([from_x, from_y]))
    grad_down_terms = down_terms(
        [r[0] for r in (own_result, near_result, far_result)],
        [grad_own, grad_near, grad_far],
        hidden_own,
    )
    grad_down = group_terms(grad_down_terms.reshape(groups, -1, width))
    far_grads = mlp_backward(
        grad_far, far_result[1], far_result[2], gate_up, down, grad_down_terms
    )
    far_sum = core_sum(far_grads[1]).astype(BF)
    near_grads = mlp_backward(grad_near, near_result[1], near_result[2], gate_up, down, far_sum)
    to_x, to_y = sum_near(*lax.optimization_barrier((near_grads[1], *send_far(far_sum))))
    gate_up_terms = gate_terms(
        normed_all, [g[0] for g in (own_grads, near_grads, far_grads)], groups, to_x
    )
    grad_normed_mlp = sum_own(own_grads[1], to_x, to_y)
    grad_normed_mlp = after(grad_normed_mlp, gate_up_terms)
    term = gate_up_terms.reshape(groups * members * shard_rows, 2 * hidden_pad)
    gate_up_share = lax.psum_scatter(term, "g", scatter_dimension=0, tiled=True)
    term = gate_up_share.reshape(members, shard_rows, 2 * hidden_pad)
    term = lax.all_to_all(term, PLANE, split_axis=0, concat_axis=0, tiled=True)

    grad_w_gate, grad_w_up = owner_rows(term, groups, piece)

    grad_middle, grad_branch, grad_queries, grad_keys, grad_values, terms = attend_backward(
        grad_normed_mlp, grad_out, middle, branch, d_gains, w_o,
        queries, keys, values, query_ids, key_ids, log_total, attn_scale,
    )
    out_terms = over_rows(attended, grad_branch).astype(BF)
    out_terms = out_terms.reshape(2, groups, 2, 2, w_out.shape[0], width)
    out_terms = plane_terms(fold(out_terms, "c", 3))
    own_weights, other_weights = mine, other
    grad_normed, returned, mine, sent = project_backward(
        places, after(grad_queries, grad_down), grad_keys, grad_values, query_raw, key_raw,
        cosine_table, sine_table, h_gains, normed, normed_before, own_weights, other_weights,
        layer_in, before, d_gains, terms, mixed_terms, shard_rows,
    )
    returned = lax.ppermute(returned, ("g", "y", "c"), [(i + 1, i) for i in range(seq_size - 1)])
    grad_in = grad_tokens(
        places, returned, grad_normed, own_weights, other_weights, layer_in, d_gains, grad_middle
    )
    mine = (mine.astype(F32) + swap(sent, "c").astype(F32)).astype(BF)
    qkv_terms = plane_terms(mine.reshape(2, groups, 2, 2 * shard_rows, half_cols))
    qkv_terms = qkv_terms.reshape(groups, -1, width)
    share = jnp.concatenate([out_terms, qkv_terms], axis=1)
    share = group_terms(after(share, gate_up_share))
    grad_w_out = share[: w_out.shape[0]]
    share = share[w_out.shape[0] :].astype(BF).reshape(2, shard_rows, half_cols)
    mine = lax.dynamic_index_in_dim(share, core, 0, keepdims=False)
    other = lax.dynamic_index_in_dim(share, 1 - core, 0, keepdims=False)
    first, second = in_order(mine, swap(other, "c"), core).astype(F32)
    half = q_cols // 2
    d_terms = first[:, half + k_cols :]
    return (
        layer_out.astype(BF)[None],
        grad_in[None],
        jnp.concatenate([first[:, :half], second[:, :half]], axis=1),
        first[:, half : half + k_cols],
        second[:, half : half + k_cols],
        grad_w_out,
        grad_w_gate,
        grad_w_up,
        grad_down,
        d_terms[:, 0],
        d_terms[:, 1],
        d_terms[:, 2],
        d_terms[:, 3],
        d_terms[:head_rows, 4],
        d_terms[:head_rows, 5],
    )


def solution(mesh):
    batch, seq = mesh.devices.shape
    fine = Mesh(mesh.devices.reshape(batch, seq // 4, 2, 2), ALL)
    rows = ("g", "y", "c")
    return jax.shard_map(
        on_device,
        mesh=fine,
        in_specs=(P("x", rows, None),) * 2
        + (P("x", None),)
        + (P(ALL, None),) * 7
        + (P(ALL),) * 6,
        out_specs=(P("x", rows, None),) * 2 + (P(ALL, None),) * 7 + (P(ALL),) * 6,
        check_vma=False,
    )
```

```python
import functools

import jax
import jax.numpy as jnp
from jax import lax
from jax.experimental import pallas as pl
from jax.experimental.pallas import tpu as pltpu
from jax.sharding import Mesh
from jax.sharding import PartitionSpec as P

HEAD = 256
WINDOW = 512
EPSILON = 1e-06
ROPE_BASE = 10000.0
ALL = ("x", "g", "y", "c")
PLANE = ("x", "y", "c")
BF = jnp.bfloat16
F32 = jnp.float32


def norm_gain(values, gain_vec):
    return (
        values * lax.rsqrt(jnp.mean(values * values, axis=-1, keepdims=True) + EPSILON) * gain_vec
    )


def rope_tables(first_row, row_count, head_size):
    places = (first_row + jnp.arange(row_count, dtype=jnp.int32)).astype(F32)
    frequency = ROPE_BASE ** (-(jnp.arange(head_size // 2, dtype=F32) * 2.0) / head_size)
    angles = places[:, None] * frequency[None, :]
    return (jnp.cos(angles), jnp.sin(angles))


def matmul(left_side, right_side):
    return jnp.dot(left_side, right_side, preferred_element_type=F32)


def over_rows(left_side, right_side):
    return lax.dot_general(
        left_side, right_side, (((0,), (0,)), ((), ())), preferred_element_type=F32
    )


def by_transpose(left_side, right_side):
    return lax.dot_general(
        left_side, right_side, (((1,), (1,)), ((), ())), preferred_element_type=F32
    )


def swap(array, axis):
    return lax.ppermute(array, axis, [(0, 1), (1, 0)])


GELU_A = 0.7978845608028654
GELU_B = 0.044715
TILE = 512
PARAMS = pltpu.CompilerParams(vmem_limit_bytes=58 << 20)


def whole_block(shape):
    return pl.BlockSpec(shape, lambda i: (0,) * len(shape), pipeline_mode=pl.Buffered(1))


def row_block(rows, columns):
    return pl.BlockSpec((rows, columns), lambda i: (i, 0))


def mlp_forward_kernel(normed, gate_up, down, _, hidden, gelu, slope, mixed):
    own = down.shape[0]
    raw = matmul(normed[...], gate_up[...])
    gate_raw, up_raw = raw[:, :own], raw[:, own:]
    square = gate_raw * gate_raw
    bend = jnp.tanh(GELU_A * (gate_raw + GELU_B * square * gate_raw))
    half = 0.5 + 0.5 * bend
    active = gate_raw * half
    turn = 0.5 * gate_raw * (1.0 - bend * bend) * (GELU_A * (1.0 + 3.0 * GELU_B * square))
    low = (active * up_raw).astype(BF)
    hidden[...] = low
    gelu[...] = active.astype(BF)
    slope[...] = ((half + turn) * up_raw).astype(BF)
    mixed[...] = matmul(low, down[...]).astype(BF)


def mlp_forward(normed, gate_up, down, earlier):
    rows, width = normed.shape
    own = down.shape[0]
    flat = jax.ShapeDtypeStruct((rows, own), BF)
    return pl.pallas_call(
        mlp_forward_kernel,
        grid=(rows // TILE,),
        in_specs=[
            row_block(TILE, width),
            whole_block(gate_up.shape),
            whole_block(down.shape),
            pl.BlockSpec(memory_space=pl.ANY),
        ],
        out_specs=[row_block(TILE, own)] * 3 + [row_block(TILE, width)],
        out_shape=[flat, flat, flat, jax.ShapeDtypeStruct((rows, width), BF)],
        compiler_params=PARAMS,
        cost_estimate=pl.CostEstimate(
            flops=6 * rows * width * own, bytes_accessed=rows * (4 * width + 6 * own), transcendentals=0
        ),
    )(normed, gate_up, down, earlier)


def mlp_backward_kernel(grad_mixed, gelu, slope, gate_up, down, _, grad_raw, grad_normed):
    own = down.shape[0]
    grad_hidden = by_transpose(grad_mixed[...], down[...])
    grad_gate = (grad_hidden * slope[...].astype(F32)).astype(BF)
    grad_up = (grad_hidden * gelu[...].astype(F32)).astype(BF)
    grad_raw[:, :own] = grad_gate
    grad_raw[:, own:] = grad_up
    grad_normed[...] = (
        by_transpose(grad_gate, gate_up[:, :own]) + by_transpose(grad_up, gate_up[:, own:])
    ).astype(BF)


def mlp_backward(grad_mixed, gelu, slope, gate_up, down, earlier):
    rows, width = grad_mixed.shape
    own = down.shape[0]
    return pl.pallas_call(
        mlp_backward_kernel,
        grid=(rows // TILE,),
        in_specs=[
            row_block(TILE, width),
            row_block(TILE, own),
            row_block(TILE, own),
            whole_block(gate_up.shape),
            whole_block(down.shape),
            pl.BlockSpec(memory_space=pl.ANY),
        ],
        out_specs=[row_block(TILE, 2 * own), row_block(TILE, width)],
        out_shape=[
            jax.ShapeDtypeStruct((rows, 2 * own), BF),
            jax.ShapeDtypeStruct((rows, width), BF),
        ],
        compiler_params=PARAMS,
        cost_estimate=pl.CostEstimate(
            flops=6 * rows * width * own, bytes_accessed=rows * (4 * width + 8 * own), transcendentals=0
        ),
    )(grad_mixed, gelu, slope, gate_up, down, earlier)


def down_terms_kernel(*refs):
    *ins, out = refs
    half = len(ins) // 2
    total = over_rows(ins[0][...], ins[half][...])
    for left, right in zip(ins[1:half], ins[half + 1 :]):
        total = total + over_rows(left[...], right[...])
    out[...] = total.astype(BF)


def down_terms(hidden, grad_mixed, keep):
    own, width = hidden[0].shape[1], grad_mixed[0].shape[1]
    rows = sum(part.shape[0] for part in hidden)
    return pl.pallas_call(
        down_terms_kernel,
        grid=(own // 128,),
        in_specs=[pl.BlockSpec((part.shape[0], 128), lambda i: (0, i)) for part in hidden]
        + [whole_block(part.shape) for part in grad_mixed],
        out_specs=row_block(128, width),
        out_shape=jax.ShapeDtypeStruct((keep, width), BF),
        compiler_params=PARAMS,
        cost_estimate=pl.CostEstimate(
            flops=2 * rows * width * own, bytes_accessed=2 * rows * (width + own), transcendentals=0
        ),
    )(*hidden, *grad_mixed)


def gate_terms_kernel(*refs):
    *ins, _, out = refs
    half = len(ins) // 2
    total = over_rows(ins[0][...], ins[half][...])
    for left, right in zip(ins[1:half], ins[half + 1 :]):
        total = total + over_rows(left[...], right[...])
    total = total.astype(BF)
    groups, sides, rows, _ = out.shape
    for side in range(sides):
        for group in range(groups):
            first = (side * groups + group) * rows
            out[group, side] = total[first : first + rows]


def gate_terms(normed, grad_raw, groups, earlier):
    width, both = normed[0].shape[1], grad_raw[0].shape[1]
    rows = sum(part.shape[0] for part in normed)
    shape = (groups, 2, width // (2 * groups))
    return pl.pallas_call(
        gate_terms_kernel,
        grid=(both // 256,),
        in_specs=[whole_block(part.shape) for part in normed]
        + [pl.BlockSpec((part.shape[0], 256), lambda i: (0, i)) for part in grad_raw]
        + [pl.BlockSpec(memory_space=pl.ANY)],
        out_specs=pl.BlockSpec(shape + (256,), lambda i: (0, 0, 0, i)),
        out_shape=jax.ShapeDtypeStruct(shape + (both,), BF),
        compiler_params=PARAMS,
        cost_estimate=pl.CostEstimate(
            flops=2 * rows * width * both, bytes_accessed=2 * rows * (width + both), transcendentals=0
        ),
    )(*normed, *grad_raw, earlier)


def after(value, *earlier):
    return lax.optimization_barrier((value, *earlier))[0]


def with_core(part):
    return jnp.concatenate([part, swap(part, "c")])


def core_sum(part):
    half = part.shape[0] // 2
    return part[:half].astype(F32) + swap(part[half:], "c").astype(F32)


def send_far(far):
    half = far.shape[0] // 2
    return swap(far[:half], "y"), swap(far[half:], "x")


def sum_near(near, top, low):
    near = core_sum(near)
    rows = near.shape[0] // 2
    half = rows // 2
    to_x = jnp.concatenate([near[:half] + top, near[half:rows]]).astype(BF)
    to_y = jnp.concatenate([near[rows : rows + half], near[rows + half :] + low]).astype(BF)
    return to_x, to_y


def sum_own(own, to_x, to_y):
    return core_sum(own) + swap(to_x, "x").astype(F32) + swap(to_y, "y").astype(F32)


def in_order(own, other, place):
    both = jnp.concatenate([own[None], other[None], own[None]])
    return lax.dynamic_slice_in_dim(both, place, 2, 0)


def group_gather(own):
    size = lax.axis_size("g")
    parts = [own] + [
        lax.ppermute(own, "g", [((i + k) % size, i) for i in range(size)]) for k in range(1, size)
    ]
    both = jnp.stack(parts + parts[:-1])
    place = lax.axis_index("g")
    return lax.dynamic_slice_in_dim(both, lax.rem(size - place, size), size, 0)


def plane_start(blocks):
    half = blocks.shape[0] // 2
    return swap(blocks[:half], "x"), swap(blocks[half:], "y")


def plane_weights(blocks, from_x, from_y):
    x, y = lax.axis_index("x"), lax.axis_index("y")
    half = blocks.shape[0] // 2
    first = in_order(blocks[:half], from_x, x)
    second = in_order(blocks[half:], from_y, y)
    first = in_order(first, swap(first, "y"), y)
    second = in_order(second, swap(second, "x"), x)
    first = first.transpose(1, 2, 0, 3, 4)
    second = second.transpose(0, 2, 1, 3, 4)
    return jnp.concatenate([first, second], axis=1)


def group_terms(term):
    size = lax.axis_size("g")
    place = lax.axis_index("g")
    total = lax.dynamic_index_in_dim(term, place, 0, keepdims=False).astype(F32)
    for k in range(1, size):
        chunk = lax.dynamic_index_in_dim(term, lax.rem(place + k, size), 0, keepdims=False)
        pairs = [(i, (i + k) % size) for i in range(size)]
        total = total + lax.ppermute(chunk, "g", pairs).astype(F32)
    return total


def fold(term, axis, dim):
    place = lax.axis_index(axis)
    mine = lax.dynamic_index_in_dim(term, place, dim, keepdims=False)
    other = lax.dynamic_index_in_dim(term, 1 - place, dim, keepdims=False)
    return (mine.astype(F32) + swap(other.astype(BF), axis).astype(F32)).astype(BF)


def plane_terms(term):
    half = term.shape[1] // 2
    first = fold(fold(term[:, :half], "x", 0), "y", 1)
    second = fold(fold(term[:, half:], "y", 2), "x", 0)
    return jnp.concatenate([first, second])


def rms_scale(values):
    return lax.rsqrt(jnp.mean(values * values, axis=-1, keepdims=True) + EPSILON)


def rms_backward(values, scale, gain, grad):
    weighted = grad * gain
    inner = jnp.mean(weighted * values, axis=-1, keepdims=True)
    terms = jnp.sum(grad * values * scale, axis=0, keepdims=True)
    return weighted * scale - values * (scale * scale * scale * inner), terms


def turn_forward(values, cosine, sine):
    half = cosine.shape[1]
    low, high = values[:, :half], values[:, half:]
    return jnp.concatenate([low * cosine - high * sine, high * cosine + low * sine], axis=1)


def turn_backward(grad, cosine, sine):
    half = cosine.shape[1]
    low, high = grad[:, :half], grad[:, half:]
    return jnp.concatenate([low * cosine + high * sine, high * cosine - low * sine], axis=1)


def gain_places(width, columns, shard_rows):
    heads = columns // (width // shard_rows)
    row = lax.broadcasted_iota(jnp.int32, (width, columns), 0)
    column = lax.broadcasted_iota(jnp.int32, (width, columns), 1)
    place = (column // heads) * shard_rows + lax.rem(column, heads)
    return jnp.where(row == place, 1.0, 0.0).astype(BF)


def project_kernel(
    shard_rows, core, tokens, earlier, own, other, cosine, sine,
    normed, normed_earlier, query_raw, key_raw, queries, keys, values, d_gains, h_gains,
):
    rows, width = tokens.shape
    pad, k_cols = earlier.shape[0], key_raw.shape[1]
    half = query_raw.shape[1] // 2
    first_is_own = core[0] == 0
    block = jnp.where(
        first_is_own, own[:, half + k_cols :].astype(F32), other[:, half + k_cols :].astype(F32)
    )
    flat = block.T[:8]
    d_gains[...] = flat
    chosen = matmul(flat.astype(BF), gain_places(width, k_cols, shard_rows))
    h_gains[...] = chosen
    before = earlier[...].astype(F32)
    low_before = (before * rms_scale(before) * flat[0:1]).astype(BF)
    normed_earlier[...] = low_before
    inputs = tokens[...].astype(F32)
    low = (inputs * rms_scale(inputs) * flat[0:1]).astype(BF)
    normed[...] = low
    raw_own = matmul(low, own[:, : half + k_cols])
    raw_other = matmul(low, other[:, : half + k_cols])
    before_own = matmul(low_before, own[:, half : half + k_cols])
    before_other = matmul(low_before, other[:, half : half + k_cols])
    first = jnp.where(first_is_own, raw_own, raw_other)
    second = jnp.where(first_is_own, raw_other, raw_own)
    raw_query = jnp.concatenate([first[:, :half], second[:, :half]], axis=1)
    query_raw[...] = raw_query
    values[:pad] = jnp.where(first_is_own, before_other, before_own).astype(BF)
    values[pad:] = second[:, half:].astype(BF)
    raw_before = jnp.where(first_is_own, before_own, before_other)
    for raw, at in ((raw_before, slice(0, pad)), (first[:, half:], slice(pad, pad + rows))):
        key_raw[at] = raw
        part = raw * rms_scale(raw) * chosen[5:6]
        keys[at] = turn_forward(part, cosine[at], sine[at]).astype(BF)
    cos, sin = cosine[pad:], sine[pad:]
    for head in range(2 * half // k_cols):
        at = slice(head * k_cols, (head + 1) * k_cols)
        part = raw_query[:, at]
        part = part * rms_scale(part) * chosen[4:5]
        queries[:, at] = turn_forward(part, cos, sin).astype(BF)


def project(core, tokens, earlier, own, other, cosine, sine, shard_rows, q_cols, k_cols):
    rows, width = tokens.shape
    seen = rows + earlier.shape[0]
    vmem = pl.BlockSpec(memory_space=pltpu.VMEM)
    return pl.pallas_call(
        functools.partial(project_kernel, shard_rows),
        in_specs=[pl.BlockSpec(memory_space=pltpu.SMEM)] + [vmem] * 6,
        out_specs=[vmem] * 9,
        out_shape=[
            jax.ShapeDtypeStruct((rows, width), BF),
            jax.ShapeDtypeStruct(earlier.shape, BF),
            jax.ShapeDtypeStruct((rows, q_cols), F32),
            jax.ShapeDtypeStruct((seen, k_cols), F32),
            jax.ShapeDtypeStruct((rows, q_cols), BF),
            jax.ShapeDtypeStruct((seen, k_cols), BF),
            jax.ShapeDtypeStruct((seen, k_cols), BF),
            jax.ShapeDtypeStruct((8, width), F32),
            jax.ShapeDtypeStruct((8, k_cols), F32),
        ],
        compiler_params=PARAMS,
        cost_estimate=pl.CostEstimate(
            flops=2 * rows * width * (q_cols + 4 * k_cols), bytes_accessed=16 * rows * width, transcendentals=0
        ),
    )(core, tokens, earlier, own, other, cosine, sine)


def tile_mask(first, rows, first_key, keys, query_ids, key_ids, pad):
    query_place = pad + first + lax.broadcasted_iota(jnp.int32, (rows, keys), 0)
    key_place = first_key + lax.broadcasted_iota(jnp.int32, (rows, keys), 1)
    distance = query_place - key_place
    same_doc = query_ids[first : first + rows, :] == key_ids[:, first_key : first_key + keys]
    return (distance >= 0) & (distance < WINDOW) & same_doc


def attend_kernel(
    scale, queries, keys, values, query_ids, key_ids, w_o, tokens, d_gains,
    attended, log_total, branch, middle, normed_mlp,
):
    rows, q_cols = queries.shape
    pad, k_cols = keys.shape[0] - rows, keys.shape[1]
    tile = rows // 2
    span = pad + tile
    lane = lax.broadcasted_iota(jnp.int32, (tile, 128), 1)
    for first in (0, tile):
        at = slice(first, first + tile)
        seen = slice(first, first + span)
        allowed = tile_mask(first, tile, first, span, query_ids, key_ids, pad)
        logs = jnp.zeros((tile, 128), F32)
        for head in range(q_cols // k_cols):
            columns = slice(head * k_cols, (head + 1) * k_cols)
            scores = by_transpose(queries[at, columns], keys[seen]) * scale
            scores = jnp.where(allowed, scores, -1e30)
            row_max = jnp.max(scores, axis=-1, keepdims=True)
            weights = jnp.exp(scores - row_max)
            row_total = jnp.sum(weights, axis=-1, keepdims=True)
            probabilities = (weights * (1.0 / row_total)).astype(BF)
            attended[at, columns] = matmul(probabilities, values[seen]).astype(BF)
            logs = jnp.where(lane == head, row_max + jnp.log(row_total), logs)
        log_total[at] = logs
    out = matmul(attended[...], w_o[...])
    branch[...] = out
    total = tokens[...].astype(F32) + out * rms_scale(out) * d_gains[1:2]
    middle[...] = total
    normed_mlp[...] = (total * rms_scale(total) * d_gains[2:3]).astype(BF)


def attend(queries, keys, values, query_ids, key_ids, w_o, tokens, d_gains, scale):
    rows, q_cols = queries.shape
    width = tokens.shape[1]
    vmem = pl.BlockSpec(memory_space=pltpu.VMEM)
    return pl.pallas_call(
        functools.partial(attend_kernel, scale),
        in_specs=[vmem] * 8,
        out_specs=[vmem] * 5,
        out_shape=[
            jax.ShapeDtypeStruct((rows, q_cols), BF),
            jax.ShapeDtypeStruct((rows, 128), F32),
            jax.ShapeDtypeStruct((rows, width), F32),
            jax.ShapeDtypeStruct((rows, width), F32),
            jax.ShapeDtypeStruct((rows, width), BF),
        ],
        compiler_params=PARAMS,
        cost_estimate=pl.CostEstimate(
            flops=2 * rows * q_cols * (width + 2 * keys.shape[0]), bytes_accessed=20 * rows * width, transcendentals=0
        ),
    )(queries, keys, values, query_ids, key_ids, w_o, tokens, d_gains)


def attend_backward_kernel(
    scale, grad_normed_mlp, cotangent, middle, branch, d_gains, w_o,
    queries, keys, values, query_ids, key_ids, log_total,
    grad_middle, grad_branch, grad_queries, grad_keys, grad_values, terms, grad_attended,
):
    rows, q_cols = queries.shape
    pad, k_cols = keys.shape[0] - rows, keys.shape[1]
    total = middle[...]
    from_mlp, mlp_terms = rms_backward(total, rms_scale(total), d_gains[2:3], grad_normed_mlp[...])
    grad_total = cotangent[...].astype(F32) + from_mlp
    grad_middle[...] = grad_total
    out = branch[...]
    grad_out, out_terms = rms_backward(out, rms_scale(out), d_gains[1:2], grad_total)
    low = grad_out.astype(BF)
    grad_branch[...] = low
    terms[...] = jnp.concatenate([out_terms, mlp_terms, jnp.zeros((6, out.shape[1]), F32)], axis=0)
    grad_attended[...] = by_transpose(low, w_o[...]).astype(BF)
    grad_keys[...] = jnp.zeros_like(grad_keys)
    grad_values[...] = jnp.zeros_like(grad_values)
    tile = rows // 2
    span = pad + tile
    for first in (0, tile):
        at = slice(first, first + tile)
        seen = slice(first, first + span)
        allowed = tile_mask(first, tile, first, span, query_ids, key_ids, pad)
        key_total = jnp.zeros((span, k_cols), F32)
        value_total = jnp.zeros((span, k_cols), F32)
        for head in range(q_cols // k_cols):
            columns = slice(head * k_cols, (head + 1) * k_cols)
            query = queries[at, columns]
            grad = grad_attended[at, columns]
            scores = by_transpose(query, keys[seen]) * scale
            probabilities = jnp.where(
                allowed, jnp.exp(scores - log_total[at, head : head + 1]), 0.0
            )
            grad_prob = by_transpose(grad, values[seen])
            inner = jnp.sum(probabilities * grad_prob, axis=-1, keepdims=True)
            grad_score = (probabilities * (grad_prob - inner)).astype(BF)
            grad_queries[at, columns] = matmul(grad_score, keys[seen]) * scale
            key_total = key_total + over_rows(grad_score, query)
            value_total = value_total + over_rows(probabilities.astype(BF), grad)
        grad_keys[seen] = grad_keys[seen] + key_total * scale
        grad_values[seen] = grad_values[seen] + value_total


def attend_backward(
    grad_normed_mlp, cotangent, middle, branch, d_gains, w_o,
    queries, keys, values, query_ids, key_ids, log_total, scale,
):
    rows, q_cols = queries.shape
    width = middle.shape[1]
    vmem = pl.BlockSpec(memory_space=pltpu.VMEM)
    return pl.pallas_call(
        functools.partial(attend_backward_kernel, scale),
        in_specs=[vmem] * 12,
        out_specs=[vmem] * 6,
        out_shape=[
            jax.ShapeDtypeStruct((rows, width), F32),
            jax.ShapeDtypeStruct((rows, width), BF),
            jax.ShapeDtypeStruct((rows, q_cols), F32),
            jax.ShapeDtypeStruct(keys.shape, F32),
            jax.ShapeDtypeStruct(keys.shape, F32),
            jax.ShapeDtypeStruct((8, width), F32),
        ],
        scratch_shapes=[pltpu.VMEM((rows, q_cols), BF)],
        compiler_params=PARAMS,
        cost_estimate=pl.CostEstimate(
            flops=2 * rows * q_cols * (width + 5 * keys.shape[0]), bytes_accessed=30 * rows * width, transcendentals=0
        ),
    )(
        grad_normed_mlp, cotangent, middle, branch, d_gains, w_o,
        queries, keys, values, query_ids, key_ids, log_total,
    )


def project_backward_kernel(
    shard_rows, core, grad_queries, grad_keys, grad_values, query_raw, key_raw, cosine, sine,
    h_gains, normed, normed_earlier, own, other, tokens, earlier, d_gains, terms, mixed_terms,
    grad_normed, returned, mine, sent,
):
    rows, width = tokens.shape
    pad, k_cols = earlier.shape[0], key_raw.shape[1]
    half = query_raw.shape[1] // 2
    cols = half + k_cols
    first_is_own = core[0] == 0
    cos, sin = cosine[pad:], sine[pad:]
    query_terms = jnp.zeros((1, k_cols), F32)
    parts = []
    for head in range(2 * half // k_cols):
        at = slice(head * k_cols, (head + 1) * k_cols)
        raw = query_raw[:, at]
        grad = turn_backward(grad_queries[:, at], cos, sin)
        grad, term = rms_backward(raw, rms_scale(raw), h_gains[4:5], grad)
        query_terms = query_terms + term
        parts.append(grad.astype(BF))
    raw = key_raw[...]
    grad = turn_backward(grad_keys[...], cosine[...], sine[...])
    grad, key_terms = rms_backward(raw, rms_scale(raw), h_gains[5:6], grad)
    grad_key, grad_value = grad.astype(BF), grad_values[...].astype(BF)
    returned[:, :k_cols] = grad_key[:pad]
    returned[:, k_cols:] = grad_value[:pad]
    kv_own = jnp.where(first_is_own, grad_key, grad_value)
    kv_other = jnp.where(first_is_own, grad_value, grad_key)
    both = len(parts) // 2
    first = jnp.concatenate(parts[:both], axis=1)
    second = jnp.concatenate(parts[both:], axis=1)
    q_own = jnp.where(first_is_own, first, second)
    q_other = jnp.where(first_is_own, second, first)
    grad_own = jnp.concatenate([q_own, kv_own[pad:]], axis=1)
    grad_other = jnp.concatenate([q_other, kv_other[pad:]], axis=1)
    total = by_transpose(grad_own, own[:, :cols]) + by_transpose(grad_other, other[:, :cols])
    grad_normed[...] = total
    values = tokens[...].astype(F32)
    in_terms = jnp.sum(total * values * rms_scale(values), axis=0, keepdims=True)
    total = by_transpose(kv_own[:pad], own[:, half:cols])
    total = total + by_transpose(kv_other[:pad], other[:, half:cols])
    values = earlier[...].astype(F32)
    in_terms = in_terms + jnp.sum(total * values * rms_scale(values), axis=0, keepdims=True)
    low, low_before = normed[...], normed_earlier[...]
    for out, query, key_value in ((mine, q_own, kv_own), (sent, q_other, kv_other)):
        out[:, :half] = over_rows(low, query).astype(BF)
        out[:, half:cols] = (
            over_rows(low, key_value[pad:]) + over_rows(low_before, key_value[:pad])
        ).astype(BF)
    heads = jnp.concatenate([query_terms, key_terms, jnp.zeros((6, k_cols), F32)], axis=0)
    placed = by_transpose(heads.astype(BF), gain_places(width, k_cols, shard_rows))
    block = jnp.concatenate(
        [in_terms, terms[0:2], mixed_terms[0:1], placed[0:2], jnp.zeros((122, width), F32)], axis=0
    ).T
    mine[:, cols:] = jnp.where(first_is_own, block, 0.0).astype(BF)
    sent[:, cols:] = jnp.where(first_is_own, 0.0, block).astype(BF)


def project_backward(
    core, grad_queries, grad_keys, grad_values, query_raw, key_raw, cosine, sine,
    h_gains, normed, normed_earlier, own, other, tokens, earlier, d_gains, terms, mixed_terms,
    shard_rows,
):
    rows, width = tokens.shape
    pad, k_cols = earlier.shape[0], key_raw.shape[1]
    vmem = pl.BlockSpec(memory_space=pltpu.VMEM)
    return pl.pallas_call(
        functools.partial(project_backward_kernel, shard_rows),
        in_specs=[pl.BlockSpec(memory_space=pltpu.SMEM)] + [vmem] * 17,
        out_specs=[vmem] * 4,
        out_shape=[
            jax.ShapeDtypeStruct((rows, width), F32),
            jax.ShapeDtypeStruct((pad, 2 * k_cols), BF),
            jax.ShapeDtypeStruct(own.shape, BF),
            jax.ShapeDtypeStruct(own.shape, BF),
        ],
        compiler_params=PARAMS,
        cost_estimate=pl.CostEstimate(
            flops=9 * rows * width * own.shape[1], bytes_accessed=30 * rows * width, transcendentals=0
        ),
    )(
        core, grad_queries, grad_keys, grad_values, query_raw, key_raw, cosine, sine,
        h_gains, normed, normed_earlier, own, other, tokens, earlier, d_gains, terms, mixed_terms,
    )


def grad_tokens_kernel(core, returned, grad_normed, own, other, tokens, d_gains, grad_middle, out):
    k_cols = returned.shape[1] // 2
    cols = own.shape[1] - 128
    half = cols - k_cols
    first_is_own = core[0] == 0
    grad_key, grad_value = returned[:, :k_cols], returned[:, k_cols:]
    kv_own = jnp.where(first_is_own, grad_key, grad_value)
    kv_other = jnp.where(first_is_own, grad_value, grad_key)
    total = grad_normed[...] + by_transpose(kv_own, own[:, half:cols])
    total = total + by_transpose(kv_other, other[:, half:cols])
    values = tokens[...].astype(F32)
    from_attn, _ = rms_backward(values, rms_scale(values), d_gains[0:1], total)
    out[...] = (grad_middle[...] + from_attn).astype(BF)


def grad_tokens(core, returned, grad_normed, own, other, tokens, d_gains, grad_middle):
    vmem = pl.BlockSpec(memory_space=pltpu.VMEM)
    return pl.pallas_call(
        grad_tokens_kernel,
        in_specs=[pl.BlockSpec(memory_space=pltpu.SMEM)] + [vmem] * 7,
        out_specs=vmem,
        out_shape=jax.ShapeDtypeStruct(tokens.shape, BF),
        compiler_params=PARAMS,
        cost_estimate=pl.CostEstimate(
            flops=2 * tokens.size * returned.shape[1], bytes_accessed=12 * tokens.size, transcendentals=0
        ),
    )(core, returned, grad_normed, own, other, tokens, d_gains, grad_middle)


def owner_rows_kernel(groups, piece, term, gate, up):
    sides, lanes = term.shape[0] // 2, term.shape[2] // 2
    for out, first in ((gate, 0), (up, lanes)):
        parts = []
        for side in range(2):
            rows = [
                term[side * sides + member, :, first : first + lanes].astype(F32)
                for member in range(sides)
            ]
            for group in range(groups):
                parts += [row[:, group * piece : (group + 1) * piece] for row in rows]
        out[...] = jnp.concatenate(parts, axis=1)


def owner_rows(term, groups, piece):
    vmem = pl.BlockSpec(memory_space=pltpu.VMEM)
    shape = jax.ShapeDtypeStruct((term.shape[1], term.shape[0] * groups * piece), F32)
    return pl.pallas_call(
        functools.partial(owner_rows_kernel, groups, piece),
        in_specs=[vmem],
        out_specs=[vmem, vmem],
        out_shape=[shape, shape],
        compiler_params=PARAMS,
        cost_estimate=pl.CostEstimate(
            flops=term.size, bytes_accessed=6 * term.size, transcendentals=0
        ),
    )(term)


def on_device(
    tokens,
    cotangent,
    doc_ids,
    w_query,
    w_key,
    w_value,
    w_out,
    w_gate,
    w_up,
    w_down,
    gain_attn_in,
    gain_attn_out,
    gain_mlp_in,
    gain_mlp_out,
    gain_query,
    gain_key,
):
    row_count = tokens.shape[1]
    width = tokens.shape[2]
    groups = lax.axis_size("g")
    members = lax.axis_size(PLANE)
    shard_rows = w_query.shape[0]
    head_rows = gain_query.shape[0]
    hidden_all = w_gate.shape[1]
    hidden_own = hidden_all // members
    hidden_pad = -(-hidden_own // 128) * 128
    piece = hidden_own // groups
    q_cols, k_cols = w_query.shape[1], w_key.shape[1]
    attn_scale = HEAD ** (-0.5)

    def gain_columns(d_gains, h_gains):
        columns = list(d_gains) + [
            jnp.pad(h, ((0, 0), (0, shard_rows - head_rows))) for h in h_gains
        ]
        block = jnp.stack(columns, axis=-1)
        return jnp.pad(block, ((0, 0), (0, 0), (0, 128 - len(columns))))

    seq_place = lax.axis_index(("g", "y", "c"))
    seq_size = lax.axis_size(("g", "y", "c"))

    def spread(weight):
        cut = weight.reshape(shard_rows, 2, groups, members // 2, piece)
        cut = cut.transpose(1, 3, 0, 2, 4).reshape(members, shard_rows, hidden_own)
        return jnp.pad(cut, ((0, 0), (0, 0), (0, hidden_pad - hidden_own)))

    sent = jnp.concatenate([spread(w_gate), spread(w_up)], axis=2)
    core = lax.axis_index("c")
    half_cols = q_cols // 2 + k_cols + 128
    gains = gain_columns(
        [g[None] for g in (gain_attn_in, gain_attn_out, gain_mlp_in, gain_mlp_out)],
        [gain_query[None], gain_key[None]],
    )
    halves = jnp.stack(
        [
            jnp.concatenate([w_query[:, : q_cols // 2], w_key, gains[0]], axis=1),
            jnp.concatenate([w_query[:, q_cols // 2 :], w_value, jnp.zeros_like(gains[0])], axis=1),
        ]
    )
    mine = lax.dynamic_index_in_dim(halves, core, 0, keepdims=False)
    other = lax.dynamic_index_in_dim(halves, 1 - core, 0, keepdims=False)
    mine = in_order(mine, swap(other, "c"), core).reshape(2 * shard_rows, half_cols)
    mine, sent = lax.optimization_barrier((mine, sent))
    sent = lax.all_to_all(sent, PLANE, split_axis=0, concat_axis=0, tiled=True)
    sent = sent.reshape(members * shard_rows, 2 * hidden_pad)
    before = lax.ppermute(
        after(tokens[0], mine), ("g", "y", "c"), [(i, i + 1) for i in range(seq_size - 1)]
    )
    mine, sent, before = lax.optimization_barrier((group_gather(mine), sent, before))
    mine = plane_weights(mine, *plane_start(mine)).reshape(width, half_cols)
    other = swap(mine, "c")

    down = lax.all_gather(jnp.concatenate([w_down, w_out]), "g", axis=0)
    w_o = down[:, w_down.shape[0] :]
    down = down[:, : w_down.shape[0]].reshape(-1, width)
    down = jnp.pad(down, ((0, hidden_pad - hidden_own), (0, 0)))

    both = lax.all_gather(sent, "g", axis=0)
    both = both.reshape(groups, 2, members // 2 * shard_rows, 2 * hidden_pad)
    gate_up = both.transpose(1, 0, 2, 3).reshape(width, 2 * hidden_pad)

    first_row = seq_place * row_count
    ids_all = doc_ids[0]
    ids_own = lax.dynamic_slice_in_dim(ids_all, first_row, row_count, 0)
    ids_prev = lax.dynamic_slice_in_dim(
        ids_all, jnp.maximum(first_row - row_count, 0), row_count, 0
    )
    ids_prev = jnp.where(seq_place > 0, ids_prev, -1)
    ids_pad = jnp.concatenate([ids_prev, ids_own])
    query_ids, key_ids = ids_own[:, None], ids_pad[None]
    cosine_table, sine_table = rope_tables(first_row - row_count, 2 * row_count, HEAD)
    places = jnp.full((1,), core, jnp.int32)
    layer_in, grad_out = tokens[0], cotangent[0]

    normed, normed_before, query_raw, key_raw, queries, keys, values, d_gains, h_gains = project(
        places, layer_in, before, mine, other, cosine_table, sine_table, shard_rows, q_cols, k_cols
    )
    w_o = plane_weights(*lax.optimization_barrier((w_o, *plane_start(w_o), keys))[:3])
    w_o = in_order(w_o, swap(w_o, "c"), core).transpose(1, 2, 3, 0, 4, 5).reshape(q_cols, width)
    attended, log_total, branch, middle, normed_mlp = attend(
        queries, keys, values, query_ids, key_ids, w_o, layer_in, d_gains, attn_scale
    )

    half = row_count // 2
    from_x, from_y, down = lax.optimization_barrier(
        (swap(normed_mlp, "x"), swap(normed_mlp, "y"), down)
    )
    normed_far = jnp.concatenate([swap(from_x[:half], "y"), swap(from_y[half:], "x")])
    normed_near = jnp.concatenate([from_x, from_y])
    normed_all = [with_core(part) for part in (normed_mlp, normed_near, normed_far)]
    far_result = mlp_forward(normed_all[2], gate_up, down, normed_all[2])
    far_sum = core_sum(far_result[3]).astype(BF)
    near_result = mlp_forward(normed_all[1], gate_up, down, far_sum)
    to_x, to_y = sum_near(*lax.optimization_barrier((near_result[3], *send_far(far_sum))))
    own_result = mlp_forward(normed_all[0], gate_up, down, to_x)
    mixed = sum_own(own_result[3], to_x, to_y)
    layer_out = middle + norm_gain(mixed, d_gains[3:4])

    _, pullback = jax.vjp(norm_gain, mixed, d_gains[3:4])
    grad_mixed, mixed_terms = pullback(grad_out.astype(F32))
    grad_mixed = grad_mixed.astype(BF)
    from_x, from_y = swap(grad_mixed, "x"), swap(grad_mixed, "y")
    grad_own = with_core(grad_mixed)
    own_grads = mlp_backward(grad_own, own_result[1], own_result[2], gate_up, down, down)
    from_x, from_y = lax.optimization_barrier((from_x, from_y, own_grads[1]))[:2]
    grad_far = with_core(jnp.concatenate([swap(from_x[:half], "y"), swap(from_y[half:], "x")]))
    grad_near = with_core(jnp.concatenate([from_x, from_y]))
    grad_down_terms = down_terms(
        [r[0] for r in (own_result, near_result, far_result)],
        [grad_own, grad_near, grad_far],
        hidden_own,
    )
    grad_down = group_terms(grad_down_terms.reshape(groups, -1, width))
    far_grads = mlp_backward(
        grad_far, far_result[1], far_result[2], gate_up, down, grad_down_terms
    )
    far_sum = core_sum(far_grads[1]).astype(BF)
    near_grads = mlp_backward(grad_near, near_result[1], near_result[2], gate_up, down, far_sum)
    to_x, to_y = sum_near(*lax.optimization_barrier((near_grads[1], *send_far(far_sum))))
    gate_up_terms = gate_terms(
        normed_all, [g[0] for g in (own_grads, near_grads, far_grads)], groups, to_x
    )
    grad_normed_mlp = sum_own(own_grads[1], to_x, to_y)
    grad_normed_mlp = after(grad_normed_mlp, gate_up_terms)
    term = gate_up_terms.reshape(groups * members * shard_rows, 2 * hidden_pad)
    gate_up_share = lax.psum_scatter(term, "g", scatter_dimension=0, tiled=True)
    term = gate_up_share.reshape(members, shard_rows, 2 * hidden_pad)
    term = lax.all_to_all(term, PLANE, split_axis=0, concat_axis=0, tiled=True)

    grad_w_gate, grad_w_up = owner_rows(term, groups, piece)

    grad_middle, grad_branch, grad_queries, grad_keys, grad_values, terms = attend_backward(
        grad_normed_mlp, grad_out, middle, branch, d_gains, w_o,
        queries, keys, values, query_ids, key_ids, log_total, attn_scale,
    )
    out_terms = over_rows(attended, grad_branch).astype(BF)
    out_terms = out_terms.reshape(2, groups, 2, 2, w_out.shape[0], width)
    out_terms = plane_terms(fold(out_terms, "c", 3))
    own_weights, other_weights = mine, other
    grad_normed, returned, mine, sent = project_backward(
        places, after(grad_queries, grad_down), grad_keys, grad_values, query_raw, key_raw,
        cosine_table, sine_table, h_gains, normed, normed_before, own_weights, other_weights,
        layer_in, before, d_gains, terms, mixed_terms, shard_rows,
    )
    returned = lax.ppermute(returned, ("g", "y", "c"), [(i + 1, i) for i in range(seq_size - 1)])
    grad_in = grad_tokens(
        places, returned, grad_normed, own_weights, other_weights, layer_in, d_gains, grad_middle
    )
    mine = (mine.astype(F32) + swap(sent, "c").astype(F32)).astype(BF)
    qkv_terms = plane_terms(mine.reshape(2, groups, 2, 2 * shard_rows, half_cols))
    qkv_terms = qkv_terms.reshape(groups, -1, width)
    share = jnp.concatenate([out_terms, qkv_terms], axis=1)
    share = group_terms(after(share, gate_up_share))
    grad_w_out = share[: w_out.shape[0]]
    share = share[w_out.shape[0] :].astype(BF).reshape(2, shard_rows, half_cols)
    mine = lax.dynamic_index_in_dim(share, core, 0, keepdims=False)
    other = lax.dynamic_index_in_dim(share, 1 - core, 0, keepdims=False)
    first, second = in_order(mine, swap(other, "c"), core).astype(F32)
    half = q_cols // 2
    d_terms = first[:, half + k_cols :]
    return (
        layer_out.astype(BF)[None],
        grad_in[None],
        jnp.concatenate([first[:, :half], second[:, :half]], axis=1),
        first[:, half : half + k_cols],
        second[:, half : half + k_cols],
        grad_w_out,
        grad_w_gate,
        grad_w_up,
        grad_down,
        d_terms[:, 0],
        d_terms[:, 1],
        d_terms[:, 2],
        d_terms[:, 3],
        d_terms[:head_rows, 4],
        d_terms[:head_rows, 5],
    )


def solution(mesh):
    batch, seq = mesh.devices.shape
    fine = Mesh(mesh.devices.reshape(batch, seq // 4, 2, 2), ALL)
    rows = ("g", "y", "c")
    return jax.shard_map(
        on_device,
        mesh=fine,
        in_specs=(P("x", rows, None),) * 2
        + (P("x", None),)
        + (P(ALL, None),) * 7
        + (P(ALL),) * 6,
        out_specs=(P("x", rows, None),) * 2 + (P(ALL, None),) * 7 + (P(ALL),) * 6,
        check_vma=False,
    )
```

```python
import functools

import jax
import jax.numpy as jnp
from jax import lax
from jax.experimental import pallas as pl
from jax.experimental.pallas import tpu as pltpu
from jax.sharding import Mesh
from jax.sharding import PartitionSpec as P

HEAD = 256
WINDOW = 512
EPSILON = 1e-06
ROPE_BASE = 10000.0
ALL = ("x", "g", "y", "c")
PLANE = ("x", "y", "c")
BF = jnp.bfloat16
F32 = jnp.float32


def norm_gain(values, gain_vec):
    return (
        values * lax.rsqrt(jnp.mean(values * values, axis=-1, keepdims=True) + EPSILON) * gain_vec
    )


def rope_tables(first_row, row_count, head_size):
    places = (first_row + jnp.arange(row_count, dtype=jnp.int32)).astype(F32)
    frequency = ROPE_BASE ** (-(jnp.arange(head_size // 2, dtype=F32) * 2.0) / head_size)
    angles = places[:, None] * frequency[None, :]
    return (jnp.cos(angles), jnp.sin(angles))


def matmul(left_side, right_side):
    return jnp.dot(left_side, right_side, preferred_element_type=F32)


def over_rows(left_side, right_side):
    return lax.dot_general(
        left_side, right_side, (((0,), (0,)), ((), ())), preferred_element_type=F32
    )


def by_transpose(left_side, right_side):
    return lax.dot_general(
        left_side, right_side, (((1,), (1,)), ((), ())), preferred_element_type=F32
    )


def swap(array, axis):
    return lax.ppermute(array, axis, [(0, 1), (1, 0)])


GELU_A = 0.7978845608028654
GELU_B = 0.044715
TILE = 512
PARAMS = pltpu.CompilerParams(vmem_limit_bytes=58 << 20)


def whole_block(shape):
    return pl.BlockSpec(shape, lambda i: (0,) * len(shape), pipeline_mode=pl.Buffered(1))


def row_block(rows, columns):
    return pl.BlockSpec((rows, columns), lambda i: (i, 0))


def mlp_forward_kernel(normed, gate_up, down, _, hidden, gelu, slope, mixed):
    own = down.shape[0]
    raw = matmul(normed[...], gate_up[...])
    gate_raw, up_raw = raw[:, :own], raw[:, own:]
    square = gate_raw * gate_raw
    bend = jnp.tanh(GELU_A * (gate_raw + GELU_B * square * gate_raw))
    half = 0.5 + 0.5 * bend
    active = gate_raw * half
    turn = 0.5 * gate_raw * (1.0 - bend * bend) * (GELU_A * (1.0 + 3.0 * GELU_B * square))
    low = (active * up_raw).astype(BF)
    hidden[...] = low
    gelu[...] = active.astype(BF)
    slope[...] = ((half + turn) * up_raw).astype(BF)
    mixed[...] = matmul(low, down[...]).astype(BF)


def mlp_forward(normed, gate_up, down, earlier):
    rows, width = normed.shape
    own = down.shape[0]
    flat = jax.ShapeDtypeStruct((rows, own), BF)
    return pl.pallas_call(
        mlp_forward_kernel,
        grid=(rows // TILE,),
        in_specs=[
            row_block(TILE, width),
            whole_block(gate_up.shape),
            whole_block(down.shape),
            pl.BlockSpec(memory_space=pl.ANY),
        ],
        out_specs=[row_block(TILE, own)] * 3 + [row_block(TILE, width)],
        out_shape=[flat, flat, flat, jax.ShapeDtypeStruct((rows, width), BF)],
        compiler_params=PARAMS,
        cost_estimate=pl.CostEstimate(
            flops=6 * rows * width * own, bytes_accessed=rows * (4 * width + 6 * own), transcendentals=0
        ),
    )(normed, gate_up, down, earlier)


def mlp_backward_kernel(grad_mixed, gelu, slope, gate_up, down, _, grad_raw, grad_normed):
    own = down.shape[0]
    grad_hidden = by_transpose(grad_mixed[...], down[...])
    grad_gate = (grad_hidden * slope[...].astype(F32)).astype(BF)
    grad_up = (grad_hidden * gelu[...].astype(F32)).astype(BF)
    grad_raw[:, :own] = grad_gate
    grad_raw[:, own:] = grad_up
    grad_normed[...] = (
        by_transpose(grad_gate, gate_up[:, :own]) + by_transpose(grad_up, gate_up[:, own:])
    ).astype(BF)


def mlp_backward(grad_mixed, gelu, slope, gate_up, down, earlier):
    rows, width = grad_mixed.shape
    own = down.shape[0]
    return pl.pallas_call(
        mlp_backward_kernel,
        grid=(rows // TILE,),
        in_specs=[
            row_block(TILE, width),
            row_block(TILE, own),
            row_block(TILE, own),
            whole_block(gate_up.shape),
            whole_block(down.shape),
            pl.BlockSpec(memory_space=pl.ANY),
        ],
        out_specs=[row_block(TILE, 2 * own), row_block(TILE, width)],
        out_shape=[
            jax.ShapeDtypeStruct((rows, 2 * own), BF),
            jax.ShapeDtypeStruct((rows, width), BF),
        ],
        compiler_params=PARAMS,
        cost_estimate=pl.CostEstimate(
            flops=6 * rows * width * own, bytes_accessed=rows * (4 * width + 8 * own), transcendentals=0
        ),
    )(grad_mixed, gelu, slope, gate_up, down, earlier)


def down_terms_kernel(count, *refs):
    *ins, out = refs
    total = None
    for left, right in zip(ins[:count], ins[count : 2 * count]):
        part = over_rows(left[...], right[...])
        total = part if total is None else total + part
    for base in ins[2 * count :]:
        total = total + base[...]
    out[...] = total.astype(out.dtype)


def down_terms(hidden, grad_mixed, base, keep, kind):
    own, width = hidden[0].shape[1], grad_mixed[0].shape[1]
    rows = sum(part.shape[0] for part in hidden)
    return pl.pallas_call(
        functools.partial(down_terms_kernel, len(hidden)),
        grid=(own // 128,),
        in_specs=[pl.BlockSpec((part.shape[0], 128), lambda i: (0, i)) for part in hidden]
        + [whole_block(part.shape) for part in grad_mixed]
        + [row_block(128, width) for _ in base],
        out_specs=row_block(128, width),
        out_shape=jax.ShapeDtypeStruct((keep, width), kind),
        compiler_params=PARAMS,
        cost_estimate=pl.CostEstimate(
            flops=2 * rows * width * own, bytes_accessed=2 * rows * (width + own), transcendentals=0
        ),
    )(*hidden, *grad_mixed, *base)


def gate_terms_kernel(*refs):
    *ins, _, out = refs
    half = len(ins) // 2
    total = over_rows(ins[0][...], ins[half][...])
    for left, right in zip(ins[1:half], ins[half + 1 :]):
        total = total + over_rows(left[...], right[...])
    total = total.astype(BF)
    groups, sides, rows, _ = out.shape
    for side in range(sides):
        for group in range(groups):
            first = (side * groups + group) * rows
            out[group, side] = total[first : first + rows]


def gate_terms(normed, grad_raw, groups, earlier):
    width, both = normed[0].shape[1], grad_raw[0].shape[1]
    rows = sum(part.shape[0] for part in normed)
    shape = (groups, 2, width // (2 * groups))
    return pl.pallas_call(
        gate_terms_kernel,
        grid=(both // 256,),
        in_specs=[whole_block(part.shape) for part in normed]
        + [pl.BlockSpec((part.shape[0], 256), lambda i: (0, i)) for part in grad_raw]
        + [pl.BlockSpec(memory_space=pl.ANY)],
        out_specs=pl.BlockSpec(shape + (256,), lambda i: (0, 0, 0, i)),
        out_shape=jax.ShapeDtypeStruct(shape + (both,), BF),
        compiler_params=PARAMS,
        cost_estimate=pl.CostEstimate(
            flops=2 * rows * width * both, bytes_accessed=2 * rows * (width + both), transcendentals=0
        ),
    )(*normed, *grad_raw, earlier)


def after(value, *earlier):
    return lax.optimization_barrier((value, *earlier))[0]


def with_core(part):
    return jnp.concatenate([part, swap(part, "c")])


def core_sum(part):
    half = part.shape[0] // 2
    return part[:half].astype(F32) + swap(part[half:], "c").astype(F32)


def send_far(far):
    half = far.shape[0] // 2
    return swap(far[:half], "y"), swap(far[half:], "x")


def sum_near(near, top, low):
    near = core_sum(near)
    rows = near.shape[0] // 2
    half = rows // 2
    to_x = jnp.concatenate([near[:half] + top, near[half:rows]]).astype(BF)
    to_y = jnp.concatenate([near[rows : rows + half], near[rows + half :] + low]).astype(BF)
    return to_x, to_y


def sum_own(own, to_x, to_y):
    return core_sum(own) + swap(to_x, "x").astype(F32) + swap(to_y, "y").astype(F32)


def in_order(own, other, place):
    both = jnp.concatenate([own[None], other[None], own[None]])
    return lax.dynamic_slice_in_dim(both, place, 2, 0)


def group_gather(own):
    size = lax.axis_size("g")
    parts = [own] + [
        lax.ppermute(own, "g", [((i + k) % size, i) for i in range(size)]) for k in range(1, size)
    ]
    both = jnp.stack(parts + parts[:-1])
    place = lax.axis_index("g")
    return lax.dynamic_slice_in_dim(both, lax.rem(size - place, size), size, 0)


def plane_start(blocks):
    half = blocks.shape[0] // 2
    return swap(blocks[:half], "x"), swap(blocks[half:], "y")


def plane_weights(blocks, from_x, from_y):
    x, y = lax.axis_index("x"), lax.axis_index("y")
    half = blocks.shape[0] // 2
    first = in_order(blocks[:half], from_x, x)
    second = in_order(blocks[half:], from_y, y)
    first = in_order(first, swap(first, "y"), y)
    second = in_order(second, swap(second, "x"), x)
    first = first.transpose(1, 2, 0, 3, 4)
    second = second.transpose(0, 2, 1, 3, 4)
    return jnp.concatenate([first, second], axis=1)


def group_terms(term):
    size = lax.axis_size("g")
    place = lax.axis_index("g")
    total = lax.dynamic_index_in_dim(term, place, 0, keepdims=False).astype(F32)
    for k in range(1, size):
        chunk = lax.dynamic_index_in_dim(term, lax.rem(place + k, size), 0, keepdims=False)
        pairs = [(i, (i + k) % size) for i in range(size)]
        total = total + lax.ppermute(chunk, "g", pairs).astype(F32)
    return total


def fold(term, axis, dim):
    place = lax.axis_index(axis)
    mine = lax.dynamic_index_in_dim(term, place, dim, keepdims=False)
    other = lax.dynamic_index_in_dim(term, 1 - place, dim, keepdims=False)
    return (mine.astype(F32) + swap(other.astype(BF), axis).astype(F32)).astype(BF)


def plane_terms(term):
    half = term.shape[1] // 2
    first = fold(fold(term[:, :half], "x", 0), "y", 1)
    second = fold(fold(term[:, half:], "y", 2), "x", 0)
    return jnp.concatenate([first, second])


def rms_scale(values):
    return lax.rsqrt(jnp.mean(values * values, axis=-1, keepdims=True) + EPSILON)


def rms_backward(values, scale, gain, grad):
    weighted = grad * gain
    inner = jnp.mean(weighted * values, axis=-1, keepdims=True)
    terms = jnp.sum(grad * values * scale, axis=0, keepdims=True)
    return weighted * scale - values * (scale * scale * scale * inner), terms


def turn_forward(values, cosine, sine):
    half = cosine.shape[1]
    low, high = values[:, :half], values[:, half:]
    return jnp.concatenate([low * cosine - high * sine, high * cosine + low * sine], axis=1)


def turn_backward(grad, cosine, sine):
    half = cosine.shape[1]
    low, high = grad[:, :half], grad[:, half:]
    return jnp.concatenate([low * cosine + high * sine, high * cosine - low * sine], axis=1)


def gain_places(width, columns, shard_rows):
    heads = columns // (width // shard_rows)
    row = lax.broadcasted_iota(jnp.int32, (width, columns), 0)
    column = lax.broadcasted_iota(jnp.int32, (width, columns), 1)
    place = (column // heads) * shard_rows + lax.rem(column, heads)
    return jnp.where(row == place, 1.0, 0.0).astype(BF)


def project_kernel(
    shard_rows, core, tokens, earlier, own, other, cosine, sine,
    normed, normed_earlier, query_raw, key_raw, queries, keys, values, d_gains, h_gains,
):
    rows, width = tokens.shape
    pad, k_cols = earlier.shape[0], key_raw.shape[1]
    half = query_raw.shape[1] // 2
    first_is_own = core[0] == 0
    block = jnp.where(
        first_is_own, own[:, half + k_cols :].astype(F32), other[:, half + k_cols :].astype(F32)
    )
    flat = block.T[:8]
    d_gains[...] = flat
    chosen = matmul(flat.astype(BF), gain_places(width, k_cols, shard_rows))
    h_gains[...] = chosen
    before = earlier[...].astype(F32)
    low_before = (before * rms_scale(before) * flat[0:1]).astype(BF)
    normed_earlier[...] = low_before
    inputs = tokens[...].astype(F32)
    low = (inputs * rms_scale(inputs) * flat[0:1]).astype(BF)
    normed[...] = low
    raw_own = matmul(low, own[:, : half + k_cols])
    raw_other = matmul(low, other[:, : half + k_cols])
    before_own = matmul(low_before, own[:, half : half + k_cols])
    before_other = matmul(low_before, other[:, half : half + k_cols])
    first = jnp.where(first_is_own, raw_own, raw_other)
    second = jnp.where(first_is_own, raw_other, raw_own)
    raw_query = jnp.concatenate([first[:, :half], second[:, :half]], axis=1)
    query_raw[...] = raw_query
    values[:pad] = jnp.where(first_is_own, before_other, before_own).astype(BF)
    values[pad:] = second[:, half:].astype(BF)
    raw_before = jnp.where(first_is_own, before_own, before_other)
    for raw, at in ((raw_before, slice(0, pad)), (first[:, half:], slice(pad, pad + rows))):
        key_raw[at] = raw
        part = raw * rms_scale(raw) * chosen[5:6]
        keys[at] = turn_forward(part, cosine[at], sine[at]).astype(BF)
    cos, sin = cosine[pad:], sine[pad:]
    for head in range(2 * half // k_cols):
        at = slice(head * k_cols, (head + 1) * k_cols)
        part = raw_query[:, at]
        part = part * rms_scale(part) * chosen[4:5]
        queries[:, at] = turn_forward(part, cos, sin).astype(BF)


def project(core, tokens, earlier, own, other, cosine, sine, shard_rows, q_cols, k_cols):
    rows, width = tokens.shape
    seen = rows + earlier.shape[0]
    vmem = pl.BlockSpec(memory_space=pltpu.VMEM)
    return pl.pallas_call(
        functools.partial(project_kernel, shard_rows),
        in_specs=[pl.BlockSpec(memory_space=pltpu.SMEM)] + [vmem] * 6,
        out_specs=[vmem] * 9,
        out_shape=[
            jax.ShapeDtypeStruct((rows, width), BF),
            jax.ShapeDtypeStruct(earlier.shape, BF),
            jax.ShapeDtypeStruct((rows, q_cols), F32),
            jax.ShapeDtypeStruct((seen, k_cols), F32),
            jax.ShapeDtypeStruct((rows, q_cols), BF),
            jax.ShapeDtypeStruct((seen, k_cols), BF),
            jax.ShapeDtypeStruct((seen, k_cols), BF),
            jax.ShapeDtypeStruct((8, width), F32),
            jax.ShapeDtypeStruct((8, k_cols), F32),
        ],
        compiler_params=PARAMS,
        cost_estimate=pl.CostEstimate(
            flops=2 * rows * width * (q_cols + 4 * k_cols), bytes_accessed=16 * rows * width, transcendentals=0
        ),
    )(core, tokens, earlier, own, other, cosine, sine)


def tile_mask(first, rows, first_key, keys, query_ids, key_ids, pad):
    query_place = pad + first + lax.broadcasted_iota(jnp.int32, (rows, keys), 0)
    key_place = first_key + lax.broadcasted_iota(jnp.int32, (rows, keys), 1)
    distance = query_place - key_place
    same_doc = query_ids[first : first + rows, :] == key_ids[:, first_key : first_key + keys]
    return (distance >= 0) & (distance < WINDOW) & same_doc


def attend_kernel(
    scale, queries, keys, values, query_ids, key_ids, w_o, tokens, d_gains,
    attended, log_total, branch, middle, normed_mlp,
):
    rows, q_cols = queries.shape
    pad, k_cols = keys.shape[0] - rows, keys.shape[1]
    tile = rows // 2
    span = pad + tile
    lane = lax.broadcasted_iota(jnp.int32, (tile, 128), 1)
    for first in (0, tile):
        at = slice(first, first + tile)
        seen = slice(first, first + span)
        allowed = tile_mask(first, tile, first, span, query_ids, key_ids, pad)
        logs = jnp.zeros((tile, 128), F32)
        for head in range(q_cols // k_cols):
            columns = slice(head * k_cols, (head + 1) * k_cols)
            scores = by_transpose(queries[at, columns], keys[seen]) * scale
            scores = jnp.where(allowed, scores, -1e30)
            row_max = jnp.max(scores, axis=-1, keepdims=True)
            weights = jnp.exp(scores - row_max)
            row_total = jnp.sum(weights, axis=-1, keepdims=True)
            probabilities = (weights * (1.0 / row_total)).astype(BF)
            attended[at, columns] = matmul(probabilities, values[seen]).astype(BF)
            logs = jnp.where(lane == head, row_max + jnp.log(row_total), logs)
        log_total[at] = logs
    out = matmul(attended[...], w_o[...])
    branch[...] = out
    total = tokens[...].astype(F32) + out * rms_scale(out) * d_gains[1:2]
    middle[...] = total
    normed_mlp[...] = (total * rms_scale(total) * d_gains[2:3]).astype(BF)


def attend(queries, keys, values, query_ids, key_ids, w_o, tokens, d_gains, scale):
    rows, q_cols = queries.shape
    width = tokens.shape[1]
    vmem = pl.BlockSpec(memory_space=pltpu.VMEM)
    return pl.pallas_call(
        functools.partial(attend_kernel, scale),
        in_specs=[vmem] * 8,
        out_specs=[vmem] * 5,
        out_shape=[
            jax.ShapeDtypeStruct((rows, q_cols), BF),
            jax.ShapeDtypeStruct((rows, 128), F32),
            jax.ShapeDtypeStruct((rows, width), F32),
            jax.ShapeDtypeStruct((rows, width), F32),
            jax.ShapeDtypeStruct((rows, width), BF),
        ],
        compiler_params=PARAMS,
        cost_estimate=pl.CostEstimate(
            flops=2 * rows * q_cols * (width + 2 * keys.shape[0]), bytes_accessed=20 * rows * width, transcendentals=0
        ),
    )(queries, keys, values, query_ids, key_ids, w_o, tokens, d_gains)


def attend_backward_kernel(
    scale, grad_normed_mlp, cotangent, middle, branch, d_gains, w_o,
    queries, keys, values, query_ids, key_ids, log_total,
    grad_middle, grad_branch, grad_queries, grad_keys, grad_values, terms, grad_attended,
):
    rows, q_cols = queries.shape
    pad, k_cols = keys.shape[0] - rows, keys.shape[1]
    total = middle[...]
    from_mlp, mlp_terms = rms_backward(total, rms_scale(total), d_gains[2:3], grad_normed_mlp[...])
    grad_total = cotangent[...].astype(F32) + from_mlp
    grad_middle[...] = grad_total
    out = branch[...]
    grad_out, out_terms = rms_backward(out, rms_scale(out), d_gains[1:2], grad_total)
    low = grad_out.astype(BF)
    grad_branch[...] = low
    terms[...] = jnp.concatenate([out_terms, mlp_terms, jnp.zeros((6, out.shape[1]), F32)], axis=0)
    grad_attended[...] = by_transpose(low, w_o[...]).astype(BF)
    grad_keys[...] = jnp.zeros_like(grad_keys)
    grad_values[...] = jnp.zeros_like(grad_values)
    tile = rows // 2
    span = pad + tile
    for first in (0, tile):
        at = slice(first, first + tile)
        seen = slice(first, first + span)
        allowed = tile_mask(first, tile, first, span, query_ids, key_ids, pad)
        key_total = jnp.zeros((span, k_cols), F32)
        value_total = jnp.zeros((span, k_cols), F32)
        for head in range(q_cols // k_cols):
            columns = slice(head * k_cols, (head + 1) * k_cols)
            query = queries[at, columns]
            grad = grad_attended[at, columns]
            scores = by_transpose(query, keys[seen]) * scale
            probabilities = jnp.where(
                allowed, jnp.exp(scores - log_total[at, head : head + 1]), 0.0
            )
            grad_prob = by_transpose(grad, values[seen])
            inner = jnp.sum(probabilities * grad_prob, axis=-1, keepdims=True)
            grad_score = (probabilities * (grad_prob - inner)).astype(BF)
            grad_queries[at, columns] = matmul(grad_score, keys[seen]) * scale
            key_total = key_total + over_rows(grad_score, query)
            value_total = value_total + over_rows(probabilities.astype(BF), grad)
        grad_keys[seen] = grad_keys[seen] + key_total * scale
        grad_values[seen] = grad_values[seen] + value_total


def attend_backward(
    grad_normed_mlp, cotangent, middle, branch, d_gains, w_o,
    queries, keys, values, query_ids, key_ids, log_total, scale,
):
    rows, q_cols = queries.shape
    width = middle.shape[1]
    vmem = pl.BlockSpec(memory_space=pltpu.VMEM)
    return pl.pallas_call(
        functools.partial(attend_backward_kernel, scale),
        in_specs=[vmem] * 12,
        out_specs=[vmem] * 6,
        out_shape=[
            jax.ShapeDtypeStruct((rows, width), F32),
            jax.ShapeDtypeStruct((rows, width), BF),
            jax.ShapeDtypeStruct((rows, q_cols), F32),
            jax.ShapeDtypeStruct(keys.shape, F32),
            jax.ShapeDtypeStruct(keys.shape, F32),
            jax.ShapeDtypeStruct((8, width), F32),
        ],
        scratch_shapes=[pltpu.VMEM((rows, q_cols), BF)],
        compiler_params=PARAMS,
        cost_estimate=pl.CostEstimate(
            flops=2 * rows * q_cols * (width + 5 * keys.shape[0]), bytes_accessed=30 * rows * width, transcendentals=0
        ),
    )(
        grad_normed_mlp, cotangent, middle, branch, d_gains, w_o,
        queries, keys, values, query_ids, key_ids, log_total,
    )


def project_backward_kernel(
    shard_rows, core, grad_queries, grad_keys, grad_values, query_raw, key_raw, cosine, sine,
    h_gains, normed, normed_earlier, own, other, tokens, earlier, d_gains, terms, mixed_terms,
    grad_normed, returned, mine, sent,
):
    rows, width = tokens.shape
    pad, k_cols = earlier.shape[0], key_raw.shape[1]
    half = query_raw.shape[1] // 2
    cols = half + k_cols
    first_is_own = core[0] == 0
    cos, sin = cosine[pad:], sine[pad:]
    query_terms = jnp.zeros((1, k_cols), F32)
    parts = []
    for head in range(2 * half // k_cols):
        at = slice(head * k_cols, (head + 1) * k_cols)
        raw = query_raw[:, at]
        grad = turn_backward(grad_queries[:, at], cos, sin)
        grad, term = rms_backward(raw, rms_scale(raw), h_gains[4:5], grad)
        query_terms = query_terms + term
        parts.append(grad.astype(BF))
    raw = key_raw[...]
    grad = turn_backward(grad_keys[...], cosine[...], sine[...])
    grad, key_terms = rms_backward(raw, rms_scale(raw), h_gains[5:6], grad)
    grad_key, grad_value = grad.astype(BF), grad_values[...].astype(BF)
    returned[:, :k_cols] = grad_key[:pad]
    returned[:, k_cols:] = grad_value[:pad]
    kv_own = jnp.where(first_is_own, grad_key, grad_value)
    kv_other = jnp.where(first_is_own, grad_value, grad_key)
    both = len(parts) // 2
    first = jnp.concatenate(parts[:both], axis=1)
    second = jnp.concatenate(parts[both:], axis=1)
    q_own = jnp.where(first_is_own, first, second)
    q_other = jnp.where(first_is_own, second, first)
    grad_own = jnp.concatenate([q_own, kv_own[pad:]], axis=1)
    grad_other = jnp.concatenate([q_other, kv_other[pad:]], axis=1)
    total = by_transpose(grad_own, own[:, :cols]) + by_transpose(grad_other, other[:, :cols])
    grad_normed[...] = total
    values = tokens[...].astype(F32)
    in_terms = jnp.sum(total * values * rms_scale(values), axis=0, keepdims=True)
    total = by_transpose(kv_own[:pad], own[:, half:cols])
    total = total + by_transpose(kv_other[:pad], other[:, half:cols])
    values = earlier[...].astype(F32)
    in_terms = in_terms + jnp.sum(total * values * rms_scale(values), axis=0, keepdims=True)
    low, low_before = normed[...], normed_earlier[...]
    for out, query, key_value in ((mine, q_own, kv_own), (sent, q_other, kv_other)):
        out[:, :half] = over_rows(low, query).astype(BF)
        out[:, half:cols] = (
            over_rows(low, key_value[pad:]) + over_rows(low_before, key_value[:pad])
        ).astype(BF)
    heads = jnp.concatenate([query_terms, key_terms, jnp.zeros((6, k_cols), F32)], axis=0)
    placed = by_transpose(heads.astype(BF), gain_places(width, k_cols, shard_rows))
    block = jnp.concatenate(
        [in_terms, terms[0:2], mixed_terms[0:1], placed[0:2], jnp.zeros((122, width), F32)], axis=0
    ).T
    mine[:, cols:] = jnp.where(first_is_own, block, 0.0).astype(BF)
    sent[:, cols:] = jnp.where(first_is_own, 0.0, block).astype(BF)


def project_backward(
    core, grad_queries, grad_keys, grad_values, query_raw, key_raw, cosine, sine,
    h_gains, normed, normed_earlier, own, other, tokens, earlier, d_gains, terms, mixed_terms,
    shard_rows,
):
    rows, width = tokens.shape
    pad, k_cols = earlier.shape[0], key_raw.shape[1]
    vmem = pl.BlockSpec(memory_space=pltpu.VMEM)
    return pl.pallas_call(
        functools.partial(project_backward_kernel, shard_rows),
        in_specs=[pl.BlockSpec(memory_space=pltpu.SMEM)] + [vmem] * 17,
        out_specs=[vmem] * 4,
        out_shape=[
            jax.ShapeDtypeStruct((rows, width), F32),
            jax.ShapeDtypeStruct((pad, 2 * k_cols), BF),
            jax.ShapeDtypeStruct(own.shape, BF),
            jax.ShapeDtypeStruct(own.shape, BF),
        ],
        compiler_params=PARAMS,
        cost_estimate=pl.CostEstimate(
            flops=9 * rows * width * own.shape[1], bytes_accessed=30 * rows * width, transcendentals=0
        ),
    )(
        core, grad_queries, grad_keys, grad_values, query_raw, key_raw, cosine, sine,
        h_gains, normed, normed_earlier, own, other, tokens, earlier, d_gains, terms, mixed_terms,
    )


def grad_tokens_kernel(core, returned, grad_normed, own, other, tokens, d_gains, grad_middle, out):
    k_cols = returned.shape[1] // 2
    cols = own.shape[1] - 128
    half = cols - k_cols
    first_is_own = core[0] == 0
    grad_key, grad_value = returned[:, :k_cols], returned[:, k_cols:]
    kv_own = jnp.where(first_is_own, grad_key, grad_value)
    kv_other = jnp.where(first_is_own, grad_value, grad_key)
    total = grad_normed[...] + by_transpose(kv_own, own[:, half:cols])
    total = total + by_transpose(kv_other, other[:, half:cols])
    values = tokens[...].astype(F32)
    from_attn, _ = rms_backward(values, rms_scale(values), d_gains[0:1], total)
    out[...] = (grad_middle[...] + from_attn).astype(BF)


def grad_tokens(core, returned, grad_normed, own, other, tokens, d_gains, grad_middle):
    vmem = pl.BlockSpec(memory_space=pltpu.VMEM)
    return pl.pallas_call(
        grad_tokens_kernel,
        in_specs=[pl.BlockSpec(memory_space=pltpu.SMEM)] + [vmem] * 7,
        out_specs=vmem,
        out_shape=jax.ShapeDtypeStruct(tokens.shape, BF),
        compiler_params=PARAMS,
        cost_estimate=pl.CostEstimate(
            flops=2 * tokens.size * returned.shape[1], bytes_accessed=12 * tokens.size, transcendentals=0
        ),
    )(core, returned, grad_normed, own, other, tokens, d_gains, grad_middle)


def owner_rows_kernel(groups, piece, term, gate, up):
    sides, lanes = term.shape[0] // 2, term.shape[2] // 2
    for out, first in ((gate, 0), (up, lanes)):
        parts = []
        for side in range(2):
            rows = [
                term[side * sides + member, :, first : first + lanes].astype(F32)
                for member in range(sides)
            ]
            for group in range(groups):
                parts += [row[:, group * piece : (group + 1) * piece] for row in rows]
        out[...] = jnp.concatenate(parts, axis=1)


def owner_rows(term, groups, piece):
    vmem = pl.BlockSpec(memory_space=pltpu.VMEM)
    shape = jax.ShapeDtypeStruct((term.shape[1], term.shape[0] * groups * piece), F32)
    return pl.pallas_call(
        functools.partial(owner_rows_kernel, groups, piece),
        in_specs=[vmem],
        out_specs=[vmem, vmem],
        out_shape=[shape, shape],
        compiler_params=PARAMS,
        cost_estimate=pl.CostEstimate(
            flops=term.size, bytes_accessed=6 * term.size, transcendentals=0
        ),
    )(term)


def on_device(
    tokens,
    cotangent,
    doc_ids,
    w_query,
    w_key,
    w_value,
    w_out,
    w_gate,
    w_up,
    w_down,
    gain_attn_in,
    gain_attn_out,
    gain_mlp_in,
    gain_mlp_out,
    gain_query,
    gain_key,
):
    row_count = tokens.shape[1]
    width = tokens.shape[2]
    groups = lax.axis_size("g")
    members = lax.axis_size(PLANE)
    shard_rows = w_query.shape[0]
    head_rows = gain_query.shape[0]
    hidden_all = w_gate.shape[1]
    hidden_own = hidden_all // members
    hidden_pad = -(-hidden_own // 128) * 128
    piece = hidden_own // groups
    q_cols, k_cols = w_query.shape[1], w_key.shape[1]
    attn_scale = HEAD ** (-0.5)

    def gain_columns(d_gains, h_gains):
        columns = list(d_gains) + [
            jnp.pad(h, ((0, 0), (0, shard_rows - head_rows))) for h in h_gains
        ]
        block = jnp.stack(columns, axis=-1)
        return jnp.pad(block, ((0, 0), (0, 0), (0, 128 - len(columns))))

    seq_place = lax.axis_index(("g", "y", "c"))
    seq_size = lax.axis_size(("g", "y", "c"))
    before = lax.ppermute(tokens[0], ("g", "y", "c"), [(i, i + 1) for i in range(seq_size - 1)])

    def spread(weight):
        cut = weight.reshape(shard_rows, 2, groups, members // 2, piece)
        cut = cut.transpose(1, 3, 0, 2, 4).reshape(members, shard_rows, hidden_own)
        return jnp.pad(cut, ((0, 0), (0, 0), (0, hidden_pad - hidden_own)))

    sent = jnp.concatenate([spread(w_gate), spread(w_up)], axis=2)
    core = lax.axis_index("c")
    half_cols = q_cols // 2 + k_cols + 128
    gains = gain_columns(
        [g[None] for g in (gain_attn_in, gain_attn_out, gain_mlp_in, gain_mlp_out)],
        [gain_query[None], gain_key[None]],
    )
    halves = jnp.stack(
        [
            jnp.concatenate([w_query[:, : q_cols // 2], w_key, gains[0]], axis=1),
            jnp.concatenate([w_query[:, q_cols // 2 :], w_value, jnp.zeros_like(gains[0])], axis=1),
        ]
    )
    mine = lax.dynamic_index_in_dim(halves, core, 0, keepdims=False)
    other = lax.dynamic_index_in_dim(halves, 1 - core, 0, keepdims=False)
    mine = in_order(mine, swap(other, "c"), core).reshape(2 * shard_rows, half_cols)
    mine, before, sent = lax.optimization_barrier((mine, before, sent))
    sent = lax.all_to_all(sent, PLANE, split_axis=0, concat_axis=0, tiled=True)
    sent = sent.reshape(members * shard_rows, 2 * hidden_pad)
    mine, sent = lax.optimization_barrier((group_gather(mine), sent))
    mine = plane_weights(mine, *plane_start(mine)).reshape(width, half_cols)
    other = swap(mine, "c")

    down = lax.all_gather(jnp.concatenate([w_down, w_out]), "g", axis=0)
    w_o = down[:, w_down.shape[0] :]
    down = down[:, : w_down.shape[0]].reshape(-1, width)
    down = jnp.pad(down, ((0, hidden_pad - hidden_own), (0, 0)))

    both = lax.all_gather(sent, "g", axis=0)
    both = both.reshape(groups, 2, members // 2 * shard_rows, 2 * hidden_pad)
    gate_up = both.transpose(1, 0, 2, 3).reshape(width, 2 * hidden_pad)

    first_row = seq_place * row_count
    ids_all = doc_ids[0]
    ids_own = lax.dynamic_slice_in_dim(ids_all, first_row, row_count, 0)
    ids_prev = lax.dynamic_slice_in_dim(
        ids_all, jnp.maximum(first_row - row_count, 0), row_count, 0
    )
    ids_prev = jnp.where(seq_place > 0, ids_prev, -1)
    ids_pad = jnp.concatenate([ids_prev, ids_own])
    query_ids, key_ids = ids_own[:, None], ids_pad[None]
    cosine_table, sine_table = rope_tables(first_row - row_count, 2 * row_count, HEAD)
    places = jnp.full((1,), core, jnp.int32)
    layer_in, grad_out = tokens[0], cotangent[0]

    normed, normed_before, query_raw, key_raw, queries, keys, values, d_gains, h_gains = project(
        places, layer_in, before, mine, other, cosine_table, sine_table, shard_rows, q_cols, k_cols
    )
    w_o = plane_weights(*lax.optimization_barrier((w_o, *plane_start(w_o), keys))[:3])
    w_o = in_order(w_o, swap(w_o, "c"), core).transpose(1, 2, 3, 0, 4, 5).reshape(q_cols, width)
    attended, log_total, branch, middle, normed_mlp = attend(
        queries, keys, values, query_ids, key_ids, w_o, layer_in, d_gains, attn_scale
    )

    half = row_count // 2
    from_x, from_y, down = lax.optimization_barrier(
        (swap(normed_mlp, "x"), swap(normed_mlp, "y"), down)
    )
    normed_far = jnp.concatenate([swap(from_x[:half], "y"), swap(from_y[half:], "x")])
    normed_near = jnp.concatenate([from_x, from_y])
    normed_all = [with_core(part) for part in (normed_mlp, normed_near, normed_far)]
    far_result = mlp_forward(normed_all[2], gate_up, down, normed_all[2])
    far_sum = core_sum(far_result[3]).astype(BF)
    near_result = mlp_forward(normed_all[1], gate_up, down, far_sum)
    to_x, to_y = sum_near(*lax.optimization_barrier((near_result[3], *send_far(far_sum))))
    own_result = mlp_forward(normed_all[0], gate_up, down, to_x)
    mixed = sum_own(own_result[3], to_x, to_y)
    layer_out = middle + norm_gain(mixed, d_gains[3:4])

    _, pullback = jax.vjp(norm_gain, mixed, d_gains[3:4])
    grad_mixed, mixed_terms = pullback(grad_out.astype(F32))
    grad_mixed = grad_mixed.astype(BF)
    from_x, from_y = swap(grad_mixed, "x"), swap(grad_mixed, "y")
    grad_own = with_core(grad_mixed)
    own_grads = mlp_backward(grad_own, own_result[1], own_result[2], gate_up, down, down)
    from_x, from_y = lax.optimization_barrier((from_x, from_y, own_grads[1]))[:2]
    grad_near = with_core(jnp.concatenate([from_x, from_y]))
    near_terms = down_terms(
        [own_result[0], near_result[0]], [grad_own, grad_near], [], hidden_pad, F32
    )
    grad_far = lax.optimization_barrier(
        (swap(from_x[:half], "y"), swap(from_y[half:], "x"), near_terms)
    )
    grad_far = with_core(jnp.concatenate(grad_far[:2]))
    grad_down_terms = down_terms([far_result[0]], [grad_far], [near_terms], hidden_own, BF)
    grad_down = group_terms(grad_down_terms.reshape(groups, -1, width))
    far_grads = mlp_backward(
        grad_far, far_result[1], far_result[2], gate_up, down, grad_down_terms
    )
    far_sum = core_sum(far_grads[1]).astype(BF)
    near_grads = mlp_backward(grad_near, near_result[1], near_result[2], gate_up, down, far_sum)
    to_x, to_y = sum_near(*lax.optimization_barrier((near_grads[1], *send_far(far_sum))))
    gate_up_terms = gate_terms(
        normed_all, [g[0] for g in (own_grads, near_grads, far_grads)], groups, to_x
    )
    grad_normed_mlp = sum_own(own_grads[1], to_x, to_y)
    grad_normed_mlp = after(grad_normed_mlp, gate_up_terms)
    term = gate_up_terms.reshape(groups * members * shard_rows, 2 * hidden_pad)
    gate_up_share = lax.psum_scatter(term, "g", scatter_dimension=0, tiled=True)
    term = gate_up_share.reshape(members, shard_rows, 2 * hidden_pad)
    term = lax.all_to_all(term, PLANE, split_axis=0, concat_axis=0, tiled=True)

    grad_w_gate, grad_w_up = owner_rows(term, groups, piece)

    grad_middle, grad_branch, grad_queries, grad_keys, grad_values, terms = attend_backward(
        grad_normed_mlp, grad_out, middle, branch, d_gains, w_o,
        queries, keys, values, query_ids, key_ids, log_total, attn_scale,
    )
    out_terms = over_rows(attended, grad_branch).astype(BF)
    out_terms = out_terms.reshape(2, groups, 2, 2, w_out.shape[0], width)
    out_terms = plane_terms(fold(out_terms, "c", 3))
    own_weights, other_weights = mine, other
    grad_normed, returned, mine, sent = project_backward(
        places, after(grad_queries, grad_down), grad_keys, grad_values, query_raw, key_raw,
        cosine_table, sine_table, h_gains, normed, normed_before, own_weights, other_weights,
        layer_in, before, d_gains, terms, mixed_terms, shard_rows,
    )
    returned = lax.ppermute(returned, ("g", "y", "c"), [(i + 1, i) for i in range(seq_size - 1)])
    grad_in = grad_tokens(
        places, returned, grad_normed, own_weights, other_weights, layer_in, d_gains, grad_middle
    )
    mine = (mine.astype(F32) + swap(sent, "c").astype(F32)).astype(BF)
    qkv_terms = plane_terms(mine.reshape(2, groups, 2, 2 * shard_rows, half_cols))
    qkv_terms = qkv_terms.reshape(groups, -1, width)
    share = jnp.concatenate([out_terms, qkv_terms], axis=1)
    share = group_terms(after(share, gate_up_share))
    grad_w_out = share[: w_out.shape[0]]
    share = share[w_out.shape[0] :].astype(BF).reshape(2, shard_rows, half_cols)
    mine = lax.dynamic_index_in_dim(share, core, 0, keepdims=False)
    other = lax.dynamic_index_in_dim(share, 1 - core, 0, keepdims=False)
    first, second = in_order(mine, swap(other, "c"), core).astype(F32)
    half = q_cols // 2
    d_terms = first[:, half + k_cols :]
    return (
        layer_out.astype(BF)[None],
        grad_in[None],
        jnp.concatenate([first[:, :half], second[:, :half]], axis=1),
        first[:, half : half + k_cols],
        second[:, half : half + k_cols],
        grad_w_out,
        grad_w_gate,
        grad_w_up,
        grad_down,
        d_terms[:, 0],
        d_terms[:, 1],
        d_terms[:, 2],
        d_terms[:, 3],
        d_terms[:head_rows, 4],
        d_terms[:head_rows, 5],
    )


def solution(mesh):
    batch, seq = mesh.devices.shape
    fine = Mesh(mesh.devices.reshape(batch, seq // 4, 2, 2), ALL)
    rows = ("g", "y", "c")
    return jax.shard_map(
        on_device,
        mesh=fine,
        in_specs=(P("x", rows, None),) * 2
        + (P("x", None),)
        + (P(ALL, None),) * 7
        + (P(ALL),) * 6,
        out_specs=(P("x", rows, None),) * 2 + (P(ALL, None),) * 7 + (P(ALL),) * 6,
        check_vma=False,
    )
```

```python
import functools

import jax
import jax.numpy as jnp
from jax import lax
from jax.experimental import pallas as pl
from jax.experimental.pallas import tpu as pltpu
from jax.sharding import Mesh
from jax.sharding import PartitionSpec as P

HEAD = 256
WINDOW = 512
EPSILON = 1e-06
ROPE_BASE = 10000.0
ALL = ("x", "g", "y", "c")
PLANE = ("x", "y", "c")
BF = jnp.bfloat16
F32 = jnp.float32


def norm_gain(values, gain_vec):
    return (
        values * lax.rsqrt(jnp.mean(values * values, axis=-1, keepdims=True) + EPSILON) * gain_vec
    )


def rope_tables(first_row, row_count, head_size):
    places = (first_row + jnp.arange(row_count, dtype=jnp.int32)).astype(F32)
    frequency = ROPE_BASE ** (-(jnp.arange(head_size // 2, dtype=F32) * 2.0) / head_size)
    angles = places[:, None] * frequency[None, :]
    return (jnp.cos(angles), jnp.sin(angles))


def matmul(left_side, right_side):
    return jnp.dot(left_side, right_side, preferred_element_type=F32)


def over_rows(left_side, right_side):
    return lax.dot_general(
        left_side, right_side, (((0,), (0,)), ((), ())), preferred_element_type=F32
    )


def by_transpose(left_side, right_side):
    return lax.dot_general(
        left_side, right_side, (((1,), (1,)), ((), ())), preferred_element_type=F32
    )


def swap(array, axis):
    return lax.ppermute(array, axis, [(0, 1), (1, 0)])


GELU_A = 0.7978845608028654
GELU_B = 0.044715
TILE = 512
PARAMS = pltpu.CompilerParams(vmem_limit_bytes=58 << 20)


def whole_block(shape):
    return pl.BlockSpec(shape, lambda i: (0,) * len(shape), pipeline_mode=pl.Buffered(1))


def row_block(rows, columns):
    return pl.BlockSpec((rows, columns), lambda i: (i, 0))


def store_half(value, mine, other):
    step, half = pl.program_id(0), pl.num_programs(0) // 2

    @pl.when(step < half)
    def _():
        mine[...] = value

    @pl.when(step >= half)
    def _():
        other[...] = value


def half_blocks(rows, columns):
    half = rows // TILE // 2
    return [
        pl.BlockSpec((TILE, columns), lambda i: (jnp.minimum(i, half - 1), 0)),
        pl.BlockSpec((TILE, columns), lambda i: (jnp.maximum(i - half, 0), 0)),
    ]


def mlp_forward_kernel(normed, gate_up, down, _, hidden, gelu, slope, mixed):
    own = down.shape[0]
    raw = matmul(normed[...], gate_up[...])
    gate_raw, up_raw = raw[:, :own], raw[:, own:]
    square = gate_raw * gate_raw
    bend = jnp.tanh(GELU_A * (gate_raw + GELU_B * square * gate_raw))
    half = 0.5 + 0.5 * bend
    active = gate_raw * half
    turn = 0.5 * gate_raw * (1.0 - bend * bend) * (GELU_A * (1.0 + 3.0 * GELU_B * square))
    low = (active * up_raw).astype(BF)
    hidden[...] = low
    gelu[...] = active.astype(BF)
    slope[...] = ((half + turn) * up_raw).astype(BF)
    mixed[...] = matmul(low, down[...]).astype(BF)


def mlp_forward(normed, gate_up, down, earlier):
    rows, width = normed.shape
    own = down.shape[0]
    flat = jax.ShapeDtypeStruct((rows, own), BF)
    return pl.pallas_call(
        mlp_forward_kernel,
        grid=(rows // TILE,),
        in_specs=[
            row_block(TILE, width),
            whole_block(gate_up.shape),
            whole_block(down.shape),
            pl.BlockSpec(memory_space=pl.ANY),
        ],
        out_specs=[row_block(TILE, own)] * 3 + [row_block(TILE, width)],
        out_shape=[flat, flat, flat, jax.ShapeDtypeStruct((rows, width), BF)],
        compiler_params=PARAMS,
        cost_estimate=pl.CostEstimate(
            flops=6 * rows * width * own, bytes_accessed=rows * (4 * width + 6 * own), transcendentals=0
        ),
    )(normed, gate_up, down, earlier)


def mlp_backward_kernel(grad_mixed, gelu, slope, gate_up, down, _, grad_raw, mine, other):
    own = down.shape[0]
    grad_hidden = by_transpose(grad_mixed[...], down[...])
    grad_gate = (grad_hidden * slope[...].astype(F32)).astype(BF)
    grad_up = (grad_hidden * gelu[...].astype(F32)).astype(BF)
    grad_raw[:, :own] = grad_gate
    grad_raw[:, own:] = grad_up
    total = by_transpose(grad_gate, gate_up[:, :own]) + by_transpose(grad_up, gate_up[:, own:])
    store_half(total.astype(BF), mine, other)


def mlp_backward(grad_mixed, gelu, slope, gate_up, down, earlier):
    rows, width = grad_mixed.shape
    own = down.shape[0]
    return pl.pallas_call(
        mlp_backward_kernel,
        grid=(rows // TILE,),
        in_specs=[
            row_block(TILE, width),
            row_block(TILE, own),
            row_block(TILE, own),
            whole_block(gate_up.shape),
            whole_block(down.shape),
            pl.BlockSpec(memory_space=pl.ANY),
        ],
        out_specs=[row_block(TILE, 2 * own)] + half_blocks(rows, width),
        out_shape=[
            jax.ShapeDtypeStruct((rows, 2 * own), BF),
            jax.ShapeDtypeStruct((rows // 2, width), BF),
            jax.ShapeDtypeStruct((rows // 2, width), BF),
        ],
        compiler_params=PARAMS,
        cost_estimate=pl.CostEstimate(
            flops=6 * rows * width * own, bytes_accessed=rows * (4 * width + 8 * own), transcendentals=0
        ),
    )(grad_mixed, gelu, slope, gate_up, down, earlier)


def down_terms_kernel(count, *refs):
    *ins, out = refs
    total = None
    for left, right in zip(ins[:count], ins[count : 2 * count]):
        part = over_rows(left[...], right[...])
        total = part if total is None else total + part
    for base in ins[2 * count :]:
        total = total + base[...]
    out[...] = total.astype(out.dtype)


def down_terms(hidden, grad_mixed, base, keep, kind):
    own, width = hidden[0].shape[1], grad_mixed[0].shape[1]
    rows = sum(part.shape[0] for part in hidden)
    return pl.pallas_call(
        functools.partial(down_terms_kernel, len(hidden)),
        grid=(own // 128,),
        in_specs=[pl.BlockSpec((part.shape[0], 128), lambda i: (0, i)) for part in hidden]
        + [whole_block(part.shape) for part in grad_mixed]
        + [row_block(128, width) for _ in base],
        out_specs=row_block(128, width),
        out_shape=jax.ShapeDtypeStruct((keep, width), kind),
        compiler_params=PARAMS,
        cost_estimate=pl.CostEstimate(
            flops=2 * rows * width * own, bytes_accessed=2 * rows * (width + own), transcendentals=0
        ),
    )(*hidden, *grad_mixed, *base)


def gate_terms_kernel(*refs):
    *ins, _, out = refs
    half = len(ins) // 2
    total = over_rows(ins[0][...], ins[half][...])
    for left, right in zip(ins[1:half], ins[half + 1 :]):
        total = total + over_rows(left[...], right[...])
    total = total.astype(BF)
    groups, sides, rows, _ = out.shape
    for side in range(sides):
        for group in range(groups):
            first = (side * groups + group) * rows
            out[group, side] = total[first : first + rows]


def gate_terms(normed, grad_raw, groups, earlier):
    width, both = normed[0].shape[1], grad_raw[0].shape[1]
    rows = sum(part.shape[0] for part in normed)
    shape = (groups, 2, width // (2 * groups))
    return pl.pallas_call(
        gate_terms_kernel,
        grid=(both // 256,),
        in_specs=[whole_block(part.shape) for part in normed]
        + [pl.BlockSpec((part.shape[0], 256), lambda i: (0, i)) for part in grad_raw]
        + [pl.BlockSpec(memory_space=pl.ANY)],
        out_specs=pl.BlockSpec(shape + (256,), lambda i: (0, 0, 0, i)),
        out_shape=jax.ShapeDtypeStruct(shape + (both,), BF),
        compiler_params=PARAMS,
        cost_estimate=pl.CostEstimate(
            flops=2 * rows * width * both, bytes_accessed=2 * rows * (width + both), transcendentals=0
        ),
    )(*normed, *grad_raw, earlier)


def after(value, *earlier):
    return lax.optimization_barrier((value, *earlier))[0]


def with_core(part):
    return jnp.concatenate([part, swap(part, "c")])


def two_cores(part):
    half = part.shape[0] // 2
    return part[:half], part[half:]


def core_sum(parts):
    return parts[0].astype(F32) + swap(parts[1], "c").astype(F32)


def send_far(far):
    half = far.shape[0] // 2
    return swap(far[:half], "y"), swap(far[half:], "x")


def sum_near(near, top, low):
    near = core_sum(near)
    rows = near.shape[0] // 2
    half = rows // 2
    to_x = jnp.concatenate([near[:half] + top, near[half:rows]]).astype(BF)
    to_y = jnp.concatenate([near[rows : rows + half], near[rows + half :] + low]).astype(BF)
    return to_x, to_y


def sum_own(own, to_x, to_y):
    return core_sum(own) + swap(to_x, "x").astype(F32) + swap(to_y, "y").astype(F32)


def in_order(own, other, place):
    both = jnp.concatenate([own[None], other[None], own[None]])
    return lax.dynamic_slice_in_dim(both, place, 2, 0)


def group_gather(own):
    size = lax.axis_size("g")
    parts = [own] + [
        lax.ppermute(own, "g", [((i + k) % size, i) for i in range(size)]) for k in range(1, size)
    ]
    both = jnp.stack(parts + parts[:-1])
    place = lax.axis_index("g")
    return lax.dynamic_slice_in_dim(both, lax.rem(size - place, size), size, 0)


def plane_start(blocks):
    half = blocks.shape[0] // 2
    return swap(blocks[:half], "x"), swap(blocks[half:], "y")


def plane_weights(blocks, from_x, from_y):
    x, y = lax.axis_index("x"), lax.axis_index("y")
    half = blocks.shape[0] // 2
    first = in_order(blocks[:half], from_x, x)
    second = in_order(blocks[half:], from_y, y)
    first = in_order(first, swap(first, "y"), y)
    second = in_order(second, swap(second, "x"), x)
    first = first.transpose(1, 2, 0, 3, 4)
    second = second.transpose(0, 2, 1, 3, 4)
    return jnp.concatenate([first, second], axis=1)


def group_terms(term):
    size = lax.axis_size("g")
    place = lax.axis_index("g")
    total = lax.dynamic_index_in_dim(term, place, 0, keepdims=False).astype(F32)
    for k in range(1, size):
        chunk = lax.dynamic_index_in_dim(term, lax.rem(place + k, size), 0, keepdims=False)
        pairs = [(i, (i + k) % size) for i in range(size)]
        total = total + lax.ppermute(chunk, "g", pairs).astype(F32)
    return total


def fold(term, axis, dim):
    place = lax.axis_index(axis)
    mine = lax.dynamic_index_in_dim(term, place, dim, keepdims=False)
    other = lax.dynamic_index_in_dim(term, 1 - place, dim, keepdims=False)
    return (mine.astype(F32) + swap(other.astype(BF), axis).astype(F32)).astype(BF)


def plane_terms(term):
    half = term.shape[1] // 2
    first = fold(fold(term[:, :half], "x", 0), "y", 1)
    second = fold(fold(term[:, half:], "y", 2), "x", 0)
    return jnp.concatenate([first, second])


def rms_scale(values):
    return lax.rsqrt(jnp.mean(values * values, axis=-1, keepdims=True) + EPSILON)


def rms_backward(values, scale, gain, grad):
    weighted = grad * gain
    inner = jnp.mean(weighted * values, axis=-1, keepdims=True)
    terms = jnp.sum(grad * values * scale, axis=0, keepdims=True)
    return weighted * scale - values * (scale * scale * scale * inner), terms


def turn_forward(values, cosine, sine):
    half = cosine.shape[1]
    low, high = values[:, :half], values[:, half:]
    return jnp.concatenate([low * cosine - high * sine, high * cosine + low * sine], axis=1)


def turn_backward(grad, cosine, sine):
    half = cosine.shape[1]
    low, high = grad[:, :half], grad[:, half:]
    return jnp.concatenate([low * cosine + high * sine, high * cosine - low * sine], axis=1)


def gain_places(width, columns, shard_rows):
    heads = columns // (width // shard_rows)
    row = lax.broadcasted_iota(jnp.int32, (width, columns), 0)
    column = lax.broadcasted_iota(jnp.int32, (width, columns), 1)
    place = (column // heads) * shard_rows + lax.rem(column, heads)
    return jnp.where(row == place, 1.0, 0.0).astype(BF)


def project_kernel(
    shard_rows, core, tokens, earlier, own, other, cosine, sine,
    normed, normed_earlier, query_raw, key_raw, queries, keys, values, d_gains, h_gains,
):
    rows, width = tokens.shape
    pad, k_cols = earlier.shape[0], key_raw.shape[1]
    half = query_raw.shape[1] // 2
    first_is_own = core[0] == 0
    block = jnp.where(
        first_is_own, own[:, half + k_cols :].astype(F32), other[:, half + k_cols :].astype(F32)
    )
    flat = block.T[:8]
    d_gains[...] = flat
    chosen = matmul(flat.astype(BF), gain_places(width, k_cols, shard_rows))
    h_gains[...] = chosen
    before = earlier[...].astype(F32)
    low_before = (before * rms_scale(before) * flat[0:1]).astype(BF)
    normed_earlier[...] = low_before
    inputs = tokens[...].astype(F32)
    low = (inputs * rms_scale(inputs) * flat[0:1]).astype(BF)
    normed[...] = low
    raw_own = matmul(low, own[:, : half + k_cols])
    raw_other = matmul(low, other[:, : half + k_cols])
    before_own = matmul(low_before, own[:, half : half + k_cols])
    before_other = matmul(low_before, other[:, half : half + k_cols])
    first = jnp.where(first_is_own, raw_own, raw_other)
    second = jnp.where(first_is_own, raw_other, raw_own)
    raw_query = jnp.concatenate([first[:, :half], second[:, :half]], axis=1)
    query_raw[...] = raw_query
    values[:pad] = jnp.where(first_is_own, before_other, before_own).astype(BF)
    values[pad:] = second[:, half:].astype(BF)
    raw_before = jnp.where(first_is_own, before_own, before_other)
    for raw, at in ((raw_before, slice(0, pad)), (first[:, half:], slice(pad, pad + rows))):
        key_raw[at] = raw
        part = raw * rms_scale(raw) * chosen[5:6]
        keys[at] = turn_forward(part, cosine[at], sine[at]).astype(BF)
    cos, sin = cosine[pad:], sine[pad:]
    for head in range(2 * half // k_cols):
        at = slice(head * k_cols, (head + 1) * k_cols)
        part = raw_query[:, at]
        part = part * rms_scale(part) * chosen[4:5]
        queries[:, at] = turn_forward(part, cos, sin).astype(BF)


def project(core, tokens, earlier, own, other, cosine, sine, shard_rows, q_cols, k_cols):
    rows, width = tokens.shape
    seen = rows + earlier.shape[0]
    vmem = pl.BlockSpec(memory_space=pltpu.VMEM)
    return pl.pallas_call(
        functools.partial(project_kernel, shard_rows),
        in_specs=[pl.BlockSpec(memory_space=pltpu.SMEM)] + [vmem] * 6,
        out_specs=[vmem] * 9,
        out_shape=[
            jax.ShapeDtypeStruct((rows, width), BF),
            jax.ShapeDtypeStruct(earlier.shape, BF),
            jax.ShapeDtypeStruct((rows, q_cols), F32),
            jax.ShapeDtypeStruct((seen, k_cols), F32),
            jax.ShapeDtypeStruct((rows, q_cols), BF),
            jax.ShapeDtypeStruct((seen, k_cols), BF),
            jax.ShapeDtypeStruct((seen, k_cols), BF),
            jax.ShapeDtypeStruct((8, width), F32),
            jax.ShapeDtypeStruct((8, k_cols), F32),
        ],
        compiler_params=PARAMS,
        cost_estimate=pl.CostEstimate(
            flops=2 * rows * width * (q_cols + 4 * k_cols), bytes_accessed=16 * rows * width, transcendentals=0
        ),
    )(core, tokens, earlier, own, other, cosine, sine)


def tile_mask(first, rows, first_key, keys, query_ids, key_ids, pad):
    query_place = pad + first + lax.broadcasted_iota(jnp.int32, (rows, keys), 0)
    key_place = first_key + lax.broadcasted_iota(jnp.int32, (rows, keys), 1)
    distance = query_place - key_place
    same_doc = query_ids[first : first + rows, :] == key_ids[:, first_key : first_key + keys]
    return (distance >= 0) & (distance < WINDOW) & same_doc


def attend_kernel(
    scale, queries, keys, values, query_ids, key_ids, w_o, tokens, d_gains,
    attended, log_total, branch, middle, normed_mlp,
):
    rows, q_cols = queries.shape
    pad, k_cols = keys.shape[0] - rows, keys.shape[1]
    tile = rows // 2
    span = pad + tile
    lane = lax.broadcasted_iota(jnp.int32, (tile, 128), 1)
    for first in (0, tile):
        at = slice(first, first + tile)
        seen = slice(first, first + span)
        allowed = tile_mask(first, tile, first, span, query_ids, key_ids, pad)
        logs = jnp.zeros((tile, 128), F32)
        for head in range(q_cols // k_cols):
            columns = slice(head * k_cols, (head + 1) * k_cols)
            scores = by_transpose(queries[at, columns], keys[seen]) * scale
            scores = jnp.where(allowed, scores, -1e30)
            row_max = jnp.max(scores, axis=-1, keepdims=True)
            weights = jnp.exp(scores - row_max)
            row_total = jnp.sum(weights, axis=-1, keepdims=True)
            probabilities = (weights * (1.0 / row_total)).astype(BF)
            attended[at, columns] = matmul(probabilities, values[seen]).astype(BF)
            logs = jnp.where(lane == head, row_max + jnp.log(row_total), logs)
        log_total[at] = logs
    out = matmul(attended[...], w_o[...])
    branch[...] = out
    total = tokens[...].astype(F32) + out * rms_scale(out) * d_gains[1:2]
    middle[...] = total
    normed_mlp[...] = (total * rms_scale(total) * d_gains[2:3]).astype(BF)


def attend(queries, keys, values, query_ids, key_ids, w_o, tokens, d_gains, scale):
    rows, q_cols = queries.shape
    width = tokens.shape[1]
    vmem = pl.BlockSpec(memory_space=pltpu.VMEM)
    return pl.pallas_call(
        functools.partial(attend_kernel, scale),
        in_specs=[vmem] * 8,
        out_specs=[vmem] * 5,
        out_shape=[
            jax.ShapeDtypeStruct((rows, q_cols), BF),
            jax.ShapeDtypeStruct((rows, 128), F32),
            jax.ShapeDtypeStruct((rows, width), F32),
            jax.ShapeDtypeStruct((rows, width), F32),
            jax.ShapeDtypeStruct((rows, width), BF),
        ],
        compiler_params=PARAMS,
        cost_estimate=pl.CostEstimate(
            flops=2 * rows * q_cols * (width + 2 * keys.shape[0]), bytes_accessed=20 * rows * width, transcendentals=0
        ),
    )(queries, keys, values, query_ids, key_ids, w_o, tokens, d_gains)


def attend_backward_kernel(
    scale, grad_normed_mlp, cotangent, middle, branch, d_gains, w_o,
    queries, keys, values, query_ids, key_ids, log_total,
    grad_middle, grad_branch, grad_queries, grad_keys, grad_values, terms, grad_attended,
):
    rows, q_cols = queries.shape
    pad, k_cols = keys.shape[0] - rows, keys.shape[1]
    total = middle[...]
    from_mlp, mlp_terms = rms_backward(total, rms_scale(total), d_gains[2:3], grad_normed_mlp[...])
    grad_total = cotangent[...].astype(F32) + from_mlp
    grad_middle[...] = grad_total
    out = branch[...]
    grad_out, out_terms = rms_backward(out, rms_scale(out), d_gains[1:2], grad_total)
    low = grad_out.astype(BF)
    grad_branch[...] = low
    terms[...] = jnp.concatenate([out_terms, mlp_terms, jnp.zeros((6, out.shape[1]), F32)], axis=0)
    grad_attended[...] = by_transpose(low, w_o[...]).astype(BF)
    grad_keys[...] = jnp.zeros_like(grad_keys)
    grad_values[...] = jnp.zeros_like(grad_values)
    tile = rows // 2
    span = pad + tile
    for first in (0, tile):
        at = slice(first, first + tile)
        seen = slice(first, first + span)
        allowed = tile_mask(first, tile, first, span, query_ids, key_ids, pad)
        key_total = jnp.zeros((span, k_cols), F32)
        value_total = jnp.zeros((span, k_cols), F32)
        for head in range(q_cols // k_cols):
            columns = slice(head * k_cols, (head + 1) * k_cols)
            query = queries[at, columns]
            grad = grad_attended[at, columns]
            scores = by_transpose(query, keys[seen]) * scale
            probabilities = jnp.where(
                allowed, jnp.exp(scores - log_total[at, head : head + 1]), 0.0
            )
            grad_prob = by_transpose(grad, values[seen])
            inner = jnp.sum(probabilities * grad_prob, axis=-1, keepdims=True)
            grad_score = (probabilities * (grad_prob - inner)).astype(BF)
            grad_queries[at, columns] = matmul(grad_score, keys[seen]) * scale
            key_total = key_total + over_rows(grad_score, query)
            value_total = value_total + over_rows(probabilities.astype(BF), grad)
        grad_keys[seen] = grad_keys[seen] + key_total * scale
        grad_values[seen] = grad_values[seen] + value_total


def attend_backward(
    grad_normed_mlp, cotangent, middle, branch, d_gains, w_o,
    queries, keys, values, query_ids, key_ids, log_total, scale,
):
    rows, q_cols = queries.shape
    width = middle.shape[1]
    vmem = pl.BlockSpec(memory_space=pltpu.VMEM)
    return pl.pallas_call(
        functools.partial(attend_backward_kernel, scale),
        in_specs=[vmem] * 12,
        out_specs=[vmem] * 6,
        out_shape=[
            jax.ShapeDtypeStruct((rows, width), F32),
            jax.ShapeDtypeStruct((rows, width), BF),
            jax.ShapeDtypeStruct((rows, q_cols), F32),
            jax.ShapeDtypeStruct(keys.shape, F32),
            jax.ShapeDtypeStruct(keys.shape, F32),
            jax.ShapeDtypeStruct((8, width), F32),
        ],
        scratch_shapes=[pltpu.VMEM((rows, q_cols), BF)],
        compiler_params=PARAMS,
        cost_estimate=pl.CostEstimate(
            flops=2 * rows * q_cols * (width + 5 * keys.shape[0]), bytes_accessed=30 * rows * width, transcendentals=0
        ),
    )(
        grad_normed_mlp, cotangent, middle, branch, d_gains, w_o,
        queries, keys, values, query_ids, key_ids, log_total,
    )


def project_backward_kernel(
    shard_rows, core, grad_queries, grad_keys, grad_values, query_raw, key_raw, cosine, sine,
    h_gains, normed, normed_earlier, own, other, tokens, earlier, d_gains, terms, mixed_terms,
    grad_normed, returned, mine, sent,
):
    rows, width = tokens.shape
    pad, k_cols = earlier.shape[0], key_raw.shape[1]
    half = query_raw.shape[1] // 2
    cols = half + k_cols
    first_is_own = core[0] == 0
    cos, sin = cosine[pad:], sine[pad:]
    query_terms = jnp.zeros((1, k_cols), F32)
    parts = []
    for head in range(2 * half // k_cols):
        at = slice(head * k_cols, (head + 1) * k_cols)
        raw = query_raw[:, at]
        grad = turn_backward(grad_queries[:, at], cos, sin)
        grad, term = rms_backward(raw, rms_scale(raw), h_gains[4:5], grad)
        query_terms = query_terms + term
        parts.append(grad.astype(BF))
    raw = key_raw[...]
    grad = turn_backward(grad_keys[...], cosine[...], sine[...])
    grad, key_terms = rms_backward(raw, rms_scale(raw), h_gains[5:6], grad)
    grad_key, grad_value = grad.astype(BF), grad_values[...].astype(BF)
    returned[:, :k_cols] = grad_key[:pad]
    returned[:, k_cols:] = grad_value[:pad]
    kv_own = jnp.where(first_is_own, grad_key, grad_value)
    kv_other = jnp.where(first_is_own, grad_value, grad_key)
    both = len(parts) // 2
    first = jnp.concatenate(parts[:both], axis=1)
    second = jnp.concatenate(parts[both:], axis=1)
    q_own = jnp.where(first_is_own, first, second)
    q_other = jnp.where(first_is_own, second, first)
    grad_own = jnp.concatenate([q_own, kv_own[pad:]], axis=1)
    grad_other = jnp.concatenate([q_other, kv_other[pad:]], axis=1)
    total = by_transpose(grad_own, own[:, :cols]) + by_transpose(grad_other, other[:, :cols])
    grad_normed[...] = total
    values = tokens[...].astype(F32)
    in_terms = jnp.sum(total * values * rms_scale(values), axis=0, keepdims=True)
    total = by_transpose(kv_own[:pad], own[:, half:cols])
    total = total + by_transpose(kv_other[:pad], other[:, half:cols])
    values = earlier[...].astype(F32)
    in_terms = in_terms + jnp.sum(total * values * rms_scale(values), axis=0, keepdims=True)
    low, low_before = normed[...], normed_earlier[...]
    for out, query, key_value in ((mine, q_own, kv_own), (sent, q_other, kv_other)):
        out[:, :half] = over_rows(low, query).astype(BF)
        out[:, half:cols] = (
            over_rows(low, key_value[pad:]) + over_rows(low_before, key_value[:pad])
        ).astype(BF)
    heads = jnp.concatenate([query_terms, key_terms, jnp.zeros((6, k_cols), F32)], axis=0)
    placed = by_transpose(heads.astype(BF), gain_places(width, k_cols, shard_rows))
    block = jnp.concatenate(
        [in_terms, terms[0:2], mixed_terms[0:1], placed[0:2], jnp.zeros((122, width), F32)], axis=0
    ).T
    mine[:, cols:] = jnp.where(first_is_own, block, 0.0).astype(BF)
    sent[:, cols:] = jnp.where(first_is_own, 0.0, block).astype(BF)


def project_backward(
    core, grad_queries, grad_keys, grad_values, query_raw, key_raw, cosine, sine,
    h_gains, normed, normed_earlier, own, other, tokens, earlier, d_gains, terms, mixed_terms,
    shard_rows,
):
    rows, width = tokens.shape
    pad, k_cols = earlier.shape[0], key_raw.shape[1]
    vmem = pl.BlockSpec(memory_space=pltpu.VMEM)
    return pl.pallas_call(
        functools.partial(project_backward_kernel, shard_rows),
        in_specs=[pl.BlockSpec(memory_space=pltpu.SMEM)] + [vmem] * 17,
        out_specs=[vmem] * 4,
        out_shape=[
            jax.ShapeDtypeStruct((rows, width), F32),
            jax.ShapeDtypeStruct((pad, 2 * k_cols), BF),
            jax.ShapeDtypeStruct(own.shape, BF),
            jax.ShapeDtypeStruct(own.shape, BF),
        ],
        compiler_params=PARAMS,
        cost_estimate=pl.CostEstimate(
            flops=9 * rows * width * own.shape[1], bytes_accessed=30 * rows * width, transcendentals=0
        ),
    )(
        core, grad_queries, grad_keys, grad_values, query_raw, key_raw, cosine, sine,
        h_gains, normed, normed_earlier, own, other, tokens, earlier, d_gains, terms, mixed_terms,
    )


def grad_tokens_kernel(core, returned, grad_normed, own, other, tokens, d_gains, grad_middle, out):
    k_cols = returned.shape[1] // 2
    cols = own.shape[1] - 128
    half = cols - k_cols
    first_is_own = core[0] == 0
    grad_key, grad_value = returned[:, :k_cols], returned[:, k_cols:]
    kv_own = jnp.where(first_is_own, grad_key, grad_value)
    kv_other = jnp.where(first_is_own, grad_value, grad_key)
    total = grad_normed[...] + by_transpose(kv_own, own[:, half:cols])
    total = total + by_transpose(kv_other, other[:, half:cols])
    values = tokens[...].astype(F32)
    from_attn, _ = rms_backward(values, rms_scale(values), d_gains[0:1], total)
    out[...] = (grad_middle[...] + from_attn).astype(BF)


def grad_tokens(core, returned, grad_normed, own, other, tokens, d_gains, grad_middle):
    vmem = pl.BlockSpec(memory_space=pltpu.VMEM)
    return pl.pallas_call(
        grad_tokens_kernel,
        in_specs=[pl.BlockSpec(memory_space=pltpu.SMEM)] + [vmem] * 7,
        out_specs=vmem,
        out_shape=jax.ShapeDtypeStruct(tokens.shape, BF),
        compiler_params=PARAMS,
        cost_estimate=pl.CostEstimate(
            flops=2 * tokens.size * returned.shape[1], bytes_accessed=12 * tokens.size, transcendentals=0
        ),
    )(core, returned, grad_normed, own, other, tokens, d_gains, grad_middle)


def owner_rows_kernel(groups, piece, term, gate, up):
    sides, lanes = term.shape[0] // 2, term.shape[2] // 2
    for out, first in ((gate, 0), (up, lanes)):
        parts = []
        for side in range(2):
            rows = [
                term[side * sides + member, :, first : first + lanes].astype(F32)
                for member in range(sides)
            ]
            for group in range(groups):
                parts += [row[:, group * piece : (group + 1) * piece] for row in rows]
        out[...] = jnp.concatenate(parts, axis=1)


def owner_rows(term, groups, piece):
    vmem = pl.BlockSpec(memory_space=pltpu.VMEM)
    shape = jax.ShapeDtypeStruct((term.shape[1], term.shape[0] * groups * piece), F32)
    return pl.pallas_call(
        functools.partial(owner_rows_kernel, groups, piece),
        in_specs=[vmem],
        out_specs=[vmem, vmem],
        out_shape=[shape, shape],
        compiler_params=PARAMS,
        cost_estimate=pl.CostEstimate(
            flops=term.size, bytes_accessed=6 * term.size, transcendentals=0
        ),
    )(term)


def on_device(
    tokens,
    cotangent,
    doc_ids,
    w_query,
    w_key,
    w_value,
    w_out,
    w_gate,
    w_up,
    w_down,
    gain_attn_in,
    gain_attn_out,
    gain_mlp_in,
    gain_mlp_out,
    gain_query,
    gain_key,
):
    row_count = tokens.shape[1]
    width = tokens.shape[2]
    groups = lax.axis_size("g")
    members = lax.axis_size(PLANE)
    shard_rows = w_query.shape[0]
    head_rows = gain_query.shape[0]
    hidden_all = w_gate.shape[1]
    hidden_own = hidden_all // members
    hidden_pad = -(-hidden_own // 128) * 128
    piece = hidden_own // groups
    q_cols, k_cols = w_query.shape[1], w_key.shape[1]
    attn_scale = HEAD ** (-0.5)

    def gain_columns(d_gains, h_gains):
        columns = list(d_gains) + [
            jnp.pad(h, ((0, 0), (0, shard_rows - head_rows))) for h in h_gains
        ]
        block = jnp.stack(columns, axis=-1)
        return jnp.pad(block, ((0, 0), (0, 0), (0, 128 - len(columns))))

    seq_place = lax.axis_index(("g", "y", "c"))
    seq_size = lax.axis_size(("g", "y", "c"))
    before = lax.ppermute(tokens[0], ("g", "y", "c"), [(i, i + 1) for i in range(seq_size - 1)])

    def spread(weight):
        cut = weight.reshape(shard_rows, 2, groups, members // 2, piece)
        cut = cut.transpose(1, 3, 0, 2, 4).reshape(members, shard_rows, hidden_own)
        return jnp.pad(cut, ((0, 0), (0, 0), (0, hidden_pad - hidden_own)))

    sent = jnp.concatenate([spread(w_gate), spread(w_up)], axis=2)
    core = lax.axis_index("c")
    half_cols = q_cols // 2 + k_cols + 128
    gains = gain_columns(
        [g[None] for g in (gain_attn_in, gain_attn_out, gain_mlp_in, gain_mlp_out)],
        [gain_query[None], gain_key[None]],
    )
    halves = jnp.stack(
        [
            jnp.concatenate([w_query[:, : q_cols // 2], w_key, gains[0]], axis=1),
            jnp.concatenate([w_query[:, q_cols // 2 :], w_value, jnp.zeros_like(gains[0])], axis=1),
        ]
    )
    mine = lax.dynamic_index_in_dim(halves, core, 0, keepdims=False)
    other = lax.dynamic_index_in_dim(halves, 1 - core, 0, keepdims=False)
    mine = in_order(mine, swap(other, "c"), core).reshape(2 * shard_rows, half_cols)
    mine, before, sent = lax.optimization_barrier((mine, before, sent))
    sent = lax.all_to_all(sent, PLANE, split_axis=0, concat_axis=0, tiled=True)
    sent = sent.reshape(members * shard_rows, 2 * hidden_pad)
    mine, sent = lax.optimization_barrier((group_gather(mine), sent))
    mine = plane_weights(mine, *plane_start(mine)).reshape(width, half_cols)
    other = swap(mine, "c")

    down = lax.all_gather(jnp.concatenate([w_down, w_out]), "g", axis=0)
    w_o = down[:, w_down.shape[0] :]
    down = down[:, : w_down.shape[0]].reshape(-1, width)
    down = jnp.pad(down, ((0, hidden_pad - hidden_own), (0, 0)))

    both = lax.all_gather(sent, "g", axis=0)
    both = both.reshape(groups, 2, members // 2 * shard_rows, 2 * hidden_pad)
    gate_up = both.transpose(1, 0, 2, 3).reshape(width, 2 * hidden_pad)

    first_row = seq_place * row_count
    ids_all = doc_ids[0]
    ids_own = lax.dynamic_slice_in_dim(ids_all, first_row, row_count, 0)
    ids_prev = lax.dynamic_slice_in_dim(
        ids_all, jnp.maximum(first_row - row_count, 0), row_count, 0
    )
    ids_prev = jnp.where(seq_place > 0, ids_prev, -1)
    ids_pad = jnp.concatenate([ids_prev, ids_own])
    query_ids, key_ids = ids_own[:, None], ids_pad[None]
    cosine_table, sine_table = rope_tables(first_row - row_count, 2 * row_count, HEAD)
    places = jnp.full((1,), core, jnp.int32)
    layer_in, grad_out = tokens[0], cotangent[0]

    normed, normed_before, query_raw, key_raw, queries, keys, values, d_gains, h_gains = project(
        places, layer_in, before, mine, other, cosine_table, sine_table, shard_rows, q_cols, k_cols
    )
    w_o = plane_weights(*lax.optimization_barrier((w_o, *plane_start(w_o), keys))[:3])
    w_o = in_order(w_o, swap(w_o, "c"), core).transpose(1, 2, 3, 0, 4, 5).reshape(q_cols, width)
    attended, log_total, branch, middle, normed_mlp = attend(
        queries, keys, values, query_ids, key_ids, w_o, layer_in, d_gains, attn_scale
    )

    half = row_count // 2
    from_x, from_y, down = lax.optimization_barrier(
        (swap(normed_mlp, "x"), swap(normed_mlp, "y"), down)
    )
    normed_far = jnp.concatenate([swap(from_x[:half], "y"), swap(from_y[half:], "x")])
    normed_near = jnp.concatenate([from_x, from_y])
    normed_all = [with_core(part) for part in (normed_mlp, normed_near, normed_far)]
    far_result = mlp_forward(normed_all[2], gate_up, down, normed_all[2])
    far_sum = core_sum(two_cores(far_result[3])).astype(BF)
    near_result = mlp_forward(normed_all[1], gate_up, down, far_sum)
    to_x, to_y = sum_near(*lax.optimization_barrier((two_cores(near_result[3]), *send_far(far_sum))))
    own_result = mlp_forward(normed_all[0], gate_up, down, to_x)
    mixed = sum_own(two_cores(own_result[3]), to_x, to_y)
    layer_out = middle + norm_gain(mixed, d_gains[3:4])

    _, pullback = jax.vjp(norm_gain, mixed, d_gains[3:4])
    grad_mixed, mixed_terms = pullback(grad_out.astype(F32))
    grad_mixed = grad_mixed.astype(BF)
    from_x, from_y = swap(grad_mixed, "x"), swap(grad_mixed, "y")
    grad_own = with_core(grad_mixed)
    own_grads = mlp_backward(grad_own, own_result[1], own_result[2], gate_up, down, down)
    from_x, from_y = lax.optimization_barrier((from_x, from_y, own_grads[1]))[:2]
    grad_near = with_core(jnp.concatenate([from_x, from_y]))
    near_terms = down_terms(
        [own_result[0], near_result[0]], [grad_own, grad_near], [], hidden_pad, F32
    )
    grad_far = lax.optimization_barrier(
        (swap(from_x[:half], "y"), swap(from_y[half:], "x"), near_terms)
    )
    grad_far = with_core(jnp.concatenate(grad_far[:2]))
    grad_down_terms = down_terms([far_result[0]], [grad_far], [near_terms], hidden_own, BF)
    grad_down = group_terms(grad_down_terms.reshape(groups, -1, width))
    far_grads = mlp_backward(
        grad_far, far_result[1], far_result[2], gate_up, down, grad_down_terms
    )
    far_sum = core_sum(far_grads[1:]).astype(BF)
    near_grads = mlp_backward(grad_near, near_result[1], near_result[2], gate_up, down, far_sum)
    to_x, to_y = sum_near(*lax.optimization_barrier((tuple(near_grads[1:]), *send_far(far_sum))))
    gate_up_terms = gate_terms(
        normed_all, [g[0] for g in (own_grads, near_grads, far_grads)], groups, to_x
    )
    grad_normed_mlp = sum_own(own_grads[1:], to_x, to_y)
    grad_normed_mlp = after(grad_normed_mlp, gate_up_terms)
    term = gate_up_terms.reshape(groups * members * shard_rows, 2 * hidden_pad)
    gate_up_share = lax.psum_scatter(term, "g", scatter_dimension=0, tiled=True)
    term = gate_up_share.reshape(members, shard_rows, 2 * hidden_pad)
    term = lax.all_to_all(term, PLANE, split_axis=0, concat_axis=0, tiled=True)

    grad_w_gate, grad_w_up = owner_rows(term, groups, piece)

    grad_middle, grad_branch, grad_queries, grad_keys, grad_values, terms = attend_backward(
        grad_normed_mlp, grad_out, middle, branch, d_gains, w_o,
        queries, keys, values, query_ids, key_ids, log_total, attn_scale,
    )
    out_terms = over_rows(attended, grad_branch).astype(BF)
    out_terms = out_terms.reshape(2, groups, 2, 2, w_out.shape[0], width)
    out_terms = plane_terms(fold(out_terms, "c", 3))
    own_weights, other_weights = mine, other
    grad_normed, returned, mine, sent = project_backward(
        places, after(grad_queries, grad_down), grad_keys, grad_values, query_raw, key_raw,
        cosine_table, sine_table, h_gains, normed, normed_before, own_weights, other_weights,
        layer_in, before, d_gains, terms, mixed_terms, shard_rows,
    )
    returned = lax.ppermute(returned, ("g", "y", "c"), [(i + 1, i) for i in range(seq_size - 1)])
    grad_in = grad_tokens(
        places, returned, grad_normed, own_weights, other_weights, layer_in, d_gains, grad_middle
    )
    mine = (mine.astype(F32) + swap(sent, "c").astype(F32)).astype(BF)
    qkv_terms = plane_terms(mine.reshape(2, groups, 2, 2 * shard_rows, half_cols))
    qkv_terms = qkv_terms.reshape(groups, -1, width)
    share = jnp.concatenate([out_terms, qkv_terms], axis=1)
    share = group_terms(after(share, gate_up_share))
    grad_w_out = share[: w_out.shape[0]]
    share = share[w_out.shape[0] :].astype(BF).reshape(2, shard_rows, half_cols)
    mine = lax.dynamic_index_in_dim(share, core, 0, keepdims=False)
    other = lax.dynamic_index_in_dim(share, 1 - core, 0, keepdims=False)
    first, second = in_order(mine, swap(other, "c"), core).astype(F32)
    half = q_cols // 2
    d_terms = first[:, half + k_cols :]
    return (
        layer_out.astype(BF)[None],
        grad_in[None],
        jnp.concatenate([first[:, :half], second[:, :half]], axis=1),
        first[:, half : half + k_cols],
        second[:, half : half + k_cols],
        grad_w_out,
        grad_w_gate,
        grad_w_up,
        grad_down,
        d_terms[:, 0],
        d_terms[:, 1],
        d_terms[:, 2],
        d_terms[:, 3],
        d_terms[:head_rows, 4],
        d_terms[:head_rows, 5],
    )


def solution(mesh):
    batch, seq = mesh.devices.shape
    fine = Mesh(mesh.devices.reshape(batch, seq // 4, 2, 2), ALL)
    rows = ("g", "y", "c")
    return jax.shard_map(
        on_device,
        mesh=fine,
        in_specs=(P("x", rows, None),) * 2
        + (P("x", None),)
        + (P(ALL, None),) * 7
        + (P(ALL),) * 6,
        out_specs=(P("x", rows, None),) * 2 + (P(ALL, None),) * 7 + (P(ALL),) * 6,
        check_vma=False,
    )
```
